32 devices in a mesh: views: 2 (over x), depth: 16 (over z, y, core).
Axes of the slice: x: 2, y: 2, z: 4, core: 2. Of those that a mesh axis runs over, the one named last changes fastest.
Arguments:
- concentration: float32 [8, 1, 512, 1024], P(None, None, 'depth'), may hold values from 0 to 1
- shear_index: int32 [4, 512, 1024], P('views', 'depth'), may hold values from 0 to 1022, as said below
- shear_weight: float32 [4, 512, 1024], P('views', 'depth'), may hold values from 0 to 1
- attenuation: float32 [4, 8], replicated, may hold values from 9.765625e-05 to 0.001953125
- yields: float32 [8], replicated, may hold values from 0.5 to 2
- line_energy: int32 [8], replicated, may hold values from 0 to 2
- measured: float32 [4, 8, 1, 1024], P('views'), may hold values from -4 to 4
Outputs:
- gradient: float32 [8, 1, 512, 1024], P(None, None, 'depth')
- signal: float32 [4, 8, 1, 1024], P('views')
The draws below stay inside these ranges and needn't reach their ends.
Inputs may be any that keep to these rules, and one draw needn't show every extreme that they name: shear_index[v, d, t] is t plus a shift of that view and depth cell, the shift between -128 and 128, clipped to the grid.
All inputs are finite; a program needn't handle non-finite values.
Results may differ from the reference program's by a relative error of at most 0.0001.
Values sent between devices are 32-bit elements; how exact they have to be, the bound alone decides.
No kernel may reach another device: no remote copies, remote signals or barrier semaphores. Data moves between devices by JAX's collectives and lax.ppermute only.
A program may use at most 64 MiB of HBM per device.

```python
import math
import jax
import jax.numpy as jnp
from jax import lax

ELEMENTS = 8
EMISSIONS = 3
ROWS = 1
DSLAB = 32
WIDTH = 1024
VIEWS = 4
NDEPTH = 512
N_DEPTH = 16


def draw_shear_index(key, part):
    key = jax.random.fold_in(key, 11)
    shifts = jax.random.randint(key, (VIEWS, NDEPTH), -(WIDTH // 8), WIDTH // 8 + 1).astype(jnp.int32)
    shifts = shifts.at[0, 0].set(0)
    positions = jnp.arange(WIDTH, dtype=jnp.int32)
    return jnp.clip(positions[None, None, :] + shifts[:, :, None], 0, WIDTH - 2).astype(jnp.int32)


def set_ends(values, stream_key, least, top_value):
    longest = values.shape.index(max(values.shape))
    spots = []
    for shift in (0, 1):
        where = [jax.random.randint(jax.random.fold_in(stream_key, axis), (), 0, length) for axis, length in enumerate(values.shape)]
        where[longest] = (where[longest] + shift) % values.shape[longest]
        spots.append(tuple(where))
    return values.at[spots[0]].set(least).at[spots[1]].set(top_value)


def block_levels(rng, dims, cuts, least, top_value):
    def one(axis_at, parts):
        draws = jax.random.uniform(jax.random.fold_in(jax.random.fold_in(rng, 6), axis_at), (parts,), jnp.float32, least / len(cuts), top_value / len(cuts))
        return jnp.repeat(jnp.exp(draws), dims[axis_at] // parts).reshape((-1,) + (1,) * (len(dims) - axis_at - 1))

    loudness = one(*cuts[0])
    for cut in cuts[1:]:
        loudness = loudness * one(*cut)
    return loudness


def noise(rng, dims, deviation, limit, cuts=(), kind=jnp.bfloat16):
    result = deviation * jax.random.normal(rng, dims, jnp.float32)
    if cuts:
        result = result * block_levels(rng, dims, cuts, -0.22, 0.18)
    return jnp.clip(result, -limit, limit).astype(kind)


def setup_inputs(seed: int = 0) -> dict:
    keys = jax.random.split(jax.random.key(seed), 8)
    return {
        "concentration": jnp.clip(1.0 * jax.random.uniform(keys[0], (ELEMENTS, ROWS, NDEPTH, WIDTH), jnp.float32) ** block_levels(keys[0], (ELEMENTS, ROWS, NDEPTH, WIDTH), ((2, 16),), -0.2, 0.2), 0.0, 1.0),
        "shear_index": draw_shear_index(jax.random.fold_in(keys[7], 71), 0),
        "shear_weight": jnp.clip(1.0 * jax.random.uniform(keys[2], (VIEWS, NDEPTH, WIDTH), jnp.float32) ** block_levels(keys[2], (VIEWS, NDEPTH, WIDTH), ((0, 2), (1, 16)), -0.2, 0.2), 0.0, 1.0),
        "attenuation": jnp.clip(jnp.exp(jax.random.uniform(keys[3], (EMISSIONS + 1, ELEMENTS), jnp.float32, math.log(9.765625145519152e-05), math.log(0.001953125))), 9.765625145519152e-05, 0.001953125),
        "yields": jnp.clip(jnp.exp(jax.random.uniform(keys[4], (ELEMENTS,), jnp.float32, math.log(0.5), math.log(2.0))), 0.5, 2.0),
        "line_energy": set_ends(jax.random.randint(keys[5], (ELEMENTS,), 0, EMISSIONS), jax.random.fold_in(keys[5], 1), 0, EMISSIONS - 1).astype(jnp.int32),
        "measured": noise(keys[6], (VIEWS, ELEMENTS, ROWS, WIDTH), 0.5, 4.0, ((0, 2),), jnp.float32),
    }


def reference(concentration, shear_index, shear_weight, attenuation, yields, line_energy, measured):
    depth_total = DSLAB * N_DEPTH
    highest = lax.Precision.HIGHEST
    selector = (line_energy[:, None] == jnp.arange(EMISSIONS, dtype=jnp.int32)[None, :]).astype(jnp.float32)
    cells = ELEMENTS * ROWS * depth_total * WIDTH
    offsets = (jnp.arange(ELEMENTS * ROWS * depth_total, dtype=jnp.int32) * WIDTH).reshape(ELEMENTS, ROWS, depth_total, 1)

    def one_view(carry, inputs):
        index_view, weight_view, measured_view = inputs
        index_full = jnp.broadcast_to(index_view[None, None], concentration.shape)
        left = jnp.take_along_axis(concentration, index_full, axis=3)
        right = jnp.take_along_axis(concentration, index_full + 1, axis=3)
        field = left * (1.0 - weight_view) + right * weight_view
        absorb = jnp.einsum('ke,erdw->krdw', attenuation, field, precision=highest)
        running = jnp.cumsum(absorb, axis=2)
        incident = jnp.exp(-(running[0] - absorb[0]))
        leaving = jnp.exp(-(running[1:, :, -1:] - running[1:]))
        leaving_line = jnp.einsum('lk,krdw->lrdw', selector, leaving, precision=highest)
        emitted = yields[:, None, None, None] * field * incident[None] * leaving_line / depth_total
        signal_view = jnp.sum(emitted, axis=2)
        misfit = signal_view - measured_view
        weighted = misfit[:, :, None, :] * emitted
        backward = jnp.sum(weighted, axis=0)
        back_run = jnp.cumsum(backward, axis=1)
        suffix = back_run[:, -1:] - back_run
        forward = jnp.einsum('lk,lrdw->krdw', selector, weighted, precision=highest)
        prefix = jnp.cumsum(forward, axis=2) - forward
        direct = misfit[:, :, None, :] * yields[:, None, None, None] * incident[None] * leaving_line
        view_grad = direct - depth_total * (attenuation[0][:, None, None, None] * suffix[None]
                                            + jnp.einsum('ke,krdw->erdw', attenuation[1:], prefix, precision=highest))
        spot = (offsets + index_full).reshape(-1)
        values = jnp.concatenate([(view_grad * (1.0 - weight_view)).reshape(-1), (view_grad * weight_view).reshape(-1)])
        places = jnp.concatenate([spot, spot + 1])
        local = jax.ops.segment_sum(values, places, num_segments=cells).reshape(concentration.shape)
        return carry + local, signal_view

    start = jnp.zeros(concentration.shape, jnp.float32)
    gradient, signal = lax.scan(one_view, start, (shear_index, shear_weight, measured))
    return gradient, signal
```

```python
import functools

import jax
import jax.numpy as jnp
from jax import lax
from jax.experimental import pallas as pl
from jax.experimental.pallas import tpu as pltpu
from jax.sharding import PartitionSpec as P

LANES = 128
SUB = 8
BLOCK = 8
GROUP = 4
F32 = jnp.float32
BF16 = jnp.bfloat16
SMEM = pl.BlockSpec(memory_space=pltpu.SMEM)


def lane_ids():
    return lax.broadcasted_iota(jnp.int32, (SUB, LANES), 1)


def row_ids():
    return lax.broadcasted_iota(jnp.int32, (SUB, LANES), 0)


def column_of(values, rows):
    tile = jnp.zeros((SUB, LANES), F32)
    for e in range(SUB):
        tile = jnp.where(rows == e, values[e], tile)
    return tile


def row_of(values, lanes):
    tile = jnp.zeros((SUB, LANES), F32)
    for e in range(SUB):
        tile = jnp.where((lanes & 7) == e, values[e], tile)
    return tile


def line_masks(line_ref, rows, emissions):
    lines = jnp.zeros(rows.shape, jnp.int32)
    for e in range(SUB):
        lines = jnp.where(rows == e, line_ref[e], lines)
    return [lines == k for k in range(emissions)]


def att_row(att_ref, k):
    return [att_ref[k, e] for e in range(SUB)]


def fill_matrix(mat_ref, first_tile, second_tile, first_incl, second_incl, lanes):
    depth = (lanes & 63) >> 3
    tiles = []
    for d in range(BLOCK):
        one = jnp.where(depth <= d if first_incl else depth < d, first_tile, 0.0)
        two = jnp.where(depth <= d if second_incl else depth < d, second_tile, 0.0)
        tiles.append(one + two)
    tiles.append(first_tile + second_tile)
    tiles.append(jnp.zeros((SUB, LANES), F32))
    whole = jnp.concatenate(tiles, axis=0)
    high = whole.astype(BF16)
    low = (whole - high.astype(F32)).astype(BF16)
    mat_ref[:, 0:LANES] = high
    mat_ref[:, LANES : 2 * LANES] = low


def multiply(mat_ref, values):
    high = values.astype(BF16)
    low = (values - high.astype(F32)).astype(BF16)
    stacked = jnp.concatenate([high, low, high], axis=0)
    return jnp.dot(mat_ref[:, 0 : 3 * BLOCK * SUB], stacked, preferred_element_type=F32)


def chunk_of(width):
    return 256 if width % 256 == 0 else LANES


def forward_kernel(with_state, parts, shift_ref, att_ref, line_ref, yield_ref, me_ref, conc_ref, weight_ref, *refs):
    if with_state:
        u_ref, n_ref = refs[:2]
        state_refs = refs[2 : 2 + parts]
        refs = refs[2 + parts :]
    else:
        u_ref, n_ref = refs[:2]
        refs = refs[2:]
    left_pad, diff_pad, field, mat, carry, field_sum, emit_sum = refs
    views, _, width = weight_ref.shape
    emissions = att_ref.shape[0] - 1
    tiles = width // LANES
    block = pl.program_id(0)
    lanes, rows = lane_ids(), row_ids()

    @pl.when(block == 0)
    def _():
        carry[...] = jnp.zeros_like(carry)
        field_sum[...] = jnp.zeros_like(field_sum)
        emit_sum[...] = jnp.zeros_like(emit_sum)
        masks = line_masks(line_ref, rows, emissions)
        own = jnp.zeros((SUB, LANES), F32)
        for k in range(emissions):
            own = jnp.where(masks[k], row_of(att_row(att_ref, k + 1), lanes), own)
        fill_matrix(mat, row_of(att_row(att_ref, 0), lanes), -own, False, True, lanes)

    by_depth = jnp.swapaxes(conc_ref[...], 0, 1)
    for d in range(BLOCK):
        cells = [by_depth[d, :, j * LANES : (j + 1) * LANES] for j in range(tiles)]
        turned = [pltpu.roll(cell, LANES - 1, 1) for cell in cells]
        after = [jnp.where(lanes < LANES - 1, turned[j], turned[min(j + 1, tiles - 1)]) for j in range(tiles)]
        steps = [after[j] - cells[j] for j in range(tiles)]
        last_cell = jnp.broadcast_to(cells[-1][:, LANES - 2 : LANES - 1], (SUB, LANES))
        last_step = jnp.broadcast_to(steps[-1][:, LANES - 2 : LANES - 1], (SUB, LANES))
        first_cell = jnp.broadcast_to(cells[0][:, 0:1], (SUB, LANES))
        first_step = jnp.broadcast_to(steps[0][:, 0:1], (SUB, LANES))
        cells[-1] = jnp.where(lanes < LANES - 1, cells[-1], last_cell)
        steps[-1] = jnp.where(lanes < LANES - 1, steps[-1], last_step)
        cells = [first_cell] + cells + [last_cell, last_cell]
        steps = [first_step] + steps + [last_step, last_step]
        for j in range(tiles + 3):
            left_pad[d, :, j * LANES : (j + 1) * LANES] = cells[j]
            diff_pad[d, :, j * LANES : (j + 1) * LANES] = steps[j]

    for v in range(views):
        for d in range(BLOCK):
            offset = shift_ref[v, block * BLOCK + d]
            whole = offset // LANES
            rest = offset % LANES
            turn = (LANES - rest) % LANES
            stay = lanes < LANES - rest

            def sheared(ref):
                turned = []
                for j in range(tiles + 1):
                    start = pl.multiple_of((whole + j) * LANES, LANES)
                    turned.append(pltpu.roll(ref[d, :, pl.ds(start, LANES)], turn, 1))
                return [jnp.where(stay, turned[j], turned[j + 1]) for j in range(tiles)]

            left, diff = sheared(left_pad), sheared(diff_pad)
            for j in range(tiles):
                span = slice(j * LANES, (j + 1) * LANES)
                weight = weight_ref[v, d : d + 1, span]
                field[v, d * SUB : (d + 1) * SUB, span] = left[j] + weight * diff[j]

    size = chunk_of(width)
    for v in range(views):
        for c in range(width // size):
            span = slice(c * size, (c + 1) * size)
            value = field[v, :, span]
            product = multiply(mat, value)
            before = carry[v, :, span]
            lines = product[: BLOCK * SUB].reshape(BLOCK, SUB, size) + before[None]
            value = value.reshape(BLOCK, SUB, size)
            through = jnp.exp(-lines)
            emit = value * through
            u_ref[v, :, span] = through.reshape(BLOCK * SUB, size)
            n_ref[v, :, span] = emit.reshape(BLOCK * SUB, size)
            carry[v, :, span] = before + product[BLOCK * SUB : (BLOCK + 1) * SUB]
            field_sum[v, :, span] += jnp.sum(value, axis=0)
            emit_sum[v, :, span] += jnp.sum(emit, axis=0)

    if with_state:

        @pl.when(block == pl.num_programs(0) - 1)
        def _():
            masks = line_masks(line_ref, rows, emissions)
            columns = [column_of(att_row(att_ref, k), rows) for k in range(emissions + 1)]
            scale = column_of([yield_ref[e] for e in range(SUB)], rows) * (1.0 / me_ref[1].astype(F32))
            here = me_ref[0]
            share = width // parts
            for r in range(parts):
                part = lax.rem(here, parts) ^ r
                for j in range(share // LANES):
                    start = pl.multiple_of(part * share + j * LANES, LANES)
                    span = slice(j * LANES, (j + 1) * LANES)
                    totals = jnp.zeros((SUB, LANES), F32)
                    for v in range(views):
                        cells = field_sum[v, :, pl.ds(start, LANES)]
                        line_total = jnp.zeros((SUB, LANES), F32)
                        for k in range(emissions + 1):
                            total = jnp.sum(columns[k] * cells, axis=0, keepdims=True)
                            totals = jnp.where(rows == v * (emissions + 1) + k, total, totals)
                            if k > 0:
                                line_total = jnp.where(masks[k - 1], total, line_total)
                        signal = scale * emit_sum[v, :, pl.ds(start, LANES)] * jnp.exp(-line_total)
                        state_refs[r][(v + 1) * SUB : (v + 2) * SUB, span] = signal
                    state_refs[r][0:SUB, span] = jnp.exp(-totals)


def forward(conc, shifts, weights, attenuation, line_energy, yields, me, parts):
    views, slab, width = weights.shape
    blocks = slab // BLOCK
    rows = BLOCK * SUB
    with_state = parts > 0
    cells = jax.ShapeDtypeStruct((views, slab * SUB, width), F32)
    spec = pl.BlockSpec((views, rows, width), lambda b: (0, b, 0))
    out_shape, out_specs = [cells, cells], [spec, spec]
    if with_state:
        shape = ((views + 1) * SUB, width // parts)
        out_shape += [jax.ShapeDtypeStruct(shape, F32)] * parts
        out_specs += [pl.BlockSpec(shape, lambda b: (0, 0))] * parts
    padded = width + 3 * LANES
    return pl.pallas_call(
        functools.partial(forward_kernel, with_state, parts),
        grid=(blocks,),
        in_specs=[
            SMEM,
            SMEM,
            SMEM,
            SMEM,
            SMEM,
            pl.BlockSpec((SUB, BLOCK, width), lambda b: (0, b, 0)),
            pl.BlockSpec((views, BLOCK, width), lambda b: (0, b, 0)),
        ],
        out_specs=out_specs,
        out_shape=out_shape,
        scratch_shapes=[
            pltpu.VMEM((BLOCK, SUB, padded), F32),
            pltpu.VMEM((BLOCK, SUB, padded), F32),
            pltpu.VMEM((views, rows, width), F32),
            pltpu.VMEM((rows + 2 * SUB, 2 * LANES), BF16),
            pltpu.VMEM((views, SUB, width), F32),
            pltpu.VMEM((views, SUB, width), F32),
            pltpu.VMEM((views, SUB, width), F32),
        ],
        compiler_params=pltpu.CompilerParams(
            dimension_semantics=("arbitrary",), vmem_limit_bytes=24 * 1024 * 1024
        ),
        cost_estimate=pl.CostEstimate(
            flops=views * slab * SUB * width * 40, bytes_accessed=4 * views * slab * SUB * width * 3, transcendentals=0
        ),
        name="forward" if with_state else "forward_other",
    )(shifts, attenuation, line_energy, yields, me, conc, weights)


def put_in_order(scratch, place, refs):
    for r, ref in enumerate(refs):
        scratch[place ^ r] = ref[...]


def rows_of_state(state, v, emissions, masks):
    base = v * (emissions + 1)
    shape = (SUB, state.shape[1])
    incident = jnp.broadcast_to(state[base : base + 1], shape)
    line = jnp.broadcast_to(state[base + 1 : base + 2], shape)
    for k in range(1, emissions):
        line = jnp.where(masks[k], jnp.broadcast_to(state[base + 1 + k : base + 2 + k], shape), line)
    return incident, line


def ordered_factors(scratch, count, v, emissions, masks):
    own = [rows_of_state(scratch[i, 0:SUB, :], v, emissions, masks) for i in range(count)]
    before, behind = [None] * count, [None] * count
    run = jnp.ones_like(own[0][0])
    for i in range(count):
        before[i] = run
        run = run * own[i][0]
    run = jnp.ones_like(own[0][0])
    for i in reversed(range(count)):
        behind[i] = run
        run = run * own[i][1]
    return own, before, behind


def wide_rows(width):
    return lax.broadcasted_iota(jnp.int32, (SUB, width), 0)


def merge_kernel(emissions, views, parts, me_ref, line_ref, *refs):
    ins, out_ref, scratch = refs[:parts], refs[parts], refs[parts + 1]
    width = out_ref.shape[1]
    place = lax.rem(me_ref[0], parts)
    put_in_order(scratch, place, ins)
    masks = line_masks(line_ref, wide_rows(width), emissions)
    product = scratch[0, 0:SUB, :]
    for i in range(1, parts):
        product = product * scratch[i, 0:SUB, :]
    out_ref[0:SUB, :] = product
    for v in range(views):
        _, before, behind = ordered_factors(scratch, parts, v, emissions, masks)
        span = slice((v + 1) * SUB, (v + 2) * SUB)
        total = jnp.zeros((SUB, width), F32)
        for i in range(parts):
            total = total + scratch[i, span, :] * (before[i] * behind[i])
        out_ref[span, :] = total


def merge(states, line_energy, me, emissions, views):
    parts = len(states)
    shape = states[0].shape
    return pl.pallas_call(
        functools.partial(merge_kernel, emissions, views, parts),
        in_specs=[SMEM, SMEM] + [pl.BlockSpec(memory_space=pltpu.VMEM)] * parts,
        out_specs=pl.BlockSpec(memory_space=pltpu.VMEM),
        out_shape=jax.ShapeDtypeStruct(shape, F32),
        scratch_shapes=[pltpu.VMEM((parts,) + shape, F32)],
        name="merge",
    )(me, line_energy, *states)


def misfit_kernel(views, parts, groups, me_ref, att_ref, line_ref, yield_ref, measured_ref, *refs):
    emissions = att_ref.shape[0] - 1
    near, refs = refs[:parts], refs[parts:]
    far, refs = refs[:groups], refs[groups:]
    outs, refs = refs[:parts], refs[parts:]
    others, refs = refs[: len(refs) - 2], refs[len(refs) - 2 :]
    near_scratch, far_scratch = refs
    width = near[0].shape[1]
    here = me_ref[0]
    place = lax.rem(here, parts)
    group = here // parts
    put_in_order(near_scratch, place, near)
    put_in_order(far_scratch, group, far)
    rows = wide_rows(width)
    masks = line_masks(line_ref, rows, emissions)

    def column(values):
        tile = jnp.zeros((SUB, width), F32)
        for e in range(SUB):
            tile = jnp.where(rows == e, values[e], tile)
        return tile

    columns = [column(att_row(att_ref, k)) for k in range(emissions + 1)]
    scale = column([yield_ref[e] for e in range(SUB)])
    cells = me_ref[1].astype(F32)
    start = pl.multiple_of(place * width, LANES)
    for v in range(views):
        span = slice((v + 1) * SUB, (v + 2) * SUB)
        _, before, behind = ordered_factors(far_scratch, groups, v, emissions, masks)
        parts_of_signal = [far_scratch[i, span, :] * (before[i] * behind[i]) for i in range(groups)]
        signal = parts_of_signal[0]
        for i in range(1, groups):
            signal = signal + parts_of_signal[i]
        misfit = signal - measured_ref[v * SUB : (v + 1) * SUB, pl.ds(start, width)]
        zero = jnp.zeros_like(signal)
        later, earlier, around = zero, zero, zero
        for i in range(groups):
            later = later + jnp.where(i > group, parts_of_signal[i], 0.0)
            earlier = earlier + jnp.where(i < group, parts_of_signal[i], 0.0)
            around = around + jnp.where(i == group, before[i] * behind[i], 0.0)
        own, near_before, near_behind = ordered_factors(near_scratch, parts, v, emissions, masks)
        factors = [around * near_before[i] * near_behind[i] for i in range(parts)]
        pieces = [near_scratch[i, span, :] * factors[i] for i in range(parts)]
        befores, laters = [], []
        run = earlier
        for i in range(parts):
            befores.append(run)
            run = run + pieces[i]
        run = later
        for i in reversed(range(parts)):
            run = run + pieces[i]
            laters.append(run)
        laters = laters[::-1]
        for r in range(parts):
            gain, back = zero, zero
            for i in range(parts):
                chosen = (place ^ r) == i
                gain = jnp.where(chosen, factors[i] * own[i][1], gain)
                total = columns[0] * jnp.sum(misfit * laters[i], axis=0, keepdims=True)
                weighted = misfit * befores[i]
                for k in range(emissions):
                    part = jnp.sum(jnp.where(masks[k], weighted, 0.0), axis=0, keepdims=True)
                    total = total + columns[k + 1] * part
                back = jnp.where(chosen, total, back)
            gain = misfit * scale * gain
            back = cells * back
            for ref in outs[r : r + 1] + others[r : r + 1]:
                ref[v * SUB : (v + 1) * SUB, :] = gain
                ref[(views + v) * SUB : (views + v + 1) * SUB, :] = back
            outs[r][(2 * views + v) * SUB : (2 * views + v + 1) * SUB, :] = signal


def misfits(near, far, measured, attenuation, line_energy, yields, me, both):
    parts, groups = len(near), len(far)
    shape = near[0].shape
    views = shape[0] // SUB - 1
    vmem = pl.BlockSpec(memory_space=pltpu.VMEM)
    out_shape = [jax.ShapeDtypeStruct((3 * views * SUB, shape[1]), F32)] * parts
    if both:
        out_shape = out_shape + [jax.ShapeDtypeStruct((2 * views * SUB, shape[1]), F32)] * parts
    outs = pl.pallas_call(
        functools.partial(misfit_kernel, views, parts, groups),
        in_specs=[SMEM] * 4 + [vmem] * (1 + parts + groups),
        out_specs=[vmem] * len(out_shape),
        out_shape=out_shape,
        scratch_shapes=[pltpu.VMEM((parts,) + shape, F32), pltpu.VMEM((groups,) + shape, F32)],
        name="misfit",
    )(me, attenuation, line_energy, yields, measured, *near, *far)
    return outs[:parts], outs[parts:]


def backward_kernel(sides, parts, att_ref, line_ref, me_ref, *refs):
    shift_refs, refs = refs[:sides], refs[sides:]
    weight_refs, refs = refs[:sides], refs[sides:]
    u_refs, refs = refs[:sides], refs[sides:]
    n_refs, refs = refs[:sides], refs[sides:]
    result_refs, refs = refs[: sides * parts], refs[sides * parts :]
    grad_ref, signal_ref, mat, gain, carry, scaled, left_pad, diff_pad = refs
    views, _, width = weight_refs[0].shape
    emissions = att_ref.shape[0] - 1
    tiles = width // LANES
    block = pl.program_id(0)
    lanes, rows = lane_ids(), row_ids()
    share = width // parts
    margin = 2 * LANES

    @pl.when(block == 0)
    def _():
        masks = line_masks(line_ref, lanes & 7, emissions)
        own = jnp.zeros((SUB, LANES), F32)
        for k in range(emissions):
            own = jnp.where(masks[k], column_of(att_row(att_ref, k + 1), rows), own)
        fill_matrix(mat, -column_of(att_row(att_ref, 0), rows), own, True, False, lanes)
        for r in range(parts):
            start = pl.multiple_of((lax.rem(me_ref[0], parts) ^ r) * share, LANES)
            for s in range(sides):
                source = result_refs[s * parts + r]
                for v in range(views):
                    gain[s * views + v, :, pl.ds(start, share)] = source[v * SUB : (v + 1) * SUB, :]
                    carry[s * views + v, :, pl.ds(start, share)] = source[(views + v) * SUB : (views + v + 1) * SUB, :]
            signal_ref[:, pl.ds(start, share)] = result_refs[r][2 * views * SUB : 3 * views * SUB, :]
        for ref in (left_pad, diff_pad):
            ref[:, :, :, 0:margin] = jnp.zeros(ref.shape[:3] + (margin,), F32)
            ref[:, :, :, margin + width + LANES :] = jnp.zeros(ref.shape[:3] + (margin,), F32)

    size = chunk_of(width)
    for s in range(sides):
        for v in range(views):
            at = s * views + v
            for c in range(width // size):
                span = slice(c * size, (c + 1) * size)
                factor = gain[at, :, span][None]
                weighted = n_refs[s][v, :, span].reshape(BLOCK, SUB, size) * factor
                direct = u_refs[s][v, :, span].reshape(BLOCK, SUB, size) * factor
                product = multiply(mat, weighted.reshape(BLOCK * SUB, size))
                before = carry[at, :, span]
                lines = product[: BLOCK * SUB].reshape(BLOCK, SUB, size) + before[None]
                scaled[at, :, span] = (direct - lines).reshape(BLOCK * SUB, size)
                carry[at, :, span] = before + product[BLOCK * SUB : (BLOCK + 1) * SUB]
            for d in range(BLOCK):
                rest = shift_refs[s][v, block * BLOCK + d] % LANES
                stay = lanes >= rest
                plain = [scaled[at, d * SUB : (d + 1) * SUB, j * LANES : (j + 1) * LANES] for j in range(tiles)]
                moved = [
                    plain[j] * weight_refs[s][v, d : d + 1, j * LANES : (j + 1) * LANES] for j in range(tiles)
                ]
                for ref, values in ((left_pad, plain), (diff_pad, moved)):
                    turned = [jnp.zeros((SUB, LANES), F32)]
                    turned += [pltpu.roll(value, rest, 1) for value in values]
                    turned += [jnp.zeros((SUB, LANES), F32)]
                    for j in range(tiles + 1):
                        span = slice(margin + j * LANES, margin + (j + 1) * LANES)
                        ref[at, d, :, span] = jnp.where(stay, turned[j + 1], turned[j])

    for d in range(BLOCK):

        def gathered(ref):
            sums = [None] * (tiles + 2)
            for s in range(sides):
                for v in range(views):
                    whole = shift_refs[s][v, block * BLOCK + d] // LANES
                    for j in range(tiles + 2):
                        start = pl.multiple_of((2 + j - whole) * LANES, LANES)
                        value = ref[s * views + v, d, :, pl.ds(start, LANES)]
                        sums[j] = value if sums[j] is None else sums[j] + value
            return sums

        left, diff = gathered(left_pad), gathered(diff_pad)
        left = [left[j] - diff[j] for j in range(tiles + 2)]

        def folded(sums):
            low = jnp.sum(sums[0], axis=1, keepdims=True)
            beyond = sums[tiles + 1] + jnp.where(lanes == LANES - 1, sums[tiles], 0.0)
            high = jnp.sum(beyond, axis=1, keepdims=True)
            core = sums[1 : tiles + 1]
            core[0] = core[0] + jnp.where(lanes == 0, low, 0.0)
            core[-1] = jnp.where(lanes == LANES - 1, 0.0, core[-1] + jnp.where(lanes == LANES - 2, high, 0.0))
            return core

        left, diff = folded(left), folded(diff)
        turned = [jnp.zeros((SUB, LANES), F32)] + [pltpu.roll(value, 1, 1) for value in diff]
        for j in range(tiles):
            value = left[j] + jnp.where(lanes == 0, turned[j], turned[j + 1])
            scaled[0, d * SUB : (d + 1) * SUB, j * LANES : (j + 1) * LANES] = value
    by_depth = scaled[0].reshape(BLOCK, SUB, width)
    grad_ref[...] = jnp.swapaxes(by_depth, 0, 1)


def backward(sides, attenuation, line_energy, me):
    views, slab, width = sides[0][1].shape
    count = len(sides)
    parts = len(sides[0][4])
    rows = BLOCK * SUB
    blocks = slab // BLOCK
    vmem = pl.BlockSpec(memory_space=pltpu.VMEM)
    cells = pl.BlockSpec((views, rows, width), lambda b: (0, b, 0))
    padded = width + 5 * LANES
    total = count * views
    return pl.pallas_call(
        functools.partial(backward_kernel, count, parts),
        grid=(blocks,),
        in_specs=[SMEM] * (3 + count)
        + [pl.BlockSpec((views, BLOCK, width), lambda b: (0, b, 0))] * count
        + [cells] * (2 * count)
        + [vmem] * (count * parts),
        out_specs=[
            pl.BlockSpec((SUB, BLOCK, width), lambda b: (0, b, 0)),
            pl.BlockSpec((views * SUB, width), lambda b: (0, 0)),
        ],
        out_shape=[
            jax.ShapeDtypeStruct((SUB, slab, width), F32),
            jax.ShapeDtypeStruct((views * SUB, width), F32),
        ],
        scratch_shapes=[
            pltpu.VMEM((rows + 2 * SUB, 2 * LANES), BF16),
            pltpu.VMEM((total, SUB, width), F32),
            pltpu.VMEM((total, SUB, width), F32),
            pltpu.VMEM((total, rows, width), F32),
            pltpu.VMEM((total, BLOCK, SUB, padded), F32),
            pltpu.VMEM((total, BLOCK, SUB, padded), F32),
        ],
        compiler_params=pltpu.CompilerParams(
            dimension_semantics=("arbitrary",), vmem_limit_bytes=40 * 1024 * 1024
        ),
        name="backward",
    )(
        attenuation,
        line_energy,
        me,
        *[side[0] for side in sides],
        *[side[1] for side in sides],
        *[side[2] for side in sides],
        *[side[3] for side in sides],
        *[part for side in sides for part in side[4]],
    )


def body(concentration, shear_index, shear_weight, attenuation, yields, line_energy, measured):
    elements, _, slab, width = concentration.shape
    views = shear_weight.shape[0]
    emissions = attenuation.shape[0] - 1
    depth = lax.axis_size("depth")
    view_groups = lax.axis_size("views")
    both = view_groups == 2
    groups = depth // GROUP
    here = lax.axis_index("depth")
    me = jnp.stack([here, jnp.int32(slab * depth)]).astype(jnp.int32)
    conc = concentration.reshape(elements, slab, width)
    shifts = shear_index[:, :, width // 2] - (width // 2 - LANES)
    target = measured.reshape(views * elements, width)

    def to_other(value):
        return lax.ppermute(value, "views", [(0, 1), (1, 0)])

    def along_depth(value, step):
        return lax.ppermute(value, "depth", [(s, s ^ step) for s in range(depth)])

    def across(value, step):
        pairs = [(v * depth + s, (1 - v) * depth + (s ^ step)) for v in range(2) for s in range(depth)]
        return lax.ppermute(value, ("views", "depth"), pairs)

    if both:
        other_weight, other_shifts = to_other(shear_weight), to_other(shifts)
    u, n, *states = forward(conc, shifts, shear_weight, attenuation, line_energy, yields, me, GROUP)
    near = [states[0]] + [along_depth(states[r], r) for r in range(1, GROUP)]
    group_state = merge(near, line_energy, me, emissions, views)
    far = [group_state] + [along_depth(group_state, r * GROUP) for r in range(1, groups)]
    if both:
        other_u, other_n = forward(conc, other_shifts, other_weight, attenuation, line_energy, yields, me, 0)
    own, others = misfits(near, far, target, attenuation, line_energy, yields, me, both)
    sides = [(shifts, shear_weight, u, n, [own[0]] + [along_depth(own[r], r) for r in range(1, GROUP)])]
    if both:
        results = [across(others[r], r) for r in range(GROUP)]
        sides.append((other_shifts, other_weight, other_u, other_n, results))
    gradient, signal = backward(sides, attenuation, line_energy, me)
    if not both:
        gradient = lax.psum(gradient, "views")
    return gradient.reshape(concentration.shape), signal.reshape(measured.shape)


def solution(mesh):
    return jax.shard_map(
        body,
        mesh=mesh,
        in_specs=(
            P(None, None, "depth", None),
            P("views", "depth", None),
            P("views", "depth", None),
            P(),
            P(),
            P(),
            P("views", None, None, None),
        ),
        out_specs=(P(None, None, "depth", None), P("views", None, None, None)),
        check_vma=False,
    )
```

```python
import functools

import jax
import jax.numpy as jnp
from jax import lax
from jax.experimental import pallas as pl
from jax.experimental.pallas import tpu as pltpu
from jax.sharding import PartitionSpec as P

LANES = 128
SUB = 8
BLOCK = 8
F32 = jnp.float32
BF16 = jnp.bfloat16
HBM = pl.BlockSpec(memory_space=pltpu.HBM)
VMEM = pl.BlockSpec(memory_space=pltpu.VMEM)


def lane_ids():
    return lax.broadcasted_iota(jnp.int32, (SUB, LANES), 1)


def row_ids():
    return lax.broadcasted_iota(jnp.int32, (SUB, LANES), 0)


def column_of(values, rows):
    tile = jnp.zeros((SUB, LANES), F32)
    for e in range(SUB):
        tile = jnp.where(rows == e, values[e], tile)
    return tile


def row_of(values, lanes):
    tile = jnp.zeros((SUB, LANES), F32)
    for e in range(SUB):
        tile = jnp.where((lanes & 7) == e, values[e], tile)
    return tile


def line_masks(line_ref, rows, emissions):
    lines = jnp.zeros(rows.shape, jnp.int32)
    for e in range(SUB):
        lines = jnp.where(rows == e, line_ref[e], lines)
    return [lines == k for k in range(emissions)]


def att_row(att_ref, k):
    return [att_ref[k, e] for e in range(SUB)]


def fill_matrix(mat_ref, first_tile, second_tile, first_incl, second_incl, lanes):
    depth = (lanes & 63) >> 3
    tiles = []
    for d in range(BLOCK):
        one = jnp.where(depth <= d if first_incl else depth < d, first_tile, 0.0)
        two = jnp.where(depth <= d if second_incl else depth < d, second_tile, 0.0)
        tiles.append(one + two)
    tiles.append(first_tile + second_tile)
    tiles.append(jnp.zeros((SUB, LANES), F32))
    whole = jnp.concatenate(tiles, axis=0)
    high = whole.astype(BF16)
    low = (whole - high.astype(F32)).astype(BF16)
    mat_ref[:, 0:LANES] = high
    mat_ref[:, LANES : 2 * LANES] = low


def multiply(mat_ref, values):
    high = values.astype(BF16)
    low = (values - high.astype(F32)).astype(BF16)
    stacked = jnp.concatenate([high, low, high], axis=0)
    return jnp.dot(mat_ref[:, 0 : 3 * BLOCK * SUB], stacked, preferred_element_type=F32)


def chunk_of(width):
    return 256 if width % 256 == 0 else LANES


def copies_in(pairs, sems):
    return [pltpu.make_async_copy(source, target, sems.at[i]) for i, (source, target) in enumerate(pairs)]


def shift_column(index_ref, width):
    return index_ref.at[:, :, pl.ds(width // 2, LANES)]


def forward_kernel(with_state, cells, att_hbm, line_hbm, yield_hbm, index_hbm, conc_ref, weight_ref, *refs):
    u_ref, n_ref = refs[:2]
    state_ref = refs[2] if with_state else None
    refs = refs[3:] if with_state else refs[2:]
    left_pad, diff_pad, field, mat, carry, field_sum, emit_sum, att_ref, line_ref, yield_ref, index_ref, sems = refs
    views, _, width = weight_ref.shape
    emissions = att_ref.shape[0] - 1
    tiles = width // LANES
    block = pl.program_id(0)
    lanes, rows = lane_ids(), row_ids()
    copies = copies_in(
        (
            (att_hbm, att_ref),
            (line_hbm, line_ref),
            (yield_hbm, yield_ref),
            (shift_column(index_hbm, width), index_ref),
        ),
        sems,
    )

    @pl.when(block == 0)
    def _():
        for copy in copies:
            copy.start()
        carry[...] = jnp.zeros_like(carry)
        field_sum[...] = jnp.zeros_like(field_sum)
        emit_sum[...] = jnp.zeros_like(emit_sum)

    by_depth = jnp.swapaxes(conc_ref[...], 0, 1)
    for d in range(BLOCK):
        pieces = [by_depth[d, :, j * LANES : (j + 1) * LANES] for j in range(tiles)]
        turned = [pltpu.roll(piece, LANES - 1, 1) for piece in pieces]
        after = [jnp.where(lanes < LANES - 1, turned[j], turned[min(j + 1, tiles - 1)]) for j in range(tiles)]
        steps = [after[j] - pieces[j] for j in range(tiles)]
        last_cell = jnp.broadcast_to(pieces[-1][:, LANES - 2 : LANES - 1], (SUB, LANES))
        last_step = jnp.broadcast_to(steps[-1][:, LANES - 2 : LANES - 1], (SUB, LANES))
        first_cell = jnp.broadcast_to(pieces[0][:, 0:1], (SUB, LANES))
        first_step = jnp.broadcast_to(steps[0][:, 0:1], (SUB, LANES))
        pieces[-1] = jnp.where(lanes < LANES - 1, pieces[-1], last_cell)
        steps[-1] = jnp.where(lanes < LANES - 1, steps[-1], last_step)
        pieces = [first_cell] + pieces + [last_cell, last_cell]
        steps = [first_step] + steps + [last_step, last_step]
        for j in range(tiles + 3):
            left_pad[d, :, j * LANES : (j + 1) * LANES] = pieces[j]
            diff_pad[d, :, j * LANES : (j + 1) * LANES] = steps[j]

    @pl.when(block == 0)
    def _():
        for copy in copies:
            copy.wait()
        masks = line_masks(line_ref, rows, emissions)
        own = jnp.zeros((SUB, LANES), F32)
        for k in range(emissions):
            own = jnp.where(masks[k], row_of(att_row(att_ref, k + 1), lanes), own)
        fill_matrix(mat, row_of(att_row(att_ref, 0), lanes), -own, False, True, lanes)

    for v in range(views):
        for d in range(BLOCK):
            offset = index_ref[v, block * BLOCK + d, 0] - (width // 2 - LANES)
            whole = offset >> 7
            rest = offset & (LANES - 1)
            turn = (LANES - rest) % LANES
            stay = lanes < LANES - rest

            def sheared(ref):
                turned = []
                for j in range(tiles + 1):
                    start = pl.multiple_of((whole + j) * LANES, LANES)
                    turned.append(pltpu.roll(ref[d, :, pl.ds(start, LANES)], turn, 1))
                return [jnp.where(stay, turned[j], turned[j + 1]) for j in range(tiles)]

            left, diff = sheared(left_pad), sheared(diff_pad)
            for j in range(tiles):
                span = slice(j * LANES, (j + 1) * LANES)
                weight = weight_ref[v, d : d + 1, span]
                field[v, d * SUB : (d + 1) * SUB, span] = left[j] + weight * diff[j]

    size = chunk_of(width)
    for v in range(views):
        for c in range(width // size):
            span = slice(c * size, (c + 1) * size)
            value = field[v, :, span]
            product = multiply(mat, value)
            before = carry[v, :, span]
            lines = product[: BLOCK * SUB].reshape(BLOCK, SUB, size) + before[None]
            value = value.reshape(BLOCK, SUB, size)
            through = jnp.exp(-lines)
            emit = value * through
            u_ref[v, :, span] = through.reshape(BLOCK * SUB, size)
            n_ref[v, :, span] = emit.reshape(BLOCK * SUB, size)
            carry[v, :, span] = before + product[BLOCK * SUB : (BLOCK + 1) * SUB]
            field_sum[v, :, span] += jnp.sum(value, axis=0)
            emit_sum[v, :, span] += jnp.sum(emit, axis=0)

    if with_state:

        @pl.when(block == pl.num_programs(0) - 1)
        def _():
            masks = line_masks(line_ref, rows, emissions)
            columns = [column_of(att_row(att_ref, k), rows) for k in range(emissions + 1)]
            scale = column_of([yield_ref[e] for e in range(SUB)], rows) * (1.0 / cells)
            for v in range(views):
                for j in range(tiles):
                    span = slice(j * LANES, (j + 1) * LANES)
                    values = field_sum[v, :, span]
                    totals = jnp.zeros((SUB, LANES), F32)
                    line_total = jnp.zeros((SUB, LANES), F32)
                    for k in range(emissions + 1):
                        total = jnp.sum(columns[k] * values, axis=0, keepdims=True)
                        totals = jnp.where(rows == k, total, totals)
                        if k > 0:
                            line_total = jnp.where(masks[k - 1], total, line_total)
                    state_ref[v * tiles + j, 0:SUB, :] = jnp.exp(-totals)
                    signal = scale * emit_sum[v, :, span] * jnp.exp(-line_total)
                    state_ref[v * tiles + j, SUB : 2 * SUB, :] = signal


def forward(conc, index, weights, attenuation, line_energy, yields, cells, with_state):
    views, slab, width = weights.shape
    blocks = slab // BLOCK
    rows = BLOCK * SUB
    values = jax.ShapeDtypeStruct((views, slab * SUB, width), F32)
    spec = pl.BlockSpec((views, rows, width), lambda b: (0, b, 0))
    out_shape, out_specs = [values, values], [spec, spec]
    if with_state:
        shape = (views * width // LANES, 2 * SUB, LANES)
        out_shape.append(jax.ShapeDtypeStruct(shape, F32))
        out_specs.append(pl.BlockSpec(shape, lambda b: (0, 0, 0)))
    padded = width + 3 * LANES
    return pl.pallas_call(
        functools.partial(forward_kernel, with_state, cells),
        grid=(blocks,),
        in_specs=[
            HBM,
            HBM,
            HBM,
            HBM,
            pl.BlockSpec((SUB, BLOCK, width), lambda b: (0, b, 0)),
            pl.BlockSpec((views, BLOCK, width), lambda b: (0, b, 0)),
        ],
        out_specs=out_specs,
        out_shape=out_shape,
        scratch_shapes=[
            pltpu.VMEM((BLOCK, SUB, padded), F32),
            pltpu.VMEM((BLOCK, SUB, padded), F32),
            pltpu.VMEM((views, rows, width), F32),
            pltpu.VMEM((rows + 2 * SUB, 2 * LANES), BF16),
            pltpu.VMEM((views, SUB, width), F32),
            pltpu.VMEM((views, SUB, width), F32),
            pltpu.VMEM((views, SUB, width), F32),
            pltpu.SMEM(attenuation.shape, F32),
            pltpu.SMEM(line_energy.shape, jnp.int32),
            pltpu.SMEM(yields.shape, F32),
            pltpu.SMEM((views, slab, LANES), jnp.int32),
            pltpu.SemaphoreType.DMA((4,)),
        ],
        compiler_params=pltpu.CompilerParams(
            dimension_semantics=("arbitrary",), vmem_limit_bytes=16 * 1024 * 1024
        ),
        cost_estimate=pl.CostEstimate(
            flops=views * slab * SUB * width * 40, bytes_accessed=4 * views * slab * SUB * width * 3, transcendentals=0
        ),
        name="forward" if with_state else "forward_other",
    )(attenuation, line_energy, yields, index, conc, weights)


def line_rows(tile, masks):
    result = jnp.broadcast_to(tile[1:2], tile.shape)
    for k in range(1, len(masks)):
        result = jnp.where(masks[k], jnp.broadcast_to(tile[k + 1 : k + 2], tile.shape), result)
    return result


def ordered_factors(factors, rows):
    count = len(factors)
    before, behind = [None] * count, [None] * count
    run = jnp.ones_like(factors[0])
    for i in range(count):
        before[i] = run
        run = run * factors[i]
    run = jnp.ones_like(factors[0])
    for i in reversed(range(count)):
        behind[i] = run
        run = run * factors[i]
    return [jnp.broadcast_to(before[i][0:1], run.shape) * behind[i] for i in range(count)]


def merge_kernel(emissions, line_hbm, near_ref, out_ref, line_ref, sems):
    copies = copies_in(((line_hbm, line_ref),), sems)
    copies[0].start()
    copies[0].wait()
    rows = row_ids()
    masks = line_masks(line_ref, rows, emissions)
    count = near_ref.shape[0]
    factors = [near_ref[i, 0:SUB, :] for i in range(count)]
    around = ordered_factors(factors, rows)
    total = factors[0]
    signal = jnp.zeros((SUB, LANES), F32)
    for i in range(count):
        if i > 0:
            total = total * factors[i]
        signal = signal + near_ref[i, SUB : 2 * SUB, :] * line_rows(around[i], masks)
    out_ref[0:SUB, :] = total
    out_ref[SUB : 2 * SUB, :] = signal


def merge(near, line_energy, emissions):
    return pl.pallas_call(
        functools.partial(merge_kernel, emissions),
        in_specs=[HBM, VMEM],
        out_specs=VMEM,
        out_shape=jax.ShapeDtypeStruct(near.shape[1:], F32),
        scratch_shapes=[pltpu.SMEM(line_energy.shape, jnp.int32), pltpu.SemaphoreType.DMA((1,))],
        name="merge",
    )(line_energy, near)


def misfit_kernel(emissions, view_groups, line_hbm, measured_hbm, near_ref, *refs):
    far, refs = refs[:-5], refs[-5:]
    out_ref, line_ref, measured_ref, far_ref, sems = refs
    count = near_ref.shape[0]
    width = measured_hbm.shape[3]
    here = lax.axis_index("depth")
    place = lax.rem(here, count)
    tiles = width // LANES
    view = place // tiles
    start = pl.multiple_of(lax.rem(place, tiles) * LANES, LANES)
    copies = copies_in(
        ((line_hbm, line_ref), (measured_hbm.at[view, :, :, pl.ds(start, LANES)], measured_ref)), sems
    )
    for copy in copies:
        copy.start()
    for copy in copies:
        copy.wait()
    rows = row_ids()
    masks = line_masks(line_ref, rows, emissions)
    zero = jnp.zeros((SUB, LANES), F32)
    factors = [near_ref[i, 0:SUB, :] for i in range(count)]
    around = ordered_factors(factors, rows)
    before_all, behind_all = None, None
    far_parts, far_order = [], []
    if far:
        group = here // count
        for r, ref in enumerate(far):
            far_ref[group ^ r] = ref[...]
        groups = len(far)
        far_factors = [far_ref[g, 0:SUB, :] for g in range(groups)]
        far_around = ordered_factors(far_factors, rows)
        outside = zero
        for g in range(groups):
            outside = outside + jnp.where(g == group, far_around[g], 0.0)
            far_parts.append(far_ref[g, SUB : 2 * SUB, :] * line_rows(far_around[g], masks))
            far_order.append(g)
        around = [value * outside for value in around]
    parts = [near_ref[i, SUB : 2 * SUB, :] * line_rows(around[i], masks) for i in range(count)]
    signal = zero
    for i in range(count):
        signal = signal + parts[i]
    for g in far_order:
        signal = signal + jnp.where(g == group, 0.0, far_parts[g])
    misfit = signal - measured_ref[...].reshape(SUB, LANES)

    def by_energy(value):
        value = misfit * value
        return [jnp.sum(jnp.where(mask, value, 0.0), axis=0, keepdims=True) for mask in masks]

    def plus(one, two):
        return [a + b for a, b in zip(one, two)]

    earlier = [jnp.zeros((1, LANES), F32)] * emissions
    later = [jnp.zeros((1, LANES), F32)] * emissions
    for g in far_order:
        sums = by_energy(far_parts[g])
        earlier = plus(earlier, [jnp.where(g < group, value, 0.0) for value in sums])
        later = plus(later, [jnp.where(g > group, value, 0.0) for value in sums])
    sums = [by_energy(part) for part in parts]
    earliers = []
    for i in range(count):
        earliers.append(earlier)
        earlier = plus(earlier, sums[i])
    laters = [None] * count
    for i in reversed(range(count)):
        later = plus(later, sums[i])
        total = later[0]
        for value in later[1:]:
            total = total + value
        laters[i] = total
    mine = lax.axis_index("views")
    for i in range(count):
        tile = around[i] * factors[i]
        tile = jnp.where(rows == 0, laters[i], tile)
        for k in range(emissions):
            tile = jnp.where(rows == emissions + 1 + k, earliers[i][k], tile)
        for x in range(view_groups):
            to_own = (x == mine) if view_groups > 1 else True
            out_ref[x * count + i, 0:SUB, :] = jnp.where(to_own, signal, misfit)
            out_ref[x * count + i, SUB : 2 * SUB, :] = tile


def misfits(near, far, measured, line_energy, emissions, view_groups):
    shape = (view_groups * near.shape[0],) + near.shape[1:]
    return pl.pallas_call(
        functools.partial(misfit_kernel, emissions, view_groups),
        in_specs=[HBM, HBM] + [VMEM] * (1 + len(far)),
        out_specs=VMEM,
        out_shape=jax.ShapeDtypeStruct(shape, F32),
        scratch_shapes=[
            pltpu.SMEM(line_energy.shape, jnp.int32),
            pltpu.VMEM((SUB, 1, LANES), F32),
            pltpu.VMEM((max(1, len(far)),) + near.shape[1:], F32),
            pltpu.SemaphoreType.DMA((2,)),
        ],
        compiler_params=pltpu.CompilerParams(vmem_limit_bytes=4 * 1024 * 1024),
        name="misfit",
    )(line_energy, measured, near, *far)


def backward_kernel(sides, cells, att_hbm, line_hbm, yield_hbm, measured_ref, *refs):
    index_hbms, refs = refs[:sides], refs[sides:]
    weight_refs, refs = refs[:sides], refs[sides:]
    u_refs, refs = refs[:sides], refs[sides:]
    n_refs, refs = refs[:sides], refs[sides:]
    result_ref, grad_ref, signal_ref, mat, gain, carry, scaled, left_pad, diff_pad = refs[:9]
    att_ref, line_ref, yield_ref = refs[9:12]
    index_refs = refs[12 : 12 + sides]
    sems = refs[-1]
    views, _, width = weight_refs[0].shape
    emissions = att_ref.shape[0] - 1
    tiles = width // LANES
    block = pl.program_id(0)
    lanes, rows = lane_ids(), row_ids()
    margin = 2 * LANES
    copies = copies_in(
        ((att_hbm, att_ref), (line_hbm, line_ref), (yield_hbm, yield_ref))
        + tuple((shift_column(index_hbms[s], width), index_refs[s]) for s in range(sides)),
        sems,
    )

    def offset(s, v, d):
        return index_refs[s][v, block * BLOCK + d, 0] - (width // 2 - LANES)

    @pl.when(block == 0)
    def _():
        for copy in copies:
            copy.start()
        for ref in (left_pad, diff_pad):
            ref[:, :, :, 0:margin] = jnp.zeros(ref.shape[:3] + (margin,), F32)
            ref[:, :, :, margin + width + LANES :] = jnp.zeros(ref.shape[:3] + (margin,), F32)
        for copy in copies:
            copy.wait()
        masks = line_masks(line_ref, lanes & 7, emissions)
        columns = [column_of(att_row(att_ref, k), rows) for k in range(emissions + 1)]
        own = jnp.zeros((SUB, LANES), F32)
        for k in range(emissions):
            own = jnp.where(masks[k], columns[k + 1], own)
        fill_matrix(mat, -columns[0], own, True, False, lanes)
        masks = line_masks(line_ref, rows, emissions)
        scale = column_of([yield_ref[e] for e in range(SUB)], rows)
        columns = [column * cells for column in columns]
        mine = lax.axis_index("views")
        for s in range(sides):
            first = (mine ^ s) * (views * tiles) if sides > 1 else 0
            for v in range(views):
                for j in range(tiles):
                    span = slice(j * LANES, (j + 1) * LANES)
                    misfit = result_ref[first + v * tiles + j, 0:SUB, :]
                    tile = result_ref[first + v * tiles + j, SUB : 2 * SUB, :]
                    if s == 0:
                        signal_ref[v, :, :, span] = misfit.reshape(SUB, 1, LANES)
                        misfit = misfit - measured_ref[v, :, :, span].reshape(SUB, LANES)
                    gain[s * views + v, :, span] = misfit * scale * line_rows(tile, masks)
                    back = columns[0] * jnp.broadcast_to(tile[0:1], tile.shape)
                    for k in range(emissions):
                        row = emissions + 1 + k
                        back = back + columns[k + 1] * jnp.broadcast_to(tile[row : row + 1], tile.shape)
                    carry[s * views + v, :, span] = back

    size = chunk_of(width)
    for s in range(sides):
        for v in range(views):
            at = s * views + v
            for c in range(width // size):
                span = slice(c * size, (c + 1) * size)
                factor = gain[at, :, span][None]
                weighted = n_refs[s][v, :, span].reshape(BLOCK, SUB, size) * factor
                direct = u_refs[s][v, :, span].reshape(BLOCK, SUB, size) * factor
                product = multiply(mat, weighted.reshape(BLOCK * SUB, size))
                before = carry[at, :, span]
                lines = product[: BLOCK * SUB].reshape(BLOCK, SUB, size) + before[None]
                scaled[at, :, span] = (direct - lines).reshape(BLOCK * SUB, size)
                carry[at, :, span] = before + product[BLOCK * SUB : (BLOCK + 1) * SUB]
            for d in range(BLOCK):
                rest = offset(s, v, d) & (LANES - 1)
                stay = lanes >= rest
                plain = [scaled[at, d * SUB : (d + 1) * SUB, j * LANES : (j + 1) * LANES] for j in range(tiles)]
                moved = [
                    plain[j] * weight_refs[s][v, d : d + 1, j * LANES : (j + 1) * LANES] for j in range(tiles)
                ]
                for ref, values in ((left_pad, plain), (diff_pad, moved)):
                    turned = [jnp.zeros((SUB, LANES), F32)]
                    turned += [pltpu.roll(value, rest, 1) for value in values]
                    turned += [jnp.zeros((SUB, LANES), F32)]
                    for j in range(tiles + 1):
                        span = slice(margin + j * LANES, margin + (j + 1) * LANES)
                        ref[at, d, :, span] = jnp.where(stay, turned[j + 1], turned[j])

    for d in range(BLOCK):

        def gathered(ref):
            sums = [None] * (tiles + 2)
            for s in range(sides):
                for v in range(views):
                    whole = offset(s, v, d) >> 7
                    for j in range(tiles + 2):
                        start = pl.multiple_of((2 + j - whole) * LANES, LANES)
                        value = ref[s * views + v, d, :, pl.ds(start, LANES)]
                        sums[j] = value if sums[j] is None else sums[j] + value
            return sums

        left, diff = gathered(left_pad), gathered(diff_pad)
        left = [left[j] - diff[j] for j in range(tiles + 2)]

        def folded(sums):
            low = jnp.sum(sums[0], axis=1, keepdims=True)
            beyond = sums[tiles + 1] + jnp.where(lanes == LANES - 1, sums[tiles], 0.0)
            high = jnp.sum(beyond, axis=1, keepdims=True)
            core = sums[1 : tiles + 1]
            core[0] = core[0] + jnp.where(lanes == 0, low, 0.0)
            core[-1] = jnp.where(lanes == LANES - 1, 0.0, core[-1] + jnp.where(lanes == LANES - 2, high, 0.0))
            return core

        left, diff = folded(left), folded(diff)
        turned = [jnp.zeros((SUB, LANES), F32)] + [pltpu.roll(value, 1, 1) for value in diff]
        for j in range(tiles):
            value = left[j] + jnp.where(lanes == 0, turned[j], turned[j + 1])
            scaled[0, d * SUB : (d + 1) * SUB, j * LANES : (j + 1) * LANES] = value
    by_depth = scaled[0].reshape(BLOCK, SUB, width)
    grad_ref[...] = jnp.swapaxes(by_depth, 0, 1)


def backward(sides, result, measured, attenuation, line_energy, yields, cells):
    views, slab, width = sides[0][1].shape
    count = len(sides)
    rows = BLOCK * SUB
    blocks = slab // BLOCK
    spec = pl.BlockSpec((views, rows, width), lambda b: (0, b, 0))
    padded = width + 5 * LANES
    total = count * views
    return pl.pallas_call(
        functools.partial(backward_kernel, count, cells),
        grid=(blocks,),
        in_specs=[HBM] * 3
        + [VMEM]
        + [HBM] * count
        + [pl.BlockSpec((views, BLOCK, width), lambda b: (0, b, 0))] * count
        + [spec] * (2 * count)
        + [VMEM],
        out_specs=[
            pl.BlockSpec((SUB, BLOCK, width), lambda b: (0, b, 0)),
            pl.BlockSpec(measured.shape, lambda b: (0, 0, 0, 0)),
        ],
        out_shape=[
            jax.ShapeDtypeStruct((SUB, slab, width), F32),
            jax.ShapeDtypeStruct(measured.shape, F32),
        ],
        scratch_shapes=[
            pltpu.VMEM((rows + 2 * SUB, 2 * LANES), BF16),
            pltpu.VMEM((total, SUB, width), F32),
            pltpu.VMEM((total, SUB, width), F32),
            pltpu.VMEM((total, rows, width), F32),
            pltpu.VMEM((total, BLOCK, SUB, padded), F32),
            pltpu.VMEM((total, BLOCK, SUB, padded), F32),
            pltpu.SMEM(attenuation.shape, F32),
            pltpu.SMEM(line_energy.shape, jnp.int32),
            pltpu.SMEM(yields.shape, F32),
        ]
        + [pltpu.SMEM((views, slab, LANES), jnp.int32)] * count
        + [pltpu.SemaphoreType.DMA((3 + count,))],
        compiler_params=pltpu.CompilerParams(
            dimension_semantics=("arbitrary",), vmem_limit_bytes=24 * 1024 * 1024
        ),
        name="backward",
    )(
        attenuation,
        line_energy,
        yields,
        measured,
        *[side[0] for side in sides],
        *[side[1] for side in sides],
        *[side[2] for side in sides],
        *[side[3] for side in sides],
        result,
    )


def body(concentration, shear_index, shear_weight, attenuation, yields, line_energy, measured):
    elements, _, slab, width = concentration.shape
    views = shear_weight.shape[0]
    emissions = attenuation.shape[0] - 1
    depth = lax.axis_size("depth")
    both = lax.axis_size("views") == 2
    near_count = views * width // LANES
    groups = depth // near_count
    cells = float(slab * depth)
    conc = concentration.reshape(elements, slab, width)

    def to_other(value):
        return lax.ppermute(value, "views", [(0, 1), (1, 0)])

    def exchange(value, axis):
        members = None
        if axis == "depth" and groups > 1:
            members = [[g * near_count + i for i in range(near_count)] for g in range(groups)]
        return lax.all_to_all(value, axis, 0, 0, axis_index_groups=members, tiled=True)

    if both:
        other_weight, other_index = to_other(shear_weight), to_other(shear_index)
    u, n, state = forward(conc, shear_index, shear_weight, attenuation, line_energy, yields, cells, True)
    near = exchange(state, "depth")
    far = []
    if groups > 1:
        merged = merge(near, line_energy, emissions)
        for r in range(groups):
            pairs = [(s, s ^ (r * near_count)) for s in range(depth)]
            far.append(lax.ppermute(merged, "depth", pairs) if r else merged)
    if both:
        other = forward(conc, other_index, other_weight, attenuation, line_energy, yields, cells, False)
    result = misfits(near, far, measured, line_energy, emissions, 2 if both else 1)
    result = exchange(result, ("views", "depth") if both else "depth")
    sides = [(shear_index, shear_weight, u, n)]
    if both:
        sides.append((other_index, other_weight, *other))
    gradient, signal = backward(sides, result, measured, attenuation, line_energy, yields, cells)
    if not both:
        gradient = lax.psum(gradient, "views")
    return gradient.reshape(concentration.shape), signal


def solution(mesh):
    return jax.shard_map(
        body,
        mesh=mesh,
        in_specs=(
            P(None, None, "depth", None),
            P("views", "depth", None),
            P("views", "depth", None),
            P(),
            P(),
            P(),
            P("views", None, None, None),
        ),
        out_specs=(P(None, None, "depth", None), P("views", None, None, None)),
        check_vma=False,
    )
```

```python
import functools

import jax
import jax.numpy as jnp
from jax import lax
from jax.experimental import pallas as pl
from jax.experimental.pallas import tpu as pltpu
from jax.sharding import PartitionSpec as P

LANES = 128
SUB = 8
BLOCK = 8
F32 = jnp.float32
BF16 = jnp.bfloat16
HBM = pl.BlockSpec(memory_space=pltpu.HBM)
VMEM = pl.BlockSpec(memory_space=pltpu.VMEM)
VMEM_BYTES = 60 * 1024 * 1024
NEAR = 4


def lane_ids():
    return lax.broadcasted_iota(jnp.int32, (SUB, LANES), 1)


def row_ids():
    return lax.broadcasted_iota(jnp.int32, (SUB, LANES), 0)


def column_of(values, rows):
    tile = jnp.zeros((SUB, LANES), F32)
    for e in range(SUB):
        tile = jnp.where(rows == e, values[e], tile)
    return tile


def row_of(values, lanes):
    tile = jnp.zeros((SUB, LANES), F32)
    for e in range(SUB):
        tile = jnp.where((lanes & 7) == e, values[e], tile)
    return tile


def line_masks(line_ref, rows, emissions):
    lines = jnp.zeros(rows.shape, jnp.int32)
    for e in range(SUB):
        lines = jnp.where(rows == e, line_ref[e], lines)
    return [lines == k for k in range(emissions)]


def att_row(att_ref, k):
    return [att_ref[k, e] for e in range(SUB)]


def fill_matrix(mat_ref, first_tile, second_tile, first_incl, second_incl, lanes):
    depth = (lanes & 63) >> 3
    tiles = []
    for d in range(BLOCK):
        one = jnp.where(depth <= d if first_incl else depth < d, first_tile, 0.0)
        two = jnp.where(depth <= d if second_incl else depth < d, second_tile, 0.0)
        tiles.append(one + two)
    tiles.append(first_tile + second_tile)
    tiles.append(jnp.zeros((SUB, LANES), F32))
    whole = jnp.concatenate(tiles, axis=0)
    high = whole.astype(BF16)
    low = (whole - high.astype(F32)).astype(BF16)
    mat_ref[:, 0:LANES] = high
    mat_ref[:, LANES : 2 * LANES] = low


def multiply(mat_ref, values):
    high = values.astype(BF16)
    low = (values - high.astype(F32)).astype(BF16)
    stacked = jnp.concatenate([high, low, high], axis=0)
    return jnp.dot(mat_ref[:, 0 : 3 * BLOCK * SUB], stacked, preferred_element_type=F32)


def chunk_of(width):
    return 256 if width % 256 == 0 else LANES


def copies_in(pairs, sems):
    return [pltpu.make_async_copy(source, target, sems.at[i]) for i, (source, target) in enumerate(pairs)]


def shift_column(index_ref):
    start = 0 if index_ref.shape[2] == LANES else index_ref.shape[2] // 2
    return index_ref.at[:, :, pl.ds(start, LANES)]


def forward_kernel(with_state, cells, att_hbm, line_hbm, yield_hbm, index_hbm, conc_ref, weight_ref, *refs):
    u_ref, n_ref = refs[:2]
    state_ref, column_hbm = refs[2:4] if with_state else (None, None)
    refs = refs[4:] if with_state else refs[2:]
    left_pad, diff_pad, field, mat, carry, field_sum, emit_sum, att_ref, line_ref, yield_ref, index_ref, sems = refs
    views, _, width = weight_ref.shape
    emissions = att_ref.shape[0] - 1
    tiles = width // LANES
    block = pl.program_id(0)
    lanes, rows = lane_ids(), row_ids()
    copies = copies_in(
        (
            (att_hbm, att_ref),
            (line_hbm, line_ref),
            (yield_hbm, yield_ref),
            (shift_column(index_hbm), index_ref),
        )
        + (((shift_column(index_hbm), column_hbm),) if with_state else ()),
        sems,
    )

    @pl.when(block == 0)
    def _():
        for copy in copies:
            copy.start()
        carry[...] = jnp.zeros_like(carry)
        field_sum[...] = jnp.zeros_like(field_sum)
        emit_sum[...] = jnp.zeros_like(emit_sum)

    by_depth = jnp.swapaxes(conc_ref[...], 0, 1)
    for d in range(BLOCK):
        pieces = [by_depth[d, :, j * LANES : (j + 1) * LANES] for j in range(tiles)]
        turned = [pltpu.roll(piece, LANES - 1, 1) for piece in pieces]
        after = [jnp.where(lanes < LANES - 1, turned[j], turned[min(j + 1, tiles - 1)]) for j in range(tiles)]
        steps = [after[j] - pieces[j] for j in range(tiles)]
        last_cell = jnp.broadcast_to(pieces[-1][:, LANES - 2 : LANES - 1], (SUB, LANES))
        last_step = jnp.broadcast_to(steps[-1][:, LANES - 2 : LANES - 1], (SUB, LANES))
        first_cell = jnp.broadcast_to(pieces[0][:, 0:1], (SUB, LANES))
        first_step = jnp.broadcast_to(steps[0][:, 0:1], (SUB, LANES))
        pieces[-1] = jnp.where(lanes < LANES - 1, pieces[-1], last_cell)
        steps[-1] = jnp.where(lanes < LANES - 1, steps[-1], last_step)
        pieces = [first_cell] + pieces + [last_cell, last_cell]
        steps = [first_step] + steps + [last_step, last_step]
        for j in range(tiles + 3):
            left_pad[d, :, j * LANES : (j + 1) * LANES] = pieces[j]
            diff_pad[d, :, j * LANES : (j + 1) * LANES] = steps[j]

    @pl.when(block == 0)
    def _():
        for copy in copies:
            copy.wait()
        masks = line_masks(line_ref, rows, emissions)
        own = jnp.zeros((SUB, LANES), F32)
        for k in range(emissions):
            own = jnp.where(masks[k], row_of(att_row(att_ref, k + 1), lanes), own)
        fill_matrix(mat, row_of(att_row(att_ref, 0), lanes), -own, False, True, lanes)

    for v in range(views):
        for d in range(BLOCK):
            offset = index_ref[v, block * BLOCK + d, 0] - (width // 2 - LANES)
            whole = offset >> 7
            rest = offset & (LANES - 1)
            turn = (LANES - rest) % LANES
            stay = lanes < LANES - rest

            def sheared(ref):
                turned = []
                for j in range(tiles + 1):
                    start = pl.multiple_of((whole + j) * LANES, LANES)
                    turned.append(pltpu.roll(ref[d, :, pl.ds(start, LANES)], turn, 1))
                return [jnp.where(stay, turned[j], turned[j + 1]) for j in range(tiles)]

            left, diff = sheared(left_pad), sheared(diff_pad)
            for j in range(tiles):
                span = slice(j * LANES, (j + 1) * LANES)
                weight = weight_ref[v, d : d + 1, span]
                field[v, d * SUB : (d + 1) * SUB, span] = left[j] + weight * diff[j]

    size = chunk_of(width)
    for v in range(views):
        for c in range(width // size):
            span = slice(c * size, (c + 1) * size)
            value = field[v, :, span]
            product = multiply(mat, value)
            before = carry[v, :, span]
            lines = product[: BLOCK * SUB].reshape(BLOCK, SUB, size) + before[None]
            value = value.reshape(BLOCK, SUB, size)
            through = jnp.exp(-lines)
            emit = value * through
            u_ref[v, :, span] = through.reshape(BLOCK * SUB, size)
            n_ref[v, :, span] = emit.reshape(BLOCK * SUB, size)
            carry[v, :, span] = before + product[BLOCK * SUB : (BLOCK + 1) * SUB]
            field_sum[v, :, span] += jnp.sum(value, axis=0)
            emit_sum[v, :, span] += jnp.sum(emit, axis=0)

    if with_state:

        @pl.when(block == pl.num_programs(0) - 1)
        def _():
            masks = line_masks(line_ref, rows, emissions)
            columns = [column_of(att_row(att_ref, k), rows) for k in range(emissions + 1)]
            scale = column_of([yield_ref[e] for e in range(SUB)], rows) * (1.0 / cells)
            share = state_ref.shape[2]
            for j in range(tiles):
                span = slice(j * LANES, (j + 1) * LANES)
                part, at = j * LANES // share, j * LANES % share
                into = slice(at, at + LANES)
                totals = jnp.zeros((SUB, LANES), F32)
                for v in range(views):
                    values = field_sum[v, :, span]
                    line_total = jnp.zeros((SUB, LANES), F32)
                    for k in range(emissions + 1):
                        total = jnp.sum(columns[k] * values, axis=0, keepdims=True)
                        totals = jnp.where(rows == v * (emissions + 1) + k, total, totals)
                        if k > 0:
                            line_total = jnp.where(masks[k - 1], total, line_total)
                    signal = scale * emit_sum[v, :, span] * jnp.exp(-line_total)
                    state_ref[part, (v + 1) * SUB : (v + 2) * SUB, into] = signal
                state_ref[part, 0:SUB, into] = jnp.exp(-totals)


def forward(conc, index, weights, attenuation, line_energy, yields, cells, with_state):
    views, slab, width = weights.shape
    blocks = slab // BLOCK
    rows = BLOCK * SUB
    values = jax.ShapeDtypeStruct((views, slab * SUB, width), F32)
    spec = pl.BlockSpec((views, rows, width), lambda b: (0, b, 0))
    out_shape, out_specs = [values, values], [spec, spec]
    if with_state:
        shape = (NEAR, (views + 1) * SUB, width // NEAR)
        out_shape += [jax.ShapeDtypeStruct(shape, F32), jax.ShapeDtypeStruct((views, slab, LANES), jnp.int32)]
        out_specs += [pl.BlockSpec(shape, lambda b: (0, 0, 0)), HBM]
    padded = width + 3 * LANES
    return pl.pallas_call(
        functools.partial(forward_kernel, with_state, cells),
        grid=(blocks,),
        in_specs=[
            HBM,
            HBM,
            HBM,
            HBM,
            pl.BlockSpec((SUB, BLOCK, width), lambda b: (0, b, 0)),
            pl.BlockSpec((views, BLOCK, width), lambda b: (0, b, 0)),
        ],
        out_specs=out_specs,
        out_shape=out_shape,
        scratch_shapes=[
            pltpu.VMEM((BLOCK, SUB, padded), F32),
            pltpu.VMEM((BLOCK, SUB, padded), F32),
            pltpu.VMEM((views, rows, width), F32),
            pltpu.VMEM((rows + 2 * SUB, 2 * LANES), BF16),
            pltpu.VMEM((views, SUB, width), F32),
            pltpu.VMEM((views, SUB, width), F32),
            pltpu.VMEM((views, SUB, width), F32),
            pltpu.SMEM(attenuation.shape, F32),
            pltpu.SMEM(line_energy.shape, jnp.int32),
            pltpu.SMEM(yields.shape, F32),
            pltpu.SMEM((views, slab, LANES), jnp.int32),
            pltpu.SemaphoreType.DMA((5,)),
        ],
        compiler_params=pltpu.CompilerParams(
            dimension_semantics=("arbitrary",), vmem_limit_bytes=VMEM_BYTES
        ),
        cost_estimate=pl.CostEstimate(
            flops=views * slab * SUB * width * 40, bytes_accessed=4 * views * slab * SUB * width * 3, transcendentals=0
        ),
        name="forward" if with_state else "forward_other",
    )(attenuation, line_energy, yields, index, conc, weights)


def line_rows(tile, base, masks):
    result = jnp.broadcast_to(tile[base + 1 : base + 2], tile.shape)
    for k in range(1, len(masks)):
        row = base + 1 + k
        result = jnp.where(masks[k], jnp.broadcast_to(tile[row : row + 1], tile.shape), result)
    return result


def ordered_factors(factors, rows, step):
    count = len(factors)
    before, behind = [None] * count, [None] * count
    run = jnp.ones_like(factors[0])
    for i in range(count):
        before[i] = run
        run = run * factors[i]
    run = jnp.ones_like(factors[0])
    for i in reversed(range(count)):
        behind[i] = run
        run = run * factors[i]

    def incident(tile):
        result = jnp.broadcast_to(tile[0:1], tile.shape)
        for base in range(step, SUB, step):
            result = jnp.where(rows >= base, jnp.broadcast_to(tile[base : base + 1], tile.shape), result)
        return result

    return [incident(before[i]) * behind[i] for i in range(count)]


def merge_kernel(emissions, line_hbm, near_ref, out_ref, line_ref, sems):
    copies = copies_in(((line_hbm, line_ref),), sems)
    copies[0].start()
    copies[0].wait()
    count, depth, width = near_ref.shape
    rows = lax.broadcasted_iota(jnp.int32, (SUB, width), 0)
    masks = line_masks(line_ref, rows, emissions)
    factors = [near_ref[i, 0:SUB, :] for i in range(count)]
    around = ordered_factors(factors, rows, emissions + 1)
    total = factors[0]
    for i in range(1, count):
        total = total * factors[i]
    results = [total]
    for v in range(depth // SUB - 1):
        signal = jnp.zeros((SUB, width), F32)
        for i in range(count):
            part = near_ref[i, (v + 1) * SUB : (v + 2) * SUB, :]
            signal = signal + part * line_rows(around[i], v * (emissions + 1), masks)
        results.append(signal)
    for g in range(out_ref.shape[0]):
        for i, result in enumerate(results):
            out_ref[g, i * SUB : (i + 1) * SUB, :] = result


def merge(near, line_energy, emissions, groups):
    return pl.pallas_call(
        functools.partial(merge_kernel, emissions),
        in_specs=[HBM, VMEM],
        out_specs=VMEM,
        out_shape=jax.ShapeDtypeStruct((groups,) + near.shape[1:], F32),
        scratch_shapes=[pltpu.SMEM(line_energy.shape, jnp.int32), pltpu.SemaphoreType.DMA((1,))],
        compiler_params=pltpu.CompilerParams(vmem_limit_bytes=VMEM_BYTES),
        name="merge",
    )(line_energy, near)


def misfit_kernel(emissions, view_groups, line_hbm, measured_hbm, near_ref, far_ref, out_ref, line_ref, measured_ref, sems):
    count, depth, width = near_ref.shape
    groups = far_ref.shape[0]
    views = depth // SUB - 1
    group = lax.axis_index("far")
    start = pl.multiple_of(lax.axis_index("near") * width, LANES)
    copies = copies_in(
        ((line_hbm, line_ref), (measured_hbm.at[:, :, :, pl.ds(start, width)], measured_ref)), sems
    )
    for copy in copies:
        copy.start()
    for copy in copies:
        copy.wait()
    rows = lax.broadcasted_iota(jnp.int32, (SUB, width), 0)
    masks = line_masks(line_ref, rows, emissions)
    zero = jnp.zeros((SUB, width), F32)
    far_around = ordered_factors([far_ref[g, 0:SUB, :] for g in range(groups)], rows, emissions + 1)
    outside = zero
    for g in range(groups):
        outside = outside + jnp.where(g == group, far_around[g], 0.0)
    factors = [near_ref[i, 0:SUB, :] for i in range(count)]
    around = [value * outside for value in ordered_factors(factors, rows, emissions + 1)]
    mine = lax.axis_index("views")
    for v in range(views):
        base = v * (emissions + 1)
        span = slice((v + 1) * SUB, (v + 2) * SUB)
        far_parts = [far_ref[g, span, :] * line_rows(far_around[g], base, masks) for g in range(groups)]
        parts = [near_ref[i, span, :] * line_rows(around[i], base, masks) for i in range(count)]
        signal = zero
        for g in range(groups):
            signal = signal + far_parts[g]
        misfit = signal - measured_ref[v].reshape(SUB, width)

        def by_energy(value):
            value = misfit * value
            return [jnp.sum(jnp.where(mask, value, 0.0), axis=0, keepdims=True) for mask in masks]

        def plus(one, two):
            return [a + b for a, b in zip(one, two)]

        lower, upper = zero, zero
        for g in range(groups):
            lower = lower + jnp.where(g < group, far_parts[g], 0.0)
            upper = upper + jnp.where(g > group, far_parts[g], 0.0)
        earlier, later = by_energy(lower), by_energy(upper)
        sums = [by_energy(part) for part in parts]
        earliers, laters = [], [None] * count
        for i in range(count):
            earliers.append(earlier)
            earlier = plus(earlier, sums[i])
        for i in reversed(range(count)):
            later = plus(later, sums[i])
            total = later[0]
            for value in later[1:]:
                total = total + value
            laters[i] = total
        for i in range(count):
            tile = around[i] * factors[i]
            tile = jnp.where(rows == base, laters[i], tile)
            for k in range(emissions):
                tile = jnp.where(rows == SUB // 2 - base + k, earliers[i][k], tile)
            for x in range(view_groups):
                to_own = (x == mine) if view_groups > 1 else True
                at = 2 * v * SUB
                out_ref[x * count + i, at : at + SUB, :] = jnp.where(to_own, signal, misfit)
                out_ref[x * count + i, at + SUB : at + 2 * SUB, :] = tile


def misfits(near, far, measured, line_energy, emissions, view_groups):
    views = near.shape[1] // SUB - 1
    shape = (view_groups * near.shape[0], 2 * views * SUB, near.shape[2])
    return pl.pallas_call(
        functools.partial(misfit_kernel, emissions, view_groups),
        in_specs=[HBM, HBM, VMEM, VMEM],
        out_specs=VMEM,
        out_shape=jax.ShapeDtypeStruct(shape, F32),
        scratch_shapes=[
            pltpu.SMEM(line_energy.shape, jnp.int32),
            pltpu.VMEM(measured.shape[:3] + near.shape[2:], F32),
            pltpu.SemaphoreType.DMA((2,)),
        ],
        compiler_params=pltpu.CompilerParams(vmem_limit_bytes=VMEM_BYTES),
        name="misfit",
    )(line_energy, measured, near, far)


def backward_kernel(sides, cells, att_hbm, line_hbm, yield_hbm, measured_ref, *refs):
    index_hbms, refs = refs[:sides], refs[sides:]
    weight_refs, refs = refs[:sides], refs[sides:]
    u_refs, refs = refs[:sides], refs[sides:]
    n_refs, refs = refs[:sides], refs[sides:]
    result_ref, grad_ref, signal_ref, mat, gain, carry, scaled, left_pad, diff_pad = refs[:9]
    att_ref, line_ref, yield_ref = refs[9:12]
    index_refs = refs[12 : 12 + sides]
    sems = refs[-1]
    views, _, width = weight_refs[0].shape
    emissions = att_ref.shape[0] - 1
    tiles = width // LANES
    block = pl.program_id(0)
    lanes, rows = lane_ids(), row_ids()
    margin = 2 * LANES
    copies = copies_in(
        ((att_hbm, att_ref), (line_hbm, line_ref), (yield_hbm, yield_ref))
        + tuple((shift_column(index_hbms[s]), index_refs[s]) for s in range(sides)),
        sems,
    )

    def offset(s, v, d):
        return index_refs[s][v, block * BLOCK + d, 0] - (width // 2 - LANES)

    @pl.when(block == 0)
    def _():
        for copy in copies:
            copy.start()
        for ref in (left_pad, diff_pad):
            ref[:, :, :, 0:margin] = jnp.zeros(ref.shape[:3] + (margin,), F32)
            ref[:, :, :, margin + width + LANES :] = jnp.zeros(ref.shape[:3] + (margin,), F32)
        for copy in copies:
            copy.wait()
        masks = line_masks(line_ref, lanes & 7, emissions)
        columns = [column_of(att_row(att_ref, k), rows) for k in range(emissions + 1)]
        own = jnp.zeros((SUB, LANES), F32)
        for k in range(emissions):
            own = jnp.where(masks[k], columns[k + 1], own)
        fill_matrix(mat, -columns[0], own, True, False, lanes)
        masks = line_masks(line_ref, rows, emissions)
        scale = column_of([yield_ref[e] for e in range(SUB)], rows)
        columns = [column * cells for column in columns]
        mine = lax.axis_index("views")
        share = result_ref.shape[2]
        for s in range(sides):
            first = (mine ^ s) * NEAR if sides > 1 else 0
            for v in range(views):
                base = v * (emissions + 1)
                for j in range(tiles):
                    span = slice(j * LANES, (j + 1) * LANES)
                    part, at = j * LANES // share, j * LANES % share
                    misfit = result_ref[first + part, 2 * v * SUB : (2 * v + 1) * SUB, at : at + LANES]
                    tile = result_ref[first + part, (2 * v + 1) * SUB : (2 * v + 2) * SUB, at : at + LANES]
                    if s == 0:
                        signal_ref[v, :, :, span] = misfit.reshape(SUB, 1, LANES)
                        misfit = misfit - measured_ref[v, :, :, span].reshape(SUB, LANES)
                    gain[s * views + v, :, span] = misfit * scale * line_rows(tile, base, masks)
                    back = columns[0] * jnp.broadcast_to(tile[base : base + 1], tile.shape)
                    for k in range(emissions):
                        row = SUB // 2 - base + k
                        back = back + columns[k + 1] * jnp.broadcast_to(tile[row : row + 1], tile.shape)
                    carry[s * views + v, :, span] = back

    size = chunk_of(width)
    for s in range(sides):
        for v in range(views):
            at = s * views + v
            for c in range(width // size):
                span = slice(c * size, (c + 1) * size)
                factor = gain[at, :, span][None]
                weighted = n_refs[s][v, :, span].reshape(BLOCK, SUB, size) * factor
                direct = u_refs[s][v, :, span].reshape(BLOCK, SUB, size) * factor
                product = multiply(mat, weighted.reshape(BLOCK * SUB, size))
                before = carry[at, :, span]
                lines = product[: BLOCK * SUB].reshape(BLOCK, SUB, size) + before[None]
                scaled[at, :, span] = (direct - lines).reshape(BLOCK * SUB, size)
                carry[at, :, span] = before + product[BLOCK * SUB : (BLOCK + 1) * SUB]
            for d in range(BLOCK):
                rest = offset(s, v, d) & (LANES - 1)
                stay = lanes >= rest
                plain = [scaled[at, d * SUB : (d + 1) * SUB, j * LANES : (j + 1) * LANES] for j in range(tiles)]
                moved = [
                    plain[j] * weight_refs[s][v, d : d + 1, j * LANES : (j + 1) * LANES] for j in range(tiles)
                ]
                for ref, values in ((left_pad, plain), (diff_pad, moved)):
                    turned = [jnp.zeros((SUB, LANES), F32)]
                    turned += [pltpu.roll(value, rest, 1) for value in values]
                    turned += [jnp.zeros((SUB, LANES), F32)]
                    for j in range(tiles + 1):
                        span = slice(margin + j * LANES, margin + (j + 1) * LANES)
                        ref[at, d, :, span] = jnp.where(stay, turned[j + 1], turned[j])

    for d in range(BLOCK):

        def gathered(ref):
            sums = [None] * (tiles + 2)
            for s in range(sides):
                for v in range(views):
                    whole = offset(s, v, d) >> 7
                    for j in range(tiles + 2):
                        start = pl.multiple_of((2 + j - whole) * LANES, LANES)
                        value = ref[s * views + v, d, :, pl.ds(start, LANES)]
                        sums[j] = value if sums[j] is None else sums[j] + value
            return sums

        left, diff = gathered(left_pad), gathered(diff_pad)
        left = [left[j] - diff[j] for j in range(tiles + 2)]

        def folded(sums):
            low = jnp.sum(sums[0], axis=1, keepdims=True)
            beyond = sums[tiles + 1] + jnp.where(lanes == LANES - 1, sums[tiles], 0.0)
            high = jnp.sum(beyond, axis=1, keepdims=True)
            core = sums[1 : tiles + 1]
            core[0] = core[0] + jnp.where(lanes == 0, low, 0.0)
            core[-1] = jnp.where(lanes == LANES - 1, 0.0, core[-1] + jnp.where(lanes == LANES - 2, high, 0.0))
            return core

        left, diff = folded(left), folded(diff)
        turned = [jnp.zeros((SUB, LANES), F32)] + [pltpu.roll(value, 1, 1) for value in diff]
        for j in range(tiles):
            value = left[j] + jnp.where(lanes == 0, turned[j], turned[j + 1])
            scaled[0, d * SUB : (d + 1) * SUB, j * LANES : (j + 1) * LANES] = value
    by_depth = scaled[0].reshape(BLOCK, SUB, width)
    grad_ref[...] = jnp.swapaxes(by_depth, 0, 1)


def backward(sides, result, measured, attenuation, line_energy, yields, cells):
    views, slab, width = sides[0][1].shape
    count = len(sides)
    rows = BLOCK * SUB
    blocks = slab // BLOCK
    spec = pl.BlockSpec((views, rows, width), lambda b: (0, b, 0))
    padded = width + 5 * LANES
    total = count * views
    return pl.pallas_call(
        functools.partial(backward_kernel, count, cells),
        grid=(blocks,),
        in_specs=[HBM] * 3
        + [VMEM]
        + [HBM] * count
        + [pl.BlockSpec((views, BLOCK, width), lambda b: (0, b, 0))] * count
        + [spec] * (2 * count)
        + [VMEM],
        out_specs=[
            pl.BlockSpec((SUB, BLOCK, width), lambda b: (0, b, 0)),
            pl.BlockSpec(measured.shape, lambda b: (0, 0, 0, 0)),
        ],
        out_shape=[
            jax.ShapeDtypeStruct((SUB, slab, width), F32),
            jax.ShapeDtypeStruct(measured.shape, F32),
        ],
        scratch_shapes=[
            pltpu.VMEM((rows + 2 * SUB, 2 * LANES), BF16),
            pltpu.VMEM((total, SUB, width), F32),
            pltpu.VMEM((total, SUB, width), F32),
            pltpu.VMEM((total, rows, width), F32),
            pltpu.VMEM((total, BLOCK, SUB, padded), F32),
            pltpu.VMEM((total, BLOCK, SUB, padded), F32),
            pltpu.SMEM(attenuation.shape, F32),
            pltpu.SMEM(line_energy.shape, jnp.int32),
            pltpu.SMEM(yields.shape, F32),
        ]
        + [pltpu.SMEM((views, slab, LANES), jnp.int32)] * count
        + [pltpu.SemaphoreType.DMA((3 + count,))],
        compiler_params=pltpu.CompilerParams(
            dimension_semantics=("arbitrary",), vmem_limit_bytes=VMEM_BYTES
        ),
        name="backward",
    )(
        attenuation,
        line_energy,
        yields,
        measured,
        *[side[0] for side in sides],
        *[side[1] for side in sides],
        *[side[2] for side in sides],
        *[side[3] for side in sides],
        result,
    )


def body(concentration, shear_index, shear_weight, attenuation, yields, line_energy, measured):
    elements, _, slab, width = concentration.shape
    emissions = attenuation.shape[0] - 1
    groups = lax.axis_size("far")
    both = lax.axis_size("views") == 2
    cells = float(slab * groups * NEAR)
    conc = concentration.reshape(elements, slab, width)

    def to_other(value):
        return lax.ppermute(value, "views", [(0, 1), (1, 0)])

    def exchange(value, axes):
        return lax.all_to_all(value, axes, 0, 0, tiled=True)

    if both:
        other_weight = to_other(shear_weight)
    u, n, state, column = forward(conc, shear_index, shear_weight, attenuation, line_energy, yields, cells, True)
    near = exchange(state, "near")
    if both:
        other_column = to_other(column)
    far = exchange(merge(near, line_energy, emissions, groups), "far")
    result = misfits(near, far, measured, line_energy, emissions, 2 if both else 1)
    if both:
        other = forward(conc, other_column, other_weight, attenuation, line_energy, yields, cells, False)
    result = exchange(result, ("views", "near") if both else "near")
    sides = [(column, shear_weight, u, n)]
    if both:
        sides.append((other_column, other_weight, *other))
    gradient, signal = backward(sides, result, measured, attenuation, line_energy, yields, cells)
    if not both:
        gradient = lax.psum(gradient, "views")
    return gradient.reshape(concentration.shape), signal


def solution(mesh):
    views, depth = mesh.shape["views"], mesh.shape["depth"]
    devices = mesh.devices.reshape(views, depth // NEAR, NEAR)
    split = jax.sharding.Mesh(devices, ("views", "far", "near"))
    depths = ("far", "near")
    return jax.shard_map(
        body,
        mesh=split,
        in_specs=(
            P(None, None, depths, None),
            P("views", depths, None),
            P("views", depths, None),
            P(),
            P(),
            P(),
            P("views", None, None, None),
        ),
        out_specs=(P(None, None, depths, None), P("views", None, None, None)),
        check_vma=False,
    )
```

```python
import functools

import jax
import jax.numpy as jnp
from jax import lax
from jax.experimental import pallas as pl
from jax.experimental.pallas import tpu as pltpu
from jax.sharding import PartitionSpec as P

LANES = 128
SUB = 8
BLOCK = 16
ROWS = BLOCK * SUB
NEAR = 4
CHUNK = 256
MIB = 1024 * 1024
F32 = jnp.float32
BF16 = jnp.bfloat16
HBM = pl.BlockSpec(memory_space=pltpu.HBM)
VMEM = pl.BlockSpec(memory_space=pltpu.VMEM)
SCALE, LINE_ROWS, LINE_LANES = 4, 5, 6


def in_hbm(value):
    return pltpu.with_memory_space_constraint(value, pltpu.HBM)


def lane_ids(width=LANES):
    return lax.broadcasted_iota(jnp.int32, (SUB, width), 1)


def row_ids(width=LANES):
    return lax.broadcasted_iota(jnp.int32, (SUB, width), 0)


def tile_of(values, ids):
    tile = jnp.zeros(ids.shape, F32)
    for e in range(SUB):
        tile = jnp.where(ids == e, values[e], tile)
    return tile


def select_line(masks, values):
    result = values[0]
    for mask, value in zip(masks[1:], values[1:]):
        result = jnp.where(mask, value, result)
    return result


def fill_matrix(mat_ref, first_tile, second_tile, first_incl, second_incl):
    depth = lane_ids() >> 3
    tiles = []
    for d in range(BLOCK):
        one = jnp.where(depth <= d if first_incl else depth < d, first_tile, 0.0)
        two = jnp.where(depth <= d if second_incl else depth < d, second_tile, 0.0)
        tiles.append(one + two)
    tiles.append(first_tile + second_tile)
    tiles.append(jnp.zeros((SUB, LANES), F32))
    whole = jnp.concatenate(tiles, axis=0)
    high = whole.astype(BF16)
    low = (whole - high.astype(F32)).astype(BF16)
    half = ROWS + 2 * SUB
    mat_ref[0:half, 0:LANES] = high
    mat_ref[0:half, LANES : 2 * LANES] = high
    mat_ref[half : 2 * half, 0:LANES] = low
    mat_ref[half : 2 * half, LANES : 2 * LANES] = jnp.zeros_like(low)


def multiply(mat_ref, values):
    high = values.astype(BF16)
    low = (values - high.astype(F32)).astype(BF16)
    product = jnp.dot(mat_ref[...], jnp.concatenate([high, low], axis=0), preferred_element_type=F32)
    half = ROWS + 2 * SUB
    lines = product[0:ROWS] + product[half : half + ROWS]
    return lines, product[ROWS : ROWS + SUB] + product[half + ROWS : half + ROWS + SUB]


def copies_in(pairs, sems):
    return [pltpu.make_async_copy(source, target, sems.at[i]) for i, (source, target) in enumerate(pairs)]


def block_rows(block):
    return pl.ds(pl.multiple_of(block * ROWS, ROWS), ROWS)


def block_cells(block):
    return pl.ds(pl.multiple_of(block * BLOCK, BLOCK), BLOCK)


def forward_kernel(with_state, cells, *refs):
    if with_state:
        att_hbm, line_hbm, yield_hbm, index_hbm, conc_hbm, weight_hbm, measured_hbm = refs[:7]
        u_ref, n_ref, const_ref, target_ref, column_hbm = refs[7:12]
        state_refs = refs[12 : 12 + NEAR]
        refs = refs[12 + NEAR :]
        measured_ref = refs[-2]
    else:
        att_hbm, line_hbm, yield_hbm, index_hbm, conc_hbm, weight_hbm, u_ref, n_ref = refs[:8]
        refs = refs[8:]
    conc_ref, weight_ref, cell_ref, left_pad, diff_pad, field, mat, carry, field_sum, emit_sum = refs[:10]
    att_ref, line_ref, yield_ref, index_ref = refs[10:14]
    sems = refs[-1]
    views, slab, width = weight_ref.shape
    emissions = att_ref.shape[0] - 1
    tiles = width // LANES
    blocks = slab // BLOCK
    lanes, rows = lane_ids(), row_ids()
    column_from = index_hbm
    if with_state:
        column_from = index_hbm.at[:, :, pl.ds(width // 2, LANES)]
    conc_copies = [
        pltpu.make_async_copy(
            conc_hbm.at[:, pl.ds(b * BLOCK, BLOCK), :], conc_ref.at[:, pl.ds(b * BLOCK, BLOCK), :], sems.at[b]
        )
        for b in range(blocks)
    ]
    pairs = [
        (att_hbm, att_ref),
        (line_hbm, line_ref),
        (yield_hbm, yield_ref),
        (column_from, index_ref),
        (weight_hbm, weight_ref),
    ]
    if with_state:
        pairs += [(measured_hbm, measured_ref), (column_from, column_hbm)]
    copies = copies_in(pairs, sems.at[pl.ds(blocks, len(pairs))])
    for copy in copies[:4] + conc_copies + copies[4:]:
        copy.start()
    for ref in (carry, field_sum, emit_sum):
        ref[...] = jnp.zeros_like(ref)
    for copy in copies[:4]:
        copy.wait()
    line_by_row = tile_of([line_ref[e].astype(F32) for e in range(SUB)], rows)
    masks = [line_by_row == k for k in range(emissions)]
    by_lane = [tile_of([att_ref[k, e] for e in range(SUB)], lanes & 7) for k in range(emissions + 1)]
    fill_matrix(mat, -by_lane[0], select_line(masks, by_lane[1:]), False, True)

    def one_block(block, _):
        for b in range(blocks):

            @pl.when(block == b)
            def _():
                conc_copies[b].wait()

        by_depth = jnp.swapaxes(conc_ref[:, block_cells(block), :], 0, 1)
        cell_ref[...] = by_depth

        def pad(d, _):
            pieces = [cell_ref[d, :, j * LANES : (j + 1) * LANES] for j in range(tiles)]
            turned = [pltpu.roll(piece, LANES - 1, 1) for piece in pieces]
            after = [jnp.where(lanes < LANES - 1, turned[j], turned[min(j + 1, tiles - 1)]) for j in range(tiles)]
            steps = [after[j] - pieces[j] for j in range(tiles)]
            last_cell = jnp.broadcast_to(pieces[-1][:, LANES - 2 : LANES - 1], (SUB, LANES))
            last_step = jnp.broadcast_to(steps[-1][:, LANES - 2 : LANES - 1], (SUB, LANES))
            first_cell = jnp.broadcast_to(pieces[0][:, 0:1], (SUB, LANES))
            first_step = jnp.broadcast_to(steps[0][:, 0:1], (SUB, LANES))
            pieces[-1] = jnp.where(lanes < LANES - 1, pieces[-1], last_cell)
            steps[-1] = jnp.where(lanes < LANES - 1, steps[-1], last_step)
            pieces = [first_cell] + pieces + [last_cell, last_cell]
            steps = [first_step] + steps + [last_step, last_step]
            for j in range(tiles + 3):
                left_pad[d, :, j * LANES : (j + 1) * LANES] = pieces[j]
                diff_pad[d, :, j * LANES : (j + 1) * LANES] = steps[j]
            return 0

        lax.fori_loop(0, BLOCK, pad, 0, unroll=4)

        @pl.when(block == 0)
        def _():
            copies[4].wait()

        def shear(octet, _):
            for i in range(SUB * views):
                v, i = i % views, i // views
                d = octet * SUB + i
                at = pl.multiple_of(block * BLOCK + octet * SUB, SUB)
                offset = index_ref[v, block * BLOCK + d, 0] - (width // 2 - LANES)
                whole = offset >> 7
                rest = offset & (LANES - 1)
                turn = (LANES - rest) & (LANES - 1)
                stay = lanes < LANES - rest

                def sheared(ref):
                    turned = []
                    for j in range(tiles + 1):
                        start = pl.multiple_of((whole + j) * LANES, LANES)
                        turned.append(pltpu.roll(ref[d, :, pl.ds(start, LANES)], turn, 1))
                    return [jnp.where(stay, turned[j], turned[j + 1]) for j in range(tiles)]

                left, diff = sheared(left_pad), sheared(diff_pad)
                into = pl.ds(pl.multiple_of(d * SUB, SUB), SUB)
                for j in range(tiles):
                    span = slice(j * LANES, (j + 1) * LANES)
                    weight = weight_ref[v, pl.ds(at, SUB), span][i : i + 1]
                    field[v, into, span] = left[j] + weight * diff[j]
            return 0

        lax.fori_loop(0, BLOCK // SUB, shear, 0)

        for v in range(views):
            for c in range(width // CHUNK):
                span = slice(c * CHUNK, (c + 1) * CHUNK)
                value = field[v, :, span]
                lines, total = multiply(mat, value)
                before = carry[v, :, span]
                through = jnp.exp(lines.reshape(BLOCK, SUB, CHUNK) + before[None])
                value = value.reshape(BLOCK, SUB, CHUNK)
                emit = value * through
                u_ref[v, block_rows(block), span] = through.reshape(ROWS, CHUNK)
                n_ref[v, block_rows(block), span] = emit.reshape(ROWS, CHUNK)
                carry[v, :, span] = before + total
                if with_state:
                    field_sum[v, :, span] += jnp.sum(value, axis=0)
                    emit_sum[v, :, span] += jnp.sum(emit, axis=0)
        return 0

    lax.fori_loop(0, blocks, one_block, 0)

    if with_state:
        columns = [tile_of([att_ref[k, e] for e in range(SUB)], rows) for k in range(emissions + 1)]
        scale = tile_of([yield_ref[e] for e in range(SUB)], rows)
        for k in range(emissions + 1):
            const_ref[k] = columns[k]
        const_ref[SCALE] = scale
        const_ref[LINE_ROWS] = line_by_row
        const_ref[LINE_LANES] = tile_of([line_ref[e].astype(F32) for e in range(SUB)], lanes & 7)
        share = width // NEAR
        place = lax.axis_index("near")
        for r in range(NEAR):
            for j in range(share // LANES):
                start = pl.multiple_of((place ^ r) * share + j * LANES, LANES)
                span = slice(j * LANES, (j + 1) * LANES)
                totals = jnp.zeros((SUB, LANES), F32)
                for v in range(views):
                    values = field_sum[v, :, pl.ds(start, LANES)]
                    sums = [jnp.sum(column * values, axis=0, keepdims=True) for column in columns]
                    for k in range(emissions + 1):
                        totals = jnp.where(rows == v * (emissions + 1) + k, sums[k], totals)
                    line_total = select_line(masks, [jnp.broadcast_to(value, rows.shape) for value in sums[1:]])
                    signal = scale * (1.0 / cells) * emit_sum[v, :, pl.ds(start, LANES)] * jnp.exp(-line_total)
                    state_refs[r][(v + 1) * SUB : (v + 2) * SUB, span] = signal
                state_refs[r][0:SUB, span] = jnp.exp(-totals)
        for copy in copies[5:]:
            copy.wait()
        for v in range(views):
            target_ref[v * SUB : (v + 1) * SUB, :] = measured_ref[v].reshape(SUB, width)


def forward(conc, index, weights, scalars, cells, measured=None):
    views, slab, width = weights.shape
    attenuation, line_energy, yields = scalars
    with_state = measured is not None
    values = pltpu.VMEM((views, slab * SUB, width), F32)
    out_shape = [values, values]
    out_specs = [VMEM, VMEM]
    operands = [attenuation, line_energy, yields, index, conc, weights]
    scratch = [
        pltpu.VMEM((SUB, slab, width), F32),
        pltpu.VMEM((views, slab, width), F32),
        pltpu.VMEM((BLOCK, SUB, width), F32),
        pltpu.VMEM((BLOCK, SUB, width + 3 * LANES), F32),
        pltpu.VMEM((BLOCK, SUB, width + 3 * LANES), F32),
        pltpu.VMEM((views, ROWS, width), F32),
        pltpu.VMEM((2 * (ROWS + 2 * SUB), 2 * LANES), BF16),
        pltpu.VMEM((views, SUB, width), F32),
        pltpu.VMEM((views, SUB, width), F32),
        pltpu.VMEM((views, SUB, width), F32),
        pltpu.SMEM(attenuation.shape, F32),
        pltpu.SMEM(line_energy.shape, jnp.int32),
        pltpu.SMEM(yields.shape, F32),
        pltpu.SMEM((views, slab, LANES), jnp.int32),
    ]
    count = slab // BLOCK + 5
    if with_state:
        operands.append(measured)
        out_shape += [
            pltpu.VMEM((LINE_LANES + 1, SUB, LANES), F32),
            pltpu.VMEM((views * SUB, width), F32),
            pltpu.HBM((views, slab, LANES), jnp.int32),
        ]
        out_specs += [VMEM, VMEM, HBM]
        out_shape += [pltpu.VMEM(((views + 1) * SUB, width // NEAR), F32)] * NEAR
        out_specs += [VMEM] * NEAR
        scratch.append(pltpu.VMEM(measured.shape, F32))
        count += 2
    return pl.pallas_call(
        functools.partial(forward_kernel, with_state, cells),
        in_specs=[HBM] * len(operands),
        out_specs=out_specs,
        out_shape=out_shape,
        scratch_shapes=scratch + [pltpu.SemaphoreType.DMA((count,))],
        compiler_params=pltpu.CompilerParams(vmem_limit_bytes=16 * MIB),
        cost_estimate=pl.CostEstimate(
            flops=views * slab * SUB * width * 40, bytes_accessed=4 * views * slab * SUB * width * 3, transcendentals=0
        ),
        name="forward" if with_state else "forward_other",
    )(*[in_hbm(operand) for operand in operands])


def line_rows(tile, base, masks):
    shape = masks[0].shape
    return select_line(masks, [jnp.broadcast_to(tile[base + 1 + k : base + 2 + k], shape) for k in range(len(masks))])


def ordered_factors(factors, rows, step):
    count = len(factors)
    before, behind = [None] * count, [None] * count
    run = jnp.ones_like(factors[0])
    for i in range(count):
        before[i] = run
        run = run * factors[i]
    run = jnp.ones_like(factors[0])
    for i in reversed(range(count)):
        behind[i] = run
        run = run * factors[i]

    def incident(tile):
        result = jnp.broadcast_to(tile[0:1], tile.shape)
        for base in range(step, SUB, step):
            result = jnp.where(rows >= base, jnp.broadcast_to(tile[base : base + 1], tile.shape), result)
        return result

    return [incident(before[i]) * behind[i] for i in range(count)]


def row_masks(const_ref, emissions, width):
    tile = const_ref[LINE_ROWS]
    return [jnp.concatenate([tile] * (width // LANES), axis=1) == k for k in range(emissions)]


def put_in_order(scratch, place, refs):
    for r, ref in enumerate(refs):
        scratch[place ^ r] = ref[...]


def merge_kernel(emissions, const_ref, *refs):
    near_refs, (out_ref, near) = refs[:NEAR], refs[NEAR:]
    put_in_order(near, lax.axis_index("near"), near_refs)
    depth, width = out_ref.shape
    masks = row_masks(const_ref, emissions, width)
    factors = [near[i, 0:SUB, :] for i in range(NEAR)]
    around = ordered_factors(factors, row_ids(width), emissions + 1)
    total = factors[0]
    for i in range(1, NEAR):
        total = total * factors[i]
    out_ref[0:SUB, :] = total
    for v in range(depth // SUB - 1):
        span = slice((v + 1) * SUB, (v + 2) * SUB)
        signal = jnp.zeros((SUB, width), F32)
        for i in range(NEAR):
            signal = signal + near[i, span, :] * line_rows(around[i], v * (emissions + 1), masks)
        out_ref[span, :] = signal


def merge(near, const, emissions):
    shape = near[0].shape
    return pl.pallas_call(
        functools.partial(merge_kernel, emissions),
        in_specs=[VMEM] * (1 + NEAR),
        out_specs=VMEM,
        out_shape=pltpu.VMEM(shape, F32),
        scratch_shapes=[pltpu.VMEM((NEAR,) + shape, F32)],
        compiler_params=pltpu.CompilerParams(vmem_limit_bytes=2 * MIB),
        name="merge",
    )(const, *near)


def misfit_kernel(emissions, groups, const_ref, target_ref, *refs):
    near_refs, refs = refs[:NEAR], refs[NEAR:]
    far_refs, refs = refs[:groups], refs[groups:]
    own_refs, refs = refs[:NEAR], refs[NEAR:]
    other_refs, (near, far, result) = refs[:-3], refs[-3:]
    depth, width = near_refs[0].shape
    views = depth // SUB - 1
    place, group = lax.axis_index("near"), lax.axis_index("far")
    put_in_order(near, place, near_refs)
    put_in_order(far, group, far_refs)
    rows = row_ids(width)
    masks = row_masks(const_ref, emissions, width)
    zero = jnp.zeros((SUB, width), F32)
    far_around = ordered_factors([far[g, 0:SUB, :] for g in range(groups)], rows, emissions + 1)
    outside = zero
    for g in range(groups):
        outside = outside + jnp.where(g == group, far_around[g], 0.0)
    factors = [near[i, 0:SUB, :] for i in range(NEAR)]
    around = [value * outside for value in ordered_factors(factors, rows, emissions + 1)]
    start = pl.multiple_of(place * width, LANES)
    for v in range(views):
        base = v * (emissions + 1)
        span = slice((v + 1) * SUB, (v + 2) * SUB)
        far_parts = [far[g, span, :] * line_rows(far_around[g], base, masks) for g in range(groups)]
        parts = [near[i, span, :] * line_rows(around[i], base, masks) for i in range(NEAR)]
        signal = zero
        for g in range(groups):
            signal = signal + far_parts[g]
        misfit = signal - target_ref[v * SUB : (v + 1) * SUB, pl.ds(start, width)]

        def by_energy(value):
            value = misfit * value
            return [jnp.sum(jnp.where(mask, value, 0.0), axis=0, keepdims=True) for mask in masks]

        def plus(one, two):
            return [a + b for a, b in zip(one, two)]

        lower, upper = zero, zero
        for g in range(groups):
            lower = lower + jnp.where(g < group, far_parts[g], 0.0)
            upper = upper + jnp.where(g > group, far_parts[g], 0.0)
        earlier, later = by_energy(lower), by_energy(upper)
        sums = [by_energy(part) for part in parts]
        earliers, laters = [], [None] * NEAR
        for i in range(NEAR):
            earliers.append(earlier)
            earlier = plus(earlier, sums[i])
        for i in reversed(range(NEAR)):
            later = plus(later, sums[i])
            total = later[0]
            for value in later[1:]:
                total = total + value
            laters[i] = total
        at = 2 * v * SUB
        for i in range(NEAR):
            tile = around[i] * factors[i]
            tile = jnp.where(rows == base, laters[i], tile)
            for k in range(emissions):
                tile = jnp.where(rows == SUB // 2 - base + k, earliers[i][k], tile)
            result[i, v * SUB : (v + 1) * SUB, :] = tile
        for ref in own_refs:
            ref[at : at + SUB, :] = signal
        for ref in other_refs:
            ref[at : at + SUB, :] = misfit
    for r in range(NEAR):
        for v in range(views):
            tile = result[place ^ r, v * SUB : (v + 1) * SUB, :]
            for refs in (own_refs, other_refs):
                if refs:
                    refs[r][(2 * v + 1) * SUB : (2 * v + 2) * SUB, :] = tile


def misfits(near, far, target, const, emissions, both):
    depth, width = near[0].shape
    views = depth // SUB - 1
    count = 2 * NEAR if both else NEAR
    groups = len(far)
    return pl.pallas_call(
        functools.partial(misfit_kernel, emissions, groups),
        in_specs=[VMEM] * (2 + NEAR + groups),
        out_specs=[VMEM] * count,
        out_shape=[pltpu.VMEM((2 * views * SUB, width), F32)] * count,
        scratch_shapes=[
            pltpu.VMEM((NEAR, depth, width), F32),
            pltpu.VMEM((groups, depth, width), F32),
            pltpu.VMEM((NEAR, views * SUB, width), F32),
        ],
        compiler_params=pltpu.CompilerParams(vmem_limit_bytes=4 * MIB),
        name="misfit",
    )(const, target, *near, *far)


def backward_kernel(sides, cells, const_ref, target_ref, *refs):
    index_hbms, refs = refs[:sides], refs[sides:]
    weight_hbms, refs = refs[:sides], refs[sides:]
    u_refs, refs = refs[:sides], refs[sides:]
    n_refs, refs = refs[:sides], refs[sides:]
    result_refs, refs = refs[: sides * NEAR], refs[sides * NEAR :]
    grad_hbm, signal_ref, mat, gain, carry, scaled, left_pad, diff_pad, cell_ref, grad_ref = refs[:10]
    index_refs, refs = refs[10 : 10 + sides], refs[10 + sides :]
    weight_refs, sems = refs[:sides], refs[-1]
    views, slab, width = weight_refs[0].shape
    emissions = SCALE - 1
    tiles = width // LANES
    blocks = slab // BLOCK
    share = width // NEAR
    lanes, rows = lane_ids(), row_ids()
    margin = 2 * LANES
    copies = copies_in(
        [(index_hbms[s], index_refs[s]) for s in range(sides)] + [(weight_hbms[s], weight_refs[s]) for s in range(sides)],
        sems.at[pl.ds(blocks, 2 * sides)],
    )
    out_copies = [
        pltpu.make_async_copy(grad_ref.at[b], grad_hbm.at[:, pl.ds(b * BLOCK, BLOCK), :], sems.at[b])
        for b in range(blocks)
    ]
    for copy in copies:
        copy.start()
    masks = [const_ref[LINE_LANES] == k for k in range(emissions)]
    columns = [const_ref[k] for k in range(emissions + 1)]
    fill_matrix(mat, -columns[0], select_line(masks, columns[1:]), True, False)
    masks = [const_ref[LINE_ROWS] == k for k in range(emissions)]
    scale = const_ref[SCALE]
    columns = [column * cells for column in columns]
    place = lax.axis_index("near")
    for r in range(NEAR):
        for j in range(share // LANES):
            span = pl.ds(pl.multiple_of((place ^ r) * share + j * LANES, LANES), LANES)
            part = slice(j * LANES, (j + 1) * LANES)
            for s in range(sides):
                for v in range(views):
                    base = v * (emissions + 1)
                    misfit = result_refs[s * NEAR + r][2 * v * SUB : (2 * v + 1) * SUB, part]
                    tile = result_refs[s * NEAR + r][(2 * v + 1) * SUB : (2 * v + 2) * SUB, part]
                    if s == 0:
                        signal_ref[v, :, :, span] = misfit.reshape(SUB, 1, LANES)
                        misfit = misfit - target_ref[v * SUB : (v + 1) * SUB, span]
                    gain[s * views + v, :, span] = misfit * scale * line_rows(tile, base, masks)
                    back = columns[0] * jnp.broadcast_to(tile[base : base + 1], tile.shape)
                    for k in range(emissions):
                        row = SUB // 2 - base + k
                        back = back + columns[k + 1] * jnp.broadcast_to(tile[row : row + 1], tile.shape)
                    carry[s * views + v, :, span] = back
    for ref in (left_pad, diff_pad):
        ref[:, :, :, 0:margin] = jnp.zeros(ref.shape[:3] + (margin,), F32)
        ref[:, :, :, margin + width + LANES :] = jnp.zeros(ref.shape[:3] + (margin,), F32)
    for copy in copies:
        copy.wait()

    def one_block(block, _):
        for s in range(sides):
            for v in range(views):
                at = s * views + v
                for c in range(width // CHUNK):
                    span = slice(c * CHUNK, (c + 1) * CHUNK)
                    factor = gain[at, :, span][None]
                    weighted = n_refs[s][v, block_rows(block), span].reshape(BLOCK, SUB, CHUNK) * factor
                    direct = u_refs[s][v, block_rows(block), span].reshape(BLOCK, SUB, CHUNK) * factor
                    lines, total = multiply(mat, weighted.reshape(ROWS, CHUNK))
                    before = carry[at, :, span]
                    lines = lines.reshape(BLOCK, SUB, CHUNK) + before[None]
                    scaled[at, :, span] = (direct - lines).reshape(ROWS, CHUNK)
                    carry[at, :, span] = before + total

                def place_octet(octet, _):
                    for i in range(SUB):
                        d = octet * SUB + i
                        cells_at = pl.ds(pl.multiple_of(block * BLOCK + octet * SUB, SUB), SUB)
                        rest = (index_refs[s][v, block * BLOCK + d, 0] - (width // 2 - LANES)) & (LANES - 1)
                        stay = lanes >= rest
                        from_rows = pl.ds(pl.multiple_of(d * SUB, SUB), SUB)
                        plain = [scaled[at, from_rows, j * LANES : (j + 1) * LANES] for j in range(tiles)]
                        moved = [
                            plain[j] * weight_refs[s][v, cells_at, j * LANES : (j + 1) * LANES][i : i + 1]
                            for j in range(tiles)
                        ]
                        for ref, values in ((left_pad, plain), (diff_pad, moved)):
                            turned = [jnp.zeros((SUB, LANES), F32)]
                            turned += [pltpu.roll(value, rest, 1) for value in values]
                            turned += [jnp.zeros((SUB, LANES), F32)]
                            for j in range(tiles + 1):
                                span = slice(margin + j * LANES, margin + (j + 1) * LANES)
                                ref[at, d, :, span] = jnp.where(stay, turned[j + 1], turned[j])
                    return 0

                lax.fori_loop(0, BLOCK // SUB, place_octet, 0)

        def gather(d, _):
            cell = block * BLOCK + d

            def gathered(ref):
                sums = [None] * (tiles + 2)
                for s in range(sides):
                    for v in range(views):
                        whole = (index_refs[s][v, cell, 0] - (width // 2 - LANES)) >> 7
                        for j in range(tiles + 2):
                            start = pl.multiple_of((2 + j - whole) * LANES, LANES)
                            value = ref[s * views + v, d, :, pl.ds(start, LANES)]
                            sums[j] = value if sums[j] is None else sums[j] + value
                return sums

            left, diff = gathered(left_pad), gathered(diff_pad)
            left = [left[j] - diff[j] for j in range(tiles + 2)]

            def folded(sums):
                low = jnp.sum(sums[0], axis=1, keepdims=True)
                beyond = sums[tiles + 1] + jnp.where(lanes == LANES - 1, sums[tiles], 0.0)
                high = jnp.sum(beyond, axis=1, keepdims=True)
                core = sums[1 : tiles + 1]
                core[0] = core[0] + jnp.where(lanes == 0, low, 0.0)
                core[-1] = jnp.where(lanes == LANES - 1, 0.0, core[-1] + jnp.where(lanes == LANES - 2, high, 0.0))
                return core

            left, diff = folded(left), folded(diff)
            turned = [jnp.zeros((SUB, LANES), F32)] + [pltpu.roll(value, 1, 1) for value in diff]
            for j in range(tiles):
                value = left[j] + jnp.where(lanes == 0, turned[j], turned[j + 1])
                cell_ref[d, :, j * LANES : (j + 1) * LANES] = value
            return 0

        lax.fori_loop(0, BLOCK, gather, 0, unroll=2)
        grad_ref[block] = jnp.swapaxes(cell_ref[...], 0, 1)
        for b in range(blocks):

            @pl.when(block == b)
            def _():
                out_copies[b].start()

        return 0

    lax.fori_loop(0, blocks, one_block, 0)
    for copy in out_copies:
        copy.wait()


def backward(sides, const, target, out_shape, cells):
    views, slab, width = sides[0][1].shape
    count = len(sides)
    total = count * views
    blocks = slab // BLOCK
    return pl.pallas_call(
        functools.partial(backward_kernel, count, cells),
        in_specs=[VMEM] * 2 + [HBM] * (2 * count) + [VMEM] * ((2 + NEAR) * count),
        out_specs=[HBM, VMEM],
        out_shape=[pltpu.HBM((SUB, slab, width), F32), jax.ShapeDtypeStruct(out_shape, F32)],
        scratch_shapes=[
            pltpu.VMEM((2 * (ROWS + 2 * SUB), 2 * LANES), BF16),
            pltpu.VMEM((total, SUB, width), F32),
            pltpu.VMEM((total, SUB, width), F32),
            pltpu.VMEM((total, ROWS, width), F32),
            pltpu.VMEM((total, BLOCK, SUB, width + 5 * LANES), F32),
            pltpu.VMEM((total, BLOCK, SUB, width + 5 * LANES), F32),
            pltpu.VMEM((BLOCK, SUB, width), F32),
            pltpu.VMEM((blocks, SUB, BLOCK, width), F32),
        ]
        + [pltpu.SMEM((views, slab, LANES), jnp.int32)] * count
        + [pltpu.VMEM((views, slab, width), F32)] * count
        + [pltpu.SemaphoreType.DMA((blocks + 2 * count,))],
        compiler_params=pltpu.CompilerParams(vmem_limit_bytes=32 * MIB),
        name="backward",
    )(
        const,
        target,
        *[in_hbm(side[0]) for side in sides],
        *[in_hbm(side[1]) for side in sides],
        *[side[2] for side in sides],
        *[side[3] for side in sides],
        *[part for side in sides for part in side[4]],
    )


def body(concentration, shear_index, shear_weight, attenuation, yields, line_energy, measured):
    elements, _, slab, width = concentration.shape
    emissions = attenuation.shape[0] - 1
    groups = lax.axis_size("far")
    both = lax.axis_size("views") == 2
    cells = float(slab * groups * NEAR)
    conc = concentration.reshape(elements, slab, width)
    scalars = (attenuation, line_energy, yields)

    def to_other(value):
        return lax.ppermute(value, "views", [(0, 1), (1, 0)])

    def to_near(value, r):
        return lax.ppermute(value, "near", [(s, s ^ r) for s in range(NEAR)]) if r else value

    def to_far(value, r):
        return lax.ppermute(value, "far", [(s, s ^ r) for s in range(groups)]) if r else value

    def across(value, r):
        pairs = [(v * NEAR + s, (1 - v) * NEAR + (s ^ r)) for v in range(2) for s in range(NEAR)]
        return lax.ppermute(value, ("views", "near"), pairs)

    if both:
        other_weight = to_other(shear_weight)
    u, n, const, target, column, *states = forward(conc, shear_index, shear_weight, scalars, cells, measured)
    near = [to_near(states[r], r) for r in range(NEAR)]
    if both:
        other_column = to_other(column)
    merged = merge(near, const, emissions)
    far = [to_far(merged, r) for r in range(groups)]
    if both:
        other = forward(conc, other_column, other_weight, scalars, cells)
    results = misfits(near, far, target, const, emissions, both)
    sides = [(column, shear_weight, u, n, [to_near(results[r], r) for r in range(NEAR)])]
    if both:
        sides.append((other_column, other_weight, *other, [across(results[NEAR + r], r) for r in range(NEAR)]))
    gradient, signal = backward(sides, const, target, measured.shape, cells)
    if not both:
        gradient = lax.psum(gradient, "views")
    return gradient.reshape(concentration.shape), signal


def solution(mesh):
    views, depth = mesh.shape["views"], mesh.shape["depth"]
    devices = mesh.devices.reshape(views, depth // NEAR, NEAR)
    split = jax.sharding.Mesh(devices, ("views", "far", "near"))
    depths = ("far", "near")
    return jax.shard_map(
        body,
        mesh=split,
        in_specs=(
            P(None, None, depths, None),
            P("views", depths, None),
            P("views", depths, None),
            P(),
            P(),
            P(),
            P("views", None, None, None),
        ),
        out_specs=(P(None, None, depths, None), P("views", None, None, None)),
        check_vma=False,
    )
```

```python
import functools

import jax
import jax.numpy as jnp
from jax import lax
from jax.experimental import pallas as pl
from jax.experimental.pallas import tpu as pltpu
from jax.sharding import PartitionSpec as P

LANES = 128
SUB = 8
BLOCK = 8
ROWS = BLOCK * SUB
NEAR = 4
CHUNK = 256
MIB = 1024 * 1024
F32 = jnp.float32
BF16 = jnp.bfloat16
HBM = pl.BlockSpec(memory_space=pltpu.HBM)
VMEM = pl.BlockSpec(memory_space=pltpu.VMEM)
SCALE, LINE_ROWS, LINE_LANES = 4, 5, 6
ANY = pl.BlockSpec(memory_space=pl.ANY)


def in_hbm(value):
    return pltpu.with_memory_space_constraint(value, pltpu.HBM)


def lane_ids(width=LANES):
    return lax.broadcasted_iota(jnp.int32, (SUB, width), 1)


def row_ids(width=LANES):
    return lax.broadcasted_iota(jnp.int32, (SUB, width), 0)


def tile_of(values, ids):
    tile = jnp.zeros(ids.shape, F32)
    for e in range(SUB):
        tile = jnp.where(ids == e, values[e], tile)
    return tile


def select_line(masks, values):
    result = values[0]
    for mask, value in zip(masks[1:], values[1:]):
        result = jnp.where(mask, value, result)
    return result


def fill_matrix(mat_ref, first_tile, second_tile, first_incl, second_incl):
    depth = (lane_ids() & (ROWS - 1)) >> 3
    tiles = []
    for d in range(BLOCK):
        one = jnp.where(depth <= d if first_incl else depth < d, first_tile, 0.0)
        two = jnp.where(depth <= d if second_incl else depth < d, second_tile, 0.0)
        tiles.append(one + two)
    tiles.append(first_tile + second_tile)
    tiles.append(jnp.zeros((SUB, LANES), F32))
    whole = jnp.concatenate(tiles, axis=0)
    high = whole.astype(BF16)
    mat_ref[:, 0:LANES] = high
    mat_ref[:, LANES : 2 * LANES] = (whole - high.astype(F32)).astype(BF16)


def multiply(mat_ref, values):
    high = values.astype(BF16)
    low = (values - high.astype(F32)).astype(BF16)
    stacked = jnp.concatenate([high, low, high], axis=0)
    product = jnp.dot(mat_ref[:, 0 : 3 * ROWS], stacked, preferred_element_type=F32)
    return product[0:ROWS], product[ROWS : ROWS + SUB]


MATRIX = (ROWS + 2 * SUB, 2 * LANES)


def copies_in(pairs, sems):
    return [pltpu.make_async_copy(source, target, sems.at[i]) for i, (source, target) in enumerate(pairs)]


def block_rows(block):
    return pl.ds(pl.multiple_of(block * ROWS, ROWS), ROWS)


def block_cells(block):
    return pl.ds(pl.multiple_of(block * BLOCK, BLOCK), BLOCK)


def shift_of(index_ref, v, cell, width):
    offset = index_ref[v, cell, 0] - (width // 2 - LANES)
    return offset >> 7, offset & (LANES - 1)


def shear(field, left_pad, diff_pad, index_ref, weight_ref, block, views, tiles):
    lanes = lane_ids()
    for i, v in enumerate(views):
        for d in range(BLOCK):
            cell = block * BLOCK + d
            whole, rest = shift_of(index_ref, v, cell, tiles * LANES)
            turn = (LANES - rest) & (LANES - 1)
            stay = lanes < LANES - rest

            def sheared(ref):
                turned = []
                for j in range(tiles + 1):
                    start = pl.multiple_of((whole + j) * LANES, LANES)
                    turned.append(pltpu.roll(ref[cell, :, pl.ds(start, LANES)], turn, 1))
                return [jnp.where(stay, turned[j], turned[j + 1]) for j in range(tiles)]

            left, diff = sheared(left_pad), sheared(diff_pad)
            for j in range(tiles):
                span = slice(j * LANES, (j + 1) * LANES)
                field[i, d * SUB : (d + 1) * SUB, span] = left[j] + weight_ref[i, d : d + 1, span] * diff[j]


def transmit(u_ref, n_ref, field, mat, carry, block, sums):
    views, _, width = field.shape
    for v in range(views):
        for c in range(width // CHUNK):
            span = slice(c * CHUNK, (c + 1) * CHUNK)
            value = field[v, :, span]
            lines, total = multiply(mat, value)
            before = carry[v, :, span]
            through = jnp.exp(lines.reshape(BLOCK, SUB, CHUNK) + before[None])
            value = value.reshape(BLOCK, SUB, CHUNK)
            emit = value * through
            u_ref[v, block_rows(block), span] = through.reshape(ROWS, CHUNK)
            n_ref[v, block_rows(block), span] = emit.reshape(ROWS, CHUNK)
            carry[v, :, span] = before + total
            if sums:
                sums[0][v, :, span] += jnp.sum(value, axis=0)
                sums[1][v, :, span] += jnp.sum(emit, axis=0)


def forward_kernel(cells, *refs):
    att_hbm, line_hbm, yield_hbm, index_hbm, conc_hbm, weight_hbm, measured_hbm = refs[:7]
    u_ref, n_ref, const_ref, target_ref, mat, left_pad, diff_pad = refs[7:14]
    state_refs = refs[14 : 14 + NEAR]
    refs = refs[14 + NEAR :]
    conc_ref, weight_ref, weight_rows, field, carry, field_sum, emit_sum, measured_ref = refs[:8]
    att_ref, line_ref, yield_ref, index_ref, sems = refs[8:]
    views, slab, width = weight_ref.shape
    emissions = att_ref.shape[0] - 1
    tiles = width // LANES
    blocks = slab // BLOCK
    lanes, rows = lane_ids(), row_ids()
    conc_copies = [
        pltpu.make_async_copy(
            conc_hbm.at[:, pl.ds(b * BLOCK, BLOCK), :], conc_ref.at[:, pl.ds(b * BLOCK, BLOCK), :], sems.at[b]
        )
        for b in range(blocks)
    ]
    pairs = [
        (att_hbm, att_ref),
        (line_hbm, line_ref),
        (yield_hbm, yield_ref),
        (index_hbm, index_ref),
        (weight_hbm, weight_ref),
        (measured_hbm, measured_ref),
    ]
    copies = copies_in(pairs, sems.at[pl.ds(blocks, len(pairs))])
    for copy in conc_copies[:1] + copies[:4] + conc_copies[1:] + copies[4:]:
        copy.start()
    for ref in (carry, field_sum, emit_sum):
        ref[...] = jnp.zeros_like(ref)

    def one_block(block, _):
        for b in range(blocks):

            @pl.when(block == b)
            def _():
                conc_copies[b].wait()

        by_depth = jnp.swapaxes(conc_ref[:, block_cells(block), :], 0, 1)
        for d in range(BLOCK):
            pieces = [by_depth[d, :, j * LANES : (j + 1) * LANES] for j in range(tiles)]
            turned = [pltpu.roll(piece, LANES - 1, 1) for piece in pieces]
            after = [jnp.where(lanes < LANES - 1, turned[j], turned[min(j + 1, tiles - 1)]) for j in range(tiles)]
            steps = [after[j] - pieces[j] for j in range(tiles)]
            last_cell = jnp.broadcast_to(pieces[-1][:, LANES - 2 : LANES - 1], (SUB, LANES))
            last_step = jnp.broadcast_to(steps[-1][:, LANES - 2 : LANES - 1], (SUB, LANES))
            first_cell = jnp.broadcast_to(pieces[0][:, 0:1], (SUB, LANES))
            first_step = jnp.broadcast_to(steps[0][:, 0:1], (SUB, LANES))
            pieces[-1] = jnp.where(lanes < LANES - 1, pieces[-1], last_cell)
            steps[-1] = jnp.where(lanes < LANES - 1, steps[-1], last_step)
            pieces = [first_cell] + pieces + [last_cell, last_cell]
            steps = [first_step] + steps + [last_step, last_step]
            for j in range(tiles + 3):
                left_pad[block * BLOCK + d, :, j * LANES : (j + 1) * LANES] = pieces[j]
                diff_pad[block * BLOCK + d, :, j * LANES : (j + 1) * LANES] = steps[j]

        @pl.when(block == 0)
        def _():
            for copy in copies:
                copy.wait()
            line_by_row = tile_of([line_ref[e].astype(F32) for e in range(SUB)], rows)
            masks = [line_by_row == k for k in range(emissions)]
            by_lane = [tile_of([att_ref[k, e] for e in range(SUB)], lanes & 7) for k in range(emissions + 1)]
            fill_matrix(mat, -by_lane[0], select_line(masks, by_lane[1:]), False, True)
            for k in range(emissions + 1):
                const_ref[k] = tile_of([att_ref[k, e] for e in range(SUB)], rows)
            const_ref[SCALE] = tile_of([yield_ref[e] for e in range(SUB)], rows)
            const_ref[LINE_ROWS] = line_by_row
            const_ref[LINE_LANES] = tile_of([line_ref[e].astype(F32) for e in range(SUB)], lanes & 7)

        weight_rows[...] = weight_ref[:, block_cells(block), :]
        shear(field, left_pad, diff_pad, index_ref, weight_rows, block, range(views), tiles)
        transmit(u_ref, n_ref, field, mat, carry, block, (field_sum, emit_sum))
        return 0

    lax.fori_loop(0, blocks, one_block, 0)
    columns = [const_ref[k] for k in range(emissions + 1)]
    masks = [const_ref[LINE_ROWS] == k for k in range(emissions)]
    scale = const_ref[SCALE] * (1.0 / cells)
    share = width // NEAR
    place = lax.axis_index("near")
    for r in range(NEAR):
        for j in range(share // LANES):
            start = pl.multiple_of((place ^ r) * share + j * LANES, LANES)
            span = slice(j * LANES, (j + 1) * LANES)
            totals = jnp.zeros((SUB, LANES), F32)
            for v in range(views):
                values = field_sum[v, :, pl.ds(start, LANES)]
                sums = [jnp.sum(column * values, axis=0, keepdims=True) for column in columns]
                for k in range(emissions + 1):
                    totals = jnp.where(rows == v * (emissions + 1) + k, sums[k], totals)
                line_total = select_line(masks, [jnp.broadcast_to(value, rows.shape) for value in sums[1:]])
                signal = scale * emit_sum[v, :, pl.ds(start, LANES)] * jnp.exp(-line_total)
                state_refs[r][(v + 1) * SUB : (v + 2) * SUB, span] = signal
            state_refs[r][0:SUB, span] = jnp.exp(-totals)
    for v in range(views):
        target_ref[v * SUB : (v + 1) * SUB, :] = measured_ref[v].reshape(SUB, width)


def forward(conc, column, weights, scalars, measured, cells):
    views, slab, width = weights.shape
    attenuation, line_energy, yields = scalars
    values = pltpu.VMEM((views, slab * SUB, width), F32)
    padded = pltpu.VMEM((slab, SUB, width + 3 * LANES), F32)
    state = pltpu.VMEM(((views + 1) * SUB, width // NEAR), F32)
    line = pltpu.VMEM((views, SUB, width), F32)
    operands = [in_hbm(value) for value in (attenuation, line_energy, yields, column, conc, weights, measured)]
    return pl.pallas_call(
        functools.partial(forward_kernel, cells),
        in_specs=[HBM] * len(operands),
        out_specs=[VMEM] * (7 + NEAR),
        out_shape=[
            values,
            values,
            pltpu.VMEM((LINE_LANES + 1, SUB, LANES), F32),
            pltpu.VMEM((views * SUB, width), F32),
            pltpu.VMEM(MATRIX, BF16),
            padded,
            padded,
        ]
        + [state] * NEAR,
        scratch_shapes=[
            pltpu.VMEM((SUB, slab, width), F32),
            pltpu.VMEM((views, slab, width), F32),
            pltpu.VMEM((views, BLOCK, width), F32),
            pltpu.VMEM((views, ROWS, width), F32),
            line,
            line,
            line,
            pltpu.VMEM(measured.shape, F32),
            pltpu.SMEM(attenuation.shape, F32),
            pltpu.SMEM(line_energy.shape, jnp.int32),
            pltpu.SMEM(yields.shape, F32),
            pltpu.SMEM((views, slab, LANES), jnp.int32),
            pltpu.SemaphoreType.DMA((slab // BLOCK + 6,)),
        ],
        compiler_params=pltpu.CompilerParams(vmem_limit_bytes=16 * MIB),
        name="forward",
    )(*operands)


def forward_other_kernel(view, index_any, weight_any, mat, left_pad, diff_pad, order_ref, *refs):
    u_ref, n_ref, token_ref, weight_ref, weight_rows, field, carry, index_ref, sems = refs
    slab, width = weight_ref.shape[1:]
    copies = copies_in(
        ((index_any.at[pl.ds(view, 1)], index_ref), (weight_any.at[pl.ds(view, 1)], weight_ref)), sems
    )
    for copy in copies:
        copy.start()
    carry[...] = jnp.zeros_like(carry)
    token_ref[...] = jnp.zeros_like(token_ref)
    for copy in copies:
        copy.wait()

    def one_block(block, _):
        weight_rows[...] = weight_ref[:, block_cells(block), :]
        shear(field, left_pad, diff_pad, index_ref, weight_rows, block, (0,), width // LANES)
        transmit(u_ref, n_ref, field, mat, carry, block, None)
        return 0

    lax.fori_loop(0, slab // BLOCK, one_block, 0)


def forward_other(view, column, weights, mat, left_pad, diff_pad, after):
    _, slab, width = weights.shape
    values = pltpu.VMEM((1, slab * SUB, width), F32)
    return pl.pallas_call(
        functools.partial(forward_other_kernel, view),
        in_specs=[ANY, ANY] + [VMEM] * 4,
        out_specs=[VMEM] * 3,
        out_shape=[values, values, pltpu.VMEM((SUB, LANES), F32)],
        scratch_shapes=[
            pltpu.VMEM((1, slab, width), F32),
            pltpu.VMEM((1, BLOCK, width), F32),
            pltpu.VMEM((1, ROWS, width), F32),
            pltpu.VMEM((1, SUB, width), F32),
            pltpu.SMEM((1, slab, LANES), jnp.int32),
            pltpu.SemaphoreType.DMA((2,)),
        ],
        compiler_params=pltpu.CompilerParams(vmem_limit_bytes=8 * MIB),
        name="forward_other",
    )(column, weights, mat, left_pad, diff_pad, after)


def line_rows(tile, base, masks):
    shape = masks[0].shape
    return select_line(masks, [jnp.broadcast_to(tile[base + 1 + k : base + 2 + k], shape) for k in range(len(masks))])


def ordered_factors(factors, rows, step):
    count = len(factors)
    before, behind = [None] * count, [None] * count
    run = jnp.ones_like(factors[0])
    for i in range(count):
        before[i] = run
        run = run * factors[i]
    run = jnp.ones_like(factors[0])
    for i in reversed(range(count)):
        behind[i] = run
        run = run * factors[i]

    def incident(tile):
        result = jnp.broadcast_to(tile[0:1], tile.shape)
        for base in range(step, SUB, step):
            result = jnp.where(rows >= base, jnp.broadcast_to(tile[base : base + 1], tile.shape), result)
        return result

    return [incident(before[i]) * behind[i] for i in range(count)]


def row_masks(const_ref, emissions, width):
    tile = const_ref[LINE_ROWS]
    return [jnp.concatenate([tile] * (width // LANES), axis=1) == k for k in range(emissions)]


def put_in_order(scratch, place, refs):
    for r, ref in enumerate(refs):
        scratch[place ^ r] = ref[...]


def merge_kernel(emissions, const_ref, *refs):
    near_refs, (out_ref, near) = refs[:NEAR], refs[-2:]
    put_in_order(near, lax.axis_index("near"), near_refs)
    depth, width = out_ref.shape
    masks = row_masks(const_ref, emissions, width)
    factors = [near[i, 0:SUB, :] for i in range(NEAR)]
    around = ordered_factors(factors, row_ids(width), emissions + 1)
    total = factors[0]
    for i in range(1, NEAR):
        total = total * factors[i]
    out_ref[0:SUB, :] = total
    for v in range(depth // SUB - 1):
        span = slice((v + 1) * SUB, (v + 2) * SUB)
        signal = jnp.zeros((SUB, width), F32)
        for i in range(NEAR):
            signal = signal + near[i, span, :] * line_rows(around[i], v * (emissions + 1), masks)
        out_ref[span, :] = signal


def merge(near, const, emissions, tokens):
    shape = near[0].shape
    return pl.pallas_call(
        functools.partial(merge_kernel, emissions),
        in_specs=[VMEM] * (1 + NEAR + len(tokens)),
        out_specs=VMEM,
        out_shape=pltpu.VMEM(shape, F32),
        scratch_shapes=[pltpu.VMEM((NEAR,) + shape, F32)],
        compiler_params=pltpu.CompilerParams(vmem_limit_bytes=2 * MIB),
        name="merge",
    )(const, *near, *tokens)


def misfit_kernel(emissions, groups, const_ref, target_ref, *refs):
    near_refs, refs = refs[:NEAR], refs[NEAR:]
    far_refs, refs = refs[:groups], refs[-3 - NEAR :]
    out_refs, (near, far, result) = refs[:NEAR], refs[NEAR:]
    depth, width = near_refs[0].shape
    views = depth // SUB - 1
    place, group = lax.axis_index("near"), lax.axis_index("far")
    put_in_order(near, place, near_refs)
    put_in_order(far, group, far_refs)
    rows = row_ids(width)
    masks = row_masks(const_ref, emissions, width)
    zero = jnp.zeros((SUB, width), F32)
    far_around = ordered_factors([far[g, 0:SUB, :] for g in range(groups)], rows, emissions + 1)
    outside = zero
    for g in range(groups):
        outside = outside + jnp.where(g == group, far_around[g], 0.0)
    factors = [near[i, 0:SUB, :] for i in range(NEAR)]
    around = [value * outside for value in ordered_factors(factors, rows, emissions + 1)]
    start = pl.multiple_of(place * width, LANES)
    for v in range(views):
        base = v * (emissions + 1)
        span = slice((v + 1) * SUB, (v + 2) * SUB)
        far_parts = [far[g, span, :] * line_rows(far_around[g], base, masks) for g in range(groups)]
        parts = [near[i, span, :] * line_rows(around[i], base, masks) for i in range(NEAR)]
        signal = zero
        for g in range(groups):
            signal = signal + far_parts[g]
        misfit = signal - target_ref[v * SUB : (v + 1) * SUB, pl.ds(start, width)]

        def by_energy(value):
            value = misfit * value
            return [jnp.sum(jnp.where(mask, value, 0.0), axis=0, keepdims=True) for mask in masks]

        def plus(one, two):
            return [a + b for a, b in zip(one, two)]

        lower, upper = zero, zero
        for g in range(groups):
            lower = lower + jnp.where(g < group, far_parts[g], 0.0)
            upper = upper + jnp.where(g > group, far_parts[g], 0.0)
        earlier, later = by_energy(lower), by_energy(upper)
        sums = [by_energy(part) for part in parts]
        earliers, laters = [], [None] * NEAR
        for i in range(NEAR):
            earliers.append(earlier)
            earlier = plus(earlier, sums[i])
        for i in reversed(range(NEAR)):
            later = plus(later, sums[i])
            total = later[0]
            for value in later[1:]:
                total = total + value
            laters[i] = total
        at = 2 * v * SUB
        for i in range(NEAR):
            tile = around[i] * factors[i]
            tile = jnp.where(rows == base, laters[i], tile)
            for k in range(emissions):
                tile = jnp.where(rows == SUB // 2 - base + k, earliers[i][k], tile)
            result[i, v * SUB : (v + 1) * SUB, :] = tile
        for ref in out_refs:
            ref[at : at + SUB, :] = signal
    for r in range(NEAR):
        for v in range(views):
            tile = result[place ^ r, v * SUB : (v + 1) * SUB, :]
            out_refs[r][(2 * v + 1) * SUB : (2 * v + 2) * SUB, :] = tile


def misfits(near, far, target, const, emissions, tokens):
    depth, width = near[0].shape
    views = depth // SUB - 1
    groups = len(far)
    return pl.pallas_call(
        functools.partial(misfit_kernel, emissions, groups),
        in_specs=[VMEM] * (2 + NEAR + groups + len(tokens)),
        out_specs=[VMEM] * NEAR,
        out_shape=[pltpu.VMEM((2 * views * SUB, width), F32)] * NEAR,
        scratch_shapes=[
            pltpu.VMEM((NEAR, depth, width), F32),
            pltpu.VMEM((groups, depth, width), F32),
            pltpu.VMEM((NEAR, views * SUB, width), F32),
        ],
        compiler_params=pltpu.CompilerParams(vmem_limit_bytes=4 * MIB),
        name="misfit",
    )(const, target, *near, *far, *tokens)


def assemble_kernel(target_ref, *refs):
    result_refs, (package_ref, signal_ref) = refs[:NEAR], refs[NEAR:]
    share = result_refs[0].shape[1]
    place = lax.axis_index("near")
    for r in range(NEAR):
        span = pl.ds(pl.multiple_of((place ^ r) * share, LANES), share)
        for v in range(signal_ref.shape[0]):
            at = 2 * v * SUB
            signal = result_refs[r][at : at + SUB, :]
            signal_ref[v, :, :, span] = signal.reshape(SUB, 1, share)
            package_ref[at : at + SUB, span] = signal - target_ref[v * SUB : (v + 1) * SUB, span]
            package_ref[at + SUB : at + 2 * SUB, span] = result_refs[r][at + SUB : at + 2 * SUB, :]


def assemble(results, target, out_shape):
    depth, share = results[0].shape
    return pl.pallas_call(
        assemble_kernel,
        in_specs=[VMEM] * (1 + NEAR),
        out_specs=[VMEM] * 2,
        out_shape=[pltpu.VMEM((depth, share * NEAR), F32), jax.ShapeDtypeStruct(out_shape, F32)],
        compiler_params=pltpu.CompilerParams(vmem_limit_bytes=2 * MIB),
        name="assemble",
    )(target, *results)


def backward_kernel(views, cells, finish, prior, const_ref, package_ref, index_any, weight_any, *refs):
    u_refs, refs = refs[: len(views)], refs[len(views) :]
    n_refs, refs = refs[: len(views)], refs[len(views) :]
    if prior:
        prior_any, prior_left, prior_diff = refs[:3]
        refs = refs[3:]
    if finish:
        grad_hbm, refs = refs[0], refs[1:]
        left_pad, diff_pad, cell_ref, grad_ref, refs = refs[:4] + (refs[4:],)
    else:
        left_pad, diff_pad, refs = refs[:2] + (refs[2:],)
    mat, gain, carry, scaled, weight_ref, weight_rows, index_ref = refs[:7]
    prior_ref, sems = refs[7] if prior else None, refs[-1]
    count, slab, width = weight_ref.shape
    emissions = SCALE - 1
    tiles = width // LANES
    blocks = slab // BLOCK
    lanes, rows = lane_ids(), row_ids()
    margin = 2 * LANES
    pairs = [(index_any, index_ref), (weight_any, weight_ref)]
    if prior:
        pairs.append((prior_any, prior_ref))
    copies = copies_in(pairs, sems.at[pl.ds(blocks, len(pairs))])
    for copy in copies:
        copy.start()
    masks = [const_ref[LINE_LANES] == k for k in range(emissions)]
    columns = [const_ref[k] for k in range(emissions + 1)]
    fill_matrix(mat, -columns[0], select_line(masks, columns[1:]), True, False)
    masks = [const_ref[LINE_ROWS] == k for k in range(emissions)]
    scale = const_ref[SCALE]
    columns = [column * cells for column in columns]
    for v in range(count):
        base = v * (emissions + 1)
        for j in range(tiles):
            span = slice(j * LANES, (j + 1) * LANES)
            tile = package_ref[(2 * v + 1) * SUB : (2 * v + 2) * SUB, span]
            gain[v, :, span] = package_ref[2 * v * SUB : (2 * v + 1) * SUB, span] * scale * line_rows(tile, base, masks)
            back = columns[0] * jnp.broadcast_to(tile[base : base + 1], tile.shape)
            for k in range(emissions):
                row = SUB // 2 - base + k
                back = back + columns[k + 1] * jnp.broadcast_to(tile[row : row + 1], tile.shape)
            carry[v, :, span] = back
    for ref in (left_pad, diff_pad):
        ref[:, :, :, 0:margin] = jnp.zeros(ref.shape[:3] + (margin,), F32)
        ref[:, :, :, margin + width + LANES :] = jnp.zeros(ref.shape[:3] + (margin,), F32)

    def one_block(block, _):
        slot = 0 if finish else block * BLOCK
        for v in range(count):
            u_ref, n_ref, at = u_refs[v], n_refs[v], views[v]
            for c in range(width // CHUNK):
                span = slice(c * CHUNK, (c + 1) * CHUNK)
                factor = gain[v, :, span][None]
                weighted = n_ref[at, block_rows(block), span].reshape(BLOCK, SUB, CHUNK) * factor
                direct = u_ref[at, block_rows(block), span].reshape(BLOCK, SUB, CHUNK) * factor
                lines, total = multiply(mat, weighted.reshape(ROWS, CHUNK))
                before = carry[v, :, span]
                lines = lines.reshape(BLOCK, SUB, CHUNK) + before[None]
                scaled[v, :, span] = (direct - lines).reshape(ROWS, CHUNK)
                carry[v, :, span] = before + total

        @pl.when(block == 0)
        def _():
            for copy in copies:
                copy.wait()

        weight_rows[...] = weight_ref[:, block_cells(block), :]
        for v in range(count):
            for d in range(BLOCK):
                _, rest = shift_of(index_ref, v, block * BLOCK + d, width)
                stay = lanes >= rest
                plain = [scaled[v, d * SUB : (d + 1) * SUB, j * LANES : (j + 1) * LANES] for j in range(tiles)]
                moved = [plain[j] * weight_rows[v, d : d + 1, j * LANES : (j + 1) * LANES] for j in range(tiles)]
                for ref, values in ((left_pad, plain), (diff_pad, moved)):
                    turned = [jnp.zeros((SUB, LANES), F32)]
                    turned += [pltpu.roll(value, rest, 1) for value in values]
                    turned += [jnp.zeros((SUB, LANES), F32)]
                    for j in range(tiles + 1):
                        span = slice(margin + j * LANES, margin + (j + 1) * LANES)
                        ref[v, slot + d, :, span] = jnp.where(stay, turned[j + 1], turned[j])
        if not finish:
            return 0
        for d in range(BLOCK):
            cell = block * BLOCK + d

            def gathered(ref, prior_pad):
                sources = [(ref, index_ref, v, d) for v in range(count)]
                if prior:
                    sources += [(prior_pad, prior_ref, v, cell) for v in range(prior)]
                sums = [None] * (tiles + 2)
                for pad, index, v, at in sources:
                    whole, _ = shift_of(index, v, cell, width)
                    for j in range(tiles + 2):
                        start = pl.multiple_of((2 + j - whole) * LANES, LANES)
                        value = pad[v, at, :, pl.ds(start, LANES)]
                        sums[j] = value if sums[j] is None else sums[j] + value
                return sums

            left = gathered(left_pad, prior_left if prior else None)
            diff = gathered(diff_pad, prior_diff if prior else None)
            left = [left[j] - diff[j] for j in range(tiles + 2)]

            def folded(sums):
                low = jnp.sum(sums[0], axis=1, keepdims=True)
                beyond = sums[tiles + 1] + jnp.where(lanes == LANES - 1, sums[tiles], 0.0)
                high = jnp.sum(beyond, axis=1, keepdims=True)
                core = sums[1 : tiles + 1]
                core[0] = core[0] + jnp.where(lanes == 0, low, 0.0)
                core[-1] = jnp.where(lanes == LANES - 1, 0.0, core[-1] + jnp.where(lanes == LANES - 2, high, 0.0))
                return core

            left, diff = folded(left), folded(diff)
            turned = [jnp.zeros((SUB, LANES), F32)] + [pltpu.roll(value, 1, 1) for value in diff]
            for j in range(tiles):
                value = left[j] + jnp.where(lanes == 0, turned[j], turned[j + 1])
                cell_ref[d, :, j * LANES : (j + 1) * LANES] = value
        grad_ref[block] = jnp.swapaxes(cell_ref[...], 0, 1)
        for b in range(blocks):

            @pl.when(block == b)
            def _():
                out_copies[b].start()

        return 0

    if finish:
        out_copies = [
            pltpu.make_async_copy(grad_ref.at[b], grad_hbm.at[:, pl.ds(b * BLOCK, BLOCK), :], sems.at[b])
            for b in range(blocks)
        ]
    lax.fori_loop(0, blocks, one_block, 0)
    if finish:
        for copy in out_copies:
            copy.wait()


def backward(package, const, column, weights, pieces, cells, finish, prior):
    views, slab, width = weights.shape
    blocks = slab // BLOCK
    line = pltpu.VMEM((views, SUB, width), F32)
    depth = BLOCK if finish else slab
    padded = pltpu.VMEM((views, depth, SUB, width + 5 * LANES), F32)
    scratch = [
        pltpu.VMEM(MATRIX, BF16),
        line,
        line,
        pltpu.VMEM((views, ROWS, width), F32),
        pltpu.VMEM((views, slab, width), F32),
        pltpu.VMEM((views, BLOCK, width), F32),
        pltpu.SMEM((views, slab, LANES), jnp.int32),
    ]
    in_specs = [VMEM, VMEM, ANY, ANY] + [VMEM] * (2 * views)
    if prior:
        in_specs += [ANY, VMEM, VMEM]
        scratch.append(pltpu.SMEM((views, slab, LANES), jnp.int32))
    scratch.append(pltpu.SemaphoreType.DMA((blocks + 3,)))
    if finish:
        scratch = [padded, padded, pltpu.VMEM((BLOCK, SUB, width), F32), pltpu.VMEM((blocks, SUB, BLOCK, width), F32)] + scratch
    return pl.pallas_call(
        functools.partial(
            backward_kernel, tuple(at for _, _, at in pieces), cells, finish, views if prior else 0
        ),
        in_specs=in_specs,
        out_specs=[HBM] if finish else [VMEM, VMEM],
        out_shape=[pltpu.HBM((SUB, slab, width), F32)] if finish else [padded, padded],
        scratch_shapes=scratch,
        compiler_params=pltpu.CompilerParams(vmem_limit_bytes=16 * MIB),
        name="backward_last" if finish else "backward_first",
    )(const, package, column, weights, *[u for u, _, _ in pieces], *[n for _, n, _ in pieces], *(prior or ()))


def body(concentration, shear_index, shear_weight, attenuation, yields, line_energy, measured):
    elements, _, slab, width = concentration.shape
    views = shear_weight.shape[0]
    emissions = attenuation.shape[0] - 1
    groups = lax.axis_size("far")
    both = lax.axis_size("views") == 2
    cells = float(slab * groups * NEAR)
    conc = concentration.reshape(elements, slab, width)
    scalars = (attenuation, line_energy, yields)
    column = shear_index[:, :, width // 2 : width // 2 + LANES]

    def to_other(value):
        return lax.ppermute(value, "views", [(0, 1), (1, 0)])

    def to_near(value, r):
        return lax.ppermute(value, "near", [(s, s ^ r) for s in range(NEAR)]) if r else value

    def to_far(value, r):
        return lax.ppermute(value, "far", [(s, s ^ r) for s in range(groups)]) if r else value

    if both:
        other_column, other_weight = to_other(column), to_other(shear_weight)
    u, n, const, target, mat, left_pad, diff_pad, *states = forward(
        conc, column, shear_weight, scalars, measured, cells
    )
    near = [to_near(states[r], r) for r in range(NEAR)]
    others, tokens = [], [(), ()]
    if both:
        after = states[0]
        others.append(forward_other(0, other_column, other_weight, mat, left_pad, diff_pad, after))
        tokens[0] = (others[0][2],)
    merged = merge(near, const, emissions, tokens[0])
    far = [to_far(merged, r) for r in range(groups)]
    if both:
        others.append(forward_other(1, other_column, other_weight, mat, left_pad, diff_pad, merged))
        tokens[1] = (others[1][2],)
    results = misfits(near, far, target, const, emissions, tokens[1])
    package, signal = assemble([to_near(results[r], r) for r in range(NEAR)], target, measured.shape)
    own = [(u, n, v) for v in range(views)]
    if both:
        other_package = to_other(package)
        pads = backward(package, const, column, shear_weight, own, cells, False, None)
        pieces = [(other[0], other[1], 0) for other in others]
        (gradient,) = backward(
            other_package, const, other_column, other_weight, pieces, cells, True, (column, *pads)
        )
    else:
        (gradient,) = backward(package, const, column, shear_weight, own, cells, True, None)
        gradient = lax.psum(gradient, "views")
    return gradient.reshape(concentration.shape), signal


def solution(mesh):
    views, depth = mesh.shape["views"], mesh.shape["depth"]
    devices = mesh.devices.reshape(views, depth // NEAR, NEAR)
    split = jax.sharding.Mesh(devices, ("views", "far", "near"))
    depths = ("far", "near")
    return jax.shard_map(
        body,
        mesh=split,
        in_specs=(
            P(None, None, depths, None),
            P("views", depths, None),
            P("views", depths, None),
            P(),
            P(),
            P(),
            P("views", None, None, None),
        ),
        out_specs=(P(None, None, depths, None), P("views", None, None, None)),
        check_vma=False,
    )
```

```python
import functools

import jax
import jax.numpy as jnp
from jax import lax
from jax.experimental import pallas as pl
from jax.experimental.pallas import tpu as pltpu
from jax.sharding import PartitionSpec as P

LANES = 128
SUB = 8
BLOCK = 8
ROWS = BLOCK * SUB
NEAR = 4
CHUNK = 256
MIB = 1024 * 1024
F32 = jnp.float32
BF16 = jnp.bfloat16
HBM = pl.BlockSpec(memory_space=pltpu.HBM)
VMEM = pl.BlockSpec(memory_space=pltpu.VMEM)
SCALE, LINE_ROWS, LINE_LANES = 4, 5, 6
ANY = pl.BlockSpec(memory_space=pl.ANY)


def in_hbm(value):
    return pltpu.with_memory_space_constraint(value, pltpu.HBM)


def lane_ids(width=LANES):
    return lax.broadcasted_iota(jnp.int32, (SUB, width), 1)


def row_ids(width=LANES):
    return lax.broadcasted_iota(jnp.int32, (SUB, width), 0)


def tile_of(values, ids):
    tile = jnp.zeros(ids.shape, F32)
    for e in range(SUB):
        tile = jnp.where(ids == e, values[e], tile)
    return tile


def select_line(masks, values):
    result = values[0]
    for mask, value in zip(masks[1:], values[1:]):
        result = jnp.where(mask, value, result)
    return result


def fill_matrix(mat_ref, first_tile, second_tile, first_incl, second_incl):
    depth = (lane_ids() & (ROWS - 1)) >> 3
    tiles = []
    for d in range(BLOCK):
        one = jnp.where(depth <= d if first_incl else depth < d, first_tile, 0.0)
        two = jnp.where(depth <= d if second_incl else depth < d, second_tile, 0.0)
        tiles.append(one + two)
    tiles.append(first_tile + second_tile)
    tiles.append(jnp.zeros((SUB, LANES), F32))
    whole = jnp.concatenate(tiles, axis=0)
    high = whole.astype(BF16)
    mat_ref[:, 0:LANES] = high
    mat_ref[:, LANES : 2 * LANES] = (whole - high.astype(F32)).astype(BF16)


def multiply(mat_ref, values):
    high = values.astype(BF16)
    low = (values - high.astype(F32)).astype(BF16)
    stacked = jnp.concatenate([high, low, high], axis=0)
    product = jnp.dot(mat_ref[:, 0 : 3 * ROWS], stacked, preferred_element_type=F32)
    return product[0:ROWS], product[ROWS : ROWS + SUB]


MATRIX = (ROWS + 2 * SUB, 2 * LANES)


def copies_in(pairs, sems):
    return [pltpu.make_async_copy(source, target, sems.at[i]) for i, (source, target) in enumerate(pairs)]


def block_rows(block):
    return pl.ds(pl.multiple_of(block * ROWS, ROWS), ROWS)


def block_cells(block):
    return pl.ds(pl.multiple_of(block * BLOCK, BLOCK), BLOCK)


def shift_of(index_ref, v, cell, width):
    offset = index_ref[v, cell, 0] - (width // 2 - LANES)
    return offset >> 7, offset & (LANES - 1)


def shear(field, left_pad, diff_pad, index_ref, weight_ref, block, views, tiles, first=0):
    lanes = lane_ids()
    for i, v in enumerate(views):
        for d in range(BLOCK):
            cell = block * BLOCK + d
            whole, rest = shift_of(index_ref, v, cell - first, tiles * LANES)
            turn = (LANES - rest) & (LANES - 1)
            stay = lanes < LANES - rest

            def sheared(ref):
                turned = []
                for j in range(tiles + 1):
                    start = pl.multiple_of((whole + j) * LANES, LANES)
                    turned.append(pltpu.roll(ref[cell, :, pl.ds(start, LANES)], turn, 1))
                return [jnp.where(stay, turned[j], turned[j + 1]) for j in range(tiles)]

            left, diff = sheared(left_pad), sheared(diff_pad)
            for j in range(tiles):
                span = slice(j * LANES, (j + 1) * LANES)
                field[i, d * SUB : (d + 1) * SUB, span] = left[j] + weight_ref[i, d : d + 1, span] * diff[j]


def transmit(u_ref, n_ref, field, mat, carry, block, sums):
    views, _, width = field.shape
    for v in range(views):
        for c in range(width // CHUNK):
            span = slice(c * CHUNK, (c + 1) * CHUNK)
            value = field[v, :, span]
            lines, total = multiply(mat, value)
            before = carry[v, :, span]
            through = jnp.exp(lines.reshape(BLOCK, SUB, CHUNK) + before[None])
            value = value.reshape(BLOCK, SUB, CHUNK)
            emit = value * through
            u_ref[v, block_rows(block), span] = through.reshape(ROWS, CHUNK)
            n_ref[v, block_rows(block), span] = emit.reshape(ROWS, CHUNK)
            carry[v, :, span] = before + total
            if sums:
                sums[0][v, :, span] += jnp.sum(value, axis=0)
                sums[1][v, :, span] += jnp.sum(emit, axis=0)


def forward_kernel(cells, *refs):
    att_hbm, line_hbm, yield_hbm, index_hbm, conc_hbm, weight_hbm, measured_hbm = refs[:7]
    u_ref, n_ref, const_ref, target_ref, mat, left_pad, diff_pad, column_ref = refs[7:15]
    state_refs = refs[15:17]
    refs = refs[17:]
    conc_ref, weight_ref, weight_rows, field, carry, field_sum, emit_sum, measured_ref = refs[:8]
    att_ref, line_ref, yield_ref, index_ref, sems = refs[8:]
    views, slab, width = weight_ref.shape
    emissions = att_ref.shape[0] - 1
    tiles = width // LANES
    blocks = slab // BLOCK
    lanes, rows = lane_ids(), row_ids()
    conc_copies = [
        pltpu.make_async_copy(
            conc_hbm.at[:, pl.ds(b * BLOCK, BLOCK), :], conc_ref.at[:, pl.ds(b * BLOCK, BLOCK), :], sems.at[b]
        )
        for b in range(blocks)
    ]
    pairs = [
        (att_hbm, att_ref),
        (line_hbm, line_ref),
        (yield_hbm, yield_ref),
        (index_hbm.at[:, :, pl.ds(width // 2, LANES)], index_ref),
        (weight_hbm, weight_ref),
        (measured_hbm, measured_ref),
        (index_hbm.at[:, :, pl.ds(width // 2, LANES)], column_ref),
    ]
    copies = copies_in(pairs, sems.at[pl.ds(blocks, len(pairs))])
    for copy in conc_copies[:1] + copies[:4] + conc_copies[1:] + copies[4:]:
        copy.start()
    for ref in (carry, field_sum, emit_sum):
        ref[...] = jnp.zeros_like(ref)

    def one_block(block, _):
        for b in range(blocks):

            @pl.when(block == b)
            def _():
                conc_copies[b].wait()

        by_depth = jnp.swapaxes(conc_ref[:, block_cells(block), :], 0, 1)
        for d in range(BLOCK):
            pieces = [by_depth[d, :, j * LANES : (j + 1) * LANES] for j in range(tiles)]
            turned = [pltpu.roll(piece, LANES - 1, 1) for piece in pieces]
            after = [jnp.where(lanes < LANES - 1, turned[j], turned[min(j + 1, tiles - 1)]) for j in range(tiles)]
            steps = [after[j] - pieces[j] for j in range(tiles)]
            last_cell = jnp.broadcast_to(pieces[-1][:, LANES - 2 : LANES - 1], (SUB, LANES))
            last_step = jnp.broadcast_to(steps[-1][:, LANES - 2 : LANES - 1], (SUB, LANES))
            first_cell = jnp.broadcast_to(pieces[0][:, 0:1], (SUB, LANES))
            first_step = jnp.broadcast_to(steps[0][:, 0:1], (SUB, LANES))
            pieces[-1] = jnp.where(lanes < LANES - 1, pieces[-1], last_cell)
            steps[-1] = jnp.where(lanes < LANES - 1, steps[-1], last_step)
            pieces = [first_cell] + pieces + [last_cell, last_cell]
            steps = [first_step] + steps + [last_step, last_step]
            for j in range(tiles + 3):
                left_pad[block * BLOCK + d, :, j * LANES : (j + 1) * LANES] = pieces[j]
                diff_pad[block * BLOCK + d, :, j * LANES : (j + 1) * LANES] = steps[j]

        @pl.when(block == 0)
        def _():
            for copy in copies:
                copy.wait()
            line_by_row = tile_of([line_ref[e].astype(F32) for e in range(SUB)], rows)
            masks = [line_by_row == k for k in range(emissions)]
            by_lane = [tile_of([att_ref[k, e] for e in range(SUB)], lanes & 7) for k in range(emissions + 1)]
            fill_matrix(mat, -by_lane[0], select_line(masks, by_lane[1:]), False, True)
            for k in range(emissions + 1):
                const_ref[k] = tile_of([att_ref[k, e] for e in range(SUB)], rows)
            const_ref[SCALE] = tile_of([yield_ref[e] for e in range(SUB)], rows)
            const_ref[LINE_ROWS] = line_by_row
            const_ref[LINE_LANES] = tile_of([line_ref[e].astype(F32) for e in range(SUB)], lanes & 7)

        weight_rows[...] = weight_ref[:, block_cells(block), :]
        shear(field, left_pad, diff_pad, index_ref, weight_rows, block, range(views), tiles)
        transmit(u_ref, n_ref, field, mat, carry, block, (field_sum, emit_sum))
        return 0

    lax.fori_loop(0, blocks, one_block, 0)
    columns = [const_ref[k] for k in range(emissions + 1)]
    masks = [const_ref[LINE_ROWS] == k for k in range(emissions)]
    scale = const_ref[SCALE] * (1.0 / cells)
    share = width // 2
    core = lax.axis_index("near") & 1
    for r in range(2):
        for j in range(share // LANES):
            start = pl.multiple_of((core ^ r) * share + j * LANES, LANES)
            span = slice(j * LANES, (j + 1) * LANES)
            totals = jnp.zeros((SUB, LANES), F32)
            for v in range(views):
                values = field_sum[v, :, pl.ds(start, LANES)]
                sums = [jnp.sum(column * values, axis=0, keepdims=True) for column in columns]
                for k in range(emissions + 1):
                    totals = jnp.where(rows == v * (emissions + 1) + k, sums[k], totals)
                line_total = select_line(masks, [jnp.broadcast_to(value, rows.shape) for value in sums[1:]])
                signal = scale * emit_sum[v, :, pl.ds(start, LANES)] * jnp.exp(-line_total)
                state_refs[r][(v + 1) * SUB : (v + 2) * SUB, span] = signal
            state_refs[r][0:SUB, span] = jnp.exp(-totals)
    for v in range(views):
        target_ref[v * SUB : (v + 1) * SUB, :] = measured_ref[v].reshape(SUB, width)


def forward(conc, index, weights, scalars, measured, cells):
    views, slab, width = weights.shape
    attenuation, line_energy, yields = scalars
    values = pltpu.VMEM((views, slab * SUB, width), F32)
    padded = pltpu.VMEM((slab, SUB, width + 3 * LANES), F32)
    state = pltpu.VMEM(((views + 1) * SUB, width // 2), F32)
    line = pltpu.VMEM((views, SUB, width), F32)
    operands = [in_hbm(value) for value in (attenuation, line_energy, yields, index, conc, weights, measured)]
    return pl.pallas_call(
        functools.partial(forward_kernel, cells),
        in_specs=[HBM] * len(operands),
        out_specs=[VMEM] * 10,
        out_shape=[
            values,
            values,
            pltpu.VMEM((LINE_LANES + 1, SUB, LANES), F32),
            pltpu.VMEM((views * SUB, width), F32),
            pltpu.VMEM(MATRIX, BF16),
            padded,
            padded,
            pltpu.VMEM((views, slab, LANES), jnp.int32),
            state,
            state,
        ],
        scratch_shapes=[
            pltpu.VMEM((SUB, slab, width), F32),
            pltpu.VMEM((views, slab, width), F32),
            pltpu.VMEM((views, BLOCK, width), F32),
            pltpu.VMEM((views, ROWS, width), F32),
            line,
            line,
            line,
            pltpu.VMEM(measured.shape, F32),
            pltpu.SMEM(attenuation.shape, F32),
            pltpu.SMEM(line_energy.shape, jnp.int32),
            pltpu.SMEM(yields.shape, F32),
            pltpu.SMEM((views, slab, LANES), jnp.int32),
            pltpu.SemaphoreType.DMA((slab // BLOCK + 7,)),
        ],
        compiler_params=pltpu.CompilerParams(vmem_limit_bytes=16 * MIB),
        name="forward",
    )(*operands)


def forward_other_kernel(view, first, index_any, weight_ref, mat, left_pad, diff_pad, order_ref, *refs):
    u_ref, n_ref, carry, token_ref, weight_rows, field, index_ref, sem = refs[-8:]
    width = weight_ref.shape[2]
    count = index_ref.shape[1]
    copy = pltpu.make_async_copy(index_any.at[pl.ds(view, 1), pl.ds(first, count)], index_ref, sem)
    copy.start()
    token_ref[...] = jnp.zeros_like(token_ref)
    if first:
        carry[...] = refs[2][...]
    else:
        carry[...] = jnp.zeros_like(carry)
    copy.wait()

    def one_block(block, _):
        weight_rows[0] = weight_ref[view, block_cells(block), :]
        shear(field, left_pad, diff_pad, index_ref, weight_rows, block, (0,), width // LANES, first)
        transmit(u_ref, n_ref, field, mat, carry, block, None)
        return 0

    lax.fori_loop(first // BLOCK, (first + count) // BLOCK, one_block, 0)


def forward_other(view, first, count, column, weights, mat, left_pad, diff_pad, after, before):
    _, slab, width = weights.shape
    values = pltpu.VMEM((1, slab * SUB, width), F32)
    return pl.pallas_call(
        functools.partial(forward_other_kernel, view, first),
        in_specs=[ANY] + [VMEM] * (5 + len(before)),
        out_specs=[VMEM] * 4,
        out_shape=[values, values, pltpu.VMEM((1, SUB, width), F32), pltpu.VMEM((SUB, LANES), F32)],
        input_output_aliases={6: 0, 7: 1} if before else {},
        scratch_shapes=[
            pltpu.VMEM((1, BLOCK, width), F32),
            pltpu.VMEM((1, ROWS, width), F32),
            pltpu.SMEM((1, count, LANES), jnp.int32),
            pltpu.SemaphoreType.DMA,
        ],
        compiler_params=pltpu.CompilerParams(vmem_limit_bytes=8 * MIB),
        name="forward_other",
    )(column, weights, mat, left_pad, diff_pad, after, *before)


def line_rows(tile, base, masks):
    shape = masks[0].shape
    return select_line(masks, [jnp.broadcast_to(tile[base + 1 + k : base + 2 + k], shape) for k in range(len(masks))])


def incident_rows(tile, step):
    rows = row_ids(tile.shape[1])
    result = jnp.broadcast_to(tile[0:1], tile.shape)
    for base in range(step, SUB, step):
        result = jnp.where(rows >= base, jnp.broadcast_to(tile[base : base + 1], tile.shape), result)
    return result


def row_masks(const_ref, width):
    tile = const_ref[LINE_ROWS]
    return [jnp.concatenate([tile] * (width // LANES), axis=1) == k for k in range(SCALE - 1)]


def factors_of(mine, theirs, bit):
    mine_factor = jnp.where(bit == 0, theirs, incident_rows(theirs, SCALE))
    return mine_factor, jnp.where(bit == 0, incident_rows(mine, SCALE), mine)


def merged_state(mine, theirs, bit, masks):
    mine_factor, theirs_factor = factors_of(mine[0:SUB], theirs[0:SUB], bit)
    result = [mine[0:SUB] * theirs[0:SUB]]
    for v in range(mine.shape[0] // SUB - 1):
        span = slice((v + 1) * SUB, (v + 2) * SUB)
        result.append(
            mine[span] * line_rows(mine_factor, v * SCALE, masks)
            + theirs[span] * line_rows(theirs_factor, v * SCALE, masks)
        )
    return result


def weighted_rows(factor, state, misfits, masks):
    rows = row_ids(state.shape[1])
    result = jnp.zeros((SUB, state.shape[1]), F32)
    for v, misfit in enumerate(misfits):
        base = v * SCALE
        value = misfit * state[(v + 1) * SUB : (v + 2) * SUB] * line_rows(factor, base, masks)
        whole = None
        for k, mask in enumerate(masks):
            part = jnp.sum(jnp.where(mask, value, 0.0), axis=0, keepdims=True)
            result = jnp.where(rows == base + 1 + k, part, result)
            whole = part if whole is None else whole + part
        result = jnp.where(rows == base, whole, result)
    return result


def children(factor, sums, mine, theirs, bit, misfits, masks):
    mine_factor, theirs_factor = factors_of(mine[0:SUB], theirs[0:SUB], bit)
    if factor is not None:
        mine_factor, theirs_factor = factor * mine_factor, factor * theirs_factor
    behind = (row_ids(mine.shape[1]) & (SCALE - 1)) == 0
    mine_sums = jnp.where(behind == (bit == 0), weighted_rows(theirs_factor, theirs, misfits, masks), 0.0)
    theirs_sums = jnp.where(behind == (bit == 1), weighted_rows(mine_factor, mine, misfits, masks), 0.0)
    if sums is not None:
        mine_sums, theirs_sums = sums + mine_sums, sums + theirs_sums
    return (mine_factor, mine_sums), (theirs_factor, theirs_sums)


def call_small(kernel, name, outs, operands, scratch=()):
    return pl.pallas_call(
        kernel,
        in_specs=[VMEM] * len(operands),
        out_specs=[VMEM] * len(outs),
        out_shape=[pltpu.VMEM(shape, F32) for shape in outs],
        scratch_shapes=[pltpu.VMEM(shape, F32) for shape in scratch],
        compiler_params=pltpu.CompilerParams(vmem_limit_bytes=4 * MIB),
        name=name,
    )(*operands)


def pair_kernel(const_ref, mine_ref, theirs_ref, keep_ref, send_ref, whole):
    width = mine_ref.shape[1]
    place = lax.axis_index("near")
    state = merged_state(mine_ref[...], theirs_ref[...], place & 1, row_masks(const_ref, width))
    for i, tile in enumerate(state):
        whole[i * SUB : (i + 1) * SUB, :] = tile
    start = pl.multiple_of((place >> 1) * (width // 2), LANES)
    keep_ref[...] = whole[:, pl.ds(start, width // 2)]
    send_ref[...] = whole[:, pl.ds(pl.multiple_of(width // 2 - start, LANES), width // 2)]


def merge_kernel(axis, shift, const_ref, mine_ref, theirs_ref, *refs):
    bit = (lax.axis_index(axis) >> shift) & 1
    state = merged_state(mine_ref[...], theirs_ref[...], bit, row_masks(const_ref, mine_ref.shape[1]))
    for i, tile in enumerate(state):
        refs[-1][i * SUB : (i + 1) * SUB, :] = tile


def context_kernel(levels, const_ref, target_ref, *refs):
    states, (mine_out, theirs_out) = refs[: 2 * levels], refs[-2:]
    depth, width = states[0].shape
    views = depth // SUB - 1
    place, far = lax.axis_index("near"), lax.axis_index("far")
    bits = [place >> 1] + [(far >> shift) & 1 for shift in range(levels - 1)]
    masks = row_masks(const_ref, width)
    start = pl.multiple_of(((place & 1) * 2 + (place >> 1)) * width, LANES)
    top, bit = [ref[...] for ref in states[-2:]], bits[-1]
    signals = merged_state(top[0], top[1], bit, masks)[1:]
    misfits = [signals[v] - target_ref[v * SUB : (v + 1) * SUB, pl.ds(start, width)] for v in range(views)]
    factor, sums = None, None
    for level in reversed(range(levels)):
        mine, theirs = states[2 * level][...], states[2 * level + 1][...]
        (factor, sums), other = children(factor, sums, mine, theirs, bits[level], misfits, masks)
    for ref, tiles in ((mine_out, (factor, sums)), (theirs_out, other)):
        for i, tile in enumerate(signals + list(tiles)):
            ref[i * SUB : (i + 1) * SUB, :] = tile


def result_kernel(const_ref, target_ref, mine_ref, theirs_ref, here_ref, there_ref, mine_out, theirs_out, whole):
    width = mine_ref.shape[1]
    views = mine_ref.shape[0] // SUB - 1
    place = lax.axis_index("near")
    half = width // 2
    at = pl.multiple_of((place >> 1) * half, LANES)
    whole[:, pl.ds(at, half)] = here_ref[...]
    whole[:, pl.ds(pl.multiple_of(half - at, LANES), half)] = there_ref[...]
    masks = row_masks(const_ref, width)
    start = pl.multiple_of((place & 1) * width, LANES)
    signals = [whole[v * SUB : (v + 1) * SUB, :] for v in range(views)]
    misfits = [signals[v] - target_ref[v * SUB : (v + 1) * SUB, pl.ds(start, width)] for v in range(views)]
    factor, sums = whole[views * SUB : (views + 1) * SUB, :], whole[(views + 1) * SUB : (views + 2) * SUB, :]
    mine, theirs = mine_ref[...], theirs_ref[...]
    contexts = children(factor, sums, mine, theirs, place & 1, misfits, masks)
    behind = (row_ids(width) & (SCALE - 1)) == 0
    for ref, state, (factor, sums) in ((mine_out, mine, contexts[0]), (theirs_out, theirs, contexts[1])):
        own = jnp.where(behind, weighted_rows(factor, state, misfits, masks), 0.0)
        for i, tile in enumerate(signals + [factor * state[0:SUB], sums + own]):
            ref[i * SUB : (i + 1) * SUB, :] = tile


def assemble_kernel(target_ref, here_ref, there_ref, package_ref, signal_ref):
    half = here_ref.shape[1]
    views = signal_ref.shape[0] // SUB
    at = pl.multiple_of((lax.axis_index("near") & 1) * half, LANES)
    for ref, start in ((here_ref, at), (there_ref, pl.multiple_of(half - at, LANES))):
        span = pl.ds(start, half)
        signal_ref[:, span] = ref[0 : views * SUB, :]
        package_ref[0 : views * SUB, span] = ref[0 : views * SUB, :] - target_ref[:, span]
        package_ref[views * SUB :, span] = ref[views * SUB :, :]


def backward_kernel(views, cells, finish, prior, const_ref, package_ref, index_any, weight_any, *refs):
    if finish:
        signal_ref, refs = refs[0], refs[1:]
    u_refs, refs = refs[: len(views)], refs[len(views) :]
    n_refs, refs = refs[: len(views)], refs[len(views) :]
    if prior:
        prior_any, prior_left, prior_diff = refs[:3]
        refs = refs[3:]
    if finish:
        grad_hbm, signal_hbm, refs = refs[0], refs[1], refs[2:]
        left_pad, diff_pad, cell_ref, grad_ref, signal_rows, refs = refs[:5] + (refs[5:],)
    else:
        left_pad, diff_pad, refs = refs[:2] + (refs[2:],)
    mat, gain, carry, scaled, weight_ref, weight_rows, index_ref = refs[:7]
    prior_ref, sems = refs[7] if prior else None, refs[-1]
    count, slab, width = weight_ref.shape
    emissions = SCALE - 1
    tiles = width // LANES
    blocks = slab // BLOCK
    lanes, rows = lane_ids(), row_ids()
    margin = 2 * LANES
    pairs = [(index_any, index_ref), (weight_any, weight_ref)]
    if prior:
        pairs.append((prior_any, prior_ref))
    copies = copies_in(pairs, sems.at[pl.ds(blocks, len(pairs))])
    for copy in copies:
        copy.start()
    if finish:
        for v in range(signal_rows.shape[0]):
            signal_rows[v] = signal_ref[v * SUB : (v + 1) * SUB, :].reshape(SUB, 1, width)
        signal_copy = pltpu.make_async_copy(signal_rows, signal_hbm, sems.at[blocks + 3])
        signal_copy.start()
    masks = [const_ref[LINE_LANES] == k for k in range(emissions)]
    columns = [const_ref[k] for k in range(emissions + 1)]
    fill_matrix(mat, -columns[0], select_line(masks, columns[1:]), True, False)
    masks = [const_ref[LINE_ROWS] == k for k in range(emissions)]
    scale = const_ref[SCALE]
    columns = [column * cells for column in columns]
    for j in range(tiles):
        span = slice(j * LANES, (j + 1) * LANES)
        factor = package_ref[count * SUB : (count + 1) * SUB, span]
        sums = package_ref[(count + 1) * SUB : (count + 2) * SUB, span]
        for v in range(count):
            base = v * SCALE
            gain[v, :, span] = package_ref[v * SUB : (v + 1) * SUB, span] * scale * line_rows(factor, base, masks)
            back = columns[0] * jnp.broadcast_to(sums[base : base + 1], rows.shape)
            for k in range(1, emissions + 1):
                back = back + columns[k] * jnp.broadcast_to(sums[base + k : base + k + 1], rows.shape)
            carry[v, :, span] = back
    for ref in (left_pad, diff_pad):
        ref[:, :, :, 0:margin] = jnp.zeros(ref.shape[:3] + (margin,), F32)
        ref[:, :, :, margin + width + LANES :] = jnp.zeros(ref.shape[:3] + (margin,), F32)

    def one_block(block, _):
        slot = 0 if finish else block * BLOCK
        for v in range(count):
            u_ref, n_ref, at = u_refs[v], n_refs[v], views[v]
            for c in range(width // CHUNK):
                span = slice(c * CHUNK, (c + 1) * CHUNK)
                factor = gain[v, :, span][None]
                weighted = n_ref[at, block_rows(block), span].reshape(BLOCK, SUB, CHUNK) * factor
                direct = u_ref[at, block_rows(block), span].reshape(BLOCK, SUB, CHUNK) * factor
                lines, total = multiply(mat, weighted.reshape(ROWS, CHUNK))
                before = carry[v, :, span]
                lines = lines.reshape(BLOCK, SUB, CHUNK) + before[None]
                scaled[v, :, span] = (direct - lines).reshape(ROWS, CHUNK)
                carry[v, :, span] = before + total

        @pl.when(block == 0)
        def _():
            for copy in copies:
                copy.wait()

        weight_rows[...] = weight_ref[:, block_cells(block), :]
        for v in range(count):
            for d in range(BLOCK):
                _, rest = shift_of(index_ref, v, block * BLOCK + d, width)
                stay = lanes >= rest
                plain = [scaled[v, d * SUB : (d + 1) * SUB, j * LANES : (j + 1) * LANES] for j in range(tiles)]
                moved = [plain[j] * weight_rows[v, d : d + 1, j * LANES : (j + 1) * LANES] for j in range(tiles)]
                for ref, values in ((left_pad, plain), (diff_pad, moved)):
                    turned = [jnp.zeros((SUB, LANES), F32)]
                    turned += [pltpu.roll(value, rest, 1) for value in values]
                    turned += [jnp.zeros((SUB, LANES), F32)]
                    for j in range(tiles + 1):
                        span = slice(margin + j * LANES, margin + (j + 1) * LANES)
                        ref[v, slot + d, :, span] = jnp.where(stay, turned[j + 1], turned[j])
        if not finish:
            return 0
        for d in range(BLOCK):
            cell = block * BLOCK + d

            def gathered(ref, prior_pad):
                sources = [(ref, index_ref, v, d) for v in range(count)]
                if prior:
                    sources += [(prior_pad, prior_ref, v, cell) for v in range(prior)]
                sums = [None] * (tiles + 2)
                for pad, index, v, at in sources:
                    whole, _ = shift_of(index, v, cell, width)
                    for j in range(tiles + 2):
                        start = pl.multiple_of((2 + j - whole) * LANES, LANES)
                        value = pad[v, at, :, pl.ds(start, LANES)]
                        sums[j] = value if sums[j] is None else sums[j] + value
                return sums

            left = gathered(left_pad, prior_left if prior else None)
            diff = gathered(diff_pad, prior_diff if prior else None)
            left = [left[j] - diff[j] for j in range(tiles + 2)]

            def folded(sums):
                low = jnp.sum(sums[0], axis=1, keepdims=True)
                beyond = sums[tiles + 1] + jnp.where(lanes == LANES - 1, sums[tiles], 0.0)
                high = jnp.sum(beyond, axis=1, keepdims=True)
                core = sums[1 : tiles + 1]
                core[0] = core[0] + jnp.where(lanes == 0, low, 0.0)
                core[-1] = jnp.where(lanes == LANES - 1, 0.0, core[-1] + jnp.where(lanes == LANES - 2, high, 0.0))
                return core

            left, diff = folded(left), folded(diff)
            turned = [jnp.zeros((SUB, LANES), F32)] + [pltpu.roll(value, 1, 1) for value in diff]
            for j in range(tiles):
                value = left[j] + jnp.where(lanes == 0, turned[j], turned[j + 1])
                cell_ref[d, :, j * LANES : (j + 1) * LANES] = value
        grad_ref[block] = jnp.swapaxes(cell_ref[...], 0, 1)
        for b in range(blocks):

            @pl.when(block == b)
            def _():
                out_copies[b].start()

        return 0

    if finish:
        out_copies = [
            pltpu.make_async_copy(grad_ref.at[b], grad_hbm.at[:, pl.ds(b * BLOCK, BLOCK), :], sems.at[b])
            for b in range(blocks)
        ]
    lax.fori_loop(0, blocks, one_block, 0)
    if finish:
        for copy in out_copies + [signal_copy]:
            copy.wait()


def backward(package, const, column, weights, pieces, cells, signal, prior):
    finish = signal is not None
    signals = [signal[0]] if finish else []
    views, slab, width = weights.shape
    blocks = slab // BLOCK
    line = pltpu.VMEM((views, SUB, width), F32)
    depth = BLOCK if finish else slab
    padded = pltpu.VMEM((views, depth, SUB, width + 5 * LANES), F32)
    scratch = [
        pltpu.VMEM(MATRIX, BF16),
        line,
        line,
        pltpu.VMEM((views, ROWS, width), F32),
        pltpu.VMEM((views, slab, width), F32),
        pltpu.VMEM((views, BLOCK, width), F32),
        pltpu.SMEM((views, slab, LANES), jnp.int32),
    ]
    in_specs = [VMEM, VMEM, ANY, ANY] + [VMEM] * (2 * views + len(signals))
    if prior:
        in_specs += [ANY, VMEM, VMEM]
        scratch.append(pltpu.SMEM((views, slab, LANES), jnp.int32))
    scratch.append(pltpu.SemaphoreType.DMA((blocks + 4,)))
    if finish:
        scratch = [
            padded,
            padded,
            pltpu.VMEM((BLOCK, SUB, width), F32),
            pltpu.VMEM((blocks, SUB, BLOCK, width), F32),
            pltpu.VMEM(signal[1], F32),
        ] + scratch
    return pl.pallas_call(
        functools.partial(
            backward_kernel, tuple(at for _, _, at in pieces), cells, finish, views if prior else 0
        ),
        in_specs=in_specs,
        out_specs=[HBM, HBM] if finish else [VMEM, VMEM],
        out_shape=[pltpu.HBM((SUB, slab, width), F32), pltpu.HBM(signal[1], F32)] if finish else [padded, padded],
        scratch_shapes=scratch,
        compiler_params=pltpu.CompilerParams(vmem_limit_bytes=16 * MIB),
        name="backward_last" if finish else "backward_first",
    )(const, package, column, weights, *signals, *[u for u, _, _ in pieces], *[n for _, n, _ in pieces], *(prior or ()))


def body(concentration, shear_index, shear_weight, attenuation, yields, line_energy, measured):
    elements, _, slab, width = concentration.shape
    views = shear_weight.shape[0]
    emissions = attenuation.shape[0] - 1
    groups = lax.axis_size("far")
    both = lax.axis_size("views") == 2
    cells = float(slab * groups * NEAR)
    conc = concentration.reshape(elements, slab, width)
    scalars = (attenuation, line_energy, yields)

    def to_other(value):
        return lax.ppermute(value, "views", [(0, 1), (1, 0)])

    def swap(value, axis, step):
        return lax.ppermute(value, axis, [(s, s ^ step) for s in range(lax.axis_size(axis))])

    fillers = []

    def fill(after):
        if not both:
            return ()
        view, first = len(fillers) // 2, len(fillers) % 2 * (slab // 2)
        before = fillers[-1][:3] if first else ()
        pads = (mat, left_pad, diff_pad, after)
        fillers.append(forward_other(view, first, slab // 2, other_column, other_weight, *pads, before))
        return (fillers[-1][3],)

    if both:
        other_weight = to_other(shear_weight)
    u, n, const, target, mat, left_pad, diff_pad, column, mine, send = forward(
        conc, shear_index, shear_weight, scalars, measured, cells
    )
    if both:
        other_column = to_other(column)
    theirs = swap(send, "near", 1)
    half, rows = width // 2, mine.shape[0]
    quarter = (rows, half // 2)
    keep, send = call_small(pair_kernel, "pair", [quarter] * 2, (const, mine, theirs), [(rows, half)])
    got = swap(send, "near", 2)
    states = [keep, got]
    tokens = fill(send)
    for shift in range(groups.bit_length() - 1):
        axis, bit = ("far", shift - 1) if shift else ("near", 1)
        (state,) = call_small(
            functools.partial(merge_kernel, axis, bit), "merge", [quarter], (const, *states[-2:], *tokens)
        )
        states += [state, swap(state, "far", 1 << shift)]
        tokens = fill(state) if shift < 2 else ()
    context = ((views + 2) * SUB, half // 2)
    here, there = call_small(
        functools.partial(context_kernel, len(states) // 2), "context", [context] * 2, (const, target, *states, *tokens)
    )
    there = swap(there, "near", 2)
    fill(here)
    context = (context[0], half)
    here, there = call_small(
        result_kernel, "result", [context] * 2, (const, target, mine, theirs, here, there), [context]
    )
    there = swap(there, "near", 1)
    package, signal = call_small(
        assemble_kernel, "assemble", [(context[0], width), (views * SUB, width)], (target, here, there)
    )
    own = [(u, n, v) for v in range(views)]
    signal = (signal, measured.shape)
    if both:
        other_package = to_other(package)
        pads = backward(package, const, column, shear_weight, own, cells, None, None)
        pieces = [(fillers[2 * v + 1][0], fillers[2 * v + 1][1], 0) for v in range(views)]
        gradient, signal = backward(
            other_package, const, other_column, other_weight, pieces, cells, signal, (column, *pads)
        )
    else:
        gradient, signal = backward(package, const, column, shear_weight, own, cells, signal, None)
        gradient = lax.psum(gradient, "views")
    return gradient.reshape(concentration.shape), signal


def solution(mesh):
    views, depth = mesh.shape["views"], mesh.shape["depth"]
    devices = mesh.devices.reshape(views, depth // NEAR, NEAR)
    split = jax.sharding.Mesh(devices, ("views", "far", "near"))
    depths = ("far", "near")
    return jax.shard_map(
        body,
        mesh=split,
        in_specs=(
            P(None, None, depths, None),
            P("views", depths, None),
            P("views", depths, None),
            P(),
            P(),
            P(),
            P("views", None, None, None),
        ),
        out_specs=(P(None, None, depths, None), P("views", None, None, None)),
        check_vma=False,
    )
```

```python
import functools

import jax
import jax.numpy as jnp
from jax import lax
from jax.experimental import pallas as pl
from jax.experimental.pallas import tpu as pltpu
from jax.sharding import PartitionSpec as P

LANES = 128
SUB = 8
BLOCK = 8
ROWS = BLOCK * SUB
NEAR = 4
CHUNK = 512
MIB = 1024 * 1024
F32 = jnp.float32
BF16 = jnp.bfloat16
HBM = pl.BlockSpec(memory_space=pltpu.HBM)
VMEM = pl.BlockSpec(memory_space=pltpu.VMEM)
SCALE, LINE_ROWS, LINE_LANES = 4, 5, 6
ANY = pl.BlockSpec(memory_space=pl.ANY)


def in_hbm(value):
    return pltpu.with_memory_space_constraint(value, pltpu.HBM)


def lane_ids(width=LANES):
    return lax.broadcasted_iota(jnp.int32, (SUB, width), 1)


def row_ids(width=LANES):
    return lax.broadcasted_iota(jnp.int32, (SUB, width), 0)


def tile_of(values, ids):
    tile = jnp.zeros(ids.shape, F32)
    for e in range(SUB):
        tile = jnp.where(ids == e, values[e], tile)
    return tile


def select_line(masks, values):
    result = values[0]
    for mask, value in zip(masks[1:], values[1:]):
        result = jnp.where(mask, value, result)
    return result


def fill_matrix(mat_ref, first_tile, second_tile, first_incl, second_incl):
    depth = (lane_ids() & (ROWS - 1)) >> 3
    tiles = []
    for d in range(BLOCK):
        one = jnp.where(depth <= d if first_incl else depth < d, first_tile, 0.0)
        two = jnp.where(depth <= d if second_incl else depth < d, second_tile, 0.0)
        tiles.append(one + two)
    tiles.append(first_tile + second_tile)
    tiles.append(jnp.zeros((SUB, LANES), F32))
    whole = jnp.concatenate(tiles, axis=0)
    high = whole.astype(BF16)
    mat_ref[:, 0:LANES] = high
    mat_ref[:, LANES : 2 * LANES] = (whole - high.astype(F32)).astype(BF16)


def multiply(mat_ref, values):
    high = values.astype(BF16)
    low = (values - high.astype(F32)).astype(BF16)
    stacked = jnp.concatenate([high, low, high], axis=0)
    product = jnp.dot(mat_ref[:, 0 : 3 * ROWS], stacked, preferred_element_type=F32)
    return product[0:ROWS], product[ROWS : ROWS + SUB]


MATRIX = (ROWS + 2 * SUB, 2 * LANES)


def copies_in(pairs, sems):
    return [pltpu.make_async_copy(source, target, sems.at[i]) for i, (source, target) in enumerate(pairs)]


def block_rows(block):
    return pl.ds(pl.multiple_of(block * ROWS, ROWS), ROWS)


def block_cells(block):
    return pl.ds(pl.multiple_of(block * BLOCK, BLOCK), BLOCK)


def shift_of(index_ref, v, cell, width):
    offset = index_ref[v, cell, 0] - (width // 2 - LANES)
    return offset >> 7, offset & (LANES - 1)


def shear(field, left_pad, diff_pad, index_ref, weight_ref, block, views, tiles, first=0):
    lanes = lane_ids()
    for i, v in enumerate(views):
        for d in range(BLOCK):
            cell = block * BLOCK + d
            whole, rest = shift_of(index_ref, v, cell - first, tiles * LANES)
            turn = (LANES - rest) & (LANES - 1)
            stay = lanes < LANES - rest

            def sheared(ref):
                turned = []
                for j in range(tiles + 1):
                    start = pl.multiple_of((whole + j) * LANES, LANES)
                    turned.append(pltpu.roll(ref[cell, :, pl.ds(start, LANES)], turn, 1))
                return [jnp.where(stay, turned[j], turned[j + 1]) for j in range(tiles)]

            left, diff = sheared(left_pad), sheared(diff_pad)
            for j in range(tiles):
                span = slice(j * LANES, (j + 1) * LANES)
                field[i, d * SUB : (d + 1) * SUB, span] = left[j] + weight_ref[i, d : d + 1, span] * diff[j]


def transmit(u_ref, n_ref, field, mat, carry, block, sums):
    views, _, width = field.shape
    for v in range(views):
        for c in range(width // CHUNK):
            span = slice(c * CHUNK, (c + 1) * CHUNK)
            value = field[v, :, span]
            lines, total = multiply(mat, value)
            before = carry[v, :, span]
            through = jnp.exp(lines.reshape(BLOCK, SUB, CHUNK) + before[None])
            value = value.reshape(BLOCK, SUB, CHUNK)
            emit = value * through
            u_ref[v, block_rows(block), span] = through.reshape(ROWS, CHUNK)
            n_ref[v, block_rows(block), span] = emit.reshape(ROWS, CHUNK)
            carry[v, :, span] = before + total
            if sums:
                sums[0][v, :, span] += jnp.sum(value, axis=0)
                sums[1][v, :, span] += jnp.sum(emit, axis=0)


def forward_kernel(cells, *refs):
    att_hbm, line_hbm, yield_hbm, index_hbm, conc_hbm, weight_hbm, measured_hbm = refs[:7]
    u_ref, n_ref, const_ref, target_ref, mat, left_pad, diff_pad, column_ref = refs[7:15]
    state_ref, refs = refs[15], refs[16:]
    conc_ref, weight_ref, weight_rows, field, carry, field_sum, emit_sum, measured_ref = refs[:8]
    att_ref, line_ref, yield_ref, index_ref, sems = refs[8:]
    views, slab, width = weight_ref.shape
    emissions = att_ref.shape[0] - 1
    tiles = width // LANES
    blocks = slab // BLOCK
    lanes, rows = lane_ids(), row_ids()
    conc_copies = [
        pltpu.make_async_copy(
            conc_hbm.at[:, pl.ds(b * BLOCK, BLOCK), :], conc_ref.at[:, pl.ds(b * BLOCK, BLOCK), :], sems.at[b]
        )
        for b in range(blocks)
    ]
    pairs = [
        (att_hbm, att_ref),
        (line_hbm, line_ref),
        (yield_hbm, yield_ref),
        (index_hbm.at[:, :, pl.ds(width // 2, LANES)], index_ref),
        (weight_hbm, weight_ref),
        (measured_hbm, measured_ref),
        (index_hbm.at[:, :, pl.ds(width // 2, LANES)], column_ref),
    ]
    copies = copies_in(pairs, sems.at[pl.ds(blocks, len(pairs))])
    for copy in conc_copies[:1] + copies[:4] + conc_copies[1:] + copies[4:]:
        copy.start()
    for ref in (carry, field_sum, emit_sum):
        ref[...] = jnp.zeros_like(ref)

    def one_block(block, _):
        for b in range(blocks):

            @pl.when(block == b)
            def _():
                conc_copies[b].wait()

        by_depth = jnp.swapaxes(conc_ref[:, block_cells(block), :], 0, 1)
        for d in range(BLOCK):
            pieces = [by_depth[d, :, j * LANES : (j + 1) * LANES] for j in range(tiles)]
            turned = [pltpu.roll(piece, LANES - 1, 1) for piece in pieces]
            after = [jnp.where(lanes < LANES - 1, turned[j], turned[min(j + 1, tiles - 1)]) for j in range(tiles)]
            steps = [after[j] - pieces[j] for j in range(tiles)]
            last_cell = jnp.broadcast_to(pieces[-1][:, LANES - 2 : LANES - 1], (SUB, LANES))
            last_step = jnp.broadcast_to(steps[-1][:, LANES - 2 : LANES - 1], (SUB, LANES))
            first_cell = jnp.broadcast_to(pieces[0][:, 0:1], (SUB, LANES))
            first_step = jnp.broadcast_to(steps[0][:, 0:1], (SUB, LANES))
            pieces[-1] = jnp.where(lanes < LANES - 1, pieces[-1], last_cell)
            steps[-1] = jnp.where(lanes < LANES - 1, steps[-1], last_step)
            pieces = [first_cell] + pieces + [last_cell, last_cell]
            steps = [first_step] + steps + [last_step, last_step]
            for j in range(tiles + 3):
                left_pad[block * BLOCK + d, :, j * LANES : (j + 1) * LANES] = pieces[j]
                diff_pad[block * BLOCK + d, :, j * LANES : (j + 1) * LANES] = steps[j]

        @pl.when(block == 0)
        def _():
            for copy in copies:
                copy.wait()
            line_by_row = tile_of([line_ref[e].astype(F32) for e in range(SUB)], rows)
            masks = [line_by_row == k for k in range(emissions)]
            by_lane = [tile_of([att_ref[k, e] for e in range(SUB)], lanes & 7) for k in range(emissions + 1)]
            fill_matrix(mat, -by_lane[0], select_line(masks, by_lane[1:]), False, True)
            for k in range(emissions + 1):
                const_ref[k] = tile_of([att_ref[k, e] for e in range(SUB)], rows)
            const_ref[SCALE] = tile_of([yield_ref[e] for e in range(SUB)], rows)
            const_ref[LINE_ROWS] = line_by_row
            const_ref[LINE_LANES] = tile_of([line_ref[e].astype(F32) for e in range(SUB)], lanes & 7)

        weight_rows[...] = weight_ref[:, block_cells(block), :]
        shear(field, left_pad, diff_pad, index_ref, weight_rows, block, range(views), tiles)
        transmit(u_ref, n_ref, field, mat, carry, block, (field_sum, emit_sum))
        return 0

    lax.fori_loop(0, blocks, one_block, 0)
    columns = [const_ref[k] for k in range(emissions + 1)]
    masks = [const_ref[LINE_ROWS] == k for k in range(emissions)]
    scale = const_ref[SCALE] * (1.0 / cells)
    for j in range(tiles):
        span = slice(j * LANES, (j + 1) * LANES)
        totals = jnp.zeros((SUB, LANES), F32)
        for v in range(views):
            values = field_sum[v, :, span]
            sums = [jnp.sum(column * values, axis=0, keepdims=True) for column in columns]
            for k in range(emissions + 1):
                totals = jnp.where(rows == v * (emissions + 1) + k, sums[k], totals)
            line_total = select_line(masks, [jnp.broadcast_to(value, rows.shape) for value in sums[1:]])
            signal = scale * emit_sum[v, :, span] * jnp.exp(-line_total)
            state_ref[(v + 1) * SUB : (v + 2) * SUB, span] = signal
        state_ref[0:SUB, span] = jnp.exp(-totals)
    for v in range(views):
        target_ref[v * SUB : (v + 1) * SUB, :] = measured_ref[v].reshape(SUB, width)


def forward(conc, index, weights, scalars, measured, cells):
    views, slab, width = weights.shape
    attenuation, line_energy, yields = scalars
    values = pltpu.VMEM((views, slab * SUB, width), F32)
    padded = pltpu.VMEM((slab, SUB, width + 3 * LANES), F32)
    state = pltpu.VMEM(((views + 1) * SUB, width), F32)
    line = pltpu.VMEM((views, SUB, width), F32)
    operands = [in_hbm(value) for value in (attenuation, line_energy, yields, index, conc, weights, measured)]
    return pl.pallas_call(
        functools.partial(forward_kernel, cells),
        in_specs=[HBM] * len(operands),
        out_specs=[VMEM] * 9,
        out_shape=[
            values,
            values,
            pltpu.VMEM((LINE_LANES + 1, SUB, LANES), F32),
            pltpu.VMEM((views * SUB, width), F32),
            pltpu.VMEM(MATRIX, BF16),
            padded,
            padded,
            pltpu.VMEM((views, slab, LANES), jnp.int32),
            state,
        ],
        scratch_shapes=[
            pltpu.VMEM((SUB, slab, width), F32),
            pltpu.VMEM((views, slab, width), F32),
            pltpu.VMEM((views, BLOCK, width), F32),
            pltpu.VMEM((views, ROWS, width), F32),
            line,
            line,
            line,
            pltpu.VMEM(measured.shape, F32),
            pltpu.SMEM(attenuation.shape, F32),
            pltpu.SMEM(line_energy.shape, jnp.int32),
            pltpu.SMEM(yields.shape, F32),
            pltpu.SMEM((views, slab, LANES), jnp.int32),
            pltpu.SemaphoreType.DMA((slab // BLOCK + 7,)),
        ],
        compiler_params=pltpu.CompilerParams(vmem_limit_bytes=16 * MIB),
        name="forward",
    )(*operands)


def forward_other_kernel(view, first, index_any, weight_ref, mat, left_pad, diff_pad, order_ref, *refs):
    u_ref, n_ref, carry, token_ref, weight_rows, field, index_ref, sem = refs[-8:]
    width = weight_ref.shape[2]
    count = index_ref.shape[1]
    copy = pltpu.make_async_copy(index_any.at[pl.ds(view, 1), pl.ds(first, count)], index_ref, sem)
    copy.start()
    token_ref[...] = jnp.zeros_like(token_ref)
    if first:
        carry[...] = refs[2][...]
    else:
        carry[...] = jnp.zeros_like(carry)
    copy.wait()

    def one_block(block, _):
        weight_rows[0] = weight_ref[view, block_cells(block), :]
        shear(field, left_pad, diff_pad, index_ref, weight_rows, block, (0,), width // LANES, first)
        transmit(u_ref, n_ref, field, mat, carry, block, None)
        return 0

    lax.fori_loop(first // BLOCK, (first + count) // BLOCK, one_block, 0)


def forward_other(view, first, count, column, weights, mat, left_pad, diff_pad, after, before):
    _, slab, width = weights.shape
    values = pltpu.VMEM((1, slab * SUB, width), F32)
    return pl.pallas_call(
        functools.partial(forward_other_kernel, view, first),
        in_specs=[ANY] + [VMEM] * (5 + len(before)),
        out_specs=[VMEM] * 4,
        out_shape=[values, values, pltpu.VMEM((1, SUB, width), F32), pltpu.VMEM((SUB, LANES), F32)],
        input_output_aliases={6: 0, 7: 1} if before else {},
        scratch_shapes=[
            pltpu.VMEM((1, BLOCK, width), F32),
            pltpu.VMEM((1, ROWS, width), F32),
            pltpu.SMEM((1, count, LANES), jnp.int32),
            pltpu.SemaphoreType.DMA,
        ],
        compiler_params=pltpu.CompilerParams(vmem_limit_bytes=8 * MIB),
        name="forward_other",
    )(column, weights, mat, left_pad, diff_pad, after, *before)


def line_rows(tile, base, masks):
    shape = masks[0].shape
    return select_line(masks, [jnp.broadcast_to(tile[base + 1 + k : base + 2 + k], shape) for k in range(len(masks))])


def incident_rows(tile, step):
    rows = row_ids(tile.shape[1])
    result = jnp.broadcast_to(tile[0:1], tile.shape)
    for base in range(step, SUB, step):
        result = jnp.where(rows >= base, jnp.broadcast_to(tile[base : base + 1], tile.shape), result)
    return result


def row_masks(const_ref, width):
    tile = const_ref[LINE_ROWS]
    return [jnp.concatenate([tile] * (width // LANES), axis=1) == k for k in range(SCALE - 1)]


def factors_of(mine, theirs, bit):
    mine_factor = jnp.where(bit == 0, theirs, incident_rows(theirs, SCALE))
    return mine_factor, jnp.where(bit == 0, incident_rows(mine, SCALE), mine)


def merged_state(mine, theirs, bit, masks):
    mine_factor, theirs_factor = factors_of(mine[0:SUB], theirs[0:SUB], bit)
    result = [mine[0:SUB] * theirs[0:SUB]]
    for v in range(mine.shape[0] // SUB - 1):
        span = slice((v + 1) * SUB, (v + 2) * SUB)
        result.append(
            mine[span] * line_rows(mine_factor, v * SCALE, masks)
            + theirs[span] * line_rows(theirs_factor, v * SCALE, masks)
        )
    return result


def weighted_rows(factor, state, misfits, masks):
    rows = row_ids(state.shape[1])
    result = jnp.zeros((SUB, state.shape[1]), F32)
    for v, misfit in enumerate(misfits):
        base = v * SCALE
        value = misfit * state[(v + 1) * SUB : (v + 2) * SUB] * line_rows(factor, base, masks)
        whole = None
        for k, mask in enumerate(masks):
            part = jnp.sum(jnp.where(mask, value, 0.0), axis=0, keepdims=True)
            result = jnp.where(rows == base + 1 + k, part, result)
            whole = part if whole is None else whole + part
        result = jnp.where(rows == base, whole, result)
    return result


def children(factor, sums, mine, theirs, bit, misfits, masks):
    mine_factor, theirs_factor = factors_of(mine[0:SUB], theirs[0:SUB], bit)
    if factor is not None:
        mine_factor, theirs_factor = factor * mine_factor, factor * theirs_factor
    behind = (row_ids(mine.shape[1]) & (SCALE - 1)) == 0
    mine_sums = jnp.where(behind == (bit == 0), weighted_rows(theirs_factor, theirs, misfits, masks), 0.0)
    theirs_sums = jnp.where(behind == (bit == 1), weighted_rows(mine_factor, mine, misfits, masks), 0.0)
    if sums is not None:
        mine_sums, theirs_sums = sums + mine_sums, sums + theirs_sums
    return (mine_factor, mine_sums), (theirs_factor, theirs_sums)


def call_small(kernel, name, outs, operands, scratch=()):
    return pl.pallas_call(
        kernel,
        in_specs=[VMEM] * len(operands),
        out_specs=[VMEM] * len(outs),
        out_shape=[pltpu.VMEM(shape, F32) for shape in outs],
        scratch_shapes=[pltpu.VMEM(shape, F32) for shape in scratch],
        compiler_params=pltpu.CompilerParams(vmem_limit_bytes=4 * MIB),
        name=name,
    )(*operands)


def merge_kernel(shift, const_ref, mine_ref, theirs_ref, *refs):
    bit = (depth_place() >> shift) & 1
    state = merged_state(mine_ref[...], theirs_ref[...], bit, row_masks(const_ref, mine_ref.shape[1]))
    for i, tile in enumerate(state):
        refs[-1][i * SUB : (i + 1) * SUB, :] = tile


def depth_place():
    return lax.axis_index("far") * NEAR + lax.axis_index("near")


def result_kernel(levels, const_ref, target_ref, *refs):
    states, outs = refs[: 2 * levels], refs[-2:]
    depth, width = states[0].shape
    views = depth // SUB - 1
    place = depth_place()
    size = 2 * LANES
    masks = row_masks(const_ref, size)
    behind = (row_ids(size) & (SCALE - 1)) == 0
    for c in range(width // size):
        span = slice(c * size, (c + 1) * size)
        factor, sums = None, None
        for level in reversed(range(levels)):
            mine, theirs = states[2 * level][:, span], states[2 * level + 1][:, span]
            bit = (place >> level) & 1
            if level == levels - 1:
                signals = merged_state(mine, theirs, bit, masks)[1:]
                misfits = [signals[v] - target_ref[v * SUB : (v + 1) * SUB, span] for v in range(views)]
            contexts = children(factor, sums, mine, theirs, bit, misfits, masks)
            factor, sums = contexts[0]
        for ref, state, (factor, sums) in zip(outs, (mine, theirs), contexts):
            own = jnp.where(behind, weighted_rows(factor, state, misfits, masks), 0.0)
            for i, tile in enumerate(signals + [factor * state[0:SUB], sums + own]):
                ref[i * SUB : (i + 1) * SUB, span] = tile


def assemble_kernel(target_ref, mine_ref, sent_ref, package_ref, signal_ref):
    leads = (lax.axis_index("near") & 1) == 1
    package = jnp.where(leads, mine_ref[...], sent_ref[...])
    count = signal_ref.shape[0]
    signal_ref[...] = package[0:count]
    package_ref[0:count, :] = package[0:count] - target_ref[...]
    package_ref[count:, :] = package[count:]


def backward_kernel(views, cells, finish, prior, const_ref, package_ref, index_any, weight_any, *refs):
    if finish:
        signal_ref, refs = refs[0], refs[1:]
    u_refs, refs = refs[: len(views)], refs[len(views) :]
    n_refs, refs = refs[: len(views)], refs[len(views) :]
    if prior:
        prior_any, prior_left, prior_diff = refs[:3]
        refs = refs[3:]
    if finish:
        grad_hbm, signal_hbm, refs = refs[0], refs[1], refs[2:]
        left_pad, diff_pad, cell_ref, grad_ref, signal_rows, refs = refs[:5] + (refs[5:],)
    else:
        left_pad, diff_pad, refs = refs[:2] + (refs[2:],)
    mat, gain, carry, scaled, weight_ref, weight_rows, index_ref = refs[:7]
    prior_ref, sems = refs[7] if prior else None, refs[-1]
    count, slab, width = weight_ref.shape
    emissions = SCALE - 1
    tiles = width // LANES
    blocks = slab // BLOCK
    lanes, rows = lane_ids(), row_ids()
    margin = 2 * LANES
    pairs = [(index_any, index_ref), (weight_any, weight_ref)]
    if prior:
        pairs.append((prior_any, prior_ref))
    copies = copies_in(pairs, sems.at[pl.ds(blocks, len(pairs))])
    for copy in copies:
        copy.start()
    if finish:
        for v in range(signal_rows.shape[0]):
            signal_rows[v] = signal_ref[v * SUB : (v + 1) * SUB, :].reshape(SUB, 1, width)
        signal_copy = pltpu.make_async_copy(signal_rows, signal_hbm, sems.at[blocks + 3])
        signal_copy.start()
    masks = [const_ref[LINE_LANES] == k for k in range(emissions)]
    columns = [const_ref[k] for k in range(emissions + 1)]
    fill_matrix(mat, -columns[0], select_line(masks, columns[1:]), True, False)
    masks = [const_ref[LINE_ROWS] == k for k in range(emissions)]
    scale = const_ref[SCALE]
    columns = [column * cells for column in columns]
    for j in range(tiles):
        span = slice(j * LANES, (j + 1) * LANES)
        factor = package_ref[count * SUB : (count + 1) * SUB, span]
        sums = package_ref[(count + 1) * SUB : (count + 2) * SUB, span]
        for v in range(count):
            base = v * SCALE
            gain[v, :, span] = package_ref[v * SUB : (v + 1) * SUB, span] * scale * line_rows(factor, base, masks)
            back = columns[0] * jnp.broadcast_to(sums[base : base + 1], rows.shape)
            for k in range(1, emissions + 1):
                back = back + columns[k] * jnp.broadcast_to(sums[base + k : base + k + 1], rows.shape)
            carry[v, :, span] = back
    for ref in (left_pad, diff_pad):
        ref[:, :, :, 0:margin] = jnp.zeros(ref.shape[:3] + (margin,), F32)
        ref[:, :, :, margin + width + LANES :] = jnp.zeros(ref.shape[:3] + (margin,), F32)

    def one_block(block, _):
        slot = 0 if finish else block * BLOCK
        for v in range(count):
            u_ref, n_ref, at = u_refs[v], n_refs[v], views[v]
            for c in range(width // CHUNK):
                span = slice(c * CHUNK, (c + 1) * CHUNK)
                factor = gain[v, :, span][None]
                weighted = n_ref[at, block_rows(block), span].reshape(BLOCK, SUB, CHUNK) * factor
                direct = u_ref[at, block_rows(block), span].reshape(BLOCK, SUB, CHUNK) * factor
                lines, total = multiply(mat, weighted.reshape(ROWS, CHUNK))
                before = carry[v, :, span]
                lines = lines.reshape(BLOCK, SUB, CHUNK) + before[None]
                scaled[v, :, span] = (direct - lines).reshape(ROWS, CHUNK)
                carry[v, :, span] = before + total

        @pl.when(block == 0)
        def _():
            for copy in copies:
                copy.wait()

        weight_rows[...] = weight_ref[:, block_cells(block), :]
        for v in range(count):
            for d in range(BLOCK):
                _, rest = shift_of(index_ref, v, block * BLOCK + d, width)
                stay = lanes >= rest
                plain = [scaled[v, d * SUB : (d + 1) * SUB, j * LANES : (j + 1) * LANES] for j in range(tiles)]
                moved = [plain[j] * weight_rows[v, d : d + 1, j * LANES : (j + 1) * LANES] for j in range(tiles)]
                for ref, values in ((left_pad, plain), (diff_pad, moved)):
                    turned = [jnp.zeros((SUB, LANES), F32)]
                    turned += [pltpu.roll(value, rest, 1) for value in values]
                    turned += [jnp.zeros((SUB, LANES), F32)]
                    for j in range(tiles + 1):
                        span = slice(margin + j * LANES, margin + (j + 1) * LANES)
                        ref[v, slot + d, :, span] = jnp.where(stay, turned[j + 1], turned[j])
        if not finish:
            return 0
        for d in range(BLOCK):
            cell = block * BLOCK + d

            def gathered(ref, prior_pad):
                sources = [(ref, index_ref, v, d) for v in range(count)]
                if prior:
                    sources += [(prior_pad, prior_ref, v, cell) for v in range(prior)]
                sums = [None] * (tiles + 2)
                for pad, index, v, at in sources:
                    whole, _ = shift_of(index, v, cell, width)
                    for j in range(tiles + 2):
                        start = pl.multiple_of((2 + j - whole) * LANES, LANES)
                        value = pad[v, at, :, pl.ds(start, LANES)]
                        sums[j] = value if sums[j] is None else sums[j] + value
                return sums

            left = gathered(left_pad, prior_left if prior else None)
            diff = gathered(diff_pad, prior_diff if prior else None)
            left = [left[j] - diff[j] for j in range(tiles + 2)]

            def folded(sums):
                low = jnp.sum(sums[0], axis=1, keepdims=True)
                beyond = sums[tiles + 1] + jnp.where(lanes == LANES - 1, sums[tiles], 0.0)
                high = jnp.sum(beyond, axis=1, keepdims=True)
                core = sums[1 : tiles + 1]
                core[0] = core[0] + jnp.where(lanes == 0, low, 0.0)
                core[-1] = jnp.where(lanes == LANES - 1, 0.0, core[-1] + jnp.where(lanes == LANES - 2, high, 0.0))
                return core

            left, diff = folded(left), folded(diff)
            turned = [jnp.zeros((SUB, LANES), F32)] + [pltpu.roll(value, 1, 1) for value in diff]
            for j in range(tiles):
                value = left[j] + jnp.where(lanes == 0, turned[j], turned[j + 1])
                cell_ref[d, :, j * LANES : (j + 1) * LANES] = value
        grad_ref[block] = jnp.swapaxes(cell_ref[...], 0, 1)
        for b in range(blocks):

            @pl.when(block == b)
            def _():
                out_copies[b].start()

        return 0

    if finish:
        out_copies = [
            pltpu.make_async_copy(grad_ref.at[b], grad_hbm.at[:, pl.ds(b * BLOCK, BLOCK), :], sems.at[b])
            for b in range(blocks)
        ]
    lax.fori_loop(0, blocks, one_block, 0)
    if finish:
        for copy in out_copies + [signal_copy]:
            copy.wait()


def backward(package, const, column, weights, pieces, cells, signal, prior):
    finish = signal is not None
    signals = [signal[0]] if finish else []
    views, slab, width = weights.shape
    blocks = slab // BLOCK
    line = pltpu.VMEM((views, SUB, width), F32)
    depth = BLOCK if finish else slab
    padded = pltpu.VMEM((views, depth, SUB, width + 5 * LANES), F32)
    scratch = [
        pltpu.VMEM(MATRIX, BF16),
        line,
        line,
        pltpu.VMEM((views, ROWS, width), F32),
        pltpu.VMEM((views, slab, width), F32),
        pltpu.VMEM((views, BLOCK, width), F32),
        pltpu.SMEM((views, slab, LANES), jnp.int32),
    ]
    in_specs = [VMEM, VMEM, ANY, ANY] + [VMEM] * (2 * views + len(signals))
    if prior:
        in_specs += [ANY, VMEM, VMEM]
        scratch.append(pltpu.SMEM((views, slab, LANES), jnp.int32))
    scratch.append(pltpu.SemaphoreType.DMA((blocks + 4,)))
    if finish:
        scratch = [
            padded,
            padded,
            pltpu.VMEM((BLOCK, SUB, width), F32),
            pltpu.VMEM((blocks, SUB, BLOCK, width), F32),
            pltpu.VMEM(signal[1], F32),
        ] + scratch
    return pl.pallas_call(
        functools.partial(
            backward_kernel, tuple(at for _, _, at in pieces), cells, finish, views if prior else 0
        ),
        in_specs=in_specs,
        out_specs=[HBM, HBM] if finish else [VMEM, VMEM],
        out_shape=[pltpu.HBM((SUB, slab, width), F32), pltpu.HBM(signal[1], F32)] if finish else [padded, padded],
        scratch_shapes=scratch,
        compiler_params=pltpu.CompilerParams(vmem_limit_bytes=16 * MIB),
        name="backward_last" if finish else "backward_first",
    )(const, package, column, weights, *signals, *[u for u, _, _ in pieces], *[n for _, n, _ in pieces], *(prior or ()))


def body(concentration, shear_index, shear_weight, attenuation, yields, line_energy, measured):
    elements, _, slab, width = concentration.shape
    views = shear_weight.shape[0]
    emissions = attenuation.shape[0] - 1
    groups = lax.axis_size("far")
    both = lax.axis_size("views") == 2
    cells = float(slab * groups * NEAR)
    conc = concentration.reshape(elements, slab, width)
    scalars = (attenuation, line_energy, yields)

    def to_other(value):
        return lax.ppermute(value, "views", [(0, 1), (1, 0)])

    fillers = []

    def fill(after):
        if not both or len(fillers) == views:
            return ()
        pads = (mat, left_pad, diff_pad, after)
        fillers.append(forward_other(len(fillers), 0, slab, other_column, other_weight, *pads, ()))
        return (fillers[-1][3],)

    if both:
        other_weight = to_other(shear_weight)
    u, n, const, target, mat, left_pad, diff_pad, column, state = forward(
        conc, shear_index, shear_weight, scalars, measured, cells
    )
    lead = [s for s in range(NEAR) if s % 2]
    states = [state, lax.ppermute(state, "near", [(s - 1, s) for s in lead])]
    if both:
        other_column = to_other(column)
    tokens = (other_weight,) if both else ()
    levels = groups.bit_length() + 1
    for level in range(levels - 1):
        (state,) = call_small(
            functools.partial(merge_kernel, level), "merge", [state.shape], (const, *states[-2:], *tokens)
        )
        if level == 0:
            states += [state, lax.ppermute(state, "near", [(s, s ^ 2) for s in lead])]
            tokens = (other_column,) if both else ()
        else:
            step = 1 << (level - 1)
            pairs = [(g * NEAR + s, (g ^ step) * NEAR + s) for g in range(groups) for s in lead]
            states += [state, lax.ppermute(state, ("far", "near"), pairs)]
            tokens = fill(state)
    package = ((views + 2) * SUB, width)
    mine, theirs = call_small(
        functools.partial(result_kernel, levels), "result", [package] * 2, (const, target, *states, *tokens)
    )
    sent = lax.ppermute(theirs, "near", [(s, s - 1) for s in lead])
    package, signal = call_small(assemble_kernel, "assemble", [package, target.shape], (target, mine, sent))
    own = [(u, n, v) for v in range(views)]
    signal = (signal, measured.shape)
    if both:
        other_package = to_other(package)
        pads = backward(package, const, column, shear_weight, own, cells, None, None)
        pieces = [(fillers[v][0], fillers[v][1], 0) for v in range(views)]
        gradient, signal = backward(
            other_package, const, other_column, other_weight, pieces, cells, signal, (column, *pads)
        )
    else:
        gradient, signal = backward(package, const, column, shear_weight, own, cells, signal, None)
        gradient = lax.psum(gradient, "views")
    return gradient.reshape(concentration.shape), signal


def solution(mesh):
    views, depth = mesh.shape["views"], mesh.shape["depth"]
    devices = mesh.devices.reshape(views, depth // NEAR, NEAR)
    split = jax.sharding.Mesh(devices, ("views", "far", "near"))
    depths = ("far", "near")
    return jax.shard_map(
        body,
        mesh=split,
        in_specs=(
            P(None, None, depths, None),
            P("views", depths, None),
            P("views", depths, None),
            P(),
            P(),
            P(),
            P("views", None, None, None),
        ),
        out_specs=(P(None, None, depths, None), P("views", None, None, None)),
        check_vma=False,
    )
```

```python
import functools

import jax
import jax.numpy as jnp
from jax import lax
from jax.experimental import pallas as pl
from jax.experimental.pallas import tpu as pltpu
from jax.sharding import PartitionSpec as P

LANES = 128
SUB = 8
BLOCK = 8
ROWS = BLOCK * SUB
NEAR = 4
CHUNK = 256
MIB = 1024 * 1024
F32 = jnp.float32
BF16 = jnp.bfloat16
HBM = pl.BlockSpec(memory_space=pltpu.HBM)
VMEM = pl.BlockSpec(memory_space=pltpu.VMEM)
SCALE, LINE_ROWS, LINE_LANES = 4, 5, 6
ANY = pl.BlockSpec(memory_space=pl.ANY)


def in_hbm(value):
    return pltpu.with_memory_space_constraint(value, pltpu.HBM)


def lane_ids(width=LANES):
    return lax.broadcasted_iota(jnp.int32, (SUB, width), 1)


def row_ids(width=LANES):
    return lax.broadcasted_iota(jnp.int32, (SUB, width), 0)


def tile_of(values, ids):
    tile = jnp.zeros(ids.shape, F32)
    for e in range(SUB):
        tile = jnp.where(ids == e, values[e], tile)
    return tile


def select_line(masks, values):
    result = values[0]
    for mask, value in zip(masks[1:], values[1:]):
        result = jnp.where(mask, value, result)
    return result


def fill_matrix(mat_ref, first_tile, second_tile, first_incl, second_incl):
    depth = (lane_ids() & (ROWS - 1)) >> 3
    tiles = []
    for d in range(BLOCK):
        one = jnp.where(depth <= d if first_incl else depth < d, first_tile, 0.0)
        two = jnp.where(depth <= d if second_incl else depth < d, second_tile, 0.0)
        tiles.append(one + two)
    tiles.append(first_tile + second_tile)
    tiles.append(jnp.zeros((SUB, LANES), F32))
    whole = jnp.concatenate(tiles, axis=0)
    high = whole.astype(BF16)
    mat_ref[:, 0:LANES] = high
    mat_ref[:, LANES : 2 * LANES] = (whole - high.astype(F32)).astype(BF16)


def multiply(mat_ref, values):
    high = values.astype(BF16)
    low = (values - high.astype(F32)).astype(BF16)
    stacked = jnp.concatenate([high, low, high], axis=0)
    product = jnp.dot(mat_ref[:, 0 : 3 * ROWS], stacked, preferred_element_type=F32)
    return product[0:ROWS], product[ROWS : ROWS + SUB]


MATRIX = (ROWS + 2 * SUB, 2 * LANES)


def copies_in(pairs, sems):
    return [pltpu.make_async_copy(source, target, sems.at[i]) for i, (source, target) in enumerate(pairs)]


def block_rows(block):
    return pl.ds(pl.multiple_of(block * ROWS, ROWS), ROWS)


def block_cells(block):
    return pl.ds(pl.multiple_of(block * BLOCK, BLOCK), BLOCK)


def shift_of(index_ref, v, cell, width):
    offset = index_ref[v, cell, 0] - (width // 2 - LANES)
    return offset >> 7, offset & (LANES - 1)


def shear(field, left_pad, diff_pad, index_ref, weight_ref, block, views, tiles, first=0):
    lanes = lane_ids()
    for i, v in enumerate(views):
        for d in range(BLOCK):
            cell = block * BLOCK + d
            whole, rest = shift_of(index_ref, v, cell - first, tiles * LANES)
            turn = (LANES - rest) & (LANES - 1)
            stay = lanes < LANES - rest

            def sheared(ref):
                turned = []
                for j in range(tiles + 1):
                    start = pl.multiple_of((whole + j) * LANES, LANES)
                    turned.append(pltpu.roll(ref[cell, :, pl.ds(start, LANES)], turn, 1))
                return [jnp.where(stay, turned[j], turned[j + 1]) for j in range(tiles)]

            left, diff = sheared(left_pad), sheared(diff_pad)
            for j in range(tiles):
                span = slice(j * LANES, (j + 1) * LANES)
                field[i, d * SUB : (d + 1) * SUB, span] = left[j] + weight_ref[i, d : d + 1, span] * diff[j]


def transmit(u_ref, n_ref, field, mat, carry, block, sums):
    views, _, width = field.shape
    for v in range(views):
        for c in range(width // CHUNK):
            span = slice(c * CHUNK, (c + 1) * CHUNK)
            value = field[v, :, span]
            lines, total = multiply(mat, value)
            before = carry[v, :, span]
            through = jnp.exp(lines.reshape(BLOCK, SUB, CHUNK) + before[None])
            value = value.reshape(BLOCK, SUB, CHUNK)
            emit = value * through
            u_ref[v, block_rows(block), span] = through.reshape(ROWS, CHUNK)
            n_ref[v, block_rows(block), span] = emit.reshape(ROWS, CHUNK)
            carry[v, :, span] = before + total
            if sums:
                sums[0][v, :, span] += jnp.sum(value, axis=0)
                sums[1][v, :, span] += jnp.sum(emit, axis=0)


def forward_kernel(cells, *refs):
    att_hbm, line_hbm, yield_hbm, index_hbm, conc_hbm, weight_hbm, measured_hbm = refs[:7]
    u_ref, n_ref, const_ref, target_ref, mat, left_pad, diff_pad, column_ref = refs[7:15]
    state_ref, refs = refs[15], refs[16:]
    conc_ref, weight_ref, weight_rows, field, carry, field_sum, emit_sum, measured_ref = refs[:8]
    att_ref, line_ref, yield_ref, index_ref, sems = refs[8:]
    views, slab, width = weight_ref.shape
    emissions = att_ref.shape[0] - 1
    tiles = width // LANES
    blocks = slab // BLOCK
    lanes, rows = lane_ids(), row_ids()
    conc_copies = [
        pltpu.make_async_copy(
            conc_hbm.at[:, pl.ds(b * BLOCK, BLOCK), :], conc_ref.at[:, pl.ds(b * BLOCK, BLOCK), :], sems.at[b]
        )
        for b in range(blocks)
    ]
    pairs = [
        (att_hbm, att_ref),
        (line_hbm, line_ref),
        (yield_hbm, yield_ref),
        (index_hbm.at[:, :, pl.ds(width // 2, LANES)], index_ref),
        (weight_hbm, weight_ref),
        (measured_hbm, measured_ref),
        (index_hbm.at[:, :, pl.ds(width // 2, LANES)], column_ref),
    ]
    copies = copies_in(pairs, sems.at[pl.ds(blocks, len(pairs))])
    for copy in conc_copies[:1] + copies[:4] + conc_copies[1:] + copies[4:]:
        copy.start()
    for ref in (carry, field_sum, emit_sum):
        ref[...] = jnp.zeros_like(ref)

    def one_block(block, _):
        for b in range(blocks):

            @pl.when(block == b)
            def _():
                conc_copies[b].wait()

        by_depth = jnp.swapaxes(conc_ref[:, block_cells(block), :], 0, 1)
        for d in range(BLOCK):
            pieces = [by_depth[d, :, j * LANES : (j + 1) * LANES] for j in range(tiles)]
            turned = [pltpu.roll(piece, LANES - 1, 1) for piece in pieces]
            after = [jnp.where(lanes < LANES - 1, turned[j], turned[min(j + 1, tiles - 1)]) for j in range(tiles)]
            steps = [after[j] - pieces[j] for j in range(tiles)]
            last_cell = jnp.broadcast_to(pieces[-1][:, LANES - 2 : LANES - 1], (SUB, LANES))
            last_step = jnp.broadcast_to(steps[-1][:, LANES - 2 : LANES - 1], (SUB, LANES))
            first_cell = jnp.broadcast_to(pieces[0][:, 0:1], (SUB, LANES))
            first_step = jnp.broadcast_to(steps[0][:, 0:1], (SUB, LANES))
            pieces[-1] = jnp.where(lanes < LANES - 1, pieces[-1], last_cell)
            steps[-1] = jnp.where(lanes < LANES - 1, steps[-1], last_step)
            pieces = [first_cell] + pieces + [last_cell, last_cell]
            steps = [first_step] + steps + [last_step, last_step]
            for j in range(tiles + 3):
                left_pad[block * BLOCK + d, :, j * LANES : (j + 1) * LANES] = pieces[j]
                diff_pad[block * BLOCK + d, :, j * LANES : (j + 1) * LANES] = steps[j]

        @pl.when(block == 0)
        def _():
            for copy in copies:
                copy.wait()
            line_by_row = tile_of([line_ref[e].astype(F32) for e in range(SUB)], rows)
            masks = [line_by_row == k for k in range(emissions)]
            by_lane = [tile_of([att_ref[k, e] for e in range(SUB)], lanes & 7) for k in range(emissions + 1)]
            fill_matrix(mat, -by_lane[0], select_line(masks, by_lane[1:]), False, True)
            for k in range(emissions + 1):
                const_ref[k] = tile_of([att_ref[k, e] for e in range(SUB)], rows)
            const_ref[SCALE] = tile_of([yield_ref[e] for e in range(SUB)], rows)
            const_ref[LINE_ROWS] = line_by_row
            const_ref[LINE_LANES] = tile_of([line_ref[e].astype(F32) for e in range(SUB)], lanes & 7)

        weight_rows[...] = weight_ref[:, block_cells(block), :]
        shear(field, left_pad, diff_pad, index_ref, weight_rows, block, range(views), tiles)
        transmit(u_ref, n_ref, field, mat, carry, block, (field_sum, emit_sum))
        return 0

    lax.fori_loop(0, blocks, one_block, 0)
    columns = [const_ref[k] for k in range(emissions + 1)]
    masks = [const_ref[LINE_ROWS] == k for k in range(emissions)]
    scale = const_ref[SCALE] * (1.0 / cells)
    for j in range(tiles):
        span = slice(j * LANES, (j + 1) * LANES)
        totals = jnp.zeros((SUB, LANES), F32)
        for v in range(views):
            values = field_sum[v, :, span]
            sums = [jnp.sum(column * values, axis=0, keepdims=True) for column in columns]
            for k in range(emissions + 1):
                totals = jnp.where(rows == v * (emissions + 1) + k, sums[k], totals)
            line_total = select_line(masks, [jnp.broadcast_to(value, rows.shape) for value in sums[1:]])
            signal = scale * emit_sum[v, :, span] * jnp.exp(-line_total)
            state_ref[(v + 1) * SUB : (v + 2) * SUB, span] = signal
        state_ref[0:SUB, span] = jnp.exp(-totals)
    for v in range(views):
        target_ref[v * SUB : (v + 1) * SUB, :] = measured_ref[v].reshape(SUB, width)


def forward(conc, index, weights, scalars, measured, cells):
    views, slab, width = weights.shape
    attenuation, line_energy, yields = scalars
    values = pltpu.VMEM((views, slab * SUB, width), F32)
    padded = pltpu.VMEM((slab, SUB, width + 3 * LANES), F32)
    state = pltpu.VMEM(((views + 1) * SUB, width), F32)
    line = pltpu.VMEM((views, SUB, width), F32)
    operands = [in_hbm(value) for value in (attenuation, line_energy, yields, index, conc, weights, measured)]
    return pl.pallas_call(
        functools.partial(forward_kernel, cells),
        in_specs=[HBM] * len(operands),
        out_specs=[VMEM] * 9,
        out_shape=[
            values,
            values,
            pltpu.VMEM((LINE_LANES + 1, SUB, LANES), F32),
            pltpu.VMEM((views * SUB, width), F32),
            pltpu.VMEM(MATRIX, BF16),
            padded,
            padded,
            pltpu.VMEM((views, slab, LANES), jnp.int32),
            state,
        ],
        scratch_shapes=[
            pltpu.VMEM((SUB, slab, width), F32),
            pltpu.VMEM((views, slab, width), F32),
            pltpu.VMEM((views, BLOCK, width), F32),
            pltpu.VMEM((views, ROWS, width), F32),
            line,
            line,
            line,
            pltpu.VMEM(measured.shape, F32),
            pltpu.SMEM(attenuation.shape, F32),
            pltpu.SMEM(line_energy.shape, jnp.int32),
            pltpu.SMEM(yields.shape, F32),
            pltpu.SMEM((views, slab, LANES), jnp.int32),
            pltpu.SemaphoreType.DMA((slab // BLOCK + 7,)),
        ],
        compiler_params=pltpu.CompilerParams(vmem_limit_bytes=16 * MIB),
        name="forward",
    )(*operands)


def forward_other_kernel(view, first, index_any, weight_ref, mat, left_pad, diff_pad, order_ref, *refs):
    u_ref, n_ref, carry, token_ref, weight_rows, field, index_ref, sem = refs[-8:]
    width = weight_ref.shape[2]
    count = index_ref.shape[1]
    copy = pltpu.make_async_copy(index_any.at[pl.ds(view, 1), pl.ds(first, count)], index_ref, sem)
    copy.start()
    token_ref[...] = jnp.zeros_like(token_ref)
    if first:
        carry[...] = refs[2][...]
    else:
        carry[...] = jnp.zeros_like(carry)
    copy.wait()

    def one_block(block, _):
        weight_rows[0] = weight_ref[view, block_cells(block), :]
        shear(field, left_pad, diff_pad, index_ref, weight_rows, block, (0,), width // LANES, first)
        transmit(u_ref, n_ref, field, mat, carry, block, None)
        return 0

    lax.fori_loop(first // BLOCK, (first + count) // BLOCK, one_block, 0)


def forward_other(view, first, count, column, weights, mat, left_pad, diff_pad, after, before):
    _, slab, width = weights.shape
    values = pltpu.VMEM((1, slab * SUB, width), F32)
    return pl.pallas_call(
        functools.partial(forward_other_kernel, view, first),
        in_specs=[ANY] + [VMEM] * (5 + len(before)),
        out_specs=[VMEM] * 4,
        out_shape=[values, values, pltpu.VMEM((1, SUB, width), F32), pltpu.VMEM((SUB, LANES), F32)],
        input_output_aliases={6: 0, 7: 1} if before else {},
        scratch_shapes=[
            pltpu.VMEM((1, BLOCK, width), F32),
            pltpu.VMEM((1, ROWS, width), F32),
            pltpu.SMEM((1, count, LANES), jnp.int32),
            pltpu.SemaphoreType.DMA,
        ],
        compiler_params=pltpu.CompilerParams(vmem_limit_bytes=8 * MIB),
        name="forward_other",
    )(column, weights, mat, left_pad, diff_pad, after, *before)


def line_rows(tile, base, masks):
    shape = masks[0].shape
    return select_line(masks, [jnp.broadcast_to(tile[base + 1 + k : base + 2 + k], shape) for k in range(len(masks))])


def incident_rows(tile, step):
    rows = row_ids(tile.shape[1])
    result = jnp.broadcast_to(tile[0:1], tile.shape)
    for base in range(step, SUB, step):
        result = jnp.where(rows >= base, jnp.broadcast_to(tile[base : base + 1], tile.shape), result)
    return result


def row_masks(const_ref, width):
    tile = const_ref[LINE_ROWS]
    return [jnp.concatenate([tile] * (width // LANES), axis=1) == k for k in range(SCALE - 1)]


def factors_of(mine, theirs, bit):
    mine_factor = jnp.where(bit == 0, theirs, incident_rows(theirs, SCALE))
    return mine_factor, jnp.where(bit == 0, incident_rows(mine, SCALE), mine)


def merged_state(mine, theirs, bit, masks):
    mine_factor, theirs_factor = factors_of(mine[0:SUB], theirs[0:SUB], bit)
    result = [mine[0:SUB] * theirs[0:SUB]]
    for v in range(mine.shape[0] // SUB - 1):
        span = slice((v + 1) * SUB, (v + 2) * SUB)
        result.append(
            mine[span] * line_rows(mine_factor, v * SCALE, masks)
            + theirs[span] * line_rows(theirs_factor, v * SCALE, masks)
        )
    return result


def weighted_rows(factor, state, misfits, masks):
    rows = row_ids(state.shape[1])
    result = jnp.zeros((SUB, state.shape[1]), F32)
    for v, misfit in enumerate(misfits):
        base = v * SCALE
        value = misfit * state[(v + 1) * SUB : (v + 2) * SUB] * line_rows(factor, base, masks)
        whole = None
        for k, mask in enumerate(masks):
            part = jnp.sum(jnp.where(mask, value, 0.0), axis=0, keepdims=True)
            result = jnp.where(rows == base + 1 + k, part, result)
            whole = part if whole is None else whole + part
        result = jnp.where(rows == base, whole, result)
    return result


def children(factor, sums, mine, theirs, bit, misfits, masks):
    mine_factor, theirs_factor = factors_of(mine[0:SUB], theirs[0:SUB], bit)
    if factor is not None:
        mine_factor, theirs_factor = factor * mine_factor, factor * theirs_factor
    behind = (row_ids(mine.shape[1]) & (SCALE - 1)) == 0
    mine_sums = jnp.where(behind == (bit == 0), weighted_rows(theirs_factor, theirs, misfits, masks), 0.0)
    theirs_sums = jnp.where(behind == (bit == 1), weighted_rows(mine_factor, mine, misfits, masks), 0.0)
    if sums is not None:
        mine_sums, theirs_sums = sums + mine_sums, sums + theirs_sums
    return (mine_factor, mine_sums), (theirs_factor, theirs_sums)


def call_small(kernel, name, outs, operands, scratch=()):
    return pl.pallas_call(
        kernel,
        in_specs=[VMEM] * len(operands),
        out_specs=[VMEM] * len(outs),
        out_shape=[pltpu.VMEM(shape, F32) for shape in outs],
        scratch_shapes=[pltpu.VMEM(shape, F32) for shape in scratch],
        compiler_params=pltpu.CompilerParams(vmem_limit_bytes=4 * MIB),
        name=name,
    )(*operands)


def merge_kernel(shift, const_ref, mine_ref, theirs_ref, *refs):
    bit = (depth_place() >> shift) & 1
    state = merged_state(mine_ref[...], theirs_ref[...], bit, row_masks(const_ref, mine_ref.shape[1]))
    for i, tile in enumerate(state):
        refs[-1][i * SUB : (i + 1) * SUB, :] = tile


def depth_place():
    return lax.axis_index("far") * NEAR + lax.axis_index("near")


def result_kernel(levels, const_ref, target_ref, *refs):
    states, outs = refs[: 2 * levels], refs[-2:]
    depth, width = states[0].shape
    views = depth // SUB - 1
    place = depth_place()
    size = 2 * LANES
    masks = row_masks(const_ref, size)
    behind = (row_ids(size) & (SCALE - 1)) == 0
    for c in range(width // size):
        span = slice(c * size, (c + 1) * size)
        factor, sums = None, None
        for level in reversed(range(levels)):
            mine, theirs = states[2 * level][:, span], states[2 * level + 1][:, span]
            bit = (place >> level) & 1
            if level == levels - 1:
                signals = merged_state(mine, theirs, bit, masks)[1:]
                misfits = [signals[v] - target_ref[v * SUB : (v + 1) * SUB, span] for v in range(views)]
            contexts = children(factor, sums, mine, theirs, bit, misfits, masks)
            factor, sums = contexts[0]
        for ref, state, (factor, sums) in zip(outs, (mine, theirs), contexts):
            own = jnp.where(behind, weighted_rows(factor, state, misfits, masks), 0.0)
            for i, tile in enumerate(signals + [factor * state[0:SUB], sums + own]):
                ref[i * SUB : (i + 1) * SUB, span] = tile


def assemble_kernel(target_ref, mine_ref, sent_ref, package_ref, signal_ref):
    leads = (lax.axis_index("near") & 1) == 1
    package = jnp.where(leads, mine_ref[...], sent_ref[...])
    count = signal_ref.shape[0]
    signal_ref[...] = package[0:count]
    package_ref[0:count, :] = package[0:count] - target_ref[...]
    package_ref[count:, :] = package[count:]


def backward_kernel(views, cells, finish, prior, const_ref, package_ref, index_any, weight_any, *refs):
    if finish:
        signal_ref, refs = refs[0], refs[1:]
    u_refs, refs = refs[: len(views)], refs[len(views) :]
    n_refs, refs = refs[: len(views)], refs[len(views) :]
    if prior:
        prior_any, prior_left, prior_diff = refs[:3]
        refs = refs[3:]
    if finish:
        grad_hbm, signal_hbm, refs = refs[0], refs[1], refs[2:]
        left_pad, diff_pad, cell_ref, grad_ref, signal_rows, refs = refs[:5] + (refs[5:],)
    else:
        left_pad, diff_pad, refs = refs[:2] + (refs[2:],)
    mat, gain, carry, scaled, weight_ref, weight_rows, index_ref = refs[:7]
    prior_ref, sems = refs[7] if prior else None, refs[-1]
    count, slab, width = weight_ref.shape
    emissions = SCALE - 1
    tiles = width // LANES
    blocks = slab // BLOCK
    lanes, rows = lane_ids(), row_ids()
    margin = 2 * LANES
    pairs = [(index_any, index_ref), (weight_any, weight_ref)]
    if prior:
        pairs.append((prior_any, prior_ref))
    copies = copies_in(pairs, sems.at[pl.ds(blocks, len(pairs))])
    for copy in copies:
        copy.start()
    if finish:
        for v in range(signal_rows.shape[0]):
            signal_rows[v] = signal_ref[v * SUB : (v + 1) * SUB, :].reshape(SUB, 1, width)
        signal_copy = pltpu.make_async_copy(signal_rows, signal_hbm, sems.at[blocks + 3])
        signal_copy.start()
    masks = [const_ref[LINE_LANES] == k for k in range(emissions)]
    columns = [const_ref[k] for k in range(emissions + 1)]
    fill_matrix(mat, -columns[0], select_line(masks, columns[1:]), True, False)
    masks = [const_ref[LINE_ROWS] == k for k in range(emissions)]
    scale = const_ref[SCALE]
    columns = [column * cells for column in columns]
    for j in range(tiles):
        span = slice(j * LANES, (j + 1) * LANES)
        factor = package_ref[count * SUB : (count + 1) * SUB, span]
        sums = package_ref[(count + 1) * SUB : (count + 2) * SUB, span]
        for v in range(count):
            base = v * SCALE
            gain[v, :, span] = package_ref[v * SUB : (v + 1) * SUB, span] * scale * line_rows(factor, base, masks)
            back = columns[0] * jnp.broadcast_to(sums[base : base + 1], rows.shape)
            for k in range(1, emissions + 1):
                back = back + columns[k] * jnp.broadcast_to(sums[base + k : base + k + 1], rows.shape)
            carry[v, :, span] = back
    for ref in (left_pad, diff_pad):
        ref[:, :, :, 0:margin] = jnp.zeros(ref.shape[:3] + (margin,), F32)
        ref[:, :, :, margin + width + LANES :] = jnp.zeros(ref.shape[:3] + (margin,), F32)

    def one_block(block, _):
        slot = 0 if finish else block * BLOCK
        for v in range(count):
            u_ref, n_ref, at = u_refs[v], n_refs[v], views[v]
            for c in range(width // CHUNK):
                span = slice(c * CHUNK, (c + 1) * CHUNK)
                factor = gain[v, :, span][None]
                weighted = n_ref[at, block_rows(block), span].reshape(BLOCK, SUB, CHUNK) * factor
                direct = u_ref[at, block_rows(block), span].reshape(BLOCK, SUB, CHUNK) * factor
                lines, total = multiply(mat, weighted.reshape(ROWS, CHUNK))
                before = carry[v, :, span]
                lines = lines.reshape(BLOCK, SUB, CHUNK) + before[None]
                scaled[v, :, span] = (direct - lines).reshape(ROWS, CHUNK)
                carry[v, :, span] = before + total

        @pl.when(block == 0)
        def _():
            for copy in copies:
                copy.wait()

        weight_rows[...] = weight_ref[:, block_cells(block), :]
        for v in range(count):
            for d in range(BLOCK):
                _, rest = shift_of(index_ref, v, block * BLOCK + d, width)
                stay = lanes >= rest
                plain = [scaled[v, d * SUB : (d + 1) * SUB, j * LANES : (j + 1) * LANES] for j in range(tiles)]
                moved = [plain[j] * weight_rows[v, d : d + 1, j * LANES : (j + 1) * LANES] for j in range(tiles)]
                for ref, values in ((left_pad, plain), (diff_pad, moved)):
                    turned = [jnp.zeros((SUB, LANES), F32)]
                    turned += [pltpu.roll(value, rest, 1) for value in values]
                    turned += [jnp.zeros((SUB, LANES), F32)]
                    for j in range(tiles + 1):
                        span = slice(margin + j * LANES, margin + (j + 1) * LANES)
                        ref[v, slot + d, :, span] = jnp.where(stay, turned[j + 1], turned[j])
        if not finish:
            return 0
        for d in range(BLOCK):
            cell = block * BLOCK + d

            def gathered(ref, prior_pad):
                sources = [(ref, index_ref, v, d) for v in range(count)]
                if prior:
                    sources += [(prior_pad, prior_ref, v, cell) for v in range(prior)]
                sums = [None] * (tiles + 2)
                for pad, index, v, at in sources:
                    whole, _ = shift_of(index, v, cell, width)
                    for j in range(tiles + 2):
                        start = pl.multiple_of((2 + j - whole) * LANES, LANES)
                        value = pad[v, at, :, pl.ds(start, LANES)]
                        sums[j] = value if sums[j] is None else sums[j] + value
                return sums

            left = gathered(left_pad, prior_left if prior else None)
            diff = gathered(diff_pad, prior_diff if prior else None)
            left = [left[j] - diff[j] for j in range(tiles + 2)]

            def folded(sums):
                low = jnp.sum(sums[0], axis=1, keepdims=True)
                beyond = sums[tiles + 1] + jnp.where(lanes == LANES - 1, sums[tiles], 0.0)
                high = jnp.sum(beyond, axis=1, keepdims=True)
                core = sums[1 : tiles + 1]
                core[0] = core[0] + jnp.where(lanes == 0, low, 0.0)
                core[-1] = jnp.where(lanes == LANES - 1, 0.0, core[-1] + jnp.where(lanes == LANES - 2, high, 0.0))
                return core

            left, diff = folded(left), folded(diff)
            turned = [jnp.zeros((SUB, LANES), F32)] + [pltpu.roll(value, 1, 1) for value in diff]
            for j in range(tiles):
                value = left[j] + jnp.where(lanes == 0, turned[j], turned[j + 1])
                cell_ref[d, :, j * LANES : (j + 1) * LANES] = value
        grad_ref[block] = jnp.swapaxes(cell_ref[...], 0, 1)
        for b in range(blocks):

            @pl.when(block == b)
            def _():
                out_copies[b].start()

        return 0

    if finish:
        out_copies = [
            pltpu.make_async_copy(grad_ref.at[b], grad_hbm.at[:, pl.ds(b * BLOCK, BLOCK), :], sems.at[b])
            for b in range(blocks)
        ]
    lax.fori_loop(0, blocks, one_block, 0)
    if finish:
        for copy in out_copies + [signal_copy]:
            copy.wait()


def backward(package, const, column, weights, pieces, cells, signal, prior):
    finish = signal is not None
    signals = [signal[0]] if finish else []
    views, slab, width = weights.shape
    blocks = slab // BLOCK
    line = pltpu.VMEM((views, SUB, width), F32)
    depth = BLOCK if finish else slab
    padded = pltpu.VMEM((views, depth, SUB, width + 5 * LANES), F32)
    scratch = [
        pltpu.VMEM(MATRIX, BF16),
        line,
        line,
        pltpu.VMEM((views, ROWS, width), F32),
        pltpu.VMEM((views, slab, width), F32),
        pltpu.VMEM((views, BLOCK, width), F32),
        pltpu.SMEM((views, slab, LANES), jnp.int32),
    ]
    in_specs = [VMEM, VMEM, ANY, ANY] + [VMEM] * (2 * views + len(signals))
    if prior:
        in_specs += [ANY, VMEM, VMEM]
        scratch.append(pltpu.SMEM((views, slab, LANES), jnp.int32))
    scratch.append(pltpu.SemaphoreType.DMA((blocks + 4,)))
    if finish:
        scratch = [
            padded,
            padded,
            pltpu.VMEM((BLOCK, SUB, width), F32),
            pltpu.VMEM((blocks, SUB, BLOCK, width), F32),
            pltpu.VMEM(signal[1], F32),
        ] + scratch
    return pl.pallas_call(
        functools.partial(
            backward_kernel, tuple(at for _, _, at in pieces), cells, finish, views if prior else 0
        ),
        in_specs=in_specs,
        out_specs=[HBM, HBM] if finish else [VMEM, VMEM],
        out_shape=[pltpu.HBM((SUB, slab, width), F32), pltpu.HBM(signal[1], F32)] if finish else [padded, padded],
        scratch_shapes=scratch,
        compiler_params=pltpu.CompilerParams(vmem_limit_bytes=16 * MIB),
        name="backward_last" if finish else "backward_first",
    )(const, package, column, weights, *signals, *[u for u, _, _ in pieces], *[n for _, n, _ in pieces], *(prior or ()))


def body(concentration, shear_index, shear_weight, attenuation, yields, line_energy, measured):
    elements, _, slab, width = concentration.shape
    views = shear_weight.shape[0]
    emissions = attenuation.shape[0] - 1
    groups = lax.axis_size("far")
    both = lax.axis_size("views") == 2
    cells = float(slab * groups * NEAR)
    conc = concentration.reshape(elements, slab, width)
    scalars = (attenuation, line_energy, yields)

    def to_other(value):
        return lax.ppermute(value, "views", [(0, 1), (1, 0)])

    fillers = []

    def fill(after):
        if not both or len(fillers) == views:
            return ()
        pads = (mat, left_pad, diff_pad, after)
        fillers.append(forward_other(len(fillers), 0, slab, other_column, other_weight, *pads, ()))
        return (fillers[-1][3],)

    if both:
        other_weight = to_other(shear_weight)
    u, n, const, target, mat, left_pad, diff_pad, column, state = forward(
        conc, shear_index, shear_weight, scalars, measured, cells
    )

    def swap_cores(value):
        return lax.ppermute(value, "near", [(s, s ^ 1) for s in range(NEAR)])

    def swap_chips(value, step):
        pairs = [(s, s ^ step if s % 2 else s) for s in range(groups * NEAR)]
        return lax.ppermute(value, ("far", "near"), pairs)

    states = [state, swap_cores(state)]
    if both:
        other_column = to_other(column)
    tokens = (other_weight,) if both else ()
    levels = groups.bit_length() + 1
    for level in range(levels - 1):
        (state,) = call_small(
            functools.partial(merge_kernel, level), "merge", [state.shape], (const, *states[-2:], *tokens)
        )
        states += [state, swap_chips(state, 2 << level)]
        tokens = fill(state) if level else (other_column,) if both else ()
    package = ((views + 2) * SUB, width)
    mine, theirs = call_small(
        functools.partial(result_kernel, levels), "result", [package] * 2, (const, target, *states, *tokens)
    )
    sent = swap_cores(theirs)
    package, signal = call_small(assemble_kernel, "assemble", [package, target.shape], (target, mine, sent))
    own = [(u, n, v) for v in range(views)]
    signal = (signal, measured.shape)
    if both:
        other_package = to_other(package)
        pads = backward(package, const, column, shear_weight, own, cells, None, None)
        pieces = [(fillers[v][0], fillers[v][1], 0) for v in range(views)]
        gradient, signal = backward(
            other_package, const, other_column, other_weight, pieces, cells, signal, (column, *pads)
        )
    else:
        gradient, signal = backward(package, const, column, shear_weight, own, cells, signal, None)
        gradient = lax.psum(gradient, "views")
    return gradient.reshape(concentration.shape), signal


def solution(mesh):
    views, depth = mesh.shape["views"], mesh.shape["depth"]
    devices = mesh.devices.reshape(views, depth // NEAR, NEAR)
    split = jax.sharding.Mesh(devices, ("views", "far", "near"))
    depths = ("far", "near")
    return jax.shard_map(
        body,
        mesh=split,
        in_specs=(
            P(None, None, depths, None),
            P("views", depths, None),
            P("views", depths, None),
            P(),
            P(),
            P(),
            P("views", None, None, None),
        ),
        out_specs=(P(None, None, depths, None), P("views", None, None, None)),
        check_vma=False,
    )
```

```python
import functools

import jax
import jax.numpy as jnp
from jax import lax
from jax.experimental import pallas as pl
from jax.experimental.pallas import tpu as pltpu
from jax.sharding import PartitionSpec as P

LANES = 128
SUB = 8
BLOCK = 8
ROWS = BLOCK * SUB
NEAR = 4
CHUNK = 256
MIB = 1024 * 1024
F32 = jnp.float32
BF16 = jnp.bfloat16
HBM = pl.BlockSpec(memory_space=pltpu.HBM)
VMEM = pl.BlockSpec(memory_space=pltpu.VMEM)
SCALE, LINE_ROWS, LINE_LANES = 4, 5, 6
ANY = pl.BlockSpec(memory_space=pl.ANY)


def in_hbm(value):
    return pltpu.with_memory_space_constraint(value, pltpu.HBM)


def lane_ids(width=LANES):
    return lax.broadcasted_iota(jnp.int32, (SUB, width), 1)


def row_ids(width=LANES):
    return lax.broadcasted_iota(jnp.int32, (SUB, width), 0)


def tile_of(values, ids):
    tile = jnp.zeros(ids.shape, F32)
    for e in range(SUB):
        tile = jnp.where(ids == e, values[e], tile)
    return tile


def select_line(masks, values):
    result = values[0]
    for mask, value in zip(masks[1:], values[1:]):
        result = jnp.where(mask, value, result)
    return result


def fill_matrix(mat_ref, first_tile, second_tile, first_incl, second_incl):
    depth = (lane_ids() & (ROWS - 1)) >> 3
    tiles = []
    for d in range(BLOCK):
        one = jnp.where(depth <= d if first_incl else depth < d, first_tile, 0.0)
        two = jnp.where(depth <= d if second_incl else depth < d, second_tile, 0.0)
        tiles.append(one + two)
    tiles.append(first_tile + second_tile)
    tiles.append(jnp.zeros((SUB, LANES), F32))
    whole = jnp.concatenate(tiles, axis=0)
    high = whole.astype(BF16)
    mat_ref[:, 0:LANES] = high
    mat_ref[:, LANES : 2 * LANES] = (whole - high.astype(F32)).astype(BF16)


def multiply(mat_ref, values):
    high = values.astype(BF16)
    low = (values - high.astype(F32)).astype(BF16)
    stacked = jnp.concatenate([high, low, high], axis=0)
    product = jnp.dot(mat_ref[:, 0 : 3 * ROWS], stacked, preferred_element_type=F32)
    return product[0:ROWS], product[ROWS : ROWS + SUB]


MATRIX = (ROWS + 2 * SUB, 2 * LANES)


def copies_in(pairs, sems):
    return [pltpu.make_async_copy(source, target, sems.at[i]) for i, (source, target) in enumerate(pairs)]


def block_rows(block):
    return pl.ds(pl.multiple_of(block * ROWS, ROWS), ROWS)


def block_cells(block):
    return pl.ds(pl.multiple_of(block * BLOCK, BLOCK), BLOCK)


def shift_of(index_ref, v, cell, width):
    offset = index_ref[v, cell, 0] - (width // 2 - LANES)
    return offset >> 7, offset & (LANES - 1)


def shear(field, left_pad, diff_pad, index_ref, weight_ref, block, views, tiles):
    lanes = lane_ids()
    for i, v in enumerate(views):
        for d in range(BLOCK):
            cell = block * BLOCK + d
            whole, rest = shift_of(index_ref, v, cell, tiles * LANES)
            turn = (LANES - rest) & (LANES - 1)
            stay = lanes < LANES - rest

            def sheared(ref):
                turned = []
                for j in range(tiles + 1):
                    start = pl.multiple_of((whole + j) * LANES, LANES)
                    turned.append(pltpu.roll(ref[cell, :, pl.ds(start, LANES)], turn, 1))
                return [jnp.where(stay, turned[j], turned[j + 1]) for j in range(tiles)]

            left, diff = sheared(left_pad), sheared(diff_pad)
            for j in range(tiles):
                span = slice(j * LANES, (j + 1) * LANES)
                field[i, d * SUB : (d + 1) * SUB, span] = left[j] + weight_ref[i, d : d + 1, span] * diff[j]


def transmit(u_ref, n_ref, field, mat, carry, block, sums):
    views, _, width = field.shape
    for v in range(views):
        for c in range(width // CHUNK):
            span = slice(c * CHUNK, (c + 1) * CHUNK)
            value = field[v, :, span]
            lines, total = multiply(mat, value)
            before = carry[v, :, span]
            through = jnp.exp(lines.reshape(BLOCK, SUB, CHUNK) + before[None])
            value = value.reshape(BLOCK, SUB, CHUNK)
            emit = value * through
            u_ref[v, block_rows(block), span] = through.reshape(ROWS, CHUNK)
            n_ref[v, block_rows(block), span] = emit.reshape(ROWS, CHUNK)
            carry[v, :, span] = before + total
            if sums:
                sums[0][v, :, span] += jnp.sum(value, axis=0)
                sums[1][v, :, span] += jnp.sum(emit, axis=0)


def forward_kernel(cells, *refs):
    att_hbm, line_hbm, yield_hbm, index_hbm, conc_hbm, weight_hbm, measured_hbm = refs[:7]
    u_ref, n_ref, const_ref, target_ref, mat, left_pad, diff_pad, column_ref = refs[7:15]
    state_refs = refs[15:17]
    refs = refs[17:]
    conc_ref, weight_ref, weight_rows, field, carry, field_sum, emit_sum, measured_ref = refs[:8]
    att_ref, line_ref, yield_ref, index_ref, sems = refs[8:]
    views, slab, width = weight_ref.shape
    emissions = att_ref.shape[0] - 1
    tiles = width // LANES
    blocks = slab // BLOCK
    lanes, rows = lane_ids(), row_ids()
    conc_copies = [
        pltpu.make_async_copy(
            conc_hbm.at[:, pl.ds(b * BLOCK, BLOCK), :], conc_ref.at[:, pl.ds(b * BLOCK, BLOCK), :], sems.at[b]
        )
        for b in range(blocks)
    ]
    pairs = [
        (att_hbm, att_ref),
        (line_hbm, line_ref),
        (yield_hbm, yield_ref),
        (index_hbm.at[:, :, pl.ds(width // 2, LANES)], index_ref),
        (weight_hbm, weight_ref),
        (measured_hbm, measured_ref),
        (index_hbm.at[:, :, pl.ds(width // 2, LANES)], column_ref),
    ]
    copies = copies_in(pairs, sems.at[pl.ds(blocks, len(pairs))])
    for copy in conc_copies[:1] + copies[:4] + conc_copies[1:] + copies[4:]:
        copy.start()
    for ref in (carry, field_sum, emit_sum):
        ref[...] = jnp.zeros_like(ref)

    def one_block(block, _):
        for b in range(blocks):

            @pl.when(block == b)
            def _():
                conc_copies[b].wait()

        by_depth = jnp.swapaxes(conc_ref[:, block_cells(block), :], 0, 1)
        for d in range(BLOCK):
            pieces = [by_depth[d, :, j * LANES : (j + 1) * LANES] for j in range(tiles)]
            turned = [pltpu.roll(piece, LANES - 1, 1) for piece in pieces]
            after = [jnp.where(lanes < LANES - 1, turned[j], turned[min(j + 1, tiles - 1)]) for j in range(tiles)]
            steps = [after[j] - pieces[j] for j in range(tiles)]
            last_cell = jnp.broadcast_to(pieces[-1][:, LANES - 2 : LANES - 1], (SUB, LANES))
            last_step = jnp.broadcast_to(steps[-1][:, LANES - 2 : LANES - 1], (SUB, LANES))
            first_cell = jnp.broadcast_to(pieces[0][:, 0:1], (SUB, LANES))
            first_step = jnp.broadcast_to(steps[0][:, 0:1], (SUB, LANES))
            pieces[-1] = jnp.where(lanes < LANES - 1, pieces[-1], last_cell)
            steps[-1] = jnp.where(lanes < LANES - 1, steps[-1], last_step)
            pieces = [first_cell] + pieces + [last_cell, last_cell]
            steps = [first_step] + steps + [last_step, last_step]
            for j in range(tiles + 3):
                left_pad[block * BLOCK + d, :, j * LANES : (j + 1) * LANES] = pieces[j]
                diff_pad[block * BLOCK + d, :, j * LANES : (j + 1) * LANES] = steps[j]

        @pl.when(block == 0)
        def _():
            for copy in copies:
                copy.wait()
            line_by_row = tile_of([line_ref[e].astype(F32) for e in range(SUB)], rows)
            masks = [line_by_row == k for k in range(emissions)]
            by_lane = [tile_of([att_ref[k, e] for e in range(SUB)], lanes & 7) for k in range(emissions + 1)]
            fill_matrix(mat, -by_lane[0], select_line(masks, by_lane[1:]), False, True)
            for k in range(emissions + 1):
                const_ref[k] = tile_of([att_ref[k, e] for e in range(SUB)], rows)
            const_ref[SCALE] = tile_of([yield_ref[e] for e in range(SUB)], rows)
            const_ref[LINE_ROWS] = line_by_row
            const_ref[LINE_LANES] = tile_of([line_ref[e].astype(F32) for e in range(SUB)], lanes & 7)

        weight_rows[...] = weight_ref[:, block_cells(block), :]
        shear(field, left_pad, diff_pad, index_ref, weight_rows, block, range(views), tiles)
        transmit(u_ref, n_ref, field, mat, carry, block, (field_sum, emit_sum))
        return 0

    lax.fori_loop(0, blocks, one_block, 0)
    columns = [const_ref[k] for k in range(emissions + 1)]
    masks = [const_ref[LINE_ROWS] == k for k in range(emissions)]
    scale = const_ref[SCALE] * (1.0 / cells)
    share = width // 2
    core = lax.axis_index("near") & 1
    for r in range(2):
        for j in range(share // LANES):
            start = pl.multiple_of((core ^ r) * share + j * LANES, LANES)
            span = slice(j * LANES, (j + 1) * LANES)
            totals = jnp.zeros((SUB, LANES), F32)
            for v in range(views):
                values = field_sum[v, :, pl.ds(start, LANES)]
                sums = [jnp.sum(column * values, axis=0, keepdims=True) for column in columns]
                for k in range(emissions + 1):
                    totals = jnp.where(rows == v * (emissions + 1) + k, sums[k], totals)
                line_total = select_line(masks, [jnp.broadcast_to(value, rows.shape) for value in sums[1:]])
                signal = scale * emit_sum[v, :, pl.ds(start, LANES)] * jnp.exp(-line_total)
                state_refs[r][(v + 1) * SUB : (v + 2) * SUB, span] = signal
            state_refs[r][0:SUB, span] = jnp.exp(-totals)
    for v in range(views):
        target_ref[v * SUB : (v + 1) * SUB, :] = measured_ref[v].reshape(SUB, width)


def forward(conc, index, weights, scalars, measured, cells):
    views, slab, width = weights.shape
    attenuation, line_energy, yields = scalars
    values = pltpu.VMEM((views, slab * SUB, width), F32)
    padded = pltpu.VMEM((slab, SUB, width + 3 * LANES), F32)
    state = pltpu.VMEM(((views + 1) * SUB, width // 2), F32)
    line = pltpu.VMEM((views, SUB, width), F32)
    operands = [in_hbm(value) for value in (attenuation, line_energy, yields, index, conc, weights, measured)]
    return pl.pallas_call(
        functools.partial(forward_kernel, cells),
        in_specs=[HBM] * len(operands),
        out_specs=[VMEM] * 10,
        out_shape=[
            values,
            values,
            pltpu.VMEM((LINE_LANES + 1, SUB, LANES), F32),
            pltpu.VMEM((views * SUB, width), F32),
            pltpu.VMEM(MATRIX, BF16),
            padded,
            padded,
            pltpu.VMEM((views, slab, LANES), jnp.int32),
            state,
            state,
        ],
        scratch_shapes=[
            pltpu.VMEM((SUB, slab, width), F32),
            pltpu.VMEM((views, slab, width), F32),
            pltpu.VMEM((views, BLOCK, width), F32),
            pltpu.VMEM((views, ROWS, width), F32),
            line,
            line,
            line,
            pltpu.VMEM(measured.shape, F32),
            pltpu.SMEM(attenuation.shape, F32),
            pltpu.SMEM(line_energy.shape, jnp.int32),
            pltpu.SMEM(yields.shape, F32),
            pltpu.SMEM((views, slab, LANES), jnp.int32),
            pltpu.SemaphoreType.DMA((slab // BLOCK + 7,)),
        ],
        compiler_params=pltpu.CompilerParams(vmem_limit_bytes=16 * MIB),
        name="forward",
    )(*operands)


def forward_other_kernel(view, index_any, weight_any, mat, left_pad, diff_pad, order_ref, *refs):
    u_ref, n_ref, token_ref, weight_ref, weight_rows, field, carry, index_ref, sems = refs
    slab, width = weight_ref.shape[1:]
    copies = copies_in(
        ((index_any.at[pl.ds(view, 1)], index_ref), (weight_any.at[pl.ds(view, 1)], weight_ref)), sems
    )
    for copy in copies:
        copy.start()
    token_ref[...] = jnp.zeros_like(token_ref)
    carry[...] = jnp.zeros_like(carry)
    for copy in copies:
        copy.wait()

    def one_block(block, _):
        weight_rows[...] = weight_ref[:, block_cells(block), :]
        shear(field, left_pad, diff_pad, index_ref, weight_rows, block, (0,), width // LANES)
        transmit(u_ref, n_ref, field, mat, carry, block, None)
        return 0

    lax.fori_loop(0, slab // BLOCK, one_block, 0)


def forward_other(view, column, weights, mat, left_pad, diff_pad, after):
    _, slab, width = weights.shape
    values = pltpu.VMEM((1, slab * SUB, width), F32)
    return pl.pallas_call(
        functools.partial(forward_other_kernel, view),
        in_specs=[ANY, ANY] + [VMEM] * 4,
        out_specs=[VMEM] * 3,
        out_shape=[values, values, pltpu.VMEM((SUB, LANES), F32)],
        scratch_shapes=[
            pltpu.VMEM((1, slab, width), F32),
            pltpu.VMEM((1, BLOCK, width), F32),
            pltpu.VMEM((1, ROWS, width), F32),
            pltpu.VMEM((1, SUB, width), F32),
            pltpu.SMEM((1, slab, LANES), jnp.int32),
            pltpu.SemaphoreType.DMA((2,)),
        ],
        compiler_params=pltpu.CompilerParams(vmem_limit_bytes=8 * MIB),
        name="forward_other",
    )(column, weights, mat, left_pad, diff_pad, after)


def line_rows(tile, base, masks):
    shape = masks[0].shape
    return select_line(masks, [jnp.broadcast_to(tile[base + 1 + k : base + 2 + k], shape) for k in range(len(masks))])


def incident_rows(tile, step):
    rows = row_ids(tile.shape[1])
    result = jnp.broadcast_to(tile[0:1], tile.shape)
    for base in range(step, SUB, step):
        result = jnp.where(rows >= base, jnp.broadcast_to(tile[base : base + 1], tile.shape), result)
    return result


def row_masks(const_ref, width):
    tile = const_ref[LINE_ROWS]
    return [jnp.concatenate([tile] * (width // LANES), axis=1) == k for k in range(SCALE - 1)]


def factors_of(mine, theirs, bit):
    mine_factor = jnp.where(bit == 0, theirs, incident_rows(theirs, SCALE))
    return mine_factor, jnp.where(bit == 0, incident_rows(mine, SCALE), mine)


def merged_state(mine, theirs, bit, masks):
    mine_factor, theirs_factor = factors_of(mine[0:SUB], theirs[0:SUB], bit)
    result = [mine[0:SUB] * theirs[0:SUB]]
    for v in range(mine.shape[0] // SUB - 1):
        span = slice((v + 1) * SUB, (v + 2) * SUB)
        result.append(
            mine[span] * line_rows(mine_factor, v * SCALE, masks)
            + theirs[span] * line_rows(theirs_factor, v * SCALE, masks)
        )
    return result


def weighted_rows(factor, state, misfits, masks):
    rows = row_ids(state.shape[1])
    result = jnp.zeros((SUB, state.shape[1]), F32)
    for v, misfit in enumerate(misfits):
        base = v * SCALE
        value = misfit * state[(v + 1) * SUB : (v + 2) * SUB] * line_rows(factor, base, masks)
        whole = None
        for k, mask in enumerate(masks):
            part = jnp.sum(jnp.where(mask, value, 0.0), axis=0, keepdims=True)
            result = jnp.where(rows == base + 1 + k, part, result)
            whole = part if whole is None else whole + part
        result = jnp.where(rows == base, whole, result)
    return result


def children(factor, sums, mine, theirs, bit, misfits, masks):
    mine_factor, theirs_factor = factors_of(mine[0:SUB], theirs[0:SUB], bit)
    if factor is not None:
        mine_factor, theirs_factor = factor * mine_factor, factor * theirs_factor
    behind = (row_ids(mine.shape[1]) & (SCALE - 1)) == 0
    mine_sums = jnp.where(behind == (bit == 0), weighted_rows(theirs_factor, theirs, misfits, masks), 0.0)
    theirs_sums = jnp.where(behind == (bit == 1), weighted_rows(mine_factor, mine, misfits, masks), 0.0)
    if sums is not None:
        mine_sums, theirs_sums = sums + mine_sums, sums + theirs_sums
    return (mine_factor, mine_sums), (theirs_factor, theirs_sums)


def call_small(kernel, name, outs, operands, scratch=()):
    return pl.pallas_call(
        kernel,
        in_specs=[VMEM] * len(operands),
        out_specs=[VMEM] * len(outs),
        out_shape=[pltpu.VMEM(shape, F32) for shape in outs],
        scratch_shapes=[pltpu.VMEM(shape, F32) for shape in scratch],
        compiler_params=pltpu.CompilerParams(vmem_limit_bytes=4 * MIB),
        name=name,
    )(*operands)


def merge_kernel(shift, const_ref, mine_ref, theirs_ref, *refs):
    bit = (depth_place() >> shift) & 1
    state = merged_state(mine_ref[...], theirs_ref[...], bit, row_masks(const_ref, mine_ref.shape[1]))
    for i, tile in enumerate(state):
        refs[-1][i * SUB : (i + 1) * SUB, :] = tile


def depth_place():
    return lax.axis_index("far") * NEAR + lax.axis_index("near")


def result_kernel(levels, const_ref, target_ref, *refs):
    states, outs = refs[: 2 * levels], refs[-2:]
    depth, width = states[0].shape
    views = depth // SUB - 1
    place = depth_place()
    size = 2 * LANES
    start = (place & 1) * width
    masks = row_masks(const_ref, size)
    behind = (row_ids(size) & (SCALE - 1)) == 0
    for c in range(width // size):
        span = slice(c * size, (c + 1) * size)
        factor, sums = None, None
        for level in reversed(range(levels)):
            mine, theirs = states[2 * level][:, span], states[2 * level + 1][:, span]
            bit = (place >> level) & 1
            if level == levels - 1:
                signals = merged_state(mine, theirs, bit, masks)[1:]
                there = pl.ds(pl.multiple_of(start + c * size, LANES), size)
                misfits = [signals[v] - target_ref[v * SUB : (v + 1) * SUB, there] for v in range(views)]
            contexts = children(factor, sums, mine, theirs, bit, misfits, masks)
            factor, sums = contexts[0]
        for ref, state, (factor, sums) in zip(outs, (mine, theirs), contexts):
            own = jnp.where(behind, weighted_rows(factor, state, misfits, masks), 0.0)
            for i, tile in enumerate(signals + [factor * state[0:SUB], sums + own]):
                ref[i * SUB : (i + 1) * SUB, span] = tile


def assemble_kernel(target_ref, here_ref, there_ref, package_ref, signal_ref):
    half = here_ref.shape[1]
    count = signal_ref.shape[0]
    at = pl.multiple_of((lax.axis_index("near") & 1) * half, LANES)
    for ref, start in ((here_ref, at), (there_ref, pl.multiple_of(half - at, LANES))):
        span = pl.ds(start, half)
        signal_ref[:, span] = ref[0:count, :]
        package_ref[0:count, span] = ref[0:count, :] - target_ref[:, span]
        package_ref[count:, span] = ref[count:, :]


def backward_kernel(views, cells, finish, prior, const_ref, package_ref, index_any, weight_any, *refs):
    if finish:
        signal_ref, refs = refs[0], refs[1:]
    u_refs, refs = refs[: len(views)], refs[len(views) :]
    n_refs, refs = refs[: len(views)], refs[len(views) :]
    if prior:
        prior_any, prior_left, prior_diff = refs[:3]
        refs = refs[3:]
    if finish:
        grad_hbm, signal_hbm, refs = refs[0], refs[1], refs[2:]
        left_pad, diff_pad, cell_ref, grad_ref, signal_rows, refs = refs[:5] + (refs[5:],)
    else:
        left_pad, diff_pad, refs = refs[:2] + (refs[2:],)
    mat, gain, carry, scaled, weight_ref, weight_rows, index_ref = refs[:7]
    prior_ref, sems = refs[7] if prior else None, refs[-1]
    count, slab, width = weight_ref.shape
    emissions = SCALE - 1
    tiles = width // LANES
    blocks = slab // BLOCK
    lanes, rows = lane_ids(), row_ids()
    margin = 2 * LANES
    pairs = [(index_any, index_ref), (weight_any, weight_ref)]
    if prior:
        pairs.append((prior_any, prior_ref))
    copies = copies_in(pairs, sems.at[pl.ds(blocks, len(pairs))])
    for copy in copies:
        copy.start()
    if finish:
        for v in range(signal_rows.shape[0]):
            signal_rows[v] = signal_ref[v * SUB : (v + 1) * SUB, :].reshape(SUB, 1, width)
        signal_copy = pltpu.make_async_copy(signal_rows, signal_hbm, sems.at[blocks + 3])
        signal_copy.start()
    masks = [const_ref[LINE_LANES] == k for k in range(emissions)]
    columns = [const_ref[k] for k in range(emissions + 1)]
    fill_matrix(mat, -columns[0], select_line(masks, columns[1:]), True, False)
    masks = [const_ref[LINE_ROWS] == k for k in range(emissions)]
    scale = const_ref[SCALE]
    columns = [column * cells for column in columns]
    for j in range(tiles):
        span = slice(j * LANES, (j + 1) * LANES)
        factor = package_ref[count * SUB : (count + 1) * SUB, span]
        sums = package_ref[(count + 1) * SUB : (count + 2) * SUB, span]
        for v in range(count):
            base = v * SCALE
            gain[v, :, span] = package_ref[v * SUB : (v + 1) * SUB, span] * scale * line_rows(factor, base, masks)
            back = columns[0] * jnp.broadcast_to(sums[base : base + 1], rows.shape)
            for k in range(1, emissions + 1):
                back = back + columns[k] * jnp.broadcast_to(sums[base + k : base + k + 1], rows.shape)
            carry[v, :, span] = back
    for ref in (left_pad, diff_pad):
        ref[:, :, :, 0:margin] = jnp.zeros(ref.shape[:3] + (margin,), F32)
        ref[:, :, :, margin + width + LANES :] = jnp.zeros(ref.shape[:3] + (margin,), F32)

    def one_block(block, _):
        slot = 0 if finish else block * BLOCK
        for v in range(count):
            u_ref, n_ref, at = u_refs[v], n_refs[v], views[v]
            for c in range(width // CHUNK):
                span = slice(c * CHUNK, (c + 1) * CHUNK)
                factor = gain[v, :, span][None]
                weighted = n_ref[at, block_rows(block), span].reshape(BLOCK, SUB, CHUNK) * factor
                direct = u_ref[at, block_rows(block), span].reshape(BLOCK, SUB, CHUNK) * factor
                lines, total = multiply(mat, weighted.reshape(ROWS, CHUNK))
                before = carry[v, :, span]
                lines = lines.reshape(BLOCK, SUB, CHUNK) + before[None]
                scaled[v, :, span] = (direct - lines).reshape(ROWS, CHUNK)
                carry[v, :, span] = before + total

        @pl.when(block == 0)
        def _():
            for copy in copies:
                copy.wait()

        weight_rows[...] = weight_ref[:, block_cells(block), :]
        for v in range(count):
            for d in range(BLOCK):
                _, rest = shift_of(index_ref, v, block * BLOCK + d, width)
                stay = lanes >= rest
                plain = [scaled[v, d * SUB : (d + 1) * SUB, j * LANES : (j + 1) * LANES] for j in range(tiles)]
                moved = [plain[j] * weight_rows[v, d : d + 1, j * LANES : (j + 1) * LANES] for j in range(tiles)]
                for ref, values in ((left_pad, plain), (diff_pad, moved)):
                    turned = [jnp.zeros((SUB, LANES), F32)]
                    turned += [pltpu.roll(value, rest, 1) for value in values]
                    turned += [jnp.zeros((SUB, LANES), F32)]
                    for j in range(tiles + 1):
                        span = slice(margin + j * LANES, margin + (j + 1) * LANES)
                        ref[v, slot + d, :, span] = jnp.where(stay, turned[j + 1], turned[j])
        if not finish:
            return 0
        for d in range(BLOCK):
            cell = block * BLOCK + d

            def gathered(ref, prior_pad):
                sources = [(ref, index_ref, v, d) for v in range(count)]
                if prior:
                    sources += [(prior_pad, prior_ref, v, cell) for v in range(prior)]
                sums = [None] * (tiles + 2)
                for pad, index, v, at in sources:
                    whole, _ = shift_of(index, v, cell, width)
                    for j in range(tiles + 2):
                        start = pl.multiple_of((2 + j - whole) * LANES, LANES)
                        value = pad[v, at, :, pl.ds(start, LANES)]
                        sums[j] = value if sums[j] is None else sums[j] + value
                return sums

            left = gathered(left_pad, prior_left if prior else None)
            diff = gathered(diff_pad, prior_diff if prior else None)
            left = [left[j] - diff[j] for j in range(tiles + 2)]

            def folded(sums):
                low = jnp.sum(sums[0], axis=1, keepdims=True)
                beyond = sums[tiles + 1] + jnp.where(lanes == LANES - 1, sums[tiles], 0.0)
                high = jnp.sum(beyond, axis=1, keepdims=True)
                core = sums[1 : tiles + 1]
                core[0] = core[0] + jnp.where(lanes == 0, low, 0.0)
                core[-1] = jnp.where(lanes == LANES - 1, 0.0, core[-1] + jnp.where(lanes == LANES - 2, high, 0.0))
                return core

            left, diff = folded(left), folded(diff)
            turned = [jnp.zeros((SUB, LANES), F32)] + [pltpu.roll(value, 1, 1) for value in diff]
            for j in range(tiles):
                value = left[j] + jnp.where(lanes == 0, turned[j], turned[j + 1])
                cell_ref[d, :, j * LANES : (j + 1) * LANES] = value
        grad_ref[block] = jnp.swapaxes(cell_ref[...], 0, 1)
        for b in range(blocks):

            @pl.when(block == b)
            def _():
                out_copies[b].start()

        return 0

    if finish:
        out_copies = [
            pltpu.make_async_copy(grad_ref.at[b], grad_hbm.at[:, pl.ds(b * BLOCK, BLOCK), :], sems.at[b])
            for b in range(blocks)
        ]
    lax.fori_loop(0, blocks, one_block, 0)
    if finish:
        for copy in out_copies + [signal_copy]:
            copy.wait()


def backward(package, const, column, weights, pieces, cells, signal, prior):
    finish = signal is not None
    signals = [signal[0]] if finish else []
    views, slab, width = weights.shape
    blocks = slab // BLOCK
    line = pltpu.VMEM((views, SUB, width), F32)
    depth = BLOCK if finish else slab
    padded = pltpu.VMEM((views, depth, SUB, width + 5 * LANES), F32)
    scratch = [
        pltpu.VMEM(MATRIX, BF16),
        line,
        line,
        pltpu.VMEM((views, ROWS, width), F32),
        pltpu.VMEM((views, slab, width), F32),
        pltpu.VMEM((views, BLOCK, width), F32),
        pltpu.SMEM((views, slab, LANES), jnp.int32),
    ]
    in_specs = [VMEM, VMEM, ANY, ANY] + [VMEM] * (2 * views + len(signals))
    if prior:
        in_specs += [ANY, VMEM, VMEM]
        scratch.append(pltpu.SMEM((views, slab, LANES), jnp.int32))
    scratch.append(pltpu.SemaphoreType.DMA((blocks + 4,)))
    if finish:
        scratch = [
            padded,
            padded,
            pltpu.VMEM((BLOCK, SUB, width), F32),
            pltpu.VMEM((blocks, SUB, BLOCK, width), F32),
            pltpu.VMEM(signal[1], F32),
        ] + scratch
    return pl.pallas_call(
        functools.partial(
            backward_kernel, tuple(at for _, _, at in pieces), cells, finish, views if prior else 0
        ),
        in_specs=in_specs,
        out_specs=[HBM, HBM] if finish else [VMEM, VMEM],
        out_shape=[pltpu.HBM((SUB, slab, width), F32), pltpu.HBM(signal[1], F32)] if finish else [padded, padded],
        scratch_shapes=scratch,
        compiler_params=pltpu.CompilerParams(vmem_limit_bytes=16 * MIB),
        name="backward_last" if finish else "backward_first",
    )(const, package, column, weights, *signals, *[u for u, _, _ in pieces], *[n for _, n, _ in pieces], *(prior or ()))


def body(concentration, shear_index, shear_weight, attenuation, yields, line_energy, measured):
    elements, _, slab, width = concentration.shape
    views = shear_weight.shape[0]
    emissions = attenuation.shape[0] - 1
    groups = lax.axis_size("far")
    both = lax.axis_size("views") == 2
    cells = float(slab * groups * NEAR)
    conc = concentration.reshape(elements, slab, width)
    scalars = (attenuation, line_energy, yields)

    def to_other(value):
        return lax.ppermute(value, "views", [(0, 1), (1, 0)])

    fillers = []

    def fill(after):
        if not both or len(fillers) == views:
            return ()
        pads = (mat, left_pad, diff_pad, after)
        fillers.append(forward_other(len(fillers), other_column, other_weight, *pads))
        return (fillers[-1][2],)

    if both:
        other_weight = to_other(shear_weight)
    u, n, const, target, mat, left_pad, diff_pad, column, state, send = forward(
        conc, shear_index, shear_weight, scalars, measured, cells
    )
    if both:
        other_column = to_other(column)

    def swap(value, axis, step):
        return lax.ppermute(value, axis, [(s, s ^ step) for s in range(lax.axis_size(axis))])

    states = [state, swap(send, "near", 1)]
    tokens = (other_weight,) if both else ()
    levels = groups.bit_length() + 1
    for level in range(levels - 1):
        (state,) = call_small(
            functools.partial(merge_kernel, level), "merge", [state.shape], (const, *states[-2:], *tokens)
        )
        if level == 0:
            states += [state, swap(state, "near", 2)]
            tokens = (other_column,) if both else ()
        else:
            states += [state, swap(state, "far", 1 << (level - 1))]
            tokens = fill(state)
    half = ((views + 2) * SUB, width // 2)
    here, there = call_small(
        functools.partial(result_kernel, levels), "result", [half] * 2, (const, target, *states, *tokens)
    )
    there = swap(there, "near", 1)
    package = (half[0], width)
    package, signal = call_small(assemble_kernel, "assemble", [package, target.shape], (target, here, there))
    own = [(u, n, v) for v in range(views)]
    signal = (signal, measured.shape)
    if both:
        other_package = to_other(package)
        pads = backward(package, const, column, shear_weight, own, cells, None, None)
        pieces = [(fillers[v][0], fillers[v][1], 0) for v in range(views)]
        gradient, signal = backward(
            other_package, const, other_column, other_weight, pieces, cells, signal, (column, *pads)
        )
    else:
        gradient, signal = backward(package, const, column, shear_weight, own, cells, signal, None)
        gradient = lax.psum(gradient, "views")
    return gradient.reshape(concentration.shape), signal


def solution(mesh):
    views, depth = mesh.shape["views"], mesh.shape["depth"]
    devices = mesh.devices.reshape(views, depth // NEAR, NEAR)
    split = jax.sharding.Mesh(devices, ("views", "far", "near"))
    depths = ("far", "near")
    return jax.shard_map(
        body,
        mesh=split,
        in_specs=(
            P(None, None, depths, None),
            P("views", depths, None),
            P("views", depths, None),
            P(),
            P(),
            P(),
            P("views", None, None, None),
        ),
        out_specs=(P(None, None, depths, None), P("views", None, None, None)),
        check_vma=False,
    )
```

```python
import functools

import jax
import jax.numpy as jnp
from jax import lax
from jax.experimental import pallas as pl
from jax.experimental.pallas import tpu as pltpu
from jax.sharding import PartitionSpec as P

LANES = 128
SUB = 8
BLOCK = 8
ROWS = BLOCK * SUB
NEAR = 4
CHUNK = 256
MIB = 1024 * 1024
F32 = jnp.float32
BF16 = jnp.bfloat16
HBM = pl.BlockSpec(memory_space=pltpu.HBM)
VMEM = pl.BlockSpec(memory_space=pltpu.VMEM)
SCALE, LINE_ROWS, LINE_LANES = 4, 5, 6
ANY = pl.BlockSpec(memory_space=pl.ANY)


def in_hbm(value):
    return pltpu.with_memory_space_constraint(value, pltpu.HBM)


def lane_ids(width=LANES):
    return lax.broadcasted_iota(jnp.int32, (SUB, width), 1)


def row_ids(width=LANES):
    return lax.broadcasted_iota(jnp.int32, (SUB, width), 0)


def tile_of(values, ids):
    tile = jnp.zeros(ids.shape, F32)
    for e in range(SUB):
        tile = jnp.where(ids == e, values[e], tile)
    return tile


def select_line(masks, values):
    result = values[0]
    for mask, value in zip(masks[1:], values[1:]):
        result = jnp.where(mask, value, result)
    return result


def fill_matrix(mat_ref, first_tile, second_tile, first_incl, second_incl):
    depth = (lane_ids() & (ROWS - 1)) >> 3
    tiles = []
    for d in range(BLOCK):
        one = jnp.where(depth <= d if first_incl else depth < d, first_tile, 0.0)
        two = jnp.where(depth <= d if second_incl else depth < d, second_tile, 0.0)
        tiles.append(one + two)
    tiles.append(first_tile + second_tile)
    tiles.append(jnp.zeros((SUB, LANES), F32))
    whole = jnp.concatenate(tiles, axis=0)
    high = whole.astype(BF16)
    mat_ref[:, 0:LANES] = high
    mat_ref[:, LANES : 2 * LANES] = (whole - high.astype(F32)).astype(BF16)


def multiply(mat_ref, values):
    high = values.astype(BF16)
    low = (values - high.astype(F32)).astype(BF16)
    stacked = jnp.concatenate([high, low, high], axis=0)
    product = jnp.dot(mat_ref[:, 0 : 3 * ROWS], stacked, preferred_element_type=F32)
    return product[0:ROWS], product[ROWS : ROWS + SUB]


MATRIX = (ROWS + 2 * SUB, 2 * LANES)


def copies_in(pairs, sems):
    return [pltpu.make_async_copy(source, target, sems.at[i]) for i, (source, target) in enumerate(pairs)]


def block_rows(block):
    return slice(block * ROWS, (block + 1) * ROWS)


def block_cells(block):
    return slice(block * BLOCK, (block + 1) * BLOCK)


def shift_of(index_ref, v, cell, width):
    offset = index_ref[v, cell, 0] - (width // 2 - LANES)
    return offset >> 7, offset & (LANES - 1)


def shear(field, left_pad, diff_pad, index_ref, weight_ref, block, views, tiles):
    lanes = lane_ids()
    for i, v in enumerate(views):
        for d in range(BLOCK):
            cell = block * BLOCK + d
            whole, rest = shift_of(index_ref, v, cell, tiles * LANES)
            turn = (LANES - rest) & (LANES - 1)
            stay = lanes < LANES - rest

            def sheared(ref):
                turned = []
                for j in range(tiles + 1):
                    start = pl.multiple_of((whole + j) * LANES, LANES)
                    turned.append(pltpu.roll(ref[cell, :, pl.ds(start, LANES)], turn, 1))
                return [jnp.where(stay, turned[j], turned[j + 1]) for j in range(tiles)]

            left, diff = sheared(left_pad), sheared(diff_pad)
            for j in range(tiles):
                span = slice(j * LANES, (j + 1) * LANES)
                field[i, d * SUB : (d + 1) * SUB, span] = left[j] + weight_ref[i, cell : cell + 1, span] * diff[j]


def transmit(u_ref, n_ref, field, mat, carry, block, sums):
    views, _, width = field.shape
    for v in range(views):
        for c in range(width // CHUNK):
            span = slice(c * CHUNK, (c + 1) * CHUNK)
            value = field[v, :, span]
            lines, total = multiply(mat, value)
            before = carry[v, :, span]
            through = jnp.exp(lines.reshape(BLOCK, SUB, CHUNK) + before[None])
            value = value.reshape(BLOCK, SUB, CHUNK)
            emit = value * through
            u_ref[v, block_rows(block), span] = through.reshape(ROWS, CHUNK)
            n_ref[v, block_rows(block), span] = emit.reshape(ROWS, CHUNK)
            carry[v, :, span] = before + total
            if sums:
                sums[0][v, :, span] += jnp.sum(value, axis=0)
                sums[1][v, :, span] += jnp.sum(emit, axis=0)


def forward_kernel(cells, *refs):
    att_hbm, line_hbm, yield_hbm, index_hbm, conc_hbm, weight_hbm, measured_hbm = refs[:7]
    u_ref, n_ref, const_ref, target_ref, mat, left_pad, diff_pad, column_ref = refs[7:15]
    state_refs = refs[15:17]
    refs = refs[17:]
    conc_ref, weight_ref, field, carry, field_sum, emit_sum, measured_ref = refs[:7]
    att_ref, line_ref, yield_ref, index_ref, sems = refs[7:]
    views, slab, width = weight_ref.shape
    emissions = att_ref.shape[0] - 1
    tiles = width // LANES
    blocks = slab // BLOCK
    lanes, rows = lane_ids(), row_ids()
    conc_copies = [
        pltpu.make_async_copy(
            conc_hbm.at[:, pl.ds(b * BLOCK, BLOCK), :], conc_ref.at[:, pl.ds(b * BLOCK, BLOCK), :], sems.at[b]
        )
        for b in range(blocks)
    ]
    pairs = [
        (att_hbm, att_ref),
        (line_hbm, line_ref),
        (yield_hbm, yield_ref),
        (index_hbm.at[:, :, pl.ds(width // 2, LANES)], index_ref),
        (weight_hbm, weight_ref),
        (measured_hbm, measured_ref),
        (index_hbm.at[:, :, pl.ds(width // 2, LANES)], column_ref),
    ]
    copies = copies_in(pairs, sems.at[pl.ds(blocks, len(pairs))])
    for copy in conc_copies[:1] + copies[:4] + conc_copies[1:] + copies[4:]:
        copy.start()
    for ref in (carry, field_sum, emit_sum):
        ref[...] = jnp.zeros_like(ref)

    def one_block(block):
        conc_copies[block].wait()
        by_depth = jnp.swapaxes(conc_ref[:, block_cells(block), :], 0, 1)
        for d in range(BLOCK):
            pieces = [by_depth[d, :, j * LANES : (j + 1) * LANES] for j in range(tiles)]
            turned = [pltpu.roll(piece, LANES - 1, 1) for piece in pieces]
            after = [jnp.where(lanes < LANES - 1, turned[j], turned[min(j + 1, tiles - 1)]) for j in range(tiles)]
            steps = [after[j] - pieces[j] for j in range(tiles)]
            last_cell = jnp.broadcast_to(pieces[-1][:, LANES - 2 : LANES - 1], (SUB, LANES))
            last_step = jnp.broadcast_to(steps[-1][:, LANES - 2 : LANES - 1], (SUB, LANES))
            first_cell = jnp.broadcast_to(pieces[0][:, 0:1], (SUB, LANES))
            first_step = jnp.broadcast_to(steps[0][:, 0:1], (SUB, LANES))
            pieces[-1] = jnp.where(lanes < LANES - 1, pieces[-1], last_cell)
            steps[-1] = jnp.where(lanes < LANES - 1, steps[-1], last_step)
            pieces = [first_cell] + pieces + [last_cell, last_cell]
            steps = [first_step] + steps + [last_step, last_step]
            for j in range(tiles + 3):
                left_pad[block * BLOCK + d, :, j * LANES : (j + 1) * LANES] = pieces[j]
                diff_pad[block * BLOCK + d, :, j * LANES : (j + 1) * LANES] = steps[j]

        if block == 0:
            for copy in copies:
                copy.wait()
            line_by_row = tile_of([line_ref[e].astype(F32) for e in range(SUB)], rows)
            masks = [line_by_row == k for k in range(emissions)]
            by_lane = [tile_of([att_ref[k, e] for e in range(SUB)], lanes & 7) for k in range(emissions + 1)]
            fill_matrix(mat, -by_lane[0], select_line(masks, by_lane[1:]), False, True)
            for k in range(emissions + 1):
                const_ref[k] = tile_of([att_ref[k, e] for e in range(SUB)], rows)
            const_ref[SCALE] = tile_of([yield_ref[e] for e in range(SUB)], rows)
            const_ref[LINE_ROWS] = line_by_row
            const_ref[LINE_LANES] = tile_of([line_ref[e].astype(F32) for e in range(SUB)], lanes & 7)

        shear(field, left_pad, diff_pad, index_ref, weight_ref, block, range(views), tiles)
        transmit(u_ref, n_ref, field, mat, carry, block, (field_sum, emit_sum))

    for block in range(blocks):
        one_block(block)
    columns = [const_ref[k] for k in range(emissions + 1)]
    masks = [const_ref[LINE_ROWS] == k for k in range(emissions)]
    scale = const_ref[SCALE] * (1.0 / cells)
    share = width // 2
    core = lax.axis_index("near") & 1
    for r in range(2):
        for j in range(share // LANES):
            start = pl.multiple_of((core ^ r) * share + j * LANES, LANES)
            span = slice(j * LANES, (j + 1) * LANES)
            totals = jnp.zeros((SUB, LANES), F32)
            for v in range(views):
                values = field_sum[v, :, pl.ds(start, LANES)]
                sums = [jnp.sum(column * values, axis=0, keepdims=True) for column in columns]
                for k in range(emissions + 1):
                    totals = jnp.where(rows == v * (emissions + 1) + k, sums[k], totals)
                line_total = select_line(masks, [jnp.broadcast_to(value, rows.shape) for value in sums[1:]])
                signal = scale * emit_sum[v, :, pl.ds(start, LANES)] * jnp.exp(-line_total)
                state_refs[r][(v + 1) * SUB : (v + 2) * SUB, span] = signal
            state_refs[r][0:SUB, span] = jnp.exp(-totals)
    for v in range(views):
        target_ref[v * SUB : (v + 1) * SUB, :] = measured_ref[v].reshape(SUB, width)


def forward(conc, index, weights, scalars, measured, cells):
    views, slab, width = weights.shape
    attenuation, line_energy, yields = scalars
    values = pltpu.VMEM((views, slab * SUB, width), F32)
    padded = pltpu.VMEM((slab, SUB, width + 3 * LANES), F32)
    state = pltpu.VMEM(((views + 1) * SUB, width // 2), F32)
    line = pltpu.VMEM((views, SUB, width), F32)
    operands = [in_hbm(value) for value in (attenuation, line_energy, yields, index, conc, weights, measured)]
    return pl.pallas_call(
        functools.partial(forward_kernel, cells),
        in_specs=[HBM] * len(operands),
        out_specs=[VMEM] * 10,
        out_shape=[
            values,
            values,
            pltpu.VMEM((LINE_LANES + 1, SUB, LANES), F32),
            pltpu.VMEM((views * SUB, width), F32),
            pltpu.VMEM(MATRIX, BF16),
            padded,
            padded,
            pltpu.VMEM((views, slab, LANES), jnp.int32),
            state,
            state,
        ],
        scratch_shapes=[
            pltpu.VMEM((SUB, slab, width), F32),
            pltpu.VMEM((views, slab, width), F32),
            pltpu.VMEM((views, ROWS, width), F32),
            line,
            line,
            line,
            pltpu.VMEM(measured.shape, F32),
            pltpu.SMEM(attenuation.shape, F32),
            pltpu.SMEM(line_energy.shape, jnp.int32),
            pltpu.SMEM(yields.shape, F32),
            pltpu.SMEM((views, slab, LANES), jnp.int32),
            pltpu.SemaphoreType.DMA((slab // BLOCK + 7,)),
        ],
        compiler_params=pltpu.CompilerParams(vmem_limit_bytes=16 * MIB),
        name="forward",
    )(*operands)


def forward_other_kernel(view, index_any, weight_any, mat, left_pad, diff_pad, order_ref, *refs):
    u_ref, n_ref, token_ref, weight_ref, field, carry, index_ref, sems = refs
    slab, width = weight_ref.shape[1:]
    copies = copies_in(
        ((index_any.at[pl.ds(view, 1)], index_ref), (weight_any.at[pl.ds(view, 1)], weight_ref)), sems
    )
    for copy in copies:
        copy.start()
    token_ref[...] = jnp.zeros_like(token_ref)
    carry[...] = jnp.zeros_like(carry)
    for copy in copies:
        copy.wait()

    for block in range(slab // BLOCK):
        shear(field, left_pad, diff_pad, index_ref, weight_ref, block, (0,), width // LANES)
        transmit(u_ref, n_ref, field, mat, carry, block, None)


def forward_other(view, column, weights, mat, left_pad, diff_pad, after):
    _, slab, width = weights.shape
    values = pltpu.VMEM((1, slab * SUB, width), F32)
    return pl.pallas_call(
        functools.partial(forward_other_kernel, view),
        in_specs=[ANY, ANY] + [VMEM] * 4,
        out_specs=[VMEM] * 3,
        out_shape=[values, values, pltpu.VMEM((SUB, LANES), F32)],
        scratch_shapes=[
            pltpu.VMEM((1, slab, width), F32),
            pltpu.VMEM((1, ROWS, width), F32),
            pltpu.VMEM((1, SUB, width), F32),
            pltpu.SMEM((1, slab, LANES), jnp.int32),
            pltpu.SemaphoreType.DMA((2,)),
        ],
        compiler_params=pltpu.CompilerParams(vmem_limit_bytes=8 * MIB),
        name="forward_other",
    )(column, weights, mat, left_pad, diff_pad, after)


def line_rows(tile, base, masks):
    shape = masks[0].shape
    return select_line(masks, [jnp.broadcast_to(tile[base + 1 + k : base + 2 + k], shape) for k in range(len(masks))])


def incident_rows(tile, step):
    rows = row_ids(tile.shape[1])
    result = jnp.broadcast_to(tile[0:1], tile.shape)
    for base in range(step, SUB, step):
        result = jnp.where(rows >= base, jnp.broadcast_to(tile[base : base + 1], tile.shape), result)
    return result


def row_masks(const_ref, width):
    tile = const_ref[LINE_ROWS]
    return [jnp.concatenate([tile] * (width // LANES), axis=1) == k for k in range(SCALE - 1)]


def factors_of(mine, theirs, bit):
    mine_factor = jnp.where(bit == 0, theirs, incident_rows(theirs, SCALE))
    return mine_factor, jnp.where(bit == 0, incident_rows(mine, SCALE), mine)


def merged_state(mine, theirs, bit, masks):
    mine_factor, theirs_factor = factors_of(mine[0:SUB], theirs[0:SUB], bit)
    result = [mine[0:SUB] * theirs[0:SUB]]
    for v in range(mine.shape[0] // SUB - 1):
        span = slice((v + 1) * SUB, (v + 2) * SUB)
        result.append(
            mine[span] * line_rows(mine_factor, v * SCALE, masks)
            + theirs[span] * line_rows(theirs_factor, v * SCALE, masks)
        )
    return result


def weighted_rows(factor, state, misfits, masks):
    rows = row_ids(state.shape[1])
    result = jnp.zeros((SUB, state.shape[1]), F32)
    for v, misfit in enumerate(misfits):
        base = v * SCALE
        value = misfit * state[(v + 1) * SUB : (v + 2) * SUB] * line_rows(factor, base, masks)
        whole = None
        for k, mask in enumerate(masks):
            part = jnp.sum(jnp.where(mask, value, 0.0), axis=0, keepdims=True)
            result = jnp.where(rows == base + 1 + k, part, result)
            whole = part if whole is None else whole + part
        result = jnp.where(rows == base, whole, result)
    return result


def children(factor, sums, mine, theirs, bit, misfits, masks):
    mine_factor, theirs_factor = factors_of(mine[0:SUB], theirs[0:SUB], bit)
    if factor is not None:
        mine_factor, theirs_factor = factor * mine_factor, factor * theirs_factor
    behind = (row_ids(mine.shape[1]) & (SCALE - 1)) == 0
    mine_sums = jnp.where(behind == (bit == 0), weighted_rows(theirs_factor, theirs, misfits, masks), 0.0)
    theirs_sums = jnp.where(behind == (bit == 1), weighted_rows(mine_factor, mine, misfits, masks), 0.0)
    if sums is not None:
        mine_sums, theirs_sums = sums + mine_sums, sums + theirs_sums
    return (mine_factor, mine_sums), (theirs_factor, theirs_sums)


def call_small(kernel, name, outs, operands, scratch=()):
    return pl.pallas_call(
        kernel,
        in_specs=[VMEM] * len(operands),
        out_specs=[VMEM] * len(outs),
        out_shape=[pltpu.VMEM(shape, F32) for shape in outs],
        scratch_shapes=[pltpu.VMEM(shape, F32) for shape in scratch],
        compiler_params=pltpu.CompilerParams(vmem_limit_bytes=4 * MIB),
        name=name,
    )(*operands)


def merge_kernel(shift, const_ref, mine_ref, theirs_ref, *refs):
    bit = (depth_place() >> shift) & 1
    state = merged_state(mine_ref[...], theirs_ref[...], bit, row_masks(const_ref, mine_ref.shape[1]))
    for i, tile in enumerate(state):
        refs[-1][i * SUB : (i + 1) * SUB, :] = tile


def depth_place():
    return lax.axis_index("far") * NEAR + lax.axis_index("near")


def result_kernel(levels, const_ref, target_ref, *refs):
    states, outs = refs[: 2 * levels], refs[-2:]
    depth, width = states[0].shape
    views = depth // SUB - 1
    place = depth_place()
    size = 2 * LANES
    start = (place & 1) * width
    masks = row_masks(const_ref, size)
    behind = (row_ids(size) & (SCALE - 1)) == 0
    for c in range(width // size):
        span = slice(c * size, (c + 1) * size)
        factor, sums = None, None
        for level in reversed(range(levels)):
            mine, theirs = states[2 * level][:, span], states[2 * level + 1][:, span]
            bit = (place >> level) & 1
            if level == levels - 1:
                signals = merged_state(mine, theirs, bit, masks)[1:]
                there = pl.ds(pl.multiple_of(start + c * size, LANES), size)
                misfits = [signals[v] - target_ref[v * SUB : (v + 1) * SUB, there] for v in range(views)]
            contexts = children(factor, sums, mine, theirs, bit, misfits, masks)
            factor, sums = contexts[0]
        for ref, state, (factor, sums) in zip(outs, (mine, theirs), contexts):
            own = jnp.where(behind, weighted_rows(factor, state, misfits, masks), 0.0)
            for i, tile in enumerate(signals + [factor * state[0:SUB], sums + own]):
                ref[i * SUB : (i + 1) * SUB, span] = tile


def assemble_kernel(target_ref, here_ref, there_ref, package_ref, signal_ref):
    half = here_ref.shape[1]
    count = signal_ref.shape[0]
    at = pl.multiple_of((lax.axis_index("near") & 1) * half, LANES)
    for ref, start in ((here_ref, at), (there_ref, pl.multiple_of(half - at, LANES))):
        span = pl.ds(start, half)
        signal_ref[:, span] = ref[0:count, :]
        package_ref[0:count, span] = ref[0:count, :] - target_ref[:, span]
        package_ref[count:, span] = ref[count:, :]


def backward_kernel(views, cells, finish, prior, const_ref, package_ref, index_any, weight_any, *refs):
    if finish:
        signal_ref, refs = refs[0], refs[1:]
    u_refs, refs = refs[: len(views)], refs[len(views) :]
    n_refs, refs = refs[: len(views)], refs[len(views) :]
    if prior:
        prior_any, prior_left, prior_diff = refs[:3]
        refs = refs[3:]
    if finish:
        grad_hbm, signal_hbm, refs = refs[0], refs[1], refs[2:]
        left_pad, diff_pad, cell_ref, grad_ref, signal_rows, refs = refs[:5] + (refs[5:],)
    else:
        left_pad, diff_pad, refs = refs[:2] + (refs[2:],)
    mat, gain, carry, scaled, weight_ref, index_ref = refs[:6]
    prior_ref, sems = refs[6] if prior else None, refs[-1]
    count, slab, width = weight_ref.shape
    emissions = SCALE - 1
    tiles = width // LANES
    blocks = slab // BLOCK
    lanes, rows = lane_ids(), row_ids()
    margin = 2 * LANES
    pairs = [(index_any, index_ref), (weight_any, weight_ref)]
    if prior:
        pairs.append((prior_any, prior_ref))
    copies = copies_in(pairs, sems.at[pl.ds(blocks, len(pairs))])
    for copy in copies:
        copy.start()
    if finish:
        for v in range(signal_rows.shape[0]):
            signal_rows[v] = signal_ref[v * SUB : (v + 1) * SUB, :].reshape(SUB, 1, width)
        signal_copy = pltpu.make_async_copy(signal_rows, signal_hbm, sems.at[blocks + 3])
        signal_copy.start()
    masks = [const_ref[LINE_LANES] == k for k in range(emissions)]
    columns = [const_ref[k] for k in range(emissions + 1)]
    fill_matrix(mat, -columns[0], select_line(masks, columns[1:]), True, False)
    masks = [const_ref[LINE_ROWS] == k for k in range(emissions)]
    scale = const_ref[SCALE]
    columns = [column * cells for column in columns]
    for j in range(tiles):
        span = slice(j * LANES, (j + 1) * LANES)
        factor = package_ref[count * SUB : (count + 1) * SUB, span]
        sums = package_ref[(count + 1) * SUB : (count + 2) * SUB, span]
        for v in range(count):
            base = v * SCALE
            gain[v, :, span] = package_ref[v * SUB : (v + 1) * SUB, span] * scale * line_rows(factor, base, masks)
            back = columns[0] * jnp.broadcast_to(sums[base : base + 1], rows.shape)
            for k in range(1, emissions + 1):
                back = back + columns[k] * jnp.broadcast_to(sums[base + k : base + k + 1], rows.shape)
            carry[v, :, span] = back
    for ref in (left_pad, diff_pad):
        ref[:, :, :, 0:margin] = jnp.zeros(ref.shape[:3] + (margin,), F32)
        ref[:, :, :, margin + width + LANES :] = jnp.zeros(ref.shape[:3] + (margin,), F32)

    def one_block(block):
        slot = 0 if finish else block * BLOCK
        for v in range(count):
            u_ref, n_ref, at = u_refs[v], n_refs[v], views[v]
            for c in range(width // CHUNK):
                span = slice(c * CHUNK, (c + 1) * CHUNK)
                factor = gain[v, :, span][None]
                weighted = n_ref[at, block_rows(block), span].reshape(BLOCK, SUB, CHUNK) * factor
                direct = u_ref[at, block_rows(block), span].reshape(BLOCK, SUB, CHUNK) * factor
                lines, total = multiply(mat, weighted.reshape(ROWS, CHUNK))
                before = carry[v, :, span]
                lines = lines.reshape(BLOCK, SUB, CHUNK) + before[None]
                scaled[v, :, span] = (direct - lines).reshape(ROWS, CHUNK)
                carry[v, :, span] = before + total

        if block == 0:
            for copy in copies:
                copy.wait()
        for v in range(count):
            for d in range(BLOCK):
                cell = block * BLOCK + d
                _, rest = shift_of(index_ref, v, cell, width)
                stay = lanes >= rest
                plain = [scaled[v, d * SUB : (d + 1) * SUB, j * LANES : (j + 1) * LANES] for j in range(tiles)]
                moved = [plain[j] * weight_ref[v, cell : cell + 1, j * LANES : (j + 1) * LANES] for j in range(tiles)]
                for ref, values in ((left_pad, plain), (diff_pad, moved)):
                    turned = [jnp.zeros((SUB, LANES), F32)]
                    turned += [pltpu.roll(value, rest, 1) for value in values]
                    turned += [jnp.zeros((SUB, LANES), F32)]
                    for j in range(tiles + 1):
                        span = slice(margin + j * LANES, margin + (j + 1) * LANES)
                        ref[v, slot + d, :, span] = jnp.where(stay, turned[j + 1], turned[j])
        if not finish:
            return
        for d in range(BLOCK):
            cell = block * BLOCK + d

            def gathered(ref, prior_pad):
                sources = [(ref, index_ref, v, d) for v in range(count)]
                if prior:
                    sources += [(prior_pad, prior_ref, v, cell) for v in range(prior)]
                sums = [None] * (tiles + 2)
                for pad, index, v, at in sources:
                    whole, _ = shift_of(index, v, cell, width)
                    for j in range(tiles + 2):
                        start = pl.multiple_of((2 + j - whole) * LANES, LANES)
                        value = pad[v, at, :, pl.ds(start, LANES)]
                        sums[j] = value if sums[j] is None else sums[j] + value
                return sums

            left = gathered(left_pad, prior_left if prior else None)
            diff = gathered(diff_pad, prior_diff if prior else None)
            left = [left[j] - diff[j] for j in range(tiles + 2)]

            def folded(sums):
                low = jnp.sum(sums[0], axis=1, keepdims=True)
                beyond = sums[tiles + 1] + jnp.where(lanes == LANES - 1, sums[tiles], 0.0)
                high = jnp.sum(beyond, axis=1, keepdims=True)
                core = sums[1 : tiles + 1]
                core[0] = core[0] + jnp.where(lanes == 0, low, 0.0)
                core[-1] = jnp.where(lanes == LANES - 1, 0.0, core[-1] + jnp.where(lanes == LANES - 2, high, 0.0))
                return core

            left, diff = folded(left), folded(diff)
            turned = [jnp.zeros((SUB, LANES), F32)] + [pltpu.roll(value, 1, 1) for value in diff]
            for j in range(tiles):
                value = left[j] + jnp.where(lanes == 0, turned[j], turned[j + 1])
                cell_ref[d, :, j * LANES : (j + 1) * LANES] = value
        grad_ref[block] = jnp.swapaxes(cell_ref[...], 0, 1)
        out_copies[block].start()

    if finish:
        out_copies = [
            pltpu.make_async_copy(grad_ref.at[b], grad_hbm.at[:, pl.ds(b * BLOCK, BLOCK), :], sems.at[b])
            for b in range(blocks)
        ]
    for block in range(blocks):
        one_block(block)
    if finish:
        for copy in out_copies + [signal_copy]:
            copy.wait()


def backward(package, const, column, weights, pieces, cells, signal, prior):
    finish = signal is not None
    signals = [signal[0]] if finish else []
    views, slab, width = weights.shape
    blocks = slab // BLOCK
    line = pltpu.VMEM((views, SUB, width), F32)
    depth = BLOCK if finish else slab
    padded = pltpu.VMEM((views, depth, SUB, width + 5 * LANES), F32)
    scratch = [
        pltpu.VMEM(MATRIX, BF16),
        line,
        line,
        pltpu.VMEM((views, ROWS, width), F32),
        pltpu.VMEM((views, slab, width), F32),
        pltpu.SMEM((views, slab, LANES), jnp.int32),
    ]
    in_specs = [VMEM, VMEM, ANY, ANY] + [VMEM] * (2 * views + len(signals))
    if prior:
        in_specs += [ANY, VMEM, VMEM]
        scratch.append(pltpu.SMEM((views, slab, LANES), jnp.int32))
    scratch.append(pltpu.SemaphoreType.DMA((blocks + 4,)))
    if finish:
        scratch = [
            padded,
            padded,
            pltpu.VMEM((BLOCK, SUB, width), F32),
            pltpu.VMEM((blocks, SUB, BLOCK, width), F32),
            pltpu.VMEM(signal[1], F32),
        ] + scratch
    return pl.pallas_call(
        functools.partial(
            backward_kernel, tuple(at for _, _, at in pieces), cells, finish, views if prior else 0
        ),
        in_specs=in_specs,
        out_specs=[HBM, HBM] if finish else [VMEM, VMEM],
        out_shape=[pltpu.HBM((SUB, slab, width), F32), pltpu.HBM(signal[1], F32)] if finish else [padded, padded],
        scratch_shapes=scratch,
        compiler_params=pltpu.CompilerParams(vmem_limit_bytes=16 * MIB),
        name="backward_last" if finish else "backward_first",
    )(const, package, column, weights, *signals, *[u for u, _, _ in pieces], *[n for _, n, _ in pieces], *(prior or ()))


def body(concentration, shear_index, shear_weight, attenuation, yields, line_energy, measured):
    elements, _, slab, width = concentration.shape
    views = shear_weight.shape[0]
    emissions = attenuation.shape[0] - 1
    groups = lax.axis_size("far")
    both = lax.axis_size("views") == 2
    cells = float(slab * groups * NEAR)
    conc = concentration.reshape(elements, slab, width)
    scalars = (attenuation, line_energy, yields)

    def to_other(value):
        return lax.ppermute(value, "views", [(0, 1), (1, 0)])

    fillers = []

    def fill(after):
        if not both or len(fillers) == views:
            return ()
        pads = (mat, left_pad, diff_pad, after)
        fillers.append(forward_other(len(fillers), other_column, other_weight, *pads))
        return (fillers[-1][2],)

    if both:
        other_weight = to_other(shear_weight)
    u, n, const, target, mat, left_pad, diff_pad, column, state, send = forward(
        conc, shear_index, shear_weight, scalars, measured, cells
    )
    if both:
        other_column = to_other(column)

    def swap(value, axis, step):
        return lax.ppermute(value, axis, [(s, s ^ step) for s in range(lax.axis_size(axis))])

    states = [state, swap(send, "near", 1)]
    tokens = (other_weight,) if both else ()
    levels = groups.bit_length() + 1
    for level in range(levels - 1):
        (state,) = call_small(
            functools.partial(merge_kernel, level), "merge", [state.shape], (const, *states[-2:], *tokens)
        )
        if level == 0:
            states += [state, swap(state, "near", 2)]
            tokens = (other_column,) if both else ()
        else:
            states += [state, swap(state, "far", 1 << (level - 1))]
            tokens = fill(state)
    half = ((views + 2) * SUB, width // 2)
    here, there = call_small(
        functools.partial(result_kernel, levels), "result", [half] * 2, (const, target, *states, *tokens)
    )
    there = swap(there, "near", 1)
    package = (half[0], width)
    package, signal = call_small(assemble_kernel, "assemble", [package, target.shape], (target, here, there))
    own = [(u, n, v) for v in range(views)]
    signal = (signal, measured.shape)
    if both:
        other_package = to_other(package)
        pads = backward(package, const, column, shear_weight, own, cells, None, None)
        pieces = [(fillers[v][0], fillers[v][1], 0) for v in range(views)]
        gradient, signal = backward(
            other_package, const, other_column, other_weight, pieces, cells, signal, (column, *pads)
        )
    else:
        gradient, signal = backward(package, const, column, shear_weight, own, cells, signal, None)
        gradient = lax.psum(gradient, "views")
    return gradient.reshape(concentration.shape), signal


def solution(mesh):
    views, depth = mesh.shape["views"], mesh.shape["depth"]
    devices = mesh.devices.reshape(views, depth // NEAR, NEAR)
    split = jax.sharding.Mesh(devices, ("views", "far", "near"))
    depths = ("far", "near")
    return jax.shard_map(
        body,
        mesh=split,
        in_specs=(
            P(None, None, depths, None),
            P("views", depths, None),
            P("views", depths, None),
            P(),
            P(),
            P(),
            P("views", None, None, None),
        ),
        out_specs=(P(None, None, depths, None), P("views", None, None, None)),
        check_vma=False,
    )
```

```python
import functools

import jax
import jax.numpy as jnp
from jax import lax
from jax.experimental import pallas as pl
from jax.experimental.pallas import tpu as pltpu
from jax.sharding import PartitionSpec as P

LANES = 128
SUB = 8
BLOCK = 8
ROWS = BLOCK * SUB
NEAR = 4
CHUNK = 256
MIB = 1024 * 1024
F32 = jnp.float32
BF16 = jnp.bfloat16
HBM = pl.BlockSpec(memory_space=pltpu.HBM)
VMEM = pl.BlockSpec(memory_space=pltpu.VMEM)
SCALE, LINE_ROWS, LINE_LANES = 4, 5, 6
ANY = pl.BlockSpec(memory_space=pl.ANY)


def in_hbm(value):
    return pltpu.with_memory_space_constraint(value, pltpu.HBM)


def lane_ids(width=LANES):
    return lax.broadcasted_iota(jnp.int32, (SUB, width), 1)


def row_ids(width=LANES):
    return lax.broadcasted_iota(jnp.int32, (SUB, width), 0)


def tile_of(values, ids):
    tile = jnp.zeros(ids.shape, F32)
    for e in range(SUB):
        tile = jnp.where(ids == e, values[e], tile)
    return tile


def select_line(masks, values):
    result = values[0]
    for mask, value in zip(masks[1:], values[1:]):
        result = jnp.where(mask, value, result)
    return result


def fill_matrix(mat_ref, first_tile, second_tile, first_incl, second_incl):
    depth = (lane_ids() & (ROWS - 1)) >> 3
    tiles = []
    for d in range(BLOCK):
        one = jnp.where(depth <= d if first_incl else depth < d, first_tile, 0.0)
        two = jnp.where(depth <= d if second_incl else depth < d, second_tile, 0.0)
        tiles.append(one + two)
    tiles.append(first_tile + second_tile)
    tiles.append(jnp.zeros((SUB, LANES), F32))
    whole = jnp.concatenate(tiles, axis=0)
    high = whole.astype(BF16)
    mat_ref[:, 0:LANES] = high
    mat_ref[:, LANES : 2 * LANES] = (whole - high.astype(F32)).astype(BF16)


def multiply(mat_ref, values):
    high = values.astype(BF16)
    low = (values - high.astype(F32)).astype(BF16)
    stacked = jnp.concatenate([high, low, high], axis=0)
    product = jnp.dot(mat_ref[:, 0 : 3 * ROWS], stacked, preferred_element_type=F32)
    return product[0:ROWS], product[ROWS : ROWS + SUB]


MATRIX = (ROWS + 2 * SUB, 2 * LANES)


def copies_in(pairs, sems):
    return [pltpu.make_async_copy(source, target, sems.at[i]) for i, (source, target) in enumerate(pairs)]


def block_rows(block):
    return slice(block * ROWS, (block + 1) * ROWS)


def block_cells(block):
    return slice(block * BLOCK, (block + 1) * BLOCK)


def shift_of(index_ref, v, cell, width):
    if index_ref.dtype == jnp.int32:
        at = index_ref[v, cell, 0]
    else:
        at = index_ref[v, cell % SUB, cell // SUB * LANES].astype(jnp.int32)
    offset = at - (width // 2 - LANES)
    whole = jnp.minimum(offset >> 7, 1)
    return whole, offset - (whole << 7)


def shear(field, left_pad, diff_pad, index_ref, weight_ref, block, views, tiles):
    lanes = lane_ids()
    for i, v in enumerate(views):
        for d in range(BLOCK):
            cell = block * BLOCK + d
            whole, rest = shift_of(index_ref, v, cell, tiles * LANES)
            turn = (LANES - rest) & (LANES - 1)
            stay = lanes < LANES - rest

            def sheared(ref):
                turned = []
                for j in range(tiles + 1):
                    start = pl.multiple_of((whole + j) * LANES, LANES)
                    turned.append(pltpu.roll(ref[cell, :, pl.ds(start, LANES)], turn, 1))
                return [jnp.where(stay, turned[j], turned[j + 1]) for j in range(tiles)]

            left, diff = sheared(left_pad), sheared(diff_pad)
            for j in range(tiles):
                span = slice(j * LANES, (j + 1) * LANES)
                field[i, d * SUB : (d + 1) * SUB, span] = left[j] + weight_ref[i, cell : cell + 1, span] * diff[j]


def transmit(u_ref, n_ref, field, mat, carry, block, sums):
    views, _, width = field.shape
    for v in range(views):
        for c in range(width // CHUNK):
            span = slice(c * CHUNK, (c + 1) * CHUNK)
            value = field[v, :, span]
            lines, total = multiply(mat, value)
            before = carry[v, :, span]
            through = jnp.exp(lines.reshape(BLOCK, SUB, CHUNK) + before[None])
            value = value.reshape(BLOCK, SUB, CHUNK)
            emit = value * through
            u_ref[v, block_rows(block), span] = through.reshape(ROWS, CHUNK)
            n_ref[v, block_rows(block), span] = emit.reshape(ROWS, CHUNK)
            carry[v, :, span] = before + total
            if sums:
                sums[0][v, :, span] += jnp.sum(value, axis=0)
                sums[1][v, :, span] += jnp.sum(emit, axis=0)


def forward_kernel(cells, *refs):
    att_hbm, line_hbm, yield_hbm, index_hbm, conc_hbm, weight_hbm, measured_hbm = refs[:7]
    u_ref, n_ref, const_ref, target_ref, mat, left_pad, diff_pad, column_ref, weight_ref = refs[7:16]
    state_refs = refs[16:18]
    refs = refs[18:]
    conc_ref, field, carry, field_sum, emit_sum, measured_ref = refs[:6]
    att_ref, line_ref, yield_ref, index_ref, sems = refs[6:]
    views, _, width = weight_ref.shape
    slab = conc_ref.shape[1]
    emissions = att_ref.shape[0] - 1
    tiles = width // LANES
    blocks = slab // BLOCK
    lanes, rows = lane_ids(), row_ids()
    pairs = [
        (att_hbm, att_ref),
        (line_hbm, line_ref),
        (yield_hbm, yield_ref),
        (index_hbm.at[:, :, pl.ds(width // 2, LANES)], index_ref),
        (weight_hbm, weight_ref.at[:, pl.ds(0, slab), :]),
        (measured_hbm, measured_ref),
        (index_hbm.at[:, :, pl.ds(width // 2, LANES)], column_ref),
    ]
    copies = copies_in([(conc_hbm, conc_ref)] + pairs, sems)
    for copy in copies:
        copy.start()
    for ref in (carry, field_sum, emit_sum):
        ref[...] = jnp.zeros_like(ref)

    copies[0].wait()
    for block in range(blocks):
        by_depth = jnp.swapaxes(conc_ref[:, block_cells(block), :], 0, 1)
        for d in range(BLOCK):
            pieces = [by_depth[d, :, j * LANES : (j + 1) * LANES] for j in range(tiles)]
            turned = [pltpu.roll(piece, LANES - 1, 1) for piece in pieces]
            after = [jnp.where(lanes < LANES - 1, turned[j], turned[min(j + 1, tiles - 1)]) for j in range(tiles)]
            steps = [after[j] - pieces[j] for j in range(tiles)]
            last_cell = jnp.broadcast_to(pieces[-1][:, LANES - 2 : LANES - 1], (SUB, LANES))
            last_step = jnp.broadcast_to(steps[-1][:, LANES - 2 : LANES - 1], (SUB, LANES))
            first_cell = jnp.broadcast_to(pieces[0][:, 0:1], (SUB, LANES))
            first_step = jnp.broadcast_to(steps[0][:, 0:1], (SUB, LANES))
            pieces[-1] = jnp.where(lanes < LANES - 1, pieces[-1], last_cell)
            steps[-1] = jnp.where(lanes < LANES - 1, steps[-1], last_step)
            pieces = [first_cell] + pieces + [last_cell, last_cell]
            steps = [first_step] + steps + [last_step, last_step]
            for j in range(tiles + 3):
                left_pad[block * BLOCK + d, :, j * LANES : (j + 1) * LANES] = pieces[j]
                diff_pad[block * BLOCK + d, :, j * LANES : (j + 1) * LANES] = steps[j]

    for copy in copies[1:]:
        copy.wait()
    line_by_row = tile_of([line_ref[e].astype(F32) for e in range(SUB)], rows)
    masks = [line_by_row == k for k in range(emissions)]
    by_lane = [tile_of([att_ref[k, e] for e in range(SUB)], lanes & 7) for k in range(emissions + 1)]
    fill_matrix(mat, -by_lane[0], select_line(masks, by_lane[1:]), False, True)
    for k in range(emissions + 1):
        const_ref[k] = tile_of([att_ref[k, e] for e in range(SUB)], rows)
    const_ref[SCALE] = tile_of([yield_ref[e] for e in range(SUB)], rows)
    const_ref[LINE_ROWS] = line_by_row
    const_ref[LINE_LANES] = tile_of([line_ref[e].astype(F32) for e in range(SUB)], lanes & 7)
    for block in range(blocks):
        shear(field, left_pad, diff_pad, index_ref, weight_ref, block, range(views), tiles)
        transmit(u_ref, n_ref, field, mat, carry, block, (field_sum, emit_sum))
    for v in range(views):
        for octet in range(slab // SUB):
            span = slice(octet * LANES, (octet + 1) * LANES)
            weight_ref[v, slab : slab + SUB, span] = column_ref[v, octet * SUB : (octet + 1) * SUB, :].astype(F32)
    columns = [const_ref[k] for k in range(emissions + 1)]
    masks = [const_ref[LINE_ROWS] == k for k in range(emissions)]
    scale = const_ref[SCALE] * (1.0 / cells)
    share = width // 2
    core = lax.axis_index("near") & 1
    for r in range(2):
        for j in range(share // LANES):
            start = pl.multiple_of((core ^ r) * share + j * LANES, LANES)
            span = slice(j * LANES, (j + 1) * LANES)
            totals = jnp.zeros((SUB, LANES), F32)
            for v in range(views):
                values = field_sum[v, :, pl.ds(start, LANES)]
                sums = [jnp.sum(column * values, axis=0, keepdims=True) for column in columns]
                for k in range(emissions + 1):
                    totals = jnp.where(rows == v * (emissions + 1) + k, sums[k], totals)
                line_total = select_line(masks, [jnp.broadcast_to(value, rows.shape) for value in sums[1:]])
                signal = scale * emit_sum[v, :, pl.ds(start, LANES)] * jnp.exp(-line_total)
                state_refs[r][(v + 1) * SUB : (v + 2) * SUB, span] = signal
            state_refs[r][0:SUB, span] = jnp.exp(-totals)
    for v in range(views):
        target_ref[v * SUB : (v + 1) * SUB, :] = measured_ref[v].reshape(SUB, width)


def forward(conc, index, weights, scalars, measured, cells):
    views, slab, width = weights.shape
    attenuation, line_energy, yields = scalars
    values = pltpu.VMEM((views, slab * SUB, width), F32)
    padded = pltpu.VMEM((slab, SUB, width + 3 * LANES), F32)
    state = pltpu.VMEM(((views + 1) * SUB, width // 2), F32)
    line = pltpu.VMEM((views, SUB, width), F32)
    operands = [in_hbm(value) for value in (attenuation, line_energy, yields, index, conc, weights, measured)]
    return pl.pallas_call(
        functools.partial(forward_kernel, cells),
        in_specs=[HBM] * len(operands),
        out_specs=[VMEM] * 11,
        out_shape=[
            values,
            values,
            pltpu.VMEM((LINE_LANES + 1, SUB, LANES), F32),
            pltpu.VMEM((views * SUB, width), F32),
            pltpu.VMEM(MATRIX, BF16),
            padded,
            padded,
            pltpu.VMEM((views, slab, LANES), jnp.int32),
            pltpu.VMEM((views, slab + SUB, width), F32),
            state,
            state,
        ],
        scratch_shapes=[
            pltpu.VMEM((SUB, slab, width), F32),
            pltpu.VMEM((views, ROWS, width), F32),
            line,
            line,
            line,
            pltpu.VMEM(measured.shape, F32),
            pltpu.SMEM(attenuation.shape, F32),
            pltpu.SMEM(line_energy.shape, jnp.int32),
            pltpu.SMEM(yields.shape, F32),
            pltpu.SMEM((views, slab, LANES), jnp.int32),
            pltpu.SemaphoreType.DMA((8,)),
        ],
        compiler_params=pltpu.CompilerParams(vmem_limit_bytes=16 * MIB),
        name="forward",
    )(*operands)


def column_in(package_any, views, index_ref, sem):
    first = package_any.shape[1] - SUB
    source = package_any.at[views, pl.ds(first, SUB), pl.ds(0, index_ref.shape[2])]
    return pltpu.make_async_copy(source, index_ref, sem)


def forward_other_kernel(view, weight_ref, mat, left_pad, diff_pad, order_ref, *refs):
    u_ref, n_ref, token_ref, field, carry, index_ref, sem = refs
    _, slab, width = weight_ref.shape
    slab = slab - SUB
    copy = column_in(weight_ref, pl.ds(view, 1), index_ref, sem)
    copy.start()
    carry[...] = jnp.zeros_like(carry)
    token_ref[...] = jnp.zeros_like(token_ref)
    copy.wait()
    for block in range(slab // BLOCK):
        shear(field, left_pad, diff_pad, index_ref, weight_ref.at[pl.ds(view, 1)], block, (0,), width // LANES)
        transmit(u_ref, n_ref, field, mat, carry, block, None)


def forward_other(view, weights, mat, left_pad, diff_pad, after):
    _, slab, width = weights.shape
    slab = slab - SUB
    values = pltpu.VMEM((1, slab * SUB, width), F32)
    return pl.pallas_call(
        functools.partial(forward_other_kernel, view),
        in_specs=[VMEM] * 5,
        out_specs=[VMEM] * 3,
        out_shape=[values, values, pltpu.VMEM((SUB, LANES), F32)],
        scratch_shapes=[
            pltpu.VMEM((1, ROWS, width), F32),
            pltpu.VMEM((1, SUB, width), F32),
            pltpu.SMEM((1, SUB, slab // SUB * LANES), F32),
            pltpu.SemaphoreType.DMA,
        ],
        compiler_params=pltpu.CompilerParams(vmem_limit_bytes=8 * MIB),
        name="forward_other",
    )(weights, mat, left_pad, diff_pad, after)


def line_rows(tile, base, masks):
    shape = masks[0].shape
    return select_line(masks, [jnp.broadcast_to(tile[base + 1 + k : base + 2 + k], shape) for k in range(len(masks))])


def incident_rows(tile, step):
    rows = row_ids(tile.shape[1])
    result = jnp.broadcast_to(tile[0:1], tile.shape)
    for base in range(step, SUB, step):
        result = jnp.where(rows >= base, jnp.broadcast_to(tile[base : base + 1], tile.shape), result)
    return result


def row_masks(const_ref, width):
    tile = const_ref[LINE_ROWS]
    return [jnp.concatenate([tile] * (width // LANES), axis=1) == k for k in range(SCALE - 1)]


def factors_of(mine, theirs, bit):
    mine_factor = jnp.where(bit == 0, theirs, incident_rows(theirs, SCALE))
    return mine_factor, jnp.where(bit == 0, incident_rows(mine, SCALE), mine)


def merged_state(mine, theirs, bit, masks):
    mine_factor, theirs_factor = factors_of(mine[0:SUB], theirs[0:SUB], bit)
    result = [mine[0:SUB] * theirs[0:SUB]]
    for v in range(mine.shape[0] // SUB - 1):
        span = slice((v + 1) * SUB, (v + 2) * SUB)
        result.append(
            mine[span] * line_rows(mine_factor, v * SCALE, masks)
            + theirs[span] * line_rows(theirs_factor, v * SCALE, masks)
        )
    return result


def weighted_rows(factor, state, misfits, masks):
    rows = row_ids(state.shape[1])
    result = jnp.zeros((SUB, state.shape[1]), F32)
    for v, misfit in enumerate(misfits):
        base = v * SCALE
        value = misfit * state[(v + 1) * SUB : (v + 2) * SUB] * line_rows(factor, base, masks)
        whole = None
        for k, mask in enumerate(masks):
            part = jnp.sum(jnp.where(mask, value, 0.0), axis=0, keepdims=True)
            result = jnp.where(rows == base + 1 + k, part, result)
            whole = part if whole is None else whole + part
        result = jnp.where(rows == base, whole, result)
    return result


def children(factor, sums, mine, theirs, bit, misfits, masks):
    mine_factor, theirs_factor = factors_of(mine[0:SUB], theirs[0:SUB], bit)
    if factor is not None:
        mine_factor, theirs_factor = factor * mine_factor, factor * theirs_factor
    behind = (row_ids(mine.shape[1]) & (SCALE - 1)) == 0
    mine_sums = jnp.where(behind == (bit == 0), weighted_rows(theirs_factor, theirs, misfits, masks), 0.0)
    theirs_sums = jnp.where(behind == (bit == 1), weighted_rows(mine_factor, mine, misfits, masks), 0.0)
    if sums is not None:
        mine_sums, theirs_sums = sums + mine_sums, sums + theirs_sums
    return (mine_factor, mine_sums), (theirs_factor, theirs_sums)


def call_small(kernel, name, outs, operands, scratch=()):
    return pl.pallas_call(
        kernel,
        in_specs=[VMEM] * len(operands),
        out_specs=[VMEM] * len(outs),
        out_shape=[pltpu.VMEM(shape, F32) for shape in outs],
        scratch_shapes=[pltpu.VMEM(shape, F32) for shape in scratch],
        compiler_params=pltpu.CompilerParams(vmem_limit_bytes=4 * MIB),
        name=name,
    )(*operands)


def merge_kernel(shift, const_ref, mine_ref, theirs_ref, *refs):
    bit = (depth_place() >> shift) & 1
    state = merged_state(mine_ref[...], theirs_ref[...], bit, row_masks(const_ref, mine_ref.shape[1]))
    for i, tile in enumerate(state):
        refs[-1][i * SUB : (i + 1) * SUB, :] = tile


def depth_place():
    return lax.axis_index("far") * NEAR + lax.axis_index("near")


def result_kernel(levels, const_ref, target_ref, *refs):
    states, outs = refs[: 2 * levels], refs[-2:]
    depth, width = states[0].shape
    views = depth // SUB - 1
    place = depth_place()
    size = 2 * LANES
    start = (place & 1) * width
    masks = row_masks(const_ref, size)
    behind = (row_ids(size) & (SCALE - 1)) == 0
    for c in range(width // size):
        span = slice(c * size, (c + 1) * size)
        factor, sums = None, None
        for level in reversed(range(levels)):
            mine, theirs = states[2 * level][:, span], states[2 * level + 1][:, span]
            bit = (place >> level) & 1
            if level == levels - 1:
                signals = merged_state(mine, theirs, bit, masks)[1:]
                there = pl.ds(pl.multiple_of(start + c * size, LANES), size)
                misfits = [signals[v] - target_ref[v * SUB : (v + 1) * SUB, there] for v in range(views)]
            contexts = children(factor, sums, mine, theirs, bit, misfits, masks)
            factor, sums = contexts[0]
        for ref, state, (factor, sums) in zip(outs, (mine, theirs), contexts):
            own = jnp.where(behind, weighted_rows(factor, state, misfits, masks), 0.0)
            for i, tile in enumerate(signals + [factor * state[0:SUB], sums + own]):
                ref[i * SUB : (i + 1) * SUB, span] = tile


def assemble_kernel(target_ref, here_ref, there_ref, package_ref, signal_ref):
    half = here_ref.shape[1]
    count = signal_ref.shape[0]
    at = pl.multiple_of((lax.axis_index("near") & 1) * half, LANES)
    for ref, start in ((here_ref, at), (there_ref, pl.multiple_of(half - at, LANES))):
        span = pl.ds(start, half)
        signal_ref[:, span] = ref[0:count, :]
        package_ref[0:count, span] = ref[0:count, :] - target_ref[:, span]
        package_ref[count:, span] = ref[count:, :]


def backward_kernel(places, cells, finish, const_ref, package_ref, weight_ref, *refs):
    count = len(places)
    u_refs, n_refs, refs = refs[:count], refs[count : 2 * count], refs[2 * count :]
    if finish:
        signal_ref, refs = refs[0], refs[1:]
        prior, refs = refs[: finish - 1], refs[finish - 1 :]
        grad_hbm, signal_hbm, cell_ref, grad_ref, signal_rows = refs[:5]
        refs = refs[5:]
    else:
        left_sum, diff_sum, refs = refs[0], refs[1], refs[2:]
    mat, gain, carry, padded, index_ref, sems = refs
    _, slab, width = weight_ref.shape
    slab = slab - SUB
    emissions = SCALE - 1
    tiles = width // LANES
    blocks = slab // BLOCK
    lanes, rows = lane_ids(), row_ids()
    column = column_in(weight_ref, pl.ds(0, count), index_ref, sems.at[blocks])
    column.start()
    if finish:
        for v in range(signal_rows.shape[0]):
            signal_rows[v] = signal_ref[v * SUB : (v + 1) * SUB, :].reshape(SUB, 1, width)
        signal_copy = pltpu.make_async_copy(signal_rows, signal_hbm, sems.at[blocks + 1])
        signal_copy.start()
        out_copies = [
            pltpu.make_async_copy(grad_ref.at[b], grad_hbm.at[:, pl.ds(b * BLOCK, BLOCK), :], sems.at[b])
            for b in range(blocks)
        ]
    masks = [const_ref[LINE_LANES] == k for k in range(emissions)]
    columns = [const_ref[k] for k in range(emissions + 1)]
    fill_matrix(mat, -columns[0], select_line(masks, columns[1:]), True, False)
    masks = [const_ref[LINE_ROWS] == k for k in range(emissions)]
    scale = const_ref[SCALE]
    columns = [column * cells for column in columns]
    for j in range(tiles):
        span = slice(j * LANES, (j + 1) * LANES)
        factor = package_ref[count * SUB : (count + 1) * SUB, span]
        sums = package_ref[(count + 1) * SUB : (count + 2) * SUB, span]
        for v in range(count):
            base = v * SCALE
            gain[v, :, span] = package_ref[v * SUB : (v + 1) * SUB, span] * scale * line_rows(factor, base, masks)
            back = columns[0] * jnp.broadcast_to(sums[base : base + 1], rows.shape)
            for k in range(1, emissions + 1):
                back = back + columns[k] * jnp.broadcast_to(sums[base + k : base + k + 1], rows.shape)
            carry[v, :, span] = back
    zero = jnp.zeros((SUB, LANES), F32)
    for v in range(count):
        for d in range(padded.shape[1]):
            padded[v, d, :, 0:LANES] = zero
            padded[v, d, :, width + LANES :] = zero
    column.wait()

    def one_cell(cell, slot):
        left, diff = [zero] * (tiles + 2), [zero] * (tiles + 2)
        if finish > 1:
            for j in range(tiles + 2):
                left[j] = prior[0][cell, :, j * LANES : (j + 1) * LANES]
                diff[j] = prior[1][cell, :, j * LANES : (j + 1) * LANES]
        for v in range(count):
            whole, rest = shift_of(index_ref, v, cell, width)
            stay = lanes >= rest
            turn = rest & (LANES - 1)
            plain, moved = [zero], [zero]
            for t in range(1, tiles + 2):
                at = t if t == 0 else t - whole
                value = padded[v, slot, :, pl.ds(pl.multiple_of(at * LANES, LANES), LANES)]
                at = 0 if t == 1 else tiles - 1 if t == tiles + 1 else t - 1 - whole
                if t in (1, tiles + 1):
                    weight = weight_ref[v, cell : cell + 1, at * LANES : (at + 1) * LANES]
                else:
                    weight = weight_ref[v, cell : cell + 1, pl.ds(pl.multiple_of(at * LANES, LANES), LANES)]
                plain.append(pltpu.roll(value, turn, 1))
                moved.append(pltpu.roll(value * weight, turn, 1))
            plain.append(zero)
            moved.append(zero)
            for j in range(tiles + 2):
                left[j] = left[j] + jnp.where(stay, plain[j + 1], plain[j])
                diff[j] = diff[j] + jnp.where(stay, moved[j + 1], moved[j])
        return left, diff

    def folded(sums):
        low = jnp.sum(sums[0], axis=1, keepdims=True)
        beyond = sums[tiles + 1] + jnp.where(lanes == LANES - 1, sums[tiles], 0.0)
        high = jnp.sum(beyond, axis=1, keepdims=True)
        core = sums[1 : tiles + 1]
        core[0] = core[0] + jnp.where(lanes == 0, low, 0.0)
        core[-1] = jnp.where(lanes == LANES - 1, 0.0, core[-1] + jnp.where(lanes == LANES - 2, high, 0.0))
        return core

    for block in range(blocks):
        first = block % 2 * BLOCK
        for v in range(count):
            for c in range(width // CHUNK):
                span = slice(c * CHUNK, (c + 1) * CHUNK)
                factor = gain[v, :, span][None]
                weighted = n_refs[v][places[v], block_rows(block), span].reshape(BLOCK, SUB, CHUNK) * factor
                direct = u_refs[v][places[v], block_rows(block), span].reshape(BLOCK, SUB, CHUNK) * factor
                lines, total = multiply(mat, weighted.reshape(ROWS, CHUNK))
                before = carry[v, :, span]
                lines = lines.reshape(BLOCK, SUB, CHUNK) + before[None]
                padded[v, first : first + BLOCK, :, LANES + c * CHUNK : LANES + (c + 1) * CHUNK] = direct - lines
                carry[v, :, span] = before + total
        for d in range(BLOCK):
            cell = block * BLOCK + d
            left, diff = one_cell(cell, first + d)
            if not finish:
                for j in range(tiles + 2):
                    left_sum[cell, :, j * LANES : (j + 1) * LANES] = left[j]
                    diff_sum[cell, :, j * LANES : (j + 1) * LANES] = diff[j]
                continue
            left, diff = folded([left[j] - diff[j] for j in range(tiles + 2)]), folded(diff)
            turned = [zero] + [pltpu.roll(value, 1, 1) for value in diff]
            for j in range(tiles):
                value = left[j] + jnp.where(lanes == 0, turned[j], turned[j + 1])
                cell_ref[first + d, :, j * LANES : (j + 1) * LANES] = value
        if finish:
            grad_ref[block] = jnp.swapaxes(cell_ref[first : first + BLOCK], 0, 1)
            out_copies[block].start()
    if finish:
        for copy in out_copies + [signal_copy]:
            copy.wait()


def backward(package, const, weights, pieces, cells, signal, prior):
    views, slab, width = weights.shape
    slab = slab - SUB
    blocks = slab // BLOCK
    finish = signal is not None
    line = pltpu.VMEM((views, SUB, width), F32)
    sums = pltpu.VMEM((slab, SUB, width + 2 * LANES), F32)
    scratch = [
        pltpu.VMEM(MATRIX, BF16),
        line,
        line,
        pltpu.VMEM((views, 2 * BLOCK, SUB, width + 2 * LANES), F32),
        pltpu.SMEM((views, SUB, slab // SUB * LANES), F32),
        pltpu.SemaphoreType.DMA((blocks + 2,)),
    ]
    operands = [const, package, weights, *[u for u, _, _ in pieces], *[n for _, n, _ in pieces]]
    if finish:
        operands += [signal[0], *prior]
        scratch = [
            pltpu.VMEM((2 * BLOCK, SUB, width), F32),
            pltpu.VMEM((blocks, SUB, BLOCK, width), F32),
            pltpu.VMEM(signal[1], F32),
        ] + scratch
    return pl.pallas_call(
        functools.partial(
            backward_kernel, tuple(at for _, _, at in pieces), cells, 1 + len(prior) if finish else 0
        ),
        in_specs=[VMEM] * len(operands),
        out_specs=[HBM, HBM] if finish else [VMEM, VMEM],
        out_shape=[pltpu.HBM((SUB, slab, width), F32), pltpu.HBM(signal[1], F32)] if finish else [sums, sums],
        scratch_shapes=scratch,
        compiler_params=pltpu.CompilerParams(vmem_limit_bytes=16 * MIB),
        name="backward_last" if finish else "backward_first",
    )(*operands)


def body(concentration, shear_index, shear_weight, attenuation, yields, line_energy, measured):
    elements, _, slab, width = concentration.shape
    views = shear_weight.shape[0]
    emissions = attenuation.shape[0] - 1
    groups = lax.axis_size("far")
    both = lax.axis_size("views") == 2
    cells = float(slab * groups * NEAR)
    conc = concentration.reshape(elements, slab, width)
    scalars = (attenuation, line_energy, yields)

    def to_other(value):
        return lax.ppermute(value, "views", [(0, 1), (1, 0)])

    fillers = []

    def fill(after):
        if not both or len(fillers) == views:
            return ()
        fillers.append(forward_other(len(fillers), other_weight, mat, left_pad, diff_pad, after))
        return (fillers[-1][2],)

    u, n, const, target, mat, left_pad, diff_pad, _, weight, state, send = forward(
        conc, shear_index, shear_weight, scalars, measured, cells
    )
    if both:
        other_weight = to_other(weight)

    def swap(value, axis, step):
        return lax.ppermute(value, axis, [(s, s ^ step) for s in range(lax.axis_size(axis))])

    states = [state, swap(send, "near", 1)]
    tokens = ()
    levels = groups.bit_length() + 1
    for level in range(levels - 1):
        (state,) = call_small(
            functools.partial(merge_kernel, level), "merge", [state.shape], (const, *states[-2:], *tokens)
        )
        step = ("near", 2) if level == 0 else ("far", 1 << (level - 1))
        states += [state, swap(state, *step)]
    for _ in range(views):
        tokens += fill(state)
    half = ((views + 2) * SUB, width // 2)
    here, there = call_small(
        functools.partial(result_kernel, levels), "result", [half] * 2, (const, target, *states, *tokens)
    )
    there = swap(there, "near", 1)
    package = (half[0], width)
    package, signal = call_small(assemble_kernel, "assemble", [package, target.shape], (target, here, there))
    own = [(u, n, v) for v in range(views)]
    signal = (signal, measured.shape)
    if both:
        other_package = to_other(package)
        sums = backward(package, const, weight, own, cells, None, ())
        pieces = [(fillers[v][0], fillers[v][1], 0) for v in range(views)]
        gradient, signal = backward(other_package, const, other_weight, pieces, cells, signal, sums)
    else:
        gradient, signal = backward(package, const, weight, own, cells, signal, ())
        gradient = lax.psum(gradient, "views")
    return gradient.reshape(concentration.shape), signal


def solution(mesh):
    views, depth = mesh.shape["views"], mesh.shape["depth"]
    devices = mesh.devices.reshape(views, depth // NEAR, NEAR)
    split = jax.sharding.Mesh(devices, ("views", "far", "near"))
    depths = ("far", "near")
    return jax.shard_map(
        body,
        mesh=split,
        in_specs=(
            P(None, None, depths, None),
            P("views", depths, None),
            P("views", depths, None),
            P(),
            P(),
            P(),
            P("views", None, None, None),
        ),
        out_specs=(P(None, None, depths, None), P("views", None, None, None)),
        check_vma=False,
    )
```

```python
import functools

import jax
import jax.numpy as jnp
from jax import lax
from jax.experimental import pallas as pl
from jax.experimental.pallas import tpu as pltpu
from jax.sharding import PartitionSpec as P

LANES = 128
SUB = 8
BLOCK = 8
ROWS = BLOCK * SUB
NEAR = 4
CHUNK = 256
MIB = 1024 * 1024
F32 = jnp.float32
BF16 = jnp.bfloat16
HBM = pl.BlockSpec(memory_space=pltpu.HBM)
VMEM = pl.BlockSpec(memory_space=pltpu.VMEM)
SCALE, LINE_ROWS, LINE_LANES = 4, 5, 6
ANY = pl.BlockSpec(memory_space=pl.ANY)


def in_hbm(value):
    return pltpu.with_memory_space_constraint(value, pltpu.HBM)


def lane_ids(width=LANES):
    return lax.broadcasted_iota(jnp.int32, (SUB, width), 1)


def row_ids(width=LANES):
    return lax.broadcasted_iota(jnp.int32, (SUB, width), 0)


def tile_of(values, ids):
    tile = jnp.zeros(ids.shape, F32)
    for e in range(SUB):
        tile = jnp.where(ids == e, values[e], tile)
    return tile


def select_line(masks, values):
    result = values[0]
    for mask, value in zip(masks[1:], values[1:]):
        result = jnp.where(mask, value, result)
    return result


def fill_matrix(mat_ref, first_tile, second_tile, first_incl, second_incl):
    depth = (lane_ids() & (ROWS - 1)) >> 3
    tiles = []
    for d in range(BLOCK):
        one = jnp.where(depth <= d if first_incl else depth < d, first_tile, 0.0)
        two = jnp.where(depth <= d if second_incl else depth < d, second_tile, 0.0)
        tiles.append(one + two)
    tiles.append(first_tile + second_tile)
    tiles.append(jnp.zeros((SUB, LANES), F32))
    whole = jnp.concatenate(tiles, axis=0)
    high = whole.astype(BF16)
    mat_ref[:, 0:LANES] = high
    mat_ref[:, LANES : 2 * LANES] = (whole - high.astype(F32)).astype(BF16)


def multiply(mat_ref, values):
    high = values.astype(BF16)
    low = (values - high.astype(F32)).astype(BF16)
    stacked = jnp.concatenate([high, low, high], axis=0)
    product = jnp.dot(mat_ref[:, 0 : 3 * ROWS], stacked, preferred_element_type=F32)
    return product[0:ROWS], product[ROWS : ROWS + SUB]


MATRIX = (ROWS + 2 * SUB, 2 * LANES)


def copies_in(pairs, sems):
    return [pltpu.make_async_copy(source, target, sems.at[i]) for i, (source, target) in enumerate(pairs)]


def block_rows(block):
    return slice(block * ROWS, (block + 1) * ROWS)


def block_cells(block):
    return slice(block * BLOCK, (block + 1) * BLOCK)


def shift_of(index_ref, v, cell, width):
    if index_ref.dtype == jnp.int32:
        at = index_ref[v, cell, 0]
    else:
        at = index_ref[v, cell % SUB, cell // SUB].astype(jnp.int32)
    offset = at - (width // 2 - LANES)
    whole = jnp.minimum(offset >> 7, 1)
    return whole, offset - (whole << 7)


def shear(field, left_pad, diff_pad, index_ref, weight_ref, block, views, tiles):
    lanes = lane_ids()
    for i, v in enumerate(views):
        for d in range(BLOCK):
            cell = block * BLOCK + d
            whole, rest = shift_of(index_ref, v, cell, tiles * LANES)
            turn = (LANES - rest) & (LANES - 1)
            stay = lanes < LANES - rest

            def sheared(ref):
                turned = []
                for j in range(tiles + 1):
                    start = pl.multiple_of((whole + j) * LANES, LANES)
                    turned.append(pltpu.roll(ref[cell, :, pl.ds(start, LANES)], turn, 1))
                return [jnp.where(stay, turned[j], turned[j + 1]) for j in range(tiles)]

            left, diff = sheared(left_pad), sheared(diff_pad)
            for j in range(tiles):
                span = slice(j * LANES, (j + 1) * LANES)
                field[i, d * SUB : (d + 1) * SUB, span] = left[j] + weight_ref[i, cell : cell + 1, span] * diff[j]


def transmit(u_ref, n_ref, field, mat, carry, block, sums):
    views, _, width = field.shape
    for v in range(views):
        for c in range(width // CHUNK):
            span = slice(c * CHUNK, (c + 1) * CHUNK)
            value = field[v, :, span]
            lines, total = multiply(mat, value)
            before = carry[v, :, span]
            through = jnp.exp(lines.reshape(BLOCK, SUB, CHUNK) + before[None])
            value = value.reshape(BLOCK, SUB, CHUNK)
            emit = value * through
            u_ref[v, block_rows(block), span] = through.reshape(ROWS, CHUNK)
            n_ref[v, block_rows(block), span] = emit.reshape(ROWS, CHUNK)
            carry[v, :, span] = before + total
            if sums:
                sums[0][v, :, span] += jnp.sum(value, axis=0)
                sums[1][v, :, span] += jnp.sum(emit, axis=0)


def forward_kernel(cells, *refs):
    att_hbm, line_hbm, yield_hbm, index_hbm, conc_hbm, weight_hbm, measured_hbm = refs[:7]
    u_ref, n_ref, const_ref, target_ref, mat, left_pad, diff_pad, weight_ref = refs[7:15]
    state_refs = refs[15:17]
    refs = refs[17:]
    conc_ref, field, carry, field_sum, emit_sum, measured_ref, column_ref = refs[:7]
    att_ref, line_ref, yield_ref, index_ref, sems = refs[7:]
    views, _, width = weight_ref.shape
    slab = conc_ref.shape[1]
    emissions = att_ref.shape[0] - 1
    tiles = width // LANES
    blocks = slab // BLOCK
    lanes, rows = lane_ids(), row_ids()
    conc_copies = [
        pltpu.make_async_copy(
            conc_hbm.at[:, pl.ds(b * BLOCK, BLOCK), :], conc_ref.at[:, pl.ds(b * BLOCK, BLOCK), :], sems.at[b]
        )
        for b in range(blocks)
    ]
    pairs = [
        (att_hbm, att_ref),
        (line_hbm, line_ref),
        (yield_hbm, yield_ref),
        (index_hbm.at[:, :, pl.ds(width // 2, LANES)], index_ref),
        (weight_hbm, weight_ref.at[:, pl.ds(0, slab), :]),
        (measured_hbm, measured_ref),
        (index_hbm.at[:, :, pl.ds(width // 2, LANES)], column_ref),
    ]
    copies = copies_in(pairs, sems.at[pl.ds(blocks, len(pairs))])
    for copy in conc_copies[:1] + copies[:5] + conc_copies[1:] + copies[5:]:
        copy.start()
    for ref in (carry, field_sum, emit_sum):
        ref[...] = jnp.zeros_like(ref)

    def pad(block):
        conc_copies[block].wait()
        by_depth = jnp.swapaxes(conc_ref[:, block_cells(block), :], 0, 1)
        for d in range(BLOCK):
            pieces = [by_depth[d, :, j * LANES : (j + 1) * LANES] for j in range(tiles)]
            turned = [pltpu.roll(piece, LANES - 1, 1) for piece in pieces]
            after = [jnp.where(lanes < LANES - 1, turned[j], turned[min(j + 1, tiles - 1)]) for j in range(tiles)]
            steps = [after[j] - pieces[j] for j in range(tiles)]
            last_cell = jnp.broadcast_to(pieces[-1][:, LANES - 2 : LANES - 1], (SUB, LANES))
            last_step = jnp.broadcast_to(steps[-1][:, LANES - 2 : LANES - 1], (SUB, LANES))
            first_cell = jnp.broadcast_to(pieces[0][:, 0:1], (SUB, LANES))
            first_step = jnp.broadcast_to(steps[0][:, 0:1], (SUB, LANES))
            pieces[-1] = jnp.where(lanes < LANES - 1, pieces[-1], last_cell)
            steps[-1] = jnp.where(lanes < LANES - 1, steps[-1], last_step)
            pieces = [first_cell] + pieces + [last_cell, last_cell]
            steps = [first_step] + steps + [last_step, last_step]
            for j in range(tiles + 3):
                left_pad[block * BLOCK + d, :, j * LANES : (j + 1) * LANES] = pieces[j]
                diff_pad[block * BLOCK + d, :, j * LANES : (j + 1) * LANES] = steps[j]

    pad(0)
    for copy in copies[:5]:
        copy.wait()
    line_by_row = tile_of([line_ref[e].astype(F32) for e in range(SUB)], rows)
    masks = [line_by_row == k for k in range(emissions)]
    by_lane = [tile_of([att_ref[k, e] for e in range(SUB)], lanes & 7) for k in range(emissions + 1)]
    fill_matrix(mat, -by_lane[0], select_line(masks, by_lane[1:]), False, True)
    for k in range(emissions + 1):
        const_ref[k] = tile_of([att_ref[k, e] for e in range(SUB)], rows)
    const_ref[SCALE] = tile_of([yield_ref[e] for e in range(SUB)], rows)
    const_ref[LINE_ROWS] = line_by_row
    const_ref[LINE_LANES] = tile_of([line_ref[e].astype(F32) for e in range(SUB)], lanes & 7)
    for block in range(blocks):
        if block:
            pad(block)
        shear(field, left_pad, diff_pad, index_ref, weight_ref, block, range(views), tiles)
        transmit(u_ref, n_ref, field, mat, carry, block, (field_sum, emit_sum))
    for copy in copies[5:]:
        copy.wait()
    for v in range(views):
        shifts = jnp.zeros((SUB, LANES), jnp.int32)
        for octet in range(slab // SUB):
            values = column_ref[v, octet * SUB : (octet + 1) * SUB, :] - lanes
            shifts = jnp.where(lanes == octet, values, shifts)
        weight_ref[v, slab : slab + SUB, 0:LANES] = shifts.astype(F32)
    columns = [const_ref[k] for k in range(emissions + 1)]
    masks = [const_ref[LINE_ROWS] == k for k in range(emissions)]
    scale = const_ref[SCALE] * (1.0 / cells)
    share = width // 2
    core = lax.axis_index("near") & 1
    for r in range(2):
        for j in range(share // LANES):
            start = pl.multiple_of((core ^ r) * share + j * LANES, LANES)
            span = slice(j * LANES, (j + 1) * LANES)
            totals = jnp.zeros((SUB, LANES), F32)
            for v in range(views):
                values = field_sum[v, :, pl.ds(start, LANES)]
                sums = [jnp.sum(column * values, axis=0, keepdims=True) for column in columns]
                for k in range(emissions + 1):
                    totals = jnp.where(rows == v * (emissions + 1) + k, sums[k], totals)
                line_total = select_line(masks, [jnp.broadcast_to(value, rows.shape) for value in sums[1:]])
                signal = scale * emit_sum[v, :, pl.ds(start, LANES)] * jnp.exp(-line_total)
                state_refs[r][(v + 1) * SUB : (v + 2) * SUB, span] = signal
            state_refs[r][0:SUB, span] = jnp.exp(-totals)
    for v in range(views):
        target_ref[v * SUB : (v + 1) * SUB, :] = measured_ref[v].reshape(SUB, width)


def forward(conc, index, weights, scalars, measured, cells):
    views, slab, width = weights.shape
    attenuation, line_energy, yields = scalars
    values = pltpu.VMEM((views, slab * SUB, width), F32)
    padded = pltpu.VMEM((slab, SUB, width + 3 * LANES), F32)
    state = pltpu.VMEM(((views + 1) * SUB, width // 2), F32)
    line = pltpu.VMEM((views, SUB, width), F32)
    operands = [in_hbm(value) for value in (attenuation, line_energy, yields, index, conc, weights, measured)]
    return pl.pallas_call(
        functools.partial(forward_kernel, cells),
        in_specs=[HBM] * len(operands),
        out_specs=[VMEM] * 10,
        out_shape=[
            values,
            values,
            pltpu.VMEM((LINE_LANES + 1, SUB, LANES), F32),
            pltpu.VMEM((views * SUB, width), F32),
            pltpu.VMEM(MATRIX, BF16),
            padded,
            padded,
            pltpu.VMEM((views, slab + SUB, width), F32),
            state,
            state,
        ],
        scratch_shapes=[
            pltpu.VMEM((SUB, slab, width), F32),
            pltpu.VMEM((views, ROWS, width), F32),
            line,
            line,
            line,
            pltpu.VMEM(measured.shape, F32),
            pltpu.VMEM((views, slab, LANES), jnp.int32),
            pltpu.SMEM(attenuation.shape, F32),
            pltpu.SMEM(line_energy.shape, jnp.int32),
            pltpu.SMEM(yields.shape, F32),
            pltpu.SMEM((views, slab, LANES), jnp.int32),
            pltpu.SemaphoreType.DMA((slab // BLOCK + 7,)),
        ],
        compiler_params=pltpu.CompilerParams(vmem_limit_bytes=16 * MIB),
        name="forward",
    )(*operands)


def column_in(package_any, views, index_ref, sem):
    first = package_any.shape[1] - SUB
    source = package_any.at[views, pl.ds(first, SUB), pl.ds(0, index_ref.shape[2])]
    return pltpu.make_async_copy(source, index_ref, sem)


def forward_other_kernel(view, weight_ref, mat, left_pad, diff_pad, order_ref, *refs):
    u_ref, n_ref, token_ref, field, carry, index_ref, sem = refs
    _, slab, width = weight_ref.shape
    slab = slab - SUB
    copy = column_in(weight_ref, pl.ds(view, 1), index_ref, sem)
    copy.start()
    carry[...] = jnp.zeros_like(carry)
    token_ref[...] = jnp.zeros_like(token_ref)
    copy.wait()
    for block in range(slab // BLOCK):
        shear(field, left_pad, diff_pad, index_ref, weight_ref.at[pl.ds(view, 1)], block, (0,), width // LANES)
        transmit(u_ref, n_ref, field, mat, carry, block, None)


def forward_other(view, weights, mat, left_pad, diff_pad, after):
    _, slab, width = weights.shape
    slab = slab - SUB
    values = pltpu.VMEM((1, slab * SUB, width), F32)
    return pl.pallas_call(
        functools.partial(forward_other_kernel, view),
        in_specs=[VMEM] * 5,
        out_specs=[VMEM] * 3,
        out_shape=[values, values, pltpu.VMEM((SUB, LANES), F32)],
        scratch_shapes=[
            pltpu.VMEM((1, ROWS, width), F32),
            pltpu.VMEM((1, SUB, width), F32),
            pltpu.SMEM((1, SUB, LANES), F32),
            pltpu.SemaphoreType.DMA,
        ],
        compiler_params=pltpu.CompilerParams(vmem_limit_bytes=8 * MIB),
        name="forward_other",
    )(weights, mat, left_pad, diff_pad, after)


def line_rows(tile, base, masks):
    shape = masks[0].shape
    return select_line(masks, [jnp.broadcast_to(tile[base + 1 + k : base + 2 + k], shape) for k in range(len(masks))])


def incident_rows(tile, step):
    rows = row_ids(tile.shape[1])
    result = jnp.broadcast_to(tile[0:1], tile.shape)
    for base in range(step, SUB, step):
        result = jnp.where(rows >= base, jnp.broadcast_to(tile[base : base + 1], tile.shape), result)
    return result


def row_masks(const_ref, width):
    tile = const_ref[LINE_ROWS]
    return [jnp.concatenate([tile] * (width // LANES), axis=1) == k for k in range(SCALE - 1)]


def factors_of(mine, theirs, bit):
    mine_factor = jnp.where(bit == 0, theirs, incident_rows(theirs, SCALE))
    return mine_factor, jnp.where(bit == 0, incident_rows(mine, SCALE), mine)


def merged_state(mine, theirs, bit, masks):
    mine_factor, theirs_factor = factors_of(mine[0:SUB], theirs[0:SUB], bit)
    result = [mine[0:SUB] * theirs[0:SUB]]
    for v in range(mine.shape[0] // SUB - 1):
        span = slice((v + 1) * SUB, (v + 2) * SUB)
        result.append(
            mine[span] * line_rows(mine_factor, v * SCALE, masks)
            + theirs[span] * line_rows(theirs_factor, v * SCALE, masks)
        )
    return result


def weighted_rows(factor, state, misfits, masks):
    rows = row_ids(state.shape[1])
    result = jnp.zeros((SUB, state.shape[1]), F32)
    for v, misfit in enumerate(misfits):
        base = v * SCALE
        value = misfit * state[(v + 1) * SUB : (v + 2) * SUB] * line_rows(factor, base, masks)
        whole = None
        for k, mask in enumerate(masks):
            part = jnp.sum(jnp.where(mask, value, 0.0), axis=0, keepdims=True)
            result = jnp.where(rows == base + 1 + k, part, result)
            whole = part if whole is None else whole + part
        result = jnp.where(rows == base, whole, result)
    return result


def children(factor, sums, mine, theirs, bit, misfits, masks):
    mine_factor, theirs_factor = factors_of(mine[0:SUB], theirs[0:SUB], bit)
    if factor is not None:
        mine_factor, theirs_factor = factor * mine_factor, factor * theirs_factor
    behind = (row_ids(mine.shape[1]) & (SCALE - 1)) == 0
    mine_sums = jnp.where(behind == (bit == 0), weighted_rows(theirs_factor, theirs, misfits, masks), 0.0)
    theirs_sums = jnp.where(behind == (bit == 1), weighted_rows(mine_factor, mine, misfits, masks), 0.0)
    if sums is not None:
        mine_sums, theirs_sums = sums + mine_sums, sums + theirs_sums
    return (mine_factor, mine_sums), (theirs_factor, theirs_sums)


def call_small(kernel, name, outs, operands, scratch=()):
    return pl.pallas_call(
        kernel,
        in_specs=[VMEM] * len(operands),
        out_specs=[VMEM] * len(outs),
        out_shape=[pltpu.VMEM(shape, F32) for shape in outs],
        scratch_shapes=[pltpu.VMEM(shape, F32) for shape in scratch],
        compiler_params=pltpu.CompilerParams(vmem_limit_bytes=4 * MIB),
        name=name,
    )(*operands)


def pass_on(value, after):
    return pl.pallas_call(
        lambda value_ref, after_ref, out_ref: None,
        in_specs=[VMEM, VMEM],
        out_specs=VMEM,
        out_shape=pltpu.VMEM(value.shape, F32),
        input_output_aliases={0: 0},
        compiler_params=pltpu.CompilerParams(vmem_limit_bytes=2 * MIB),
        cost_estimate=pl.CostEstimate(flops=0, bytes_accessed=8 * MIB, transcendentals=0),
        name="pass_on",
    )(value, after)


def merge_kernel(shift, const_ref, mine_ref, theirs_ref, *refs):
    bit = (depth_place() >> shift) & 1
    state = merged_state(mine_ref[...], theirs_ref[...], bit, row_masks(const_ref, mine_ref.shape[1]))
    for i, tile in enumerate(state):
        refs[-1][i * SUB : (i + 1) * SUB, :] = tile


def depth_place():
    return lax.axis_index("far") * NEAR + lax.axis_index("near")


def result_kernel(levels, const_ref, target_ref, *refs):
    states, outs = refs[: 2 * levels], refs[-2:]
    depth, width = states[0].shape
    views = depth // SUB - 1
    place = depth_place()
    size = 2 * LANES
    start = (place & 1) * width
    masks = row_masks(const_ref, size)
    behind = (row_ids(size) & (SCALE - 1)) == 0
    for c in range(width // size):
        span = slice(c * size, (c + 1) * size)
        factor, sums = None, None
        for level in reversed(range(levels)):
            mine, theirs = states[2 * level][:, span], states[2 * level + 1][:, span]
            bit = (place >> level) & 1
            if level == levels - 1:
                signals = merged_state(mine, theirs, bit, masks)[1:]
                there = pl.ds(pl.multiple_of(start + c * size, LANES), size)
                misfits = [signals[v] - target_ref[v * SUB : (v + 1) * SUB, there] for v in range(views)]
            contexts = children(factor, sums, mine, theirs, bit, misfits, masks)
            factor, sums = contexts[0]
        for ref, state, (factor, sums) in zip(outs, (mine, theirs), contexts):
            own = jnp.where(behind, weighted_rows(factor, state, misfits, masks), 0.0)
            for i, tile in enumerate(signals + [factor * state[0:SUB], sums + own]):
                ref[i * SUB : (i + 1) * SUB, span] = tile


def assemble_kernel(target_ref, here_ref, there_ref, package_ref, signal_ref):
    half = here_ref.shape[1]
    count = signal_ref.shape[0]
    at = pl.multiple_of((lax.axis_index("near") & 1) * half, LANES)
    for ref, start in ((here_ref, at), (there_ref, pl.multiple_of(half - at, LANES))):
        span = pl.ds(start, half)
        signal_ref[:, span] = ref[0:count, :]
        package_ref[0:count, span] = ref[0:count, :] - target_ref[:, span]
        package_ref[count:, span] = ref[count:, :]


def backward_kernel(places, cells, finish, const_ref, package_ref, weight_ref, *refs):
    count = len(places)
    u_refs, n_refs, refs = refs[:count], refs[count : 2 * count], refs[2 * count :]
    if finish:
        signal_ref, refs = refs[0], refs[1:]
        prior, refs = refs[: finish - 1], refs[finish - 1 :]
        grad_hbm, signal_hbm, cell_ref, grad_ref, signal_rows = refs[:5]
        refs = refs[5:]
    else:
        left_sum, diff_sum, refs = refs[0], refs[1], refs[2:]
    mat, gain, carry, scaled, left_pad, diff_pad, index_ref, sems = refs
    _, slab, width = weight_ref.shape
    slab = slab - SUB
    emissions = SCALE - 1
    tiles = width // LANES
    blocks = slab // BLOCK
    lanes, rows = lane_ids(), row_ids()
    column = column_in(weight_ref, pl.ds(0, count), index_ref, sems.at[blocks])
    column.start()
    if finish:
        for v in range(signal_rows.shape[0]):
            signal_rows[v] = signal_ref[v * SUB : (v + 1) * SUB, :].reshape(SUB, 1, width)
        signal_copy = pltpu.make_async_copy(signal_rows, signal_hbm, sems.at[blocks + 1])
        signal_copy.start()
        out_copies = [
            pltpu.make_async_copy(grad_ref.at[b], grad_hbm.at[:, pl.ds(b * BLOCK, BLOCK), :], sems.at[b])
            for b in range(blocks)
        ]
    masks = [const_ref[LINE_LANES] == k for k in range(emissions)]
    columns = [const_ref[k] for k in range(emissions + 1)]
    fill_matrix(mat, -columns[0], select_line(masks, columns[1:]), True, False)
    masks = [const_ref[LINE_ROWS] == k for k in range(emissions)]
    scale = const_ref[SCALE]
    columns = [column * cells for column in columns]
    for j in range(tiles):
        span = slice(j * LANES, (j + 1) * LANES)
        factor = package_ref[count * SUB : (count + 1) * SUB, span]
        sums = package_ref[(count + 1) * SUB : (count + 2) * SUB, span]
        for v in range(count):
            base = v * SCALE
            gain[v, :, span] = package_ref[v * SUB : (v + 1) * SUB, span] * scale * line_rows(factor, base, masks)
            back = columns[0] * jnp.broadcast_to(sums[base : base + 1], rows.shape)
            for k in range(1, emissions + 1):
                back = back + columns[k] * jnp.broadcast_to(sums[base + k : base + k + 1], rows.shape)
            carry[v, :, span] = back
    zero = jnp.zeros((SUB, LANES), F32)
    for ref in (left_pad, diff_pad):
        edge = jnp.zeros(ref.shape[:3] + (LANES,), F32)
        ref[:, :, :, 0:LANES] = edge
        ref[:, :, :, width + 2 * LANES :] = edge
    column.wait()

    def place(v, d, cell, first):
        _, rest = shift_of(index_ref, v, cell, width)
        stay = lanes >= rest
        turn = rest & (LANES - 1)
        at = (first + d) * SUB
        plain = [scaled[v, at : at + SUB, j * LANES : (j + 1) * LANES] for j in range(tiles)]
        moved = [plain[j] * weight_ref[v, cell : cell + 1, j * LANES : (j + 1) * LANES] for j in range(tiles)]
        for ref, values in ((left_pad, plain), (diff_pad, moved)):
            turned = [zero] + [pltpu.roll(value, turn, 1) for value in values] + [zero]
            for j in range(tiles + 1):
                ref[v, first + d, :, (j + 1) * LANES : (j + 2) * LANES] = jnp.where(stay, turned[j + 1], turned[j])

    def gathered(ref, before, cell, slot):
        sums = [None] * (tiles + 2)
        if before is not None:
            sums = [before[cell, :, j * LANES : (j + 1) * LANES] for j in range(tiles + 2)]
        for v in range(count):
            whole, _ = shift_of(index_ref, v, cell, width)
            for j in range(tiles + 2):
                start = pl.multiple_of((1 + j - whole) * LANES, LANES)
                value = ref[v, slot, :, pl.ds(start, LANES)]
                sums[j] = value if sums[j] is None else sums[j] + value
        return sums

    def folded(sums):
        low = jnp.sum(sums[0], axis=1, keepdims=True)
        beyond = sums[tiles + 1] + jnp.where(lanes == LANES - 1, sums[tiles], 0.0)
        high = jnp.sum(beyond, axis=1, keepdims=True)
        core = sums[1 : tiles + 1]
        core[0] = core[0] + jnp.where(lanes == 0, low, 0.0)
        core[-1] = jnp.where(lanes == LANES - 1, 0.0, core[-1] + jnp.where(lanes == LANES - 2, high, 0.0))
        return core

    for block in range(blocks):
        first = block % 2 * BLOCK
        for v in range(count):
            for c in range(width // CHUNK):
                span = slice(c * CHUNK, (c + 1) * CHUNK)
                factor = gain[v, :, span][None]
                weighted = n_refs[v][places[v], block_rows(block), span].reshape(BLOCK, SUB, CHUNK) * factor
                direct = u_refs[v][places[v], block_rows(block), span].reshape(BLOCK, SUB, CHUNK) * factor
                lines, total = multiply(mat, weighted.reshape(ROWS, CHUNK))
                before = carry[v, :, span]
                lines = lines.reshape(BLOCK, SUB, CHUNK) + before[None]
                scaled[v, first * SUB : first * SUB + ROWS, span] = (direct - lines).reshape(ROWS, CHUNK)
                carry[v, :, span] = before + total
        for v in range(count):
            for d in range(BLOCK):
                place(v, d, block * BLOCK + d, first)
        for d in range(BLOCK):
            cell = block * BLOCK + d
            left = gathered(left_pad, prior[0] if finish > 1 else None, cell, first + d)
            diff = gathered(diff_pad, prior[1] if finish > 1 else None, cell, first + d)
            if not finish:
                for j in range(tiles + 2):
                    left_sum[cell, :, j * LANES : (j + 1) * LANES] = left[j]
                    diff_sum[cell, :, j * LANES : (j + 1) * LANES] = diff[j]
                continue
            left, diff = folded([left[j] - diff[j] for j in range(tiles + 2)]), folded(diff)
            turned = [zero] + [pltpu.roll(value, 1, 1) for value in diff]
            for j in range(tiles):
                value = left[j] + jnp.where(lanes == 0, turned[j], turned[j + 1])
                cell_ref[first + d, :, j * LANES : (j + 1) * LANES] = value
        if finish:
            grad_ref[block] = jnp.swapaxes(cell_ref[first : first + BLOCK], 0, 1)
            out_copies[block].start()
    if finish:
        for copy in out_copies + [signal_copy]:
            copy.wait()


def backward(package, const, weights, pieces, cells, signal, prior):
    views, slab, width = weights.shape
    slab = slab - SUB
    blocks = slab // BLOCK
    finish = signal is not None
    line = pltpu.VMEM((views, SUB, width), F32)
    sums = pltpu.VMEM((slab, SUB, width + 2 * LANES), F32)
    scratch = [
        pltpu.VMEM(MATRIX, BF16),
        line,
        line,
        pltpu.VMEM((views, 2 * ROWS, width), F32),
        pltpu.VMEM((views, 2 * BLOCK, SUB, width + 3 * LANES), F32),
        pltpu.VMEM((views, 2 * BLOCK, SUB, width + 3 * LANES), F32),
        pltpu.SMEM((views, SUB, LANES), F32),
        pltpu.SemaphoreType.DMA((blocks + 2,)),
    ]
    operands = [const, package, weights, *[u for u, _, _ in pieces], *[n for _, n, _ in pieces]]
    if finish:
        operands += [signal[0], *prior]
        scratch = [
            pltpu.VMEM((2 * BLOCK, SUB, width), F32),
            pltpu.VMEM((blocks, SUB, BLOCK, width), F32),
            pltpu.VMEM(signal[1], F32),
        ] + scratch
    return pl.pallas_call(
        functools.partial(
            backward_kernel, tuple(at for _, _, at in pieces), cells, 1 + len(prior) if finish else 0
        ),
        in_specs=[VMEM] * len(operands),
        out_specs=[HBM, HBM] if finish else [VMEM, VMEM],
        out_shape=[pltpu.HBM((SUB, slab, width), F32), pltpu.HBM(signal[1], F32)] if finish else [sums, sums],
        scratch_shapes=scratch,
        compiler_params=pltpu.CompilerParams(vmem_limit_bytes=16 * MIB),
        name="backward_last" if finish else "backward_first",
    )(*operands)


def body(concentration, shear_index, shear_weight, attenuation, yields, line_energy, measured):
    elements, _, slab, width = concentration.shape
    views = shear_weight.shape[0]
    emissions = attenuation.shape[0] - 1
    groups = lax.axis_size("far")
    both = lax.axis_size("views") == 2
    cells = float(slab * groups * NEAR)
    conc = concentration.reshape(elements, slab, width)
    scalars = (attenuation, line_energy, yields)

    def to_other(value):
        return lax.ppermute(value, "views", [(0, 1), (1, 0)])

    fillers = []

    def fill(after):
        if not both or len(fillers) == views:
            return ()
        fillers.append(forward_other(len(fillers), other_weight, mat, left_pad, diff_pad, after))
        return (fillers[-1][2],)

    u, n, const, target, mat, left_pad, diff_pad, weight, state, send = forward(
        conc, shear_index, shear_weight, scalars, measured, cells
    )
    def swap(value, axis, step):
        return lax.ppermute(value, axis, [(s, s ^ step) for s in range(lax.axis_size(axis))])

    states = [state, swap(send, "near", 1)]
    if both:
        weight = pass_on(weight, state)
        other_weight = to_other(weight)
    tokens = ()
    levels = groups.bit_length() + 1
    for level in range(levels - 1):
        (state,) = call_small(
            functools.partial(merge_kernel, level), "merge", [state.shape], (const, *states[-2:], *tokens)
        )
        step = ("near", 2) if level == 0 else ("far", 1 << (level - 1))
        states += [state, swap(state, *step)]
    for _ in range(views):
        tokens += fill(state)
    half = ((views + 2) * SUB, width // 2)
    here, there = call_small(
        functools.partial(result_kernel, levels), "result", [half] * 2, (const, target, *states, *tokens)
    )
    there = swap(there, "near", 1)
    package = (half[0], width)
    package, signal = call_small(assemble_kernel, "assemble", [package, target.shape], (target, here, there))
    own = [(u, n, v) for v in range(views)]
    signal = (signal, measured.shape)
    if both:
        other_package = to_other(package)
        sums = backward(package, const, weight, own, cells, None, ())
        pieces = [(fillers[v][0], fillers[v][1], 0) for v in range(views)]
        gradient, signal = backward(other_package, const, other_weight, pieces, cells, signal, sums)
    else:
        gradient, signal = backward(package, const, weight, own, cells, signal, ())
        gradient = lax.psum(gradient, "views")
    return gradient.reshape(concentration.shape), signal


def solution(mesh):
    views, depth = mesh.shape["views"], mesh.shape["depth"]
    devices = mesh.devices.reshape(views, depth // NEAR, NEAR)
    split = jax.sharding.Mesh(devices, ("views", "far", "near"))
    depths = ("far", "near")
    return jax.shard_map(
        body,
        mesh=split,
        in_specs=(
            P(None, None, depths, None),
            P("views", depths, None),
            P("views", depths, None),
            P(),
            P(),
            P(),
            P("views", None, None, None),
        ),
        out_specs=(P(None, None, depths, None), P("views", None, None, None)),
        check_vma=False,
    )
```

```python
import functools

import jax
import jax.numpy as jnp
from jax import lax
from jax.experimental import pallas as pl
from jax.experimental.pallas import tpu as pltpu
from jax.sharding import PartitionSpec as P

LANES = 128
SUB = 8
BLOCK = 8
ROWS = BLOCK * SUB
NEAR = 4
CHUNK = 256
MIB = 1024 * 1024
F32 = jnp.float32
BF16 = jnp.bfloat16
HBM = pl.BlockSpec(memory_space=pltpu.HBM)
VMEM = pl.BlockSpec(memory_space=pltpu.VMEM)
SCALE, LINE_ROWS, LINE_LANES = 4, 5, 6
ANY = pl.BlockSpec(memory_space=pl.ANY)


def in_hbm(value):
    return pltpu.with_memory_space_constraint(value, pltpu.HBM)


def lane_ids(width=LANES):
    return lax.broadcasted_iota(jnp.int32, (SUB, width), 1)


def row_ids(width=LANES):
    return lax.broadcasted_iota(jnp.int32, (SUB, width), 0)


def tile_of(values, ids):
    tile = jnp.zeros(ids.shape, F32)
    for e in range(SUB):
        tile = jnp.where(ids == e, values[e], tile)
    return tile


def select_line(masks, values):
    result = values[0]
    for mask, value in zip(masks[1:], values[1:]):
        result = jnp.where(mask, value, result)
    return result


def fill_matrix(mat_ref, first_tile, second_tile, first_incl, second_incl):
    depth = (lane_ids() & (ROWS - 1)) >> 3
    tiles = []
    for d in range(BLOCK):
        one = jnp.where(depth <= d if first_incl else depth < d, first_tile, 0.0)
        two = jnp.where(depth <= d if second_incl else depth < d, second_tile, 0.0)
        tiles.append(one + two)
    tiles.append(first_tile + second_tile)
    tiles.append(jnp.zeros((SUB, LANES), F32))
    whole = jnp.concatenate(tiles, axis=0)
    high = whole.astype(BF16)
    mat_ref[:, 0:LANES] = high
    mat_ref[:, LANES : 2 * LANES] = (whole - high.astype(F32)).astype(BF16)


def multiply(mat_ref, values):
    high = values.astype(BF16)
    low = (values - high.astype(F32)).astype(BF16)
    stacked = jnp.concatenate([high, low, high], axis=0)
    product = jnp.dot(mat_ref[:, 0 : 3 * ROWS], stacked, preferred_element_type=F32)
    return product[0:ROWS], product[ROWS : ROWS + SUB]


MATRIX = (ROWS + 2 * SUB, 2 * LANES)


def copies_in(pairs, sems):
    return [pltpu.make_async_copy(source, target, sems.at[i]) for i, (source, target) in enumerate(pairs)]


def block_rows(block):
    return slice(block * ROWS, (block + 1) * ROWS)


def block_cells(block):
    return slice(block * BLOCK, (block + 1) * BLOCK)


def shift_of(index_ref, v, cell, width):
    if index_ref.dtype == jnp.int32:
        at = index_ref[v, cell, 0]
    else:
        at = index_ref[v, cell % SUB, cell // SUB].astype(jnp.int32)
    offset = at - (width // 2 - LANES)
    whole = jnp.minimum(offset >> 7, 1)
    return whole, offset - (whole << 7)


def shear(field, left_pad, diff_pad, index_ref, weight_ref, block, views, tiles):
    lanes = lane_ids()
    for i, v in enumerate(views):
        for d in range(BLOCK):
            cell = block * BLOCK + d
            whole, rest = shift_of(index_ref, v, cell, tiles * LANES)
            turn = (LANES - rest) & (LANES - 1)
            stay = lanes < LANES - rest

            def sheared(ref):
                turned = []
                for j in range(tiles + 1):
                    start = pl.multiple_of((whole + j) * LANES, LANES)
                    turned.append(pltpu.roll(ref[cell, :, pl.ds(start, LANES)], turn, 1))
                return [jnp.where(stay, turned[j], turned[j + 1]) for j in range(tiles)]

            left, diff = sheared(left_pad), sheared(diff_pad)
            for j in range(tiles):
                span = slice(j * LANES, (j + 1) * LANES)
                field[i, d * SUB : (d + 1) * SUB, span] = left[j] + weight_ref[i, cell : cell + 1, span] * diff[j]


def transmit(u_ref, n_ref, field, mat, carry, block, sums):
    views, _, width = field.shape
    for v in range(views):
        for c in range(width // CHUNK):
            span = slice(c * CHUNK, (c + 1) * CHUNK)
            value = field[v, :, span]
            lines, total = multiply(mat, value)
            before = carry[v, :, span]
            through = jnp.exp(lines.reshape(BLOCK, SUB, CHUNK) + before[None])
            value = value.reshape(BLOCK, SUB, CHUNK)
            emit = value * through
            u_ref[v, block_rows(block), span] = through.reshape(ROWS, CHUNK)
            n_ref[v, block_rows(block), span] = emit.reshape(ROWS, CHUNK)
            carry[v, :, span] = before + total
            if sums:
                sums[0][v, :, span] += jnp.sum(value, axis=0)
                sums[1][v, :, span] += jnp.sum(emit, axis=0)


def forward_kernel(cells, *refs):
    att_hbm, line_hbm, yield_hbm, index_hbm, conc_hbm, weight_hbm, measured_hbm = refs[:7]
    u_ref, n_ref, const_ref, target_ref, mat, left_pad, diff_pad, weight_ref = refs[7:15]
    state_refs = refs[15:17]
    refs = refs[17:]
    conc_ref, field, carry, field_sum, emit_sum, measured_ref, column_ref = refs[:7]
    att_ref, line_ref, yield_ref, index_ref, sems = refs[7:]
    views, _, width = weight_ref.shape
    slab = conc_ref.shape[1]
    emissions = att_ref.shape[0] - 1
    tiles = width // LANES
    blocks = slab // BLOCK
    lanes, rows = lane_ids(), row_ids()
    conc_copies = [
        pltpu.make_async_copy(
            conc_hbm.at[:, pl.ds(b * BLOCK, BLOCK), :], conc_ref.at[:, pl.ds(b * BLOCK, BLOCK), :], sems.at[b]
        )
        for b in range(blocks)
    ]
    pairs = [
        (att_hbm, att_ref),
        (line_hbm, line_ref),
        (yield_hbm, yield_ref),
        (index_hbm.at[:, :, pl.ds(width // 2, LANES)], index_ref),
        (weight_hbm, weight_ref.at[:, pl.ds(0, slab), :]),
        (measured_hbm, measured_ref),
        (index_hbm.at[:, :, pl.ds(width // 2, LANES)], column_ref),
    ]
    copies = copies_in(pairs, sems.at[pl.ds(blocks, len(pairs))])
    for copy in conc_copies[:1] + copies[:5] + conc_copies[1:] + copies[5:]:
        copy.start()
    for ref in (carry, field_sum, emit_sum):
        ref[...] = jnp.zeros_like(ref)

    def pad(block):
        conc_copies[block].wait()
        by_depth = jnp.swapaxes(conc_ref[:, block_cells(block), :], 0, 1)
        for d in range(BLOCK):
            pieces = [by_depth[d, :, j * LANES : (j + 1) * LANES] for j in range(tiles)]
            turned = [pltpu.roll(piece, LANES - 1, 1) for piece in pieces]
            after = [jnp.where(lanes < LANES - 1, turned[j], turned[min(j + 1, tiles - 1)]) for j in range(tiles)]
            steps = [after[j] - pieces[j] for j in range(tiles)]
            last_cell = jnp.broadcast_to(pieces[-1][:, LANES - 2 : LANES - 1], (SUB, LANES))
            last_step = jnp.broadcast_to(steps[-1][:, LANES - 2 : LANES - 1], (SUB, LANES))
            first_cell = jnp.broadcast_to(pieces[0][:, 0:1], (SUB, LANES))
            first_step = jnp.broadcast_to(steps[0][:, 0:1], (SUB, LANES))
            pieces[-1] = jnp.where(lanes < LANES - 1, pieces[-1], last_cell)
            steps[-1] = jnp.where(lanes < LANES - 1, steps[-1], last_step)
            pieces = [first_cell] + pieces + [last_cell, last_cell]
            steps = [first_step] + steps + [last_step, last_step]
            for j in range(tiles + 3):
                left_pad[block * BLOCK + d, :, j * LANES : (j + 1) * LANES] = pieces[j]
                diff_pad[block * BLOCK + d, :, j * LANES : (j + 1) * LANES] = steps[j]

    pad(0)
    for copy in copies[:5]:
        copy.wait()
    line_by_row = tile_of([line_ref[e].astype(F32) for e in range(SUB)], rows)
    masks = [line_by_row == k for k in range(emissions)]
    by_lane = [tile_of([att_ref[k, e] for e in range(SUB)], lanes & 7) for k in range(emissions + 1)]
    fill_matrix(mat, -by_lane[0], select_line(masks, by_lane[1:]), False, True)
    for k in range(emissions + 1):
        const_ref[k] = tile_of([att_ref[k, e] for e in range(SUB)], rows)
    const_ref[SCALE] = tile_of([yield_ref[e] for e in range(SUB)], rows)
    const_ref[LINE_ROWS] = line_by_row
    const_ref[LINE_LANES] = tile_of([line_ref[e].astype(F32) for e in range(SUB)], lanes & 7)
    for block in range(blocks):
        if block:
            pad(block)
        shear(field, left_pad, diff_pad, index_ref, weight_ref, block, range(views), tiles)
        transmit(u_ref, n_ref, field, mat, carry, block, (field_sum, emit_sum))
    for copy in copies[5:]:
        copy.wait()
    for v in range(views):
        shifts = jnp.zeros((SUB, LANES), jnp.int32)
        for octet in range(slab // SUB):
            values = column_ref[v, octet * SUB : (octet + 1) * SUB, :] - lanes
            shifts = jnp.where(lanes == octet, values, shifts)
        weight_ref[v, slab : slab + SUB, 0:LANES] = shifts.astype(F32)
    columns = [const_ref[k] for k in range(emissions + 1)]
    masks = [const_ref[LINE_ROWS] == k for k in range(emissions)]
    scale = const_ref[SCALE] * (1.0 / cells)
    share = width // 2
    core = lax.axis_index("near") & 1
    for r in range(2):
        for j in range(share // LANES):
            start = pl.multiple_of((core ^ r) * share + j * LANES, LANES)
            span = slice(j * LANES, (j + 1) * LANES)
            totals = jnp.zeros((SUB, LANES), F32)
            for v in range(views):
                values = field_sum[v, :, pl.ds(start, LANES)]
                sums = [jnp.sum(column * values, axis=0, keepdims=True) for column in columns]
                for k in range(emissions + 1):
                    totals = jnp.where(rows == v * (emissions + 1) + k, sums[k], totals)
                line_total = select_line(masks, [jnp.broadcast_to(value, rows.shape) for value in sums[1:]])
                signal = scale * emit_sum[v, :, pl.ds(start, LANES)] * jnp.exp(-line_total)
                state_refs[r][(v + 1) * SUB : (v + 2) * SUB, span] = signal
            state_refs[r][0:SUB, span] = jnp.exp(-totals)
    for v in range(views):
        target_ref[v * SUB : (v + 1) * SUB, :] = measured_ref[v].reshape(SUB, width)


def forward(conc, index, weights, scalars, measured, cells):
    views, slab, width = weights.shape
    attenuation, line_energy, yields = scalars
    values = pltpu.VMEM((views, slab * SUB, width), F32)
    padded = pltpu.VMEM((slab, SUB, width + 3 * LANES), F32)
    state = pltpu.VMEM(((views + 1) * SUB, width // 2), F32)
    line = pltpu.VMEM((views, SUB, width), F32)
    operands = [in_hbm(value) for value in (attenuation, line_energy, yields, index, conc, weights, measured)]
    return pl.pallas_call(
        functools.partial(forward_kernel, cells),
        in_specs=[HBM] * len(operands),
        out_specs=[VMEM] * 10,
        out_shape=[
            values,
            values,
            pltpu.VMEM((LINE_LANES + 1, SUB, LANES), F32),
            pltpu.VMEM((views * SUB, width), F32),
            pltpu.VMEM(MATRIX, BF16),
            padded,
            padded,
            pltpu.VMEM((views, slab + SUB, width), F32),
            state,
            state,
        ],
        scratch_shapes=[
            pltpu.VMEM((SUB, slab, width), F32),
            pltpu.VMEM((views, ROWS, width), F32),
            line,
            line,
            line,
            pltpu.VMEM(measured.shape, F32),
            pltpu.VMEM((views, slab, LANES), jnp.int32),
            pltpu.SMEM(attenuation.shape, F32),
            pltpu.SMEM(line_energy.shape, jnp.int32),
            pltpu.SMEM(yields.shape, F32),
            pltpu.SMEM((views, slab, LANES), jnp.int32),
            pltpu.SemaphoreType.DMA((slab // BLOCK + 7,)),
        ],
        compiler_params=pltpu.CompilerParams(vmem_limit_bytes=16 * MIB),
        name="forward",
    )(*operands)


def column_in(package_any, views, index_ref, sem):
    first = package_any.shape[1] - SUB
    source = package_any.at[views, pl.ds(first, SUB), pl.ds(0, index_ref.shape[2])]
    return pltpu.make_async_copy(source, index_ref, sem)


def forward_other_kernel(view, weight_ref, mat, left_pad, diff_pad, order_ref, *refs):
    u_ref, n_ref, token_ref, field, carry, index_ref, sem = refs
    _, slab, width = weight_ref.shape
    slab = slab - SUB
    copy = column_in(weight_ref, pl.ds(view, 1), index_ref, sem)
    copy.start()
    carry[...] = jnp.zeros_like(carry)
    token_ref[...] = jnp.zeros_like(token_ref)
    copy.wait()
    for block in range(slab // BLOCK):
        shear(field, left_pad, diff_pad, index_ref, weight_ref.at[pl.ds(view, 1)], block, (0,), width // LANES)
        transmit(u_ref, n_ref, field, mat, carry, block, None)


def forward_other(view, weights, mat, left_pad, diff_pad, after):
    _, slab, width = weights.shape
    slab = slab - SUB
    values = pltpu.VMEM((1, slab * SUB, width), F32)
    return pl.pallas_call(
        functools.partial(forward_other_kernel, view),
        in_specs=[VMEM] * 5,
        out_specs=[VMEM] * 3,
        out_shape=[values, values, pltpu.VMEM((SUB, LANES), F32)],
        scratch_shapes=[
            pltpu.VMEM((1, ROWS, width), F32),
            pltpu.VMEM((1, SUB, width), F32),
            pltpu.SMEM((1, SUB, LANES), F32),
            pltpu.SemaphoreType.DMA,
        ],
        compiler_params=pltpu.CompilerParams(vmem_limit_bytes=8 * MIB),
        name="forward_other",
    )(weights, mat, left_pad, diff_pad, after)


def line_rows(tile, base, masks):
    shape = masks[0].shape
    return select_line(masks, [jnp.broadcast_to(tile[base + 1 + k : base + 2 + k], shape) for k in range(len(masks))])


def incident_rows(tile, step):
    rows = row_ids(tile.shape[1])
    result = jnp.broadcast_to(tile[0:1], tile.shape)
    for base in range(step, SUB, step):
        result = jnp.where(rows >= base, jnp.broadcast_to(tile[base : base + 1], tile.shape), result)
    return result


def row_masks(const_ref, width):
    tile = const_ref[LINE_ROWS]
    return [jnp.concatenate([tile] * (width // LANES), axis=1) == k for k in range(SCALE - 1)]


def factors_of(mine, theirs, bit):
    mine_factor = jnp.where(bit == 0, theirs, incident_rows(theirs, SCALE))
    return mine_factor, jnp.where(bit == 0, incident_rows(mine, SCALE), mine)


def merged_state(mine, theirs, bit, masks):
    mine_factor, theirs_factor = factors_of(mine[0:SUB], theirs[0:SUB], bit)
    result = [mine[0:SUB] * theirs[0:SUB]]
    for v in range(mine.shape[0] // SUB - 1):
        span = slice((v + 1) * SUB, (v + 2) * SUB)
        result.append(
            mine[span] * line_rows(mine_factor, v * SCALE, masks)
            + theirs[span] * line_rows(theirs_factor, v * SCALE, masks)
        )
    return result


def weighted_rows(factor, state, misfits, masks):
    rows = row_ids(state.shape[1])
    result = jnp.zeros((SUB, state.shape[1]), F32)
    for v, misfit in enumerate(misfits):
        base = v * SCALE
        value = misfit * state[(v + 1) * SUB : (v + 2) * SUB] * line_rows(factor, base, masks)
        whole = None
        for k, mask in enumerate(masks):
            part = jnp.sum(jnp.where(mask, value, 0.0), axis=0, keepdims=True)
            result = jnp.where(rows == base + 1 + k, part, result)
            whole = part if whole is None else whole + part
        result = jnp.where(rows == base, whole, result)
    return result


def children(factor, sums, mine, theirs, bit, misfits, masks):
    mine_factor, theirs_factor = factors_of(mine[0:SUB], theirs[0:SUB], bit)
    if factor is not None:
        mine_factor, theirs_factor = factor * mine_factor, factor * theirs_factor
    behind = (row_ids(mine.shape[1]) & (SCALE - 1)) == 0
    mine_sums = jnp.where(behind == (bit == 0), weighted_rows(theirs_factor, theirs, misfits, masks), 0.0)
    theirs_sums = jnp.where(behind == (bit == 1), weighted_rows(mine_factor, mine, misfits, masks), 0.0)
    if sums is not None:
        mine_sums, theirs_sums = sums + mine_sums, sums + theirs_sums
    return (mine_factor, mine_sums), (theirs_factor, theirs_sums)


def call_small(kernel, name, outs, operands, scratch=()):
    return pl.pallas_call(
        kernel,
        in_specs=[VMEM] * len(operands),
        out_specs=[VMEM] * len(outs),
        out_shape=[pltpu.VMEM(shape, F32) for shape in outs],
        scratch_shapes=[pltpu.VMEM(shape, F32) for shape in scratch],
        compiler_params=pltpu.CompilerParams(vmem_limit_bytes=4 * MIB),
        name=name,
    )(*operands)


def pass_on(value, after):
    return pl.pallas_call(
        lambda value_ref, after_ref, out_ref: None,
        in_specs=[VMEM, VMEM],
        out_specs=VMEM,
        out_shape=pltpu.VMEM(value.shape, F32),
        input_output_aliases={0: 0},
        compiler_params=pltpu.CompilerParams(vmem_limit_bytes=2 * MIB),
        cost_estimate=pl.CostEstimate(flops=0, bytes_accessed=8 * MIB, transcendentals=0),
        name="pass_on",
    )(value, after)


def store_rows(ref, tiles):
    for i, tile in enumerate(tiles):
        ref[i * SUB : (i + 1) * SUB, :] = tile


def merge_kernel(shift, const_ref, mine_ref, theirs_ref, *refs):
    bit = (depth_place() >> shift) & 1
    store_rows(refs[-1], merged_state(mine_ref[...], theirs_ref[...], bit, row_masks(const_ref, mine_ref.shape[1])))


def merge_four_kernel(const_ref, mine_ref, near_ref, far_ref, both_ref, pair_ref, other_ref, whole_ref):
    place = depth_place()
    masks = row_masks(const_ref, mine_ref.shape[1])
    pair = merged_state(mine_ref[...], near_ref[...], (place >> 1) & 1, masks)
    other = merged_state(far_ref[...], both_ref[...], (place >> 1) & 1, masks)
    store_rows(pair_ref, pair)
    store_rows(other_ref, other)
    store_rows(whole_ref, merged_state(pair_ref[...], other_ref[...], (place >> 2) & 1, masks))


def depth_place():
    return lax.axis_index("far") * NEAR + lax.axis_index("near")


def result_kernel(levels, const_ref, target_ref, *refs):
    states, outs = refs[: 2 * levels], refs[-4:]
    depth, width = states[0].shape
    views = depth // SUB - 1
    place = depth_place()
    size = 2 * LANES
    start = (place & 1) * width
    masks = row_masks(const_ref, size)
    behind = (row_ids(size) & (SCALE - 1)) == 0
    for c in range(width // size):
        span = slice(c * size, (c + 1) * size)
        factor, sums = None, None
        for level in reversed(range(levels)):
            mine, theirs = states[2 * level][:, span], states[2 * level + 1][:, span]
            bit = (place >> level) & 1
            if level == levels - 1:
                signals = merged_state(mine, theirs, bit, masks)[1:]
                there = pl.ds(pl.multiple_of(start + c * size, LANES), size)
                misfits = [signals[v] - target_ref[v * SUB : (v + 1) * SUB, there] for v in range(views)]
            contexts = children(factor, sums, mine, theirs, bit, misfits, masks)
            factor, sums = contexts[0]
        for i, (state, (factor, sums)) in enumerate(zip((mine, theirs), contexts)):
            own = jnp.where(behind, weighted_rows(factor, state, misfits, masks), 0.0)
            rest = [factor * state[0:SUB], sums + own]
            for ref, first in ((outs[i], signals), (outs[2 + i], misfits)):
                for j, tile in enumerate(first + rest):
                    ref[j * SUB : (j + 1) * SUB, span] = tile


def assemble_kernel(target_ref, here_ref, there_ref, package_ref, signal_ref):
    half = here_ref.shape[1]
    count = signal_ref.shape[0]
    at = pl.multiple_of((lax.axis_index("near") & 1) * half, LANES)
    for ref, start in ((here_ref, at), (there_ref, pl.multiple_of(half - at, LANES))):
        span = pl.ds(start, half)
        signal_ref[:, span] = ref[0:count, :]
        package_ref[0:count, span] = ref[0:count, :] - target_ref[:, span]
        package_ref[count:, span] = ref[count:, :]


def assemble_other_kernel(here_ref, there_ref, package_ref):
    half = here_ref.shape[1]
    at = pl.multiple_of((lax.axis_index("near") & 1) * half, LANES)
    package_ref[:, pl.ds(at, half)] = here_ref[...]
    package_ref[:, pl.ds(pl.multiple_of(half - at, LANES), half)] = there_ref[...]


def backward_kernel(places, cells, finish, const_ref, package_ref, weight_ref, *refs):
    count = len(places)
    u_refs, n_refs, refs = refs[:count], refs[count : 2 * count], refs[2 * count :]
    if finish:
        signal_ref, refs = refs[0], refs[1:]
        prior, refs = refs[: finish - 1], refs[finish - 1 :]
        grad_hbm, signal_hbm, cell_ref, grad_ref, signal_rows = refs[:5]
        refs = refs[5:]
    else:
        left_sum, diff_sum, refs = refs[0], refs[1], refs[2:]
    mat, gain, carry, scaled, left_pad, diff_pad, index_ref, sems = refs
    _, slab, width = weight_ref.shape
    slab = slab - SUB
    emissions = SCALE - 1
    tiles = width // LANES
    blocks = slab // BLOCK
    lanes, rows = lane_ids(), row_ids()
    column = column_in(weight_ref, pl.ds(0, count), index_ref, sems.at[blocks])
    column.start()
    if finish:
        for v in range(signal_rows.shape[0]):
            signal_rows[v] = signal_ref[v * SUB : (v + 1) * SUB, :].reshape(SUB, 1, width)
        signal_copy = pltpu.make_async_copy(signal_rows, signal_hbm, sems.at[blocks + 1])
        signal_copy.start()
        out_copies = [
            pltpu.make_async_copy(grad_ref.at[b], grad_hbm.at[:, pl.ds(b * BLOCK, BLOCK), :], sems.at[b])
            for b in range(blocks)
        ]
    masks = [const_ref[LINE_LANES] == k for k in range(emissions)]
    columns = [const_ref[k] for k in range(emissions + 1)]
    fill_matrix(mat, -columns[0], select_line(masks, columns[1:]), True, False)
    masks = [const_ref[LINE_ROWS] == k for k in range(emissions)]
    scale = const_ref[SCALE]
    columns = [column * cells for column in columns]
    for j in range(tiles):
        span = slice(j * LANES, (j + 1) * LANES)
        factor = package_ref[count * SUB : (count + 1) * SUB, span]
        sums = package_ref[(count + 1) * SUB : (count + 2) * SUB, span]
        for v in range(count):
            base = v * SCALE
            gain[v, :, span] = package_ref[v * SUB : (v + 1) * SUB, span] * scale * line_rows(factor, base, masks)
            back = columns[0] * jnp.broadcast_to(sums[base : base + 1], rows.shape)
            for k in range(1, emissions + 1):
                back = back + columns[k] * jnp.broadcast_to(sums[base + k : base + k + 1], rows.shape)
            carry[v, :, span] = back
    zero = jnp.zeros((SUB, LANES), F32)
    for ref in (left_pad, diff_pad):
        edge = jnp.zeros(ref.shape[:3] + (LANES,), F32)
        ref[:, :, :, 0:LANES] = edge
        ref[:, :, :, width + 2 * LANES :] = edge
    column.wait()

    def place(v, d, cell, first):
        _, rest = shift_of(index_ref, v, cell, width)
        stay = lanes >= rest
        turn = rest & (LANES - 1)
        at = (first + d) * SUB
        plain = [scaled[v, at : at + SUB, j * LANES : (j + 1) * LANES] for j in range(tiles)]
        moved = [plain[j] * weight_ref[v, cell : cell + 1, j * LANES : (j + 1) * LANES] for j in range(tiles)]
        for ref, values in ((left_pad, plain), (diff_pad, moved)):
            turned = [zero] + [pltpu.roll(value, turn, 1) for value in values] + [zero]
            for j in range(tiles + 1):
                ref[v, first + d, :, (j + 1) * LANES : (j + 2) * LANES] = jnp.where(stay, turned[j + 1], turned[j])

    def gathered(ref, before, cell, slot):
        sums = [None] * (tiles + 2)
        if before is not None:
            sums = [before[cell, :, j * LANES : (j + 1) * LANES] for j in range(tiles + 2)]
        for v in range(count):
            whole, _ = shift_of(index_ref, v, cell, width)
            for j in range(tiles + 2):
                start = pl.multiple_of((1 + j - whole) * LANES, LANES)
                value = ref[v, slot, :, pl.ds(start, LANES)]
                sums[j] = value if sums[j] is None else sums[j] + value
        return sums

    def folded(sums):
        low = jnp.sum(sums[0], axis=1, keepdims=True)
        beyond = sums[tiles + 1] + jnp.where(lanes == LANES - 1, sums[tiles], 0.0)
        high = jnp.sum(beyond, axis=1, keepdims=True)
        core = sums[1 : tiles + 1]
        core[0] = core[0] + jnp.where(lanes == 0, low, 0.0)
        core[-1] = jnp.where(lanes == LANES - 1, 0.0, core[-1] + jnp.where(lanes == LANES - 2, high, 0.0))
        return core

    for block in range(blocks):
        first = block % 2 * BLOCK
        for v in range(count):
            for c in range(width // CHUNK):
                span = slice(c * CHUNK, (c + 1) * CHUNK)
                factor = gain[v, :, span][None]
                weighted = n_refs[v][places[v], block_rows(block), span].reshape(BLOCK, SUB, CHUNK) * factor
                direct = u_refs[v][places[v], block_rows(block), span].reshape(BLOCK, SUB, CHUNK) * factor
                lines, total = multiply(mat, weighted.reshape(ROWS, CHUNK))
                before = carry[v, :, span]
                lines = lines.reshape(BLOCK, SUB, CHUNK) + before[None]
                scaled[v, first * SUB : first * SUB + ROWS, span] = (direct - lines).reshape(ROWS, CHUNK)
                carry[v, :, span] = before + total
        for v in range(count):
            for d in range(BLOCK):
                place(v, d, block * BLOCK + d, first)
        for d in range(BLOCK):
            cell = block * BLOCK + d
            left = gathered(left_pad, prior[0] if finish > 1 else None, cell, first + d)
            diff = gathered(diff_pad, prior[1] if finish > 1 else None, cell, first + d)
            if not finish:
                for j in range(tiles + 2):
                    left_sum[cell, :, j * LANES : (j + 1) * LANES] = left[j]
                    diff_sum[cell, :, j * LANES : (j + 1) * LANES] = diff[j]
                continue
            left, diff = folded([left[j] - diff[j] for j in range(tiles + 2)]), folded(diff)
            turned = [zero] + [pltpu.roll(value, 1, 1) for value in diff]
            for j in range(tiles):
                value = left[j] + jnp.where(lanes == 0, turned[j], turned[j + 1])
                cell_ref[first + d, :, j * LANES : (j + 1) * LANES] = value
        if finish:
            grad_ref[block] = jnp.swapaxes(cell_ref[first : first + BLOCK], 0, 1)
            out_copies[block].start()
    if finish:
        for copy in out_copies + [signal_copy]:
            copy.wait()


def backward(package, const, weights, pieces, cells, signal, prior):
    views, slab, width = weights.shape
    slab = slab - SUB
    blocks = slab // BLOCK
    finish = signal is not None
    line = pltpu.VMEM((views, SUB, width), F32)
    sums = pltpu.VMEM((slab, SUB, width + 2 * LANES), F32)
    scratch = [
        pltpu.VMEM(MATRIX, BF16),
        line,
        line,
        pltpu.VMEM((views, 2 * ROWS, width), F32),
        pltpu.VMEM((views, 2 * BLOCK, SUB, width + 3 * LANES), F32),
        pltpu.VMEM((views, 2 * BLOCK, SUB, width + 3 * LANES), F32),
        pltpu.SMEM((views, SUB, LANES), F32),
        pltpu.SemaphoreType.DMA((blocks + 2,)),
    ]
    operands = [const, package, weights, *[u for u, _, _ in pieces], *[n for _, n, _ in pieces]]
    if finish:
        operands += [signal[0], *prior]
        scratch = [
            pltpu.VMEM((2 * BLOCK, SUB, width), F32),
            pltpu.VMEM((blocks, SUB, BLOCK, width), F32),
            pltpu.VMEM(signal[1], F32),
        ] + scratch
    return pl.pallas_call(
        functools.partial(
            backward_kernel, tuple(at for _, _, at in pieces), cells, 1 + len(prior) if finish else 0
        ),
        in_specs=[VMEM] * len(operands),
        out_specs=[HBM, HBM] if finish else [VMEM, VMEM],
        out_shape=[pltpu.HBM((SUB, slab, width), F32), pltpu.HBM(signal[1], F32)] if finish else [sums, sums],
        scratch_shapes=scratch,
        compiler_params=pltpu.CompilerParams(vmem_limit_bytes=16 * MIB),
        name="backward_last" if finish else "backward_first",
    )(*operands)


def body(concentration, shear_index, shear_weight, attenuation, yields, line_energy, measured):
    elements, _, slab, width = concentration.shape
    views = shear_weight.shape[0]
    emissions = attenuation.shape[0] - 1
    groups = lax.axis_size("far")
    both = lax.axis_size("views") == 2
    cells = float(slab * groups * NEAR)
    conc = concentration.reshape(elements, slab, width)
    scalars = (attenuation, line_energy, yields)

    def to_other(value):
        return lax.ppermute(value, "views", [(0, 1), (1, 0)])

    fillers = []

    def fill(after):
        if not both or len(fillers) == views:
            return ()
        fillers.append(forward_other(len(fillers), other_weight, mat, left_pad, diff_pad, after))
        return (fillers[-1][2],)

    u, n, const, target, mat, left_pad, diff_pad, weight, state, send = forward(
        conc, shear_index, shear_weight, scalars, measured, cells
    )
    def swap(value, axis, step):
        return lax.ppermute(value, axis, [(s, s ^ step) for s in range(lax.axis_size(axis))])

    states = [state, swap(send, "near", 1)]
    if both:
        weight = pass_on(weight, state)
        other_weight = to_other(weight)
    tokens = ()
    levels = groups.bit_length() + 1

    def merge(level):
        (merged,) = call_small(
            functools.partial(merge_kernel, level), "merge", [state.shape], (const, *states[-2:])
        )
        return merged

    state = merge(0)
    pairs = [(s, s ^ 6) for s in range(groups * NEAR)]
    four = (state, swap(state, "near", 2), swap(state, "far", 1), lax.ppermute(state, ("far", "near"), pairs))
    pair, other, whole = call_small(merge_four_kernel, "merge_four", [state.shape] * 3, (const, *four))
    states += [*four[:2], pair, other]
    state = whole
    for level in range(3, levels):
        states += [state, swap(state, "far", 1 << (level - 2))]
        if level < levels - 1:
            state = merge(level)
    for _ in range(views):
        tokens += fill(state)
    half = ((views + 2) * SUB, width // 2)
    here, there, here_other, there_other = call_small(
        functools.partial(result_kernel, levels), "result", [half] * 4, (const, target, *states, *tokens)
    )
    there = swap(there, "near", 1)
    if both:
        pairs = [(v * NEAR + s, (1 - v) * NEAR + (s ^ 1)) for v in range(2) for s in range(NEAR)]
        here_other = to_other(here_other)
        there_other = lax.ppermute(there_other, ("views", "near"), pairs)
    package = (half[0], width)
    shapes = [package, target.shape]
    package, signal = call_small(assemble_kernel, "assemble", shapes, (target, here, there))
    own = [(u, n, v) for v in range(views)]
    signal = (signal, measured.shape)
    if both:
        sums = backward(package, const, weight, own, cells, None, ())
        (other_package,) = call_small(
            assemble_other_kernel, "assemble_other", [package.shape], (here_other, there_other)
        )
        pieces = [(fillers[v][0], fillers[v][1], 0) for v in range(views)]
        gradient, signal = backward(other_package, const, other_weight, pieces, cells, signal, sums)
    else:
        gradient, signal = backward(package, const, weight, own, cells, signal, ())
        gradient = lax.psum(gradient, "views")
    return gradient.reshape(concentration.shape), signal


def solution(mesh):
    views, depth = mesh.shape["views"], mesh.shape["depth"]
    devices = mesh.devices.reshape(views, depth // NEAR, NEAR)
    split = jax.sharding.Mesh(devices, ("views", "far", "near"))
    depths = ("far", "near")
    return jax.shard_map(
        body,
        mesh=split,
        in_specs=(
            P(None, None, depths, None),
            P("views", depths, None),
            P("views", depths, None),
            P(),
            P(),
            P(),
            P("views", None, None, None),
        ),
        out_specs=(P(None, None, depths, None), P("views", None, None, None)),
        check_vma=False,
    )
```

```python
import functools

import jax
import jax.numpy as jnp
from jax import lax
from jax.experimental import pallas as pl
from jax.experimental.pallas import tpu as pltpu
from jax.sharding import PartitionSpec as P

LANES = 128
SUB = 8
BLOCK = 8
ROWS = BLOCK * SUB
NEAR = 4
CHUNK = 256
MIB = 1024 * 1024
F32 = jnp.float32
BF16 = jnp.bfloat16
HBM = pl.BlockSpec(memory_space=pltpu.HBM)
VMEM = pl.BlockSpec(memory_space=pltpu.VMEM)
SCALE, LINE_ROWS, LINE_LANES = 4, 5, 6
ANY = pl.BlockSpec(memory_space=pl.ANY)


def in_hbm(value):
    return pltpu.with_memory_space_constraint(value, pltpu.HBM)


def lane_ids(width=LANES):
    return lax.broadcasted_iota(jnp.int32, (SUB, width), 1)


def row_ids(width=LANES):
    return lax.broadcasted_iota(jnp.int32, (SUB, width), 0)


def tile_of(values, ids):
    tile = jnp.zeros(ids.shape, F32)
    for e in range(SUB):
        tile = jnp.where(ids == e, values[e], tile)
    return tile


def select_line(masks, values):
    result = values[0]
    for mask, value in zip(masks[1:], values[1:]):
        result = jnp.where(mask, value, result)
    return result


def fill_matrix(mat_ref, first_tile, second_tile, first_incl, second_incl):
    depth = (lane_ids() & (ROWS - 1)) >> 3
    tiles = []
    for d in range(BLOCK):
        one = jnp.where(depth <= d if first_incl else depth < d, first_tile, 0.0)
        two = jnp.where(depth <= d if second_incl else depth < d, second_tile, 0.0)
        tiles.append(one + two)
    tiles.append(first_tile + second_tile)
    tiles.append(jnp.zeros((SUB, LANES), F32))
    whole = jnp.concatenate(tiles, axis=0)
    high = whole.astype(BF16)
    mat_ref[:, 0:LANES] = high
    mat_ref[:, LANES : 2 * LANES] = (whole - high.astype(F32)).astype(BF16)


def multiply(mat_ref, values):
    high = values.astype(BF16)
    low = (values - high.astype(F32)).astype(BF16)
    stacked = jnp.concatenate([high, low, high], axis=0)
    product = jnp.dot(mat_ref[:, 0 : 3 * ROWS], stacked, preferred_element_type=F32)
    return product[0:ROWS], product[ROWS : ROWS + SUB]


MATRIX = (ROWS + 2 * SUB, 2 * LANES)


def copies_in(pairs, sems):
    return [pltpu.make_async_copy(source, target, sems.at[i]) for i, (source, target) in enumerate(pairs)]


def block_rows(block):
    return slice(block * ROWS, (block + 1) * ROWS)


def block_cells(block):
    return slice(block * BLOCK, (block + 1) * BLOCK)


def offset_of(index_ref, v, cell, width):
    if index_ref.dtype == jnp.int32:
        at = index_ref[v, cell, 0]
    else:
        at = index_ref[v, cell % SUB, cell // SUB].astype(jnp.int32)
    return at - (width // 2 - LANES)


def shift_of(index_ref, v, cell, width):
    offset = offset_of(index_ref, v, cell, width)
    whole = jnp.minimum(offset >> 7, 1)
    return whole, offset - (whole << 7)


def pad_cells(pad_ref, cell, pieces):
    tiles = len(pieces)

    def spread(piece, lane):
        return jnp.broadcast_to(piece[:, lane : lane + 1], (SUB, LANES))

    last = spread(pieces[-1], LANES - 1)
    edges = [spread(pieces[0], 1), spread(pieces[-1], LANES - 2)]
    for j, piece in enumerate([spread(pieces[0], 0)] + pieces + [last, last] + edges):
        pad_ref[cell, :, j * LANES : (j + 1) * LANES] = piece


def shear(field, pad_ref, index_ref, weight_ref, block, views, tiles):
    lanes = lane_ids()
    for i, v in enumerate(views):
        for d in range(BLOCK):
            cell = block * BLOCK + d
            offset = offset_of(index_ref, v, cell, tiles * LANES)
            whole, rest = offset >> 7, offset & (LANES - 1)
            starts = [pl.multiple_of((whole + j) * LANES, LANES) for j in range(tiles + 1)]
            values = [pad_ref[cell, :, pl.ds(start, LANES)] for start in starts]

            def turned(rest):
                stay = lanes < LANES - rest
                turn = (LANES - rest) & (LANES - 1)
                rolled = [pltpu.roll(value, turn, 1) for value in values]
                return [jnp.where(stay, rolled[j], rolled[j + 1]) for j in range(tiles)]

            left, right = turned(rest), turned(rest + 1)
            second, last_but_one = [
                pad_ref[cell, :, (tiles + 3 + j) * LANES : (tiles + 4 + j) * LANES] for j in range(2)
            ]
            right[0] = jnp.where(lanes < LANES - offset, second, right[0])
            for j in (tiles - 2, tiles - 1):
                first = (tiles + 1 - j) * LANES - 1 - offset
                left[j] = jnp.where(lanes >= first, last_but_one, left[j])
            for j in range(tiles):
                span = slice(j * LANES, (j + 1) * LANES)
                weight = weight_ref[i, cell : cell + 1, span]
                field[i, d * SUB : (d + 1) * SUB, span] = left[j] + weight * (right[j] - left[j])


def transmit(u_ref, n_ref, field, mat, carry, block, sums):
    views, _, width = field.shape
    for v in range(views):
        for c in range(width // CHUNK):
            span = slice(c * CHUNK, (c + 1) * CHUNK)
            value = field[v, :, span]
            lines, total = multiply(mat, value)
            before = carry[v, :, span]
            through = jnp.exp(lines.reshape(BLOCK, SUB, CHUNK) + before[None])
            value = value.reshape(BLOCK, SUB, CHUNK)
            emit = value * through
            u_ref[v, block_rows(block), span] = through.reshape(ROWS, CHUNK)
            n_ref[v, block_rows(block), span] = emit.reshape(ROWS, CHUNK)
            carry[v, :, span] = before + total
            if sums:
                sums[0][v, :, span] += jnp.sum(value, axis=0)
                sums[1][v, :, span] += jnp.sum(emit, axis=0)


def forward_kernel(cells, *refs):
    att_hbm, line_hbm, yield_hbm, index_hbm, conc_hbm, weight_hbm, measured_hbm = refs[:7]
    u_ref, n_ref, const_ref, target_ref, mat, pad_ref, weight_ref = refs[7:14]
    state_refs = refs[14:16]
    refs = refs[16:]
    conc_ref, field, carry, field_sum, emit_sum, measured_ref, column_ref = refs[:7]
    att_ref, line_ref, yield_ref, index_ref, sems = refs[7:]
    views, _, width = weight_ref.shape
    slab = conc_ref.shape[1]
    emissions = att_ref.shape[0] - 1
    tiles = width // LANES
    blocks = slab // BLOCK
    lanes, rows = lane_ids(), row_ids()
    conc_copies = [
        pltpu.make_async_copy(
            conc_hbm.at[:, pl.ds(b * BLOCK, BLOCK), :], conc_ref.at[:, pl.ds(b * BLOCK, BLOCK), :], sems.at[b]
        )
        for b in range(blocks)
    ]
    pairs = [
        (att_hbm, att_ref),
        (line_hbm, line_ref),
        (yield_hbm, yield_ref),
        (weight_hbm, weight_ref.at[:, pl.ds(0, slab), :]),
        (measured_hbm, measured_ref),
        (index_hbm.at[:, :, pl.ds(width // 2, LANES)], column_ref),
    ]
    copies = copies_in(pairs, sems.at[pl.ds(2 * blocks, len(pairs))])
    index_copies = [
        pltpu.make_async_copy(
            index_hbm.at[:, pl.ds(b * BLOCK, BLOCK), pl.ds(width // 2, LANES)],
            index_ref.at[:, pl.ds(b * BLOCK, BLOCK), :],
            sems.at[blocks + b],
        )
        for b in range(blocks)
    ]
    for copy in conc_copies[:1] + copies[:3] + index_copies[:1] + copies[3:4]:
        copy.start()
    for copy in conc_copies[1:] + index_copies[1:] + copies[4:]:
        copy.start()
    for ref in (carry, field_sum, emit_sum):
        ref[...] = jnp.zeros_like(ref)

    def pad(block):
        conc_copies[block].wait()
        by_depth = jnp.swapaxes(conc_ref[:, block_cells(block), :], 0, 1)
        for d in range(BLOCK):
            pieces = [by_depth[d, :, j * LANES : (j + 1) * LANES] for j in range(tiles)]
            pad_cells(pad_ref, block * BLOCK + d, pieces)

    pad(0)
    for copy in copies[:3]:
        copy.wait()
    line_by_row = tile_of([line_ref[e].astype(F32) for e in range(SUB)], rows)
    masks = [line_by_row == k for k in range(emissions)]
    by_lane = [tile_of([att_ref[k, e] for e in range(SUB)], lanes & 7) for k in range(emissions + 1)]
    fill_matrix(mat, -by_lane[0], select_line(masks, by_lane[1:]), False, True)
    for k in range(emissions + 1):
        const_ref[k] = tile_of([att_ref[k, e] for e in range(SUB)], rows)
    const_ref[SCALE] = tile_of([yield_ref[e] for e in range(SUB)], rows)
    const_ref[LINE_ROWS] = line_by_row
    const_ref[LINE_LANES] = tile_of([line_ref[e].astype(F32) for e in range(SUB)], lanes & 7)
    copies[3].wait()
    for block in range(blocks):
        if block:
            pad(block)
        index_copies[block].wait()
        shear(field, pad_ref, index_ref, weight_ref, block, range(views), tiles)
        transmit(u_ref, n_ref, field, mat, carry, block, (field_sum, emit_sum))
    for copy in copies[4:]:
        copy.wait()
    for v in range(views):
        shifts = jnp.zeros((SUB, LANES), jnp.int32)
        for octet in range(slab // SUB):
            values = column_ref[v, octet * SUB : (octet + 1) * SUB, :] - lanes
            shifts = jnp.where(lanes == octet, values, shifts)
        weight_ref[v, slab : slab + SUB, 0:LANES] = shifts.astype(F32)
    columns = [const_ref[k] for k in range(emissions + 1)]
    masks = [const_ref[LINE_ROWS] == k for k in range(emissions)]
    scale = const_ref[SCALE] * (1.0 / cells)
    share = width // 2
    core = lax.axis_index("near") & 1
    for r in range(2):
        for j in range(share // LANES):
            start = pl.multiple_of((core ^ r) * share + j * LANES, LANES)
            span = slice(j * LANES, (j + 1) * LANES)
            totals = jnp.zeros((SUB, LANES), F32)
            for v in range(views):
                values = field_sum[v, :, pl.ds(start, LANES)]
                sums = [jnp.sum(column * values, axis=0, keepdims=True) for column in columns]
                for k in range(emissions + 1):
                    totals = jnp.where(rows == v * (emissions + 1) + k, sums[k], totals)
                line_total = select_line(masks, [jnp.broadcast_to(value, rows.shape) for value in sums[1:]])
                signal = scale * emit_sum[v, :, pl.ds(start, LANES)] * jnp.exp(-line_total)
                state_refs[r][(v + 1) * SUB : (v + 2) * SUB, span] = signal
            state_refs[r][0:SUB, span] = jnp.exp(-totals)
    for v in range(views):
        target_ref[v * SUB : (v + 1) * SUB, :] = measured_ref[v].reshape(SUB, width)


def forward(conc, index, weights, scalars, measured, cells):
    views, slab, width = weights.shape
    attenuation, line_energy, yields = scalars
    values = pltpu.VMEM((views, slab * SUB, width), F32)
    padded = pltpu.VMEM((slab, SUB, width + 5 * LANES), F32)
    state = pltpu.VMEM(((views + 1) * SUB, width // 2), F32)
    line = pltpu.VMEM((views, SUB, width), F32)
    operands = [in_hbm(value) for value in (attenuation, line_energy, yields, index, conc, weights, measured)]
    return pl.pallas_call(
        functools.partial(forward_kernel, cells),
        in_specs=[HBM] * len(operands),
        out_specs=[VMEM] * 9,
        out_shape=[
            values,
            values,
            pltpu.VMEM((LINE_LANES + 1, SUB, LANES), F32),
            pltpu.VMEM((views * SUB, width), F32),
            pltpu.VMEM(MATRIX, BF16),
            padded,
            pltpu.VMEM((views, slab + SUB, width), F32),
            state,
            state,
        ],
        scratch_shapes=[
            pltpu.VMEM((SUB, slab, width), F32),
            pltpu.VMEM((views, ROWS, width), F32),
            line,
            line,
            line,
            pltpu.VMEM(measured.shape, F32),
            pltpu.VMEM((views, slab, LANES), jnp.int32),
            pltpu.SMEM(attenuation.shape, F32),
            pltpu.SMEM(line_energy.shape, jnp.int32),
            pltpu.SMEM(yields.shape, F32),
            pltpu.SMEM((views, slab, LANES), jnp.int32),
            pltpu.SemaphoreType.DMA((2 * (slab // BLOCK) + 6,)),
        ],
        compiler_params=pltpu.CompilerParams(vmem_limit_bytes=16 * MIB),
        name="forward",
    )(*operands)


def column_in(package_any, views, index_ref, sem):
    first = package_any.shape[1] - SUB
    source = package_any.at[views, pl.ds(first, SUB), pl.ds(0, index_ref.shape[2])]
    return pltpu.make_async_copy(source, index_ref, sem)


def forward_other_kernel(view, weight_ref, mat, pad_ref, order_ref, *refs):
    u_ref, n_ref, token_ref, field, carry, index_ref, sem = refs
    _, slab, width = weight_ref.shape
    slab = slab - SUB
    copy = column_in(weight_ref, pl.ds(view, 1), index_ref, sem)
    copy.start()
    carry[...] = jnp.zeros_like(carry)
    token_ref[...] = jnp.zeros_like(token_ref)
    copy.wait()
    for block in range(slab // BLOCK):
        shear(field, pad_ref, index_ref, weight_ref.at[pl.ds(view, 1)], block, (0,), width // LANES)
        transmit(u_ref, n_ref, field, mat, carry, block, None)


def forward_other(view, weights, mat, pads, after):
    _, slab, width = weights.shape
    slab = slab - SUB
    values = pltpu.VMEM((1, slab * SUB, width), F32)
    return pl.pallas_call(
        functools.partial(forward_other_kernel, view),
        in_specs=[VMEM] * 4,
        out_specs=[VMEM] * 3,
        out_shape=[values, values, pltpu.VMEM((SUB, LANES), F32)],
        scratch_shapes=[
            pltpu.VMEM((1, ROWS, width), F32),
            pltpu.VMEM((1, SUB, width), F32),
            pltpu.SMEM((1, SUB, LANES), F32),
            pltpu.SemaphoreType.DMA,
        ],
        compiler_params=pltpu.CompilerParams(vmem_limit_bytes=8 * MIB),
        name="forward_other",
    )(weights, mat, pads, after)


def line_rows(tile, base, masks):
    shape = masks[0].shape
    return select_line(masks, [jnp.broadcast_to(tile[base + 1 + k : base + 2 + k], shape) for k in range(len(masks))])


def incident_rows(tile, step):
    rows = row_ids(tile.shape[1])
    result = jnp.broadcast_to(tile[0:1], tile.shape)
    for base in range(step, SUB, step):
        result = jnp.where(rows >= base, jnp.broadcast_to(tile[base : base + 1], tile.shape), result)
    return result


def row_masks(const_ref, width):
    tile = const_ref[LINE_ROWS]
    return [jnp.concatenate([tile] * (width // LANES), axis=1) == k for k in range(SCALE - 1)]


def factors_of(mine, theirs, bit):
    mine_factor = jnp.where(bit == 0, theirs, incident_rows(theirs, SCALE))
    return mine_factor, jnp.where(bit == 0, incident_rows(mine, SCALE), mine)


def merged_state(mine, theirs, bit, masks):
    mine_factor, theirs_factor = factors_of(mine[0:SUB], theirs[0:SUB], bit)
    result = [mine[0:SUB] * theirs[0:SUB]]
    for v in range(mine.shape[0] // SUB - 1):
        span = slice((v + 1) * SUB, (v + 2) * SUB)
        result.append(
            mine[span] * line_rows(mine_factor, v * SCALE, masks)
            + theirs[span] * line_rows(theirs_factor, v * SCALE, masks)
        )
    return result


def weighted_rows(factor, state, misfits, masks):
    rows = row_ids(state.shape[1])
    result = jnp.zeros((SUB, state.shape[1]), F32)
    for v, misfit in enumerate(misfits):
        base = v * SCALE
        value = misfit * state[(v + 1) * SUB : (v + 2) * SUB] * line_rows(factor, base, masks)
        whole = None
        for k, mask in enumerate(masks):
            part = jnp.sum(jnp.where(mask, value, 0.0), axis=0, keepdims=True)
            result = jnp.where(rows == base + 1 + k, part, result)
            whole = part if whole is None else whole + part
        result = jnp.where(rows == base, whole, result)
    return result


def children(factor, sums, mine, theirs, bit, misfits, masks):
    mine_factor, theirs_factor = factors_of(mine[0:SUB], theirs[0:SUB], bit)
    if factor is not None:
        mine_factor, theirs_factor = factor * mine_factor, factor * theirs_factor
    behind = (row_ids(mine.shape[1]) & (SCALE - 1)) == 0
    mine_sums = jnp.where(behind == (bit == 0), weighted_rows(theirs_factor, theirs, misfits, masks), 0.0)
    theirs_sums = jnp.where(behind == (bit == 1), weighted_rows(mine_factor, mine, misfits, masks), 0.0)
    if sums is not None:
        mine_sums, theirs_sums = sums + mine_sums, sums + theirs_sums
    return (mine_factor, mine_sums), (theirs_factor, theirs_sums)


def call_small(kernel, name, outs, operands, scratch=()):
    return pl.pallas_call(
        kernel,
        in_specs=[VMEM] * len(operands),
        out_specs=[VMEM] * len(outs),
        out_shape=[pltpu.VMEM(shape, F32) for shape in outs],
        scratch_shapes=[pltpu.VMEM(shape, F32) for shape in scratch],
        compiler_params=pltpu.CompilerParams(vmem_limit_bytes=4 * MIB),
        name=name,
    )(*operands)


def pass_on(value, after):
    return pl.pallas_call(
        lambda value_ref, after_ref, out_ref: None,
        in_specs=[VMEM, VMEM],
        out_specs=VMEM,
        out_shape=pltpu.VMEM(value.shape, F32),
        input_output_aliases={0: 0},
        compiler_params=pltpu.CompilerParams(vmem_limit_bytes=2 * MIB),
        cost_estimate=pl.CostEstimate(flops=0, bytes_accessed=8 * MIB, transcendentals=0),
        name="pass_on",
    )(value, after)


def store_rows(ref, tiles):
    for i, tile in enumerate(tiles):
        ref[i * SUB : (i + 1) * SUB, :] = tile


def merge_kernel(shift, const_ref, mine_ref, theirs_ref, *refs):
    bit = (depth_place() >> shift) & 1
    store_rows(refs[-1], merged_state(mine_ref[...], theirs_ref[...], bit, row_masks(const_ref, mine_ref.shape[1])))


def merge_four_kernel(const_ref, mine_ref, near_ref, far_ref, both_ref, pair_ref, other_ref, whole_ref):
    place = depth_place()
    masks = row_masks(const_ref, mine_ref.shape[1])
    pair = merged_state(mine_ref[...], near_ref[...], (place >> 1) & 1, masks)
    other = merged_state(far_ref[...], both_ref[...], (place >> 1) & 1, masks)
    store_rows(pair_ref, pair)
    store_rows(other_ref, other)
    store_rows(whole_ref, merged_state(pair_ref[...], other_ref[...], (place >> 2) & 1, masks))


def depth_place():
    return lax.axis_index("far") * NEAR + lax.axis_index("near")


def result_kernel(levels, const_ref, target_ref, *refs):
    states, outs = refs[: 2 * levels], refs[-4:]
    depth, width = states[0].shape
    views = depth // SUB - 1
    place = depth_place()
    size = 2 * LANES
    start = (place & 1) * width
    masks = row_masks(const_ref, size)
    behind = (row_ids(size) & (SCALE - 1)) == 0
    for c in range(width // size):
        span = slice(c * size, (c + 1) * size)
        factor, sums = None, None
        for level in reversed(range(levels)):
            mine, theirs = states[2 * level][:, span], states[2 * level + 1][:, span]
            bit = (place >> level) & 1
            if level == levels - 1:
                signals = merged_state(mine, theirs, bit, masks)[1:]
                there = pl.ds(pl.multiple_of(start + c * size, LANES), size)
                misfits = [signals[v] - target_ref[v * SUB : (v + 1) * SUB, there] for v in range(views)]
            contexts = children(factor, sums, mine, theirs, bit, misfits, masks)
            factor, sums = contexts[0]
        for i, (state, (factor, sums)) in enumerate(zip((mine, theirs), contexts)):
            own = jnp.where(behind, weighted_rows(factor, state, misfits, masks), 0.0)
            rest = [factor * state[0:SUB], sums + own]
            for ref, first in ((outs[i], signals), (outs[2 + i], misfits)):
                for j, tile in enumerate(first + rest):
                    ref[j * SUB : (j + 1) * SUB, span] = tile


def assemble_kernel(target_ref, here_ref, there_ref, package_ref, signal_ref):
    half = here_ref.shape[1]
    count = signal_ref.shape[0]
    at = pl.multiple_of((lax.axis_index("near") & 1) * half, LANES)
    for ref, start in ((here_ref, at), (there_ref, pl.multiple_of(half - at, LANES))):
        span = pl.ds(start, half)
        signal_ref[:, span] = ref[0:count, :]
        package_ref[0:count, span] = ref[0:count, :] - target_ref[:, span]
        package_ref[count:, span] = ref[count:, :]


def assemble_other_kernel(here_ref, there_ref, package_ref):
    half = here_ref.shape[1]
    at = pl.multiple_of((lax.axis_index("near") & 1) * half, LANES)
    package_ref[:, pl.ds(at, half)] = here_ref[...]
    package_ref[:, pl.ds(pl.multiple_of(half - at, LANES), half)] = there_ref[...]


def backward_kernel(places, cells, finish, const_ref, package_ref, weight_ref, *refs):
    count = len(places)
    u_refs, n_refs, refs = refs[:count], refs[count : 2 * count], refs[2 * count :]
    if finish:
        signal_ref, refs = refs[0], refs[1:]
        prior, refs = refs[: finish - 1], refs[finish - 1 :]
        grad_hbm, signal_hbm, cell_ref, grad_ref, signal_rows = refs[:5]
        refs = refs[5:]
    else:
        left_sum, diff_sum, refs = refs[0], refs[1], refs[2:]
    mat, gain, carry, scaled, left_pad, diff_pad, index_ref, sems = refs
    _, slab, width = weight_ref.shape
    slab = slab - SUB
    emissions = SCALE - 1
    tiles = width // LANES
    blocks = slab // BLOCK
    lanes, rows = lane_ids(), row_ids()
    column = column_in(weight_ref, pl.ds(0, count), index_ref, sems.at[blocks])
    column.start()
    if finish:
        for v in range(signal_rows.shape[0]):
            signal_rows[v] = signal_ref[v * SUB : (v + 1) * SUB, :].reshape(SUB, 1, width)
        signal_copy = pltpu.make_async_copy(signal_rows, signal_hbm, sems.at[blocks + 1])
        signal_copy.start()
        out_copies = [
            pltpu.make_async_copy(grad_ref.at[b], grad_hbm.at[:, pl.ds(b * BLOCK, BLOCK), :], sems.at[b])
            for b in range(blocks)
        ]
    masks = [const_ref[LINE_LANES] == k for k in range(emissions)]
    columns = [const_ref[k] for k in range(emissions + 1)]
    fill_matrix(mat, -columns[0], select_line(masks, columns[1:]), True, False)
    masks = [const_ref[LINE_ROWS] == k for k in range(emissions)]
    scale = const_ref[SCALE]
    columns = [column * cells for column in columns]
    for j in range(tiles):
        span = slice(j * LANES, (j + 1) * LANES)
        factor = package_ref[count * SUB : (count + 1) * SUB, span]
        sums = package_ref[(count + 1) * SUB : (count + 2) * SUB, span]
        for v in range(count):
            base = v * SCALE
            gain[v, :, span] = package_ref[v * SUB : (v + 1) * SUB, span] * scale * line_rows(factor, base, masks)
            back = columns[0] * jnp.broadcast_to(sums[base : base + 1], rows.shape)
            for k in range(1, emissions + 1):
                back = back + columns[k] * jnp.broadcast_to(sums[base + k : base + k + 1], rows.shape)
            carry[v, :, span] = back
    zero = jnp.zeros((SUB, LANES), F32)
    for ref in (left_pad, diff_pad):
        edge = jnp.zeros(ref.shape[:3] + (LANES,), F32)
        ref[:, :, :, 0:LANES] = edge
        ref[:, :, :, width + 2 * LANES :] = edge
    column.wait()

    def place(v, d, cell, first):
        _, rest = shift_of(index_ref, v, cell, width)
        stay = lanes >= rest
        turn = rest & (LANES - 1)
        at = (first + d) * SUB
        plain = [scaled[v, at : at + SUB, j * LANES : (j + 1) * LANES] for j in range(tiles)]
        moved = [plain[j] * weight_ref[v, cell : cell + 1, j * LANES : (j + 1) * LANES] for j in range(tiles)]
        for ref, values in ((left_pad, plain), (diff_pad, moved)):
            turned = [zero] + [pltpu.roll(value, turn, 1) for value in values] + [zero]
            for j in range(tiles + 1):
                ref[v, first + d, :, (j + 1) * LANES : (j + 2) * LANES] = jnp.where(stay, turned[j + 1], turned[j])

    def gathered(ref, before, cell, slot):
        sums = [None] * (tiles + 2)
        if before is not None:
            sums = [before[cell, :, j * LANES : (j + 1) * LANES] for j in range(tiles + 2)]
        for v in range(count):
            whole, _ = shift_of(index_ref, v, cell, width)
            for j in range(tiles + 2):
                start = pl.multiple_of((1 + j - whole) * LANES, LANES)
                value = ref[v, slot, :, pl.ds(start, LANES)]
                sums[j] = value if sums[j] is None else sums[j] + value
        return sums

    def folded(sums):
        low = jnp.sum(sums[0], axis=1, keepdims=True)
        beyond = sums[tiles + 1] + jnp.where(lanes == LANES - 1, sums[tiles], 0.0)
        high = jnp.sum(beyond, axis=1, keepdims=True)
        core = sums[1 : tiles + 1]
        core[0] = core[0] + jnp.where(lanes == 0, low, 0.0)
        core[-1] = jnp.where(lanes == LANES - 1, 0.0, core[-1] + jnp.where(lanes == LANES - 2, high, 0.0))
        return core

    for block in range(blocks):
        first = block % 2 * BLOCK
        for v in range(count):
            for c in range(width // CHUNK):
                span = slice(c * CHUNK, (c + 1) * CHUNK)
                factor = gain[v, :, span][None]
                weighted = n_refs[v][places[v], block_rows(block), span].reshape(BLOCK, SUB, CHUNK) * factor
                direct = u_refs[v][places[v], block_rows(block), span].reshape(BLOCK, SUB, CHUNK) * factor
                lines, total = multiply(mat, weighted.reshape(ROWS, CHUNK))
                before = carry[v, :, span]
                lines = lines.reshape(BLOCK, SUB, CHUNK) + before[None]
                scaled[v, first * SUB : first * SUB + ROWS, span] = (direct - lines).reshape(ROWS, CHUNK)
                carry[v, :, span] = before + total
        for v in range(count):
            for d in range(BLOCK):
                place(v, d, block * BLOCK + d, first)
        for d in range(BLOCK):
            cell = block * BLOCK + d
            left = gathered(left_pad, prior[0] if finish > 1 else None, cell, first + d)
            diff = gathered(diff_pad, prior[1] if finish > 1 else None, cell, first + d)
            if not finish:
                for j in range(tiles + 2):
                    left_sum[cell, :, j * LANES : (j + 1) * LANES] = left[j]
                    diff_sum[cell, :, j * LANES : (j + 1) * LANES] = diff[j]
                continue
            left, diff = folded([left[j] - diff[j] for j in range(tiles + 2)]), folded(diff)
            turned = [zero] + [pltpu.roll(value, 1, 1) for value in diff]
            for j in range(tiles):
                value = left[j] + jnp.where(lanes == 0, turned[j], turned[j + 1])
                cell_ref[first + d, :, j * LANES : (j + 1) * LANES] = value
        if finish:
            grad_ref[block] = jnp.swapaxes(cell_ref[first : first + BLOCK], 0, 1)
            out_copies[block].start()
    if finish:
        for copy in out_copies + [signal_copy]:
            copy.wait()


def backward(package, const, weights, pieces, cells, signal, prior):
    views, slab, width = weights.shape
    slab = slab - SUB
    blocks = slab // BLOCK
    finish = signal is not None
    line = pltpu.VMEM((views, SUB, width), F32)
    sums = pltpu.VMEM((slab, SUB, width + 2 * LANES), F32)
    scratch = [
        pltpu.VMEM(MATRIX, BF16),
        line,
        line,
        pltpu.VMEM((views, 2 * ROWS, width), F32),
        pltpu.VMEM((views, 2 * BLOCK, SUB, width + 3 * LANES), F32),
        pltpu.VMEM((views, 2 * BLOCK, SUB, width + 3 * LANES), F32),
        pltpu.SMEM((views, SUB, LANES), F32),
        pltpu.SemaphoreType.DMA((blocks + 2,)),
    ]
    operands = [const, package, weights, *[u for u, _, _ in pieces], *[n for _, n, _ in pieces]]
    if finish:
        operands += [signal[0], *prior]
        scratch = [
            pltpu.VMEM((2 * BLOCK, SUB, width), F32),
            pltpu.VMEM((blocks, SUB, BLOCK, width), F32),
            pltpu.VMEM(signal[1], F32),
        ] + scratch
    return pl.pallas_call(
        functools.partial(
            backward_kernel, tuple(at for _, _, at in pieces), cells, 1 + len(prior) if finish else 0
        ),
        in_specs=[VMEM] * len(operands),
        out_specs=[HBM, HBM] if finish else [VMEM, VMEM],
        out_shape=[pltpu.HBM((SUB, slab, width), F32), pltpu.HBM(signal[1], F32)] if finish else [sums, sums],
        scratch_shapes=scratch,
        compiler_params=pltpu.CompilerParams(vmem_limit_bytes=16 * MIB),
        name="backward_last" if finish else "backward_first",
    )(*operands)


def body(concentration, shear_index, shear_weight, attenuation, yields, line_energy, measured):
    elements, _, slab, width = concentration.shape
    views = shear_weight.shape[0]
    emissions = attenuation.shape[0] - 1
    groups = lax.axis_size("far")
    both = lax.axis_size("views") == 2
    cells = float(slab * groups * NEAR)
    conc = concentration.reshape(elements, slab, width)
    scalars = (attenuation, line_energy, yields)

    def to_other(value):
        return lax.ppermute(value, "views", [(0, 1), (1, 0)])

    fillers = []

    def fill(after):
        if not both or len(fillers) == views:
            return ()
        fillers.append(forward_other(len(fillers), other_weight, mat, pads, after))
        return (fillers[-1][2],)

    u, n, const, target, mat, pads, weight, state, send = forward(
        conc, shear_index, shear_weight, scalars, measured, cells
    )
    def swap(value, axis, step):
        return lax.ppermute(value, axis, [(s, s ^ step) for s in range(lax.axis_size(axis))])

    states = [state, swap(send, "near", 1)]
    if both:
        weight = pass_on(weight, state)
        other_weight = to_other(weight)
    tokens = ()
    levels = groups.bit_length() + 1

    def merge(level):
        (merged,) = call_small(
            functools.partial(merge_kernel, level), "merge", [state.shape], (const, *states[-2:])
        )
        return merged

    state = merge(0)
    pairs = [(s, s ^ 6) for s in range(groups * NEAR)]
    four = (state, swap(state, "near", 2), swap(state, "far", 1), lax.ppermute(state, ("far", "near"), pairs))
    pair, other, whole = call_small(merge_four_kernel, "merge_four", [state.shape] * 3, (const, *four))
    states += [*four[:2], pair, other]
    state = whole
    for level in range(3, levels):
        states += [state, swap(state, "far", 1 << (level - 2))]
        if level < levels - 1:
            state = merge(level)
    for _ in range(views):
        tokens += fill(state)
    half = ((views + 2) * SUB, width // 2)
    here, there, here_other, there_other = call_small(
        functools.partial(result_kernel, levels), "result", [half] * 4, (const, target, *states, *tokens)
    )
    there = swap(there, "near", 1)
    if both:
        pairs = [(v * NEAR + s, (1 - v) * NEAR + (s ^ 1)) for v in range(2) for s in range(NEAR)]
        here_other = to_other(here_other)
        there_other = lax.ppermute(there_other, ("views", "near"), pairs)
    package = (half[0], width)
    shapes = [package, target.shape]
    package, signal = call_small(assemble_kernel, "assemble", shapes, (target, here, there))
    own = [(u, n, v) for v in range(views)]
    signal = (signal, measured.shape)
    if both:
        sums = backward(package, const, weight, own, cells, None, ())
        (other_package,) = call_small(
            assemble_other_kernel, "assemble_other", [package.shape], (here_other, there_other)
        )
        pieces = [(fillers[v][0], fillers[v][1], 0) for v in range(views)]
        gradient, signal = backward(other_package, const, other_weight, pieces, cells, signal, sums)
    else:
        gradient, signal = backward(package, const, weight, own, cells, signal, ())
        gradient = lax.psum(gradient, "views")
    return gradient.reshape(concentration.shape), signal


def solution(mesh):
    views, depth = mesh.shape["views"], mesh.shape["depth"]
    devices = mesh.devices.reshape(views, depth // NEAR, NEAR)
    split = jax.sharding.Mesh(devices, ("views", "far", "near"))
    depths = ("far", "near")
    return jax.shard_map(
        body,
        mesh=split,
        in_specs=(
            P(None, None, depths, None),
            P("views", depths, None),
            P("views", depths, None),
            P(),
            P(),
            P(),
            P("views", None, None, None),
        ),
        out_specs=(P(None, None, depths, None), P("views", None, None, None)),
        check_vma=False,
    )
```

```python
import functools

import jax
import jax.numpy as jnp
from jax import lax
from jax.experimental import pallas as pl
from jax.experimental.pallas import tpu as pltpu
from jax.sharding import PartitionSpec as P

LANES = 128
SUB = 8
BLOCK = 8
ROWS = BLOCK * SUB
NEAR = 4
CHUNK = 256
MIB = 1024 * 1024
F32 = jnp.float32
BF16 = jnp.bfloat16
HBM = pl.BlockSpec(memory_space=pltpu.HBM)
VMEM = pl.BlockSpec(memory_space=pltpu.VMEM)
SCALE, LINE_ROWS, LINE_LANES = 4, 5, 6
ANY = pl.BlockSpec(memory_space=pl.ANY)


def in_hbm(value):
    return pltpu.with_memory_space_constraint(value, pltpu.HBM)


def lane_ids(width=LANES):
    return lax.broadcasted_iota(jnp.int32, (SUB, width), 1)


def row_ids(width=LANES):
    return lax.broadcasted_iota(jnp.int32, (SUB, width), 0)


def tile_of(values, ids):
    tile = jnp.zeros(ids.shape, F32)
    for e in range(SUB):
        tile = jnp.where(ids == e, values[e], tile)
    return tile


def select_line(masks, values):
    result = values[0]
    for mask, value in zip(masks[1:], values[1:]):
        result = jnp.where(mask, value, result)
    return result


def fill_matrix(mat_ref, first_tile, second_tile, first_incl, second_incl):
    depth = (lane_ids() & (ROWS - 1)) >> 3
    tiles = []
    for d in range(BLOCK):
        one = jnp.where(depth <= d if first_incl else depth < d, first_tile, 0.0)
        two = jnp.where(depth <= d if second_incl else depth < d, second_tile, 0.0)
        tiles.append(one + two)
    tiles.append(first_tile + second_tile)
    tiles.append(jnp.zeros((SUB, LANES), F32))
    whole = jnp.concatenate(tiles, axis=0)
    high = whole.astype(BF16)
    mat_ref[:, 0:LANES] = high
    mat_ref[:, LANES : 2 * LANES] = (whole - high.astype(F32)).astype(BF16)


def multiply(mat_ref, values):
    high = values.astype(BF16)
    low = (values - high.astype(F32)).astype(BF16)
    stacked = jnp.concatenate([high, low, high], axis=0)
    product = jnp.dot(mat_ref[:, 0 : 3 * ROWS], stacked, preferred_element_type=F32)
    return product[0:ROWS], product[ROWS : ROWS + SUB]


MATRIX = (ROWS + 2 * SUB, 2 * LANES)


def copies_in(pairs, sems):
    return [pltpu.make_async_copy(source, target, sems.at[i]) for i, (source, target) in enumerate(pairs)]


def block_rows(block):
    return slice(block * ROWS, (block + 1) * ROWS)


def block_cells(block):
    return slice(block * BLOCK, (block + 1) * BLOCK)


def offset_of(index_ref, v, cell, width):
    if index_ref.dtype == jnp.int32:
        at = index_ref[v, cell, 0]
    else:
        at = index_ref[v, cell % SUB, cell // SUB].astype(jnp.int32)
    return at - (width // 2 - LANES)


def shift_of(index_ref, v, cell, width):
    offset = offset_of(index_ref, v, cell, width)
    whole = jnp.minimum(offset >> 7, 1)
    return whole, offset - (whole << 7)


def pad_cells(pad_ref, cell, pieces):
    tiles = len(pieces)

    def spread(piece, lane):
        return jnp.broadcast_to(piece[:, lane : lane + 1], (SUB, LANES))

    last = spread(pieces[-1], LANES - 1)
    edges = [spread(pieces[0], 1), spread(pieces[-1], LANES - 2)]
    for j, piece in enumerate([spread(pieces[0], 0)] + pieces + [last, last] + edges):
        pad_ref[cell, :, j * LANES : (j + 1) * LANES] = piece


def shear(field, pad_ref, index_ref, weight_ref, block, views, tiles):
    lanes = lane_ids()
    for i, v in enumerate(views):
        for d in range(BLOCK):
            cell = block * BLOCK + d
            offset = offset_of(index_ref, v, cell, tiles * LANES)
            whole, rest = offset >> 7, offset & (LANES - 1)
            starts = [pl.multiple_of((whole + j) * LANES, LANES) for j in range(tiles + 1)]
            values = [pad_ref[cell, :, pl.ds(start, LANES)] for start in starts]

            def turned(rest):
                stay = lanes < LANES - rest
                turn = (LANES - rest) & (LANES - 1)
                rolled = [pltpu.roll(value, turn, 1) for value in values]
                return [jnp.where(stay, rolled[j], rolled[j + 1]) for j in range(tiles)]

            left, right = turned(rest), turned(rest + 1)
            second, last_but_one = [
                pad_ref[cell, :, (tiles + 3 + j) * LANES : (tiles + 4 + j) * LANES] for j in range(2)
            ]
            right[0] = jnp.where(lanes < LANES - offset, second, right[0])
            for j in (tiles - 2, tiles - 1):
                first = (tiles + 1 - j) * LANES - 1 - offset
                left[j] = jnp.where(lanes >= first, last_but_one, left[j])
            for j in range(tiles):
                span = slice(j * LANES, (j + 1) * LANES)
                weight = weight_ref[i, cell : cell + 1, span]
                field[i, d * SUB : (d + 1) * SUB, span] = left[j] + weight * (right[j] - left[j])


def transmit(u_ref, n_ref, field, mat, carry, block, sums):
    views, _, width = field.shape
    for v in range(views):
        for c in range(width // CHUNK):
            span = slice(c * CHUNK, (c + 1) * CHUNK)
            value = field[v, :, span]
            lines, total = multiply(mat, value)
            before = carry[v, :, span]
            through = jnp.exp(lines.reshape(BLOCK, SUB, CHUNK) + before[None])
            value = value.reshape(BLOCK, SUB, CHUNK)
            emit = value * through
            u_ref[v, block_rows(block), span] = through.reshape(ROWS, CHUNK)
            n_ref[v, block_rows(block), span] = emit.reshape(ROWS, CHUNK)
            carry[v, :, span] = before + total
            if sums:
                sums[0][v, :, span] += jnp.sum(value, axis=0)
                sums[1][v, :, span] += jnp.sum(emit, axis=0)


def forward_kernel(cells, *refs):
    att_hbm, line_hbm, yield_hbm, index_hbm, conc_hbm, weight_hbm, measured_hbm = refs[:7]
    u_ref, n_ref, const_ref, target_ref, mat, pad_ref, weight_ref = refs[7:14]
    state_refs = refs[14:16]
    refs = refs[16:]
    conc_ref, field, carry, field_sum, emit_sum, measured_ref, column_ref = refs[:7]
    att_ref, line_ref, yield_ref, index_ref, sems = refs[7:]
    views, _, width = weight_ref.shape
    slab = conc_ref.shape[1]
    emissions = att_ref.shape[0] - 1
    tiles = width // LANES
    blocks = slab // BLOCK
    lanes, rows = lane_ids(), row_ids()
    conc_copies = [
        pltpu.make_async_copy(
            conc_hbm.at[:, pl.ds(b * BLOCK, BLOCK), :], conc_ref.at[:, pl.ds(b * BLOCK, BLOCK), :], sems.at[b]
        )
        for b in range(blocks)
    ]
    pairs = [
        (att_hbm, att_ref),
        (line_hbm, line_ref),
        (yield_hbm, yield_ref),
        (weight_hbm, weight_ref.at[:, pl.ds(0, slab), :]),
        (measured_hbm, measured_ref),
        (index_hbm.at[:, :, pl.ds(width // 2, LANES)], column_ref),
    ]
    copies = copies_in(pairs, sems.at[pl.ds(2 * blocks, len(pairs))])
    index_copies = [
        pltpu.make_async_copy(
            index_hbm.at[:, pl.ds(b * BLOCK, BLOCK), pl.ds(width // 2, LANES)],
            index_ref.at[:, pl.ds(b * BLOCK, BLOCK), :],
            sems.at[blocks + b],
        )
        for b in range(blocks)
    ]
    for copy in conc_copies[:1] + copies[:3] + index_copies[:1] + copies[3:4]:
        copy.start()
    for copy in conc_copies[1:] + index_copies[1:] + copies[4:]:
        copy.start()
    for ref in (carry, field_sum, emit_sum):
        ref[...] = jnp.zeros_like(ref)

    def pad(block):
        conc_copies[block].wait()
        by_depth = jnp.swapaxes(conc_ref[:, block_cells(block), :], 0, 1)
        for d in range(BLOCK):
            pieces = [by_depth[d, :, j * LANES : (j + 1) * LANES] for j in range(tiles)]
            pad_cells(pad_ref, block * BLOCK + d, pieces)

    pad(0)
    for copy in copies[:3]:
        copy.wait()
    line_by_row = tile_of([line_ref[e].astype(F32) for e in range(SUB)], rows)
    masks = [line_by_row == k for k in range(emissions)]
    by_lane = [tile_of([att_ref[k, e] for e in range(SUB)], lanes & 7) for k in range(emissions + 1)]
    fill_matrix(mat, -by_lane[0], select_line(masks, by_lane[1:]), False, True)
    for k in range(emissions + 1):
        const_ref[k] = tile_of([att_ref[k, e] for e in range(SUB)], rows)
    const_ref[SCALE] = tile_of([yield_ref[e] for e in range(SUB)], rows)
    const_ref[LINE_ROWS] = line_by_row
    const_ref[LINE_LANES] = tile_of([line_ref[e].astype(F32) for e in range(SUB)], lanes & 7)
    copies[3].wait()
    for block in range(blocks):
        if block:
            pad(block)
        index_copies[block].wait()
        shear(field, pad_ref, index_ref, weight_ref, block, range(views), tiles)
        transmit(u_ref, n_ref, field, mat, carry, block, (field_sum, emit_sum))
    for copy in copies[4:]:
        copy.wait()
    for v in range(views):
        shifts = jnp.zeros((SUB, LANES), jnp.int32)
        for octet in range(slab // SUB):
            values = column_ref[v, octet * SUB : (octet + 1) * SUB, :] - lanes
            shifts = jnp.where(lanes == octet, values, shifts)
        weight_ref[v, slab : slab + SUB, 0:LANES] = shifts.astype(F32)
    columns = [const_ref[k] for k in range(emissions + 1)]
    masks = [const_ref[LINE_ROWS] == k for k in range(emissions)]
    scale = const_ref[SCALE] * (1.0 / cells)
    share = width // 2
    core = lax.axis_index("near") & 1
    for r in range(2):
        for j in range(share // LANES):
            start = pl.multiple_of((core ^ r) * share + j * LANES, LANES)
            span = slice(j * LANES, (j + 1) * LANES)
            totals = jnp.zeros((SUB, LANES), F32)
            for v in range(views):
                values = field_sum[v, :, pl.ds(start, LANES)]
                sums = [jnp.sum(column * values, axis=0, keepdims=True) for column in columns]
                for k in range(emissions + 1):
                    totals = jnp.where(rows == v * (emissions + 1) + k, sums[k], totals)
                line_total = select_line(masks, [jnp.broadcast_to(value, rows.shape) for value in sums[1:]])
                signal = scale * emit_sum[v, :, pl.ds(start, LANES)] * jnp.exp(-line_total)
                state_refs[r][(v + 1) * SUB : (v + 2) * SUB, span] = signal
            state_refs[r][0:SUB, span] = jnp.exp(-totals)
    for v in range(views):
        target_ref[v * SUB : (v + 1) * SUB, :] = measured_ref[v].reshape(SUB, width)


def forward(conc, index, weights, scalars, measured, cells):
    views, slab, width = weights.shape
    attenuation, line_energy, yields = scalars
    values = pltpu.VMEM((views, slab * SUB, width), F32)
    padded = pltpu.VMEM((slab, SUB, width + 5 * LANES), F32)
    state = pltpu.VMEM(((views + 1) * SUB, width // 2), F32)
    line = pltpu.VMEM((views, SUB, width), F32)
    operands = [in_hbm(value) for value in (attenuation, line_energy, yields, index, conc, weights, measured)]
    return pl.pallas_call(
        functools.partial(forward_kernel, cells),
        in_specs=[HBM] * len(operands),
        out_specs=[VMEM] * 9,
        out_shape=[
            values,
            values,
            pltpu.VMEM((LINE_LANES + 1, SUB, LANES), F32),
            pltpu.VMEM((views * SUB, width), F32),
            pltpu.VMEM(MATRIX, BF16),
            padded,
            pltpu.VMEM((views, slab + SUB, width), F32),
            state,
            state,
        ],
        scratch_shapes=[
            pltpu.VMEM((SUB, slab, width), F32),
            pltpu.VMEM((views, ROWS, width), F32),
            line,
            line,
            line,
            pltpu.VMEM(measured.shape, F32),
            pltpu.VMEM((views, slab, LANES), jnp.int32),
            pltpu.SMEM(attenuation.shape, F32),
            pltpu.SMEM(line_energy.shape, jnp.int32),
            pltpu.SMEM(yields.shape, F32),
            pltpu.SMEM((views, slab, LANES), jnp.int32),
            pltpu.SemaphoreType.DMA((2 * (slab // BLOCK) + 6,)),
        ],
        compiler_params=pltpu.CompilerParams(vmem_limit_bytes=16 * MIB),
        name="forward",
    )(*operands)


def column_in(package_any, views, index_ref, sem):
    first = package_any.shape[1] - SUB
    source = package_any.at[views, pl.ds(first, SUB), pl.ds(0, index_ref.shape[2])]
    return pltpu.make_async_copy(source, index_ref, sem)


def backward_matrix(mat_ref, const_ref):
    masks = [const_ref[LINE_LANES] == k for k in range(SCALE - 1)]
    columns = [const_ref[k] for k in range(SCALE)]
    fill_matrix(mat_ref, -columns[0], select_line(masks, columns[1:]), True, False)


def forward_other_kernel(view, weight_ref, mat, pad_ref, const_ref, order_ref, *refs):
    u_ref, n_ref, back_mat, field, carry, index_ref, sem = refs
    _, slab, width = weight_ref.shape
    slab = slab - SUB
    copy = column_in(weight_ref, pl.ds(view, 1), index_ref, sem)
    copy.start()
    carry[...] = jnp.zeros_like(carry)
    backward_matrix(back_mat, const_ref)
    copy.wait()
    for block in range(slab // BLOCK):
        shear(field, pad_ref, index_ref, weight_ref.at[pl.ds(view, 1)], block, (0,), width // LANES)
        transmit(u_ref, n_ref, field, mat, carry, block, None)


def forward_other(view, weights, mat, pads, const, after):
    _, slab, width = weights.shape
    slab = slab - SUB
    values = pltpu.VMEM((1, slab * SUB, width), F32)
    return pl.pallas_call(
        functools.partial(forward_other_kernel, view),
        in_specs=[VMEM] * 5,
        out_specs=[VMEM] * 3,
        out_shape=[values, values, pltpu.VMEM(MATRIX, BF16)],
        scratch_shapes=[
            pltpu.VMEM((1, ROWS, width), F32),
            pltpu.VMEM((1, SUB, width), F32),
            pltpu.SMEM((1, SUB, LANES), F32),
            pltpu.SemaphoreType.DMA,
        ],
        compiler_params=pltpu.CompilerParams(vmem_limit_bytes=8 * MIB),
        name="forward_other",
    )(weights, mat, pads, const, after)


def line_rows(tile, base, masks):
    shape = masks[0].shape
    return select_line(masks, [jnp.broadcast_to(tile[base + 1 + k : base + 2 + k], shape) for k in range(len(masks))])


def incident_rows(tile, step):
    rows = row_ids(tile.shape[1])
    result = jnp.broadcast_to(tile[0:1], tile.shape)
    for base in range(step, SUB, step):
        result = jnp.where(rows >= base, jnp.broadcast_to(tile[base : base + 1], tile.shape), result)
    return result


def row_masks(const_ref, width):
    tile = const_ref[LINE_ROWS]
    return [jnp.concatenate([tile] * (width // LANES), axis=1) == k for k in range(SCALE - 1)]


def factors_of(mine, theirs, bit):
    mine_factor = jnp.where(bit == 0, theirs, incident_rows(theirs, SCALE))
    return mine_factor, jnp.where(bit == 0, incident_rows(mine, SCALE), mine)


def merged_state(mine, theirs, bit, masks):
    mine_factor, theirs_factor = factors_of(mine[0:SUB], theirs[0:SUB], bit)
    result = [mine[0:SUB] * theirs[0:SUB]]
    for v in range(mine.shape[0] // SUB - 1):
        span = slice((v + 1) * SUB, (v + 2) * SUB)
        result.append(
            mine[span] * line_rows(mine_factor, v * SCALE, masks)
            + theirs[span] * line_rows(theirs_factor, v * SCALE, masks)
        )
    return result


def weighted_rows(factor, state, misfits, masks):
    rows = row_ids(state.shape[1])
    result = jnp.zeros((SUB, state.shape[1]), F32)
    for v, misfit in enumerate(misfits):
        base = v * SCALE
        value = misfit * state[(v + 1) * SUB : (v + 2) * SUB] * line_rows(factor, base, masks)
        whole = None
        for k, mask in enumerate(masks):
            part = jnp.sum(jnp.where(mask, value, 0.0), axis=0, keepdims=True)
            result = jnp.where(rows == base + 1 + k, part, result)
            whole = part if whole is None else whole + part
        result = jnp.where(rows == base, whole, result)
    return result


def children(factor, sums, mine, theirs, bit, misfits, masks):
    mine_factor, theirs_factor = factors_of(mine[0:SUB], theirs[0:SUB], bit)
    if factor is not None:
        mine_factor, theirs_factor = factor * mine_factor, factor * theirs_factor
    behind = (row_ids(mine.shape[1]) & (SCALE - 1)) == 0
    mine_sums = jnp.where(behind == (bit == 0), weighted_rows(theirs_factor, theirs, misfits, masks), 0.0)
    theirs_sums = jnp.where(behind == (bit == 1), weighted_rows(mine_factor, mine, misfits, masks), 0.0)
    if sums is not None:
        mine_sums, theirs_sums = sums + mine_sums, sums + theirs_sums
    return (mine_factor, mine_sums), (theirs_factor, theirs_sums)


def call_small(kernel, name, outs, operands, scratch=()):
    return pl.pallas_call(
        kernel,
        in_specs=[VMEM] * len(operands),
        out_specs=[VMEM] * len(outs),
        out_shape=[pltpu.VMEM(shape, F32) for shape in outs],
        scratch_shapes=[pltpu.VMEM(shape, F32) for shape in scratch],
        compiler_params=pltpu.CompilerParams(vmem_limit_bytes=4 * MIB),
        name=name,
    )(*operands)


def store_rows(ref, tiles):
    for i, tile in enumerate(tiles):
        ref[i * SUB : (i + 1) * SUB, :] = tile


def merge_kernel(shift, const_ref, mine_ref, theirs_ref, *refs):
    bit = (depth_place() >> shift) & 1
    store_rows(refs[-1], merged_state(mine_ref[...], theirs_ref[...], bit, row_masks(const_ref, mine_ref.shape[1])))


def merge_four_kernel(const_ref, mine_ref, near_ref, far_ref, both_ref, pair_ref, other_ref, whole_ref):
    place = depth_place()
    masks = row_masks(const_ref, mine_ref.shape[1])
    pair = merged_state(mine_ref[...], near_ref[...], (place >> 1) & 1, masks)
    other = merged_state(far_ref[...], both_ref[...], (place >> 1) & 1, masks)
    store_rows(pair_ref, pair)
    store_rows(other_ref, other)
    store_rows(whole_ref, merged_state(pair_ref[...], other_ref[...], (place >> 2) & 1, masks))


def depth_place():
    return lax.axis_index("far") * NEAR + lax.axis_index("near")


def result_kernel(levels, const_ref, target_ref, *refs):
    states, outs = refs[: 2 * levels], refs[-4:]
    depth, width = states[0].shape
    views = depth // SUB - 1
    place = depth_place()
    size = 2 * LANES
    start = (place & 1) * width
    masks = row_masks(const_ref, size)
    behind = (row_ids(size) & (SCALE - 1)) == 0
    for c in range(width // size):
        span = slice(c * size, (c + 1) * size)
        factor, sums = None, None
        for level in reversed(range(levels)):
            mine, theirs = states[2 * level][:, span], states[2 * level + 1][:, span]
            bit = (place >> level) & 1
            if level == levels - 1:
                signals = merged_state(mine, theirs, bit, masks)[1:]
                there = pl.ds(pl.multiple_of(start + c * size, LANES), size)
                misfits = [signals[v] - target_ref[v * SUB : (v + 1) * SUB, there] for v in range(views)]
            contexts = children(factor, sums, mine, theirs, bit, misfits, masks)
            factor, sums = contexts[0]
        for i, (state, (factor, sums)) in enumerate(zip((mine, theirs), contexts)):
            own = jnp.where(behind, weighted_rows(factor, state, misfits, masks), 0.0)
            rest = [factor * state[0:SUB], sums + own]
            for ref, first in ((outs[i], signals), (outs[2 + i], misfits)):
                for j, tile in enumerate(first + rest):
                    ref[j * SUB : (j + 1) * SUB, span] = tile


def assemble_kernel(target_ref, here_ref, there_ref, package_ref, signal_ref):
    half = here_ref.shape[1]
    count = signal_ref.shape[0]
    at = pl.multiple_of((lax.axis_index("near") & 1) * half, LANES)
    for ref, start in ((here_ref, at), (there_ref, pl.multiple_of(half - at, LANES))):
        span = pl.ds(start, half)
        signal_ref[:, span] = ref[0:count, :]
        package_ref[0:count, span] = ref[0:count, :] - target_ref[:, span]
        package_ref[count:, span] = ref[count:, :]


def assemble_other_kernel(here_ref, there_ref, package_ref):
    half = here_ref.shape[1]
    at = pl.multiple_of((lax.axis_index("near") & 1) * half, LANES)
    package_ref[:, pl.ds(at, half)] = here_ref[...]
    package_ref[:, pl.ds(pl.multiple_of(half - at, LANES), half)] = there_ref[...]


def backward_kernel(places, cells, finish, given, const_ref, package_ref, weight_ref, *refs):
    count = len(places)
    if given:
        mat, refs = refs[0], refs[1:]
    u_refs, n_refs, refs = refs[:count], refs[count : 2 * count], refs[2 * count :]
    if finish:
        signal_ref, refs = refs[0], refs[1:]
        prior, refs = refs[: finish - 1], refs[finish - 1 :]
        grad_hbm, signal_hbm, cell_ref, grad_ref, signal_rows = refs[:5]
        refs = refs[5:]
    else:
        left_sum, diff_sum, refs = refs[0], refs[1], refs[2:]
    gain, carry, scaled, left_pad, diff_pad, index_ref, sems = refs[-7:]
    _, slab, width = weight_ref.shape
    slab = slab - SUB
    emissions = SCALE - 1
    tiles = width // LANES
    blocks = slab // BLOCK
    lanes, rows = lane_ids(), row_ids()
    column = column_in(weight_ref, pl.ds(0, count), index_ref, sems.at[blocks])
    column.start()
    if finish:
        for v in range(signal_rows.shape[0]):
            signal_rows[v] = signal_ref[v * SUB : (v + 1) * SUB, :].reshape(SUB, 1, width)
        signal_copy = pltpu.make_async_copy(signal_rows, signal_hbm, sems.at[blocks + 1])
        signal_copy.start()
        out_copies = [
            pltpu.make_async_copy(grad_ref.at[b], grad_hbm.at[:, pl.ds(b * BLOCK, BLOCK), :], sems.at[b])
            for b in range(blocks)
        ]
    if not given:
        mat = refs[0]
        backward_matrix(mat, const_ref)
    masks = [const_ref[LINE_ROWS] == k for k in range(emissions)]
    scale = const_ref[SCALE]
    columns = [const_ref[k] * cells for k in range(emissions + 1)]
    for j in range(tiles):
        span = slice(j * LANES, (j + 1) * LANES)
        factor = package_ref[count * SUB : (count + 1) * SUB, span]
        sums = package_ref[(count + 1) * SUB : (count + 2) * SUB, span]
        for v in range(count):
            base = v * SCALE
            gain[v, :, span] = package_ref[v * SUB : (v + 1) * SUB, span] * scale * line_rows(factor, base, masks)
            back = columns[0] * jnp.broadcast_to(sums[base : base + 1], rows.shape)
            for k in range(1, emissions + 1):
                back = back + columns[k] * jnp.broadcast_to(sums[base + k : base + k + 1], rows.shape)
            carry[v, :, span] = back
    zero = jnp.zeros((SUB, LANES), F32)
    for ref in (left_pad, diff_pad):
        edge = jnp.zeros(ref.shape[:3] + (LANES,), F32)
        ref[:, :, :, 0:LANES] = edge
        ref[:, :, :, width + 2 * LANES :] = edge

    def place(v, d, cell, first):
        _, rest = shift_of(index_ref, v, cell, width)
        stay = lanes >= rest
        turn = rest & (LANES - 1)
        at = (first + d) * SUB
        plain = [scaled[v, at : at + SUB, j * LANES : (j + 1) * LANES] for j in range(tiles)]
        moved = [plain[j] * weight_ref[v, cell : cell + 1, j * LANES : (j + 1) * LANES] for j in range(tiles)]
        for ref, values in ((left_pad, plain), (diff_pad, moved)):
            turned = [zero] + [pltpu.roll(value, turn, 1) for value in values] + [zero]
            for j in range(tiles + 1):
                ref[v, first + d, :, (j + 1) * LANES : (j + 2) * LANES] = jnp.where(stay, turned[j + 1], turned[j])

    def gathered(ref, before, cell, slot):
        sums = [None] * (tiles + 2)
        if before is not None:
            sums = [before[cell, :, j * LANES : (j + 1) * LANES] for j in range(tiles + 2)]
        for v in range(count):
            whole, _ = shift_of(index_ref, v, cell, width)
            for j in range(tiles + 2):
                start = pl.multiple_of((1 + j - whole) * LANES, LANES)
                value = ref[v, slot, :, pl.ds(start, LANES)]
                sums[j] = value if sums[j] is None else sums[j] + value
        return sums

    def folded(sums):
        low = jnp.sum(sums[0], axis=1, keepdims=True)
        beyond = sums[tiles + 1] + jnp.where(lanes == LANES - 1, sums[tiles], 0.0)
        high = jnp.sum(beyond, axis=1, keepdims=True)
        core = sums[1 : tiles + 1]
        core[0] = core[0] + jnp.where(lanes == 0, low, 0.0)
        core[-1] = jnp.where(lanes == LANES - 1, 0.0, core[-1] + jnp.where(lanes == LANES - 2, high, 0.0))
        return core

    for block in range(blocks):
        first = block % 2 * BLOCK
        for v in range(count):
            for c in range(width // CHUNK):
                span = slice(c * CHUNK, (c + 1) * CHUNK)
                factor = gain[v, :, span][None]
                weighted = n_refs[v][places[v], block_rows(block), span].reshape(BLOCK, SUB, CHUNK) * factor
                direct = u_refs[v][places[v], block_rows(block), span].reshape(BLOCK, SUB, CHUNK) * factor
                lines, total = multiply(mat, weighted.reshape(ROWS, CHUNK))
                before = carry[v, :, span]
                lines = lines.reshape(BLOCK, SUB, CHUNK) + before[None]
                scaled[v, first * SUB : first * SUB + ROWS, span] = (direct - lines).reshape(ROWS, CHUNK)
                carry[v, :, span] = before + total
        if block == 0:
            column.wait()
        for v in range(count):
            for d in range(BLOCK):
                place(v, d, block * BLOCK + d, first)
        for d in range(BLOCK):
            cell = block * BLOCK + d
            left = gathered(left_pad, prior[0] if finish > 1 else None, cell, first + d)
            diff = gathered(diff_pad, prior[1] if finish > 1 else None, cell, first + d)
            if not finish:
                for j in range(tiles + 2):
                    left_sum[cell, :, j * LANES : (j + 1) * LANES] = left[j]
                    diff_sum[cell, :, j * LANES : (j + 1) * LANES] = diff[j]
                continue
            left, diff = folded([left[j] - diff[j] for j in range(tiles + 2)]), folded(diff)
            turned = [zero] + [pltpu.roll(value, 1, 1) for value in diff]
            for j in range(tiles):
                value = left[j] + jnp.where(lanes == 0, turned[j], turned[j + 1])
                cell_ref[first + d, :, j * LANES : (j + 1) * LANES] = value
        if finish:
            grad_ref[block] = jnp.swapaxes(cell_ref[first : first + BLOCK], 0, 1)
            out_copies[block].start()
    if finish:
        for copy in out_copies + [signal_copy]:
            copy.wait()


def backward(package, const, weights, mats, pieces, cells, signal, prior):
    views, slab, width = weights.shape
    slab = slab - SUB
    blocks = slab // BLOCK
    finish = signal is not None
    line = pltpu.VMEM((views, SUB, width), F32)
    sums = pltpu.VMEM((slab, SUB, width + 2 * LANES), F32)
    scratch = [] if mats else [pltpu.VMEM(MATRIX, BF16)]
    scratch += [
        line,
        line,
        pltpu.VMEM((views, 2 * ROWS, width), F32),
        pltpu.VMEM((views, 2 * BLOCK, SUB, width + 3 * LANES), F32),
        pltpu.VMEM((views, 2 * BLOCK, SUB, width + 3 * LANES), F32),
        pltpu.SMEM((views, SUB, LANES), F32),
        pltpu.SemaphoreType.DMA((blocks + 2,)),
    ]
    operands = [const, package, weights, *mats, *[u for u, _, _ in pieces], *[n for _, n, _ in pieces]]
    if finish:
        operands += [signal[0], *prior]
        scratch = [
            pltpu.VMEM((2 * BLOCK, SUB, width), F32),
            pltpu.VMEM((blocks, SUB, BLOCK, width), F32),
            pltpu.VMEM(signal[1], F32),
        ] + scratch
    return pl.pallas_call(
        functools.partial(
            backward_kernel, tuple(at for _, _, at in pieces), cells, 1 + len(prior) if finish else 0, len(mats)
        ),
        in_specs=[VMEM] * len(operands),
        out_specs=[HBM, HBM] if finish else [VMEM, VMEM],
        out_shape=[pltpu.HBM((SUB, slab, width), F32), pltpu.HBM(signal[1], F32)] if finish else [sums, sums],
        scratch_shapes=scratch,
        compiler_params=pltpu.CompilerParams(vmem_limit_bytes=16 * MIB),
        name="backward_last" if finish else "backward_first",
    )(*operands)


def body(concentration, shear_index, shear_weight, attenuation, yields, line_energy, measured):
    elements, _, slab, width = concentration.shape
    views = shear_weight.shape[0]
    emissions = attenuation.shape[0] - 1
    groups = lax.axis_size("far")
    both = lax.axis_size("views") == 2
    cells = float(slab * groups * NEAR)
    conc = concentration.reshape(elements, slab, width)
    scalars = (attenuation, line_energy, yields)

    def to_other(value):
        return lax.ppermute(value, "views", [(0, 1), (1, 0)])

    fillers = []

    def fill(after):
        if not both or len(fillers) == views:
            return ()
        fillers.append(forward_other(len(fillers), other_weight, mat, pads, const, after))
        return (fillers[-1][2],)

    u, n, const, target, mat, pads, weight, state, send = forward(
        conc, shear_index, shear_weight, scalars, measured, cells
    )
    def swap(value, axis, step):
        return lax.ppermute(value, axis, [(s, s ^ step) for s in range(lax.axis_size(axis))])

    states = [state, swap(send, "near", 1)]
    if both:
        other_weight = to_other(weight)
    tokens = ()
    levels = groups.bit_length() + 1

    def merge(level):
        (merged,) = call_small(
            functools.partial(merge_kernel, level), "merge", [state.shape], (const, *states[-2:])
        )
        return merged

    state = merge(0)
    pairs = [(s, s ^ 6) for s in range(groups * NEAR)]
    four = (state, swap(state, "near", 2), swap(state, "far", 1), lax.ppermute(state, ("far", "near"), pairs))
    pair, other, whole = call_small(merge_four_kernel, "merge_four", [state.shape] * 3, (const, *four))
    states += [*four[:2], pair, other]
    state = whole
    for level in range(3, levels):
        states += [state, swap(state, "far", 1 << (level - 2))]
        if level < levels - 1:
            state = merge(level)
    for _ in range(views):
        tokens += fill(state)
    half = ((views + 2) * SUB, width // 2)
    here, there, here_other, there_other = call_small(
        functools.partial(result_kernel, levels), "result", [half] * 4, (const, target, *states, *tokens)
    )
    there = swap(there, "near", 1)
    if both:
        pairs = [(v * NEAR + s, (1 - v) * NEAR + (s ^ 1)) for v in range(2) for s in range(NEAR)]
        here_other = to_other(here_other)
        there_other = lax.ppermute(there_other, ("views", "near"), pairs)
    package = (half[0], width)
    shapes = [package, target.shape]
    package, signal = call_small(assemble_kernel, "assemble", shapes, (target, here, there))
    own = [(u, n, v) for v in range(views)]
    signal = (signal, measured.shape)
    if both:
        sums = backward(package, const, weight, tokens[:1], own, cells, None, ())
        (other_package,) = call_small(
            assemble_other_kernel, "assemble_other", [package.shape], (here_other, there_other)
        )
        pieces = [(fillers[v][0], fillers[v][1], 0) for v in range(views)]
        gradient, signal = backward(other_package, const, other_weight, tokens[:1], pieces, cells, signal, sums)
    else:
        gradient, signal = backward(package, const, weight, (), own, cells, signal, ())
        gradient = lax.psum(gradient, "views")
    return gradient.reshape(concentration.shape), signal


def solution(mesh):
    views, depth = mesh.shape["views"], mesh.shape["depth"]
    devices = mesh.devices.reshape(views, depth // NEAR, NEAR)
    split = jax.sharding.Mesh(devices, ("views", "far", "near"))
    depths = ("far", "near")
    return jax.shard_map(
        body,
        mesh=split,
        in_specs=(
            P(None, None, depths, None),
            P("views", depths, None),
            P("views", depths, None),
            P(),
            P(),
            P(),
            P("views", None, None, None),
        ),
        out_specs=(P(None, None, depths, None), P("views", None, None, None)),
        check_vma=False,
    )
```

```python
import functools

import jax
import jax.numpy as jnp
from jax import lax
from jax.experimental import pallas as pl
from jax.experimental.pallas import tpu as pltpu
from jax.sharding import PartitionSpec as P

LANES = 128
SUB = 8
BLOCK = 8
ROWS = BLOCK * SUB
NEAR = 4
CHUNK = 256
MIB = 1024 * 1024
F32 = jnp.float32
BF16 = jnp.bfloat16
HBM = pl.BlockSpec(memory_space=pltpu.HBM)
VMEM = pl.BlockSpec(memory_space=pltpu.VMEM)
SCALE, LINE_ROWS, LINE_LANES = 4, 5, 6
ANY = pl.BlockSpec(memory_space=pl.ANY)


def in_hbm(value):
    return pltpu.with_memory_space_constraint(value, pltpu.HBM)


def lane_ids(width=LANES):
    return lax.broadcasted_iota(jnp.int32, (SUB, width), 1)


def row_ids(width=LANES):
    return lax.broadcasted_iota(jnp.int32, (SUB, width), 0)


def tile_of(values, ids):
    tile = jnp.zeros(ids.shape, F32)
    for e in range(SUB):
        tile = jnp.where(ids == e, values[e], tile)
    return tile


def select_line(masks, values):
    result = values[0]
    for mask, value in zip(masks[1:], values[1:]):
        result = jnp.where(mask, value, result)
    return result


def fill_matrix(mat_ref, first_tile, second_tile, first_incl, second_incl):
    depth = (lane_ids() & (ROWS - 1)) >> 3
    tiles = []
    for d in range(BLOCK):
        one = jnp.where(depth <= d if first_incl else depth < d, first_tile, 0.0)
        two = jnp.where(depth <= d if second_incl else depth < d, second_tile, 0.0)
        tiles.append(one + two)
    whole = jnp.concatenate(tiles, axis=0)
    high = whole.astype(BF16)
    mat_ref[:, 0:LANES] = high
    mat_ref[:, LANES : 2 * LANES] = (whole - high.astype(F32)).astype(BF16)


def multiply(mat_ref, values):
    high = values.astype(BF16)
    low = (values - high.astype(F32)).astype(BF16)
    stacked = jnp.concatenate([high, low, high], axis=0)
    return jnp.dot(mat_ref[:, 0 : 3 * ROWS], stacked, preferred_element_type=F32)


MATRIX = (ROWS, 2 * LANES)


def copies_in(pairs, sems):
    return [pltpu.make_async_copy(source, target, sems.at[i]) for i, (source, target) in enumerate(pairs)]


def block_rows(block):
    return slice(block * ROWS, (block + 1) * ROWS)


def block_cells(block):
    return slice(block * BLOCK, (block + 1) * BLOCK)


def offset_of(index_ref, v, cell, width):
    if index_ref.dtype == jnp.int32:
        at = index_ref[v, cell, 0]
    else:
        at = index_ref[v, cell % SUB, cell // SUB].astype(jnp.int32)
    return at - (width // 2 - LANES)


def shift_of(index_ref, v, cell, width):
    offset = offset_of(index_ref, v, cell, width)
    whole = jnp.minimum(offset >> 7, 1)
    return whole, offset - (whole << 7)


def pad_cells(pad_ref, cell, pieces):
    tiles = len(pieces)

    def spread(piece, lane):
        return jnp.broadcast_to(piece[:, lane : lane + 1], (SUB, LANES))

    last = spread(pieces[-1], LANES - 1)
    edges = [spread(pieces[0], 1), spread(pieces[-1], LANES - 2)]
    for j, piece in enumerate([spread(pieces[0], 0)] + pieces + [last, last] + edges):
        pad_ref[cell, :, j * LANES : (j + 1) * LANES] = piece


def shear(field, pad_ref, index_ref, weight_ref, block, views, tiles):
    lanes = lane_ids()
    for i, v in enumerate(views):
        for d in range(BLOCK):
            cell = block * BLOCK + d
            offset = offset_of(index_ref, v, cell, tiles * LANES)
            whole, rest = offset >> 7, offset & (LANES - 1)
            starts = [pl.multiple_of((whole + j) * LANES, LANES) for j in range(tiles + 1)]
            values = [pad_ref[cell, :, pl.ds(start, LANES)] for start in starts]

            def turned(rest):
                stay = lanes < LANES - rest
                turn = (LANES - rest) & (LANES - 1)
                rolled = [pltpu.roll(value, turn, 1) for value in values]
                return [jnp.where(stay, rolled[j], rolled[j + 1]) for j in range(tiles)]

            left, right = turned(rest), turned(rest + 1)
            second, last_but_one = [
                pad_ref[cell, :, (tiles + 3 + j) * LANES : (tiles + 4 + j) * LANES] for j in range(2)
            ]
            right[0] = jnp.where(lanes < LANES - offset, second, right[0])
            for j in (tiles - 2, tiles - 1):
                first = (tiles + 1 - j) * LANES - 1 - offset
                left[j] = jnp.where(lanes >= first, last_but_one, left[j])
            for j in range(tiles):
                span = slice(j * LANES, (j + 1) * LANES)
                weight = weight_ref[i, cell : cell + 1, span]
                field[i, d * SUB : (d + 1) * SUB, span] = left[j] + weight * (right[j] - left[j])


def transmit(u_ref, n_ref, field, mat, const_ref, carry, block, sums):
    views, _, width = field.shape
    column = jnp.concatenate([const_ref[0]] * (CHUNK // LANES), axis=1)
    for v in range(views):
        for c in range(width // CHUNK):
            span = slice(c * CHUNK, (c + 1) * CHUNK)
            value = field[v, :, span]
            lines = multiply(mat, value).reshape(BLOCK, SUB, CHUNK) + carry[v, :, span][None]
            through = jnp.exp(lines)
            value = value.reshape(BLOCK, SUB, CHUNK)
            carry[v, :, span] = lines[-1] - jnp.sum(column * value[-1], axis=0, keepdims=True)
            emit = value * through
            u_ref[v, block_rows(block), span] = through.reshape(ROWS, CHUNK)
            n_ref[v, block_rows(block), span] = emit.reshape(ROWS, CHUNK)
            if sums:
                sums[0][v, :, span] += jnp.sum(value, axis=0)
                sums[1][v, :, span] += jnp.sum(emit, axis=0)


def forward_kernel(cells, *refs):
    att_hbm, line_hbm, yield_hbm, index_hbm, conc_hbm, weight_hbm, measured_hbm = refs[:7]
    u_ref, n_ref, const_ref, target_ref, mat, pad_ref, weight_ref = refs[7:14]
    state_refs = refs[14:16]
    refs = refs[16:]
    conc_ref, field, carry, field_sum, emit_sum, measured_ref, column_ref = refs[:7]
    att_ref, line_ref, yield_ref, index_ref, sems = refs[7:]
    views, _, width = weight_ref.shape
    slab = conc_ref.shape[1]
    emissions = att_ref.shape[0] - 1
    tiles = width // LANES
    blocks = slab // BLOCK
    lanes, rows = lane_ids(), row_ids()
    conc_copies = [
        pltpu.make_async_copy(
            conc_hbm.at[:, pl.ds(b * BLOCK, BLOCK), :], conc_ref.at[:, pl.ds(b * BLOCK, BLOCK), :], sems.at[b]
        )
        for b in range(blocks)
    ]
    pairs = [
        (att_hbm, att_ref),
        (line_hbm, line_ref),
        (yield_hbm, yield_ref),
        (weight_hbm, weight_ref.at[:, pl.ds(0, slab), :]),
        (measured_hbm, measured_ref),
        (index_hbm.at[:, :, pl.ds(width // 2, LANES)], column_ref),
    ]
    copies = copies_in(pairs, sems.at[pl.ds(2 * blocks, len(pairs))])
    index_copies = [
        pltpu.make_async_copy(
            index_hbm.at[:, pl.ds(b * BLOCK, BLOCK), pl.ds(width // 2, LANES)],
            index_ref.at[:, pl.ds(b * BLOCK, BLOCK), :],
            sems.at[blocks + b],
        )
        for b in range(blocks)
    ]
    for copy in conc_copies[:1] + copies[:3] + index_copies[:1] + copies[3:4]:
        copy.start()
    for copy in conc_copies[1:] + index_copies[1:] + copies[4:]:
        copy.start()
    for ref in (carry, field_sum, emit_sum):
        ref[...] = jnp.zeros_like(ref)

    def pad(block):
        conc_copies[block].wait()
        by_depth = jnp.swapaxes(conc_ref[:, block_cells(block), :], 0, 1)
        for d in range(BLOCK):
            pieces = [by_depth[d, :, j * LANES : (j + 1) * LANES] for j in range(tiles)]
            pad_cells(pad_ref, block * BLOCK + d, pieces)

    pad(0)
    for copy in copies[:3]:
        copy.wait()
    line_by_row = tile_of([line_ref[e].astype(F32) for e in range(SUB)], rows)
    masks = [line_by_row == k for k in range(emissions)]
    by_lane = [tile_of([att_ref[k, e] for e in range(SUB)], lanes & 7) for k in range(emissions + 1)]
    fill_matrix(mat, -by_lane[0], select_line(masks, by_lane[1:]), False, True)
    for k in range(emissions + 1):
        const_ref[k] = tile_of([att_ref[k, e] for e in range(SUB)], rows)
    const_ref[SCALE] = tile_of([yield_ref[e] for e in range(SUB)], rows)
    const_ref[LINE_ROWS] = line_by_row
    const_ref[LINE_LANES] = tile_of([line_ref[e].astype(F32) for e in range(SUB)], lanes & 7)
    copies[3].wait()
    for block in range(blocks):
        if block:
            pad(block)
        index_copies[block].wait()
        shear(field, pad_ref, index_ref, weight_ref, block, range(views), tiles)
        transmit(u_ref, n_ref, field, mat, const_ref, carry, block, (field_sum, emit_sum))
    for copy in copies[4:]:
        copy.wait()
    for v in range(views):
        shifts = jnp.zeros((SUB, LANES), jnp.int32)
        for octet in range(slab // SUB):
            values = column_ref[v, octet * SUB : (octet + 1) * SUB, :] - lanes
            shifts = jnp.where(lanes == octet, values, shifts)
        weight_ref[v, slab : slab + SUB, 0:LANES] = shifts.astype(F32)
    columns = [const_ref[k] for k in range(emissions + 1)]
    masks = [const_ref[LINE_ROWS] == k for k in range(emissions)]
    scale = const_ref[SCALE] * (1.0 / cells)
    share = width // 2
    core = lax.axis_index("near") & 1
    for r in range(2):
        for j in range(share // LANES):
            start = pl.multiple_of((core ^ r) * share + j * LANES, LANES)
            span = slice(j * LANES, (j + 1) * LANES)
            totals = jnp.zeros((SUB, LANES), F32)
            for v in range(views):
                values = field_sum[v, :, pl.ds(start, LANES)]
                sums = [jnp.sum(column * values, axis=0, keepdims=True) for column in columns]
                for k in range(emissions + 1):
                    totals = jnp.where(rows == v * (emissions + 1) + k, sums[k], totals)
                line_total = select_line(masks, [jnp.broadcast_to(value, rows.shape) for value in sums[1:]])
                signal = scale * emit_sum[v, :, pl.ds(start, LANES)] * jnp.exp(-line_total)
                state_refs[r][(v + 1) * SUB : (v + 2) * SUB, span] = signal
            state_refs[r][0:SUB, span] = jnp.exp(-totals)
    for v in range(views):
        target_ref[v * SUB : (v + 1) * SUB, :] = measured_ref[v].reshape(SUB, width)


def forward(conc, index, weights, scalars, measured, cells):
    views, slab, width = weights.shape
    attenuation, line_energy, yields = scalars
    values = pltpu.VMEM((views, slab * SUB, width), F32)
    padded = pltpu.VMEM((slab, SUB, width + 5 * LANES), F32)
    state = pltpu.VMEM(((views + 1) * SUB, width // 2), F32)
    line = pltpu.VMEM((views, SUB, width), F32)
    operands = [in_hbm(value) for value in (attenuation, line_energy, yields, index, conc, weights, measured)]
    return pl.pallas_call(
        functools.partial(forward_kernel, cells),
        in_specs=[HBM] * len(operands),
        out_specs=[VMEM] * 9,
        out_shape=[
            values,
            values,
            pltpu.VMEM((LINE_LANES + 1, SUB, LANES), F32),
            pltpu.VMEM((views * SUB, width), F32),
            pltpu.VMEM(MATRIX, BF16),
            padded,
            pltpu.VMEM((views, slab + SUB, width), F32),
            state,
            state,
        ],
        scratch_shapes=[
            pltpu.VMEM((SUB, slab, width), F32),
            pltpu.VMEM((views, ROWS, width), F32),
            line,
            line,
            line,
            pltpu.VMEM(measured.shape, F32),
            pltpu.VMEM((views, slab, LANES), jnp.int32),
            pltpu.SMEM(attenuation.shape, F32),
            pltpu.SMEM(line_energy.shape, jnp.int32),
            pltpu.SMEM(yields.shape, F32),
            pltpu.SMEM((views, slab, LANES), jnp.int32),
            pltpu.SemaphoreType.DMA((2 * (slab // BLOCK) + 6,)),
        ],
        compiler_params=pltpu.CompilerParams(vmem_limit_bytes=16 * MIB),
        name="forward",
    )(*operands)


def column_in(package_any, views, index_ref, sem):
    first = package_any.shape[1] - SUB
    source = package_any.at[views, pl.ds(first, SUB), pl.ds(0, index_ref.shape[2])]
    return pltpu.make_async_copy(source, index_ref, sem)


def backward_matrix(mat_ref, const_ref):
    masks = [const_ref[LINE_LANES] == k for k in range(SCALE - 1)]
    columns = [const_ref[k] for k in range(SCALE)]
    fill_matrix(mat_ref, -columns[0], select_line(masks, columns[1:]), True, False)


def forward_other_kernel(view, weight_ref, mat, pad_ref, const_ref, order_ref, *refs):
    u_ref, n_ref, back_mat, field, carry, index_ref, sem = refs
    _, slab, width = weight_ref.shape
    slab = slab - SUB
    copy = column_in(weight_ref, pl.ds(view, 1), index_ref, sem)
    copy.start()
    carry[...] = jnp.zeros_like(carry)
    backward_matrix(back_mat, const_ref)
    copy.wait()
    for block in range(slab // BLOCK):
        shear(field, pad_ref, index_ref, weight_ref.at[pl.ds(view, 1)], block, (0,), width // LANES)
        transmit(u_ref, n_ref, field, mat, const_ref, carry, block, None)


def forward_other(view, weights, mat, pads, const, after):
    _, slab, width = weights.shape
    slab = slab - SUB
    values = pltpu.VMEM((1, slab * SUB, width), F32)
    return pl.pallas_call(
        functools.partial(forward_other_kernel, view),
        in_specs=[VMEM] * 5,
        out_specs=[VMEM] * 3,
        out_shape=[values, values, pltpu.VMEM(MATRIX, BF16)],
        scratch_shapes=[
            pltpu.VMEM((1, ROWS, width), F32),
            pltpu.VMEM((1, SUB, width), F32),
            pltpu.SMEM((1, SUB, LANES), F32),
            pltpu.SemaphoreType.DMA,
        ],
        compiler_params=pltpu.CompilerParams(vmem_limit_bytes=8 * MIB),
        name="forward_other",
    )(weights, mat, pads, const, after)


def line_rows(tile, base, masks):
    shape = masks[0].shape
    return select_line(masks, [jnp.broadcast_to(tile[base + 1 + k : base + 2 + k], shape) for k in range(len(masks))])


def incident_rows(tile, step):
    rows = row_ids(tile.shape[1])
    result = jnp.broadcast_to(tile[0:1], tile.shape)
    for base in range(step, SUB, step):
        result = jnp.where(rows >= base, jnp.broadcast_to(tile[base : base + 1], tile.shape), result)
    return result


def row_masks(const_ref, width):
    tile = const_ref[LINE_ROWS]
    return [jnp.concatenate([tile] * (width // LANES), axis=1) == k for k in range(SCALE - 1)]


def factors_of(mine, theirs, bit):
    mine_factor = jnp.where(bit == 0, theirs, incident_rows(theirs, SCALE))
    return mine_factor, jnp.where(bit == 0, incident_rows(mine, SCALE), mine)


def merged_state(mine, theirs, bit, masks):
    mine_factor, theirs_factor = factors_of(mine[0:SUB], theirs[0:SUB], bit)
    result = [mine[0:SUB] * theirs[0:SUB]]
    for v in range(mine.shape[0] // SUB - 1):
        span = slice((v + 1) * SUB, (v + 2) * SUB)
        result.append(
            mine[span] * line_rows(mine_factor, v * SCALE, masks)
            + theirs[span] * line_rows(theirs_factor, v * SCALE, masks)
        )
    return result


def weighted_rows(factor, state, misfits, masks):
    rows = row_ids(state.shape[1])
    result = jnp.zeros((SUB, state.shape[1]), F32)
    for v, misfit in enumerate(misfits):
        base = v * SCALE
        value = misfit * state[(v + 1) * SUB : (v + 2) * SUB] * line_rows(factor, base, masks)
        whole = None
        for k, mask in enumerate(masks):
            part = jnp.sum(jnp.where(mask, value, 0.0), axis=0, keepdims=True)
            result = jnp.where(rows == base + 1 + k, part, result)
            whole = part if whole is None else whole + part
        result = jnp.where(rows == base, whole, result)
    return result


def children(factor, sums, mine, theirs, bit, misfits, masks):
    mine_factor, theirs_factor = factors_of(mine[0:SUB], theirs[0:SUB], bit)
    if factor is not None:
        mine_factor, theirs_factor = factor * mine_factor, factor * theirs_factor
    behind = (row_ids(mine.shape[1]) & (SCALE - 1)) == 0
    mine_sums = jnp.where(behind == (bit == 0), weighted_rows(theirs_factor, theirs, misfits, masks), 0.0)
    theirs_sums = jnp.where(behind == (bit == 1), weighted_rows(mine_factor, mine, misfits, masks), 0.0)
    if sums is not None:
        mine_sums, theirs_sums = sums + mine_sums, sums + theirs_sums
    return (mine_factor, mine_sums), (theirs_factor, theirs_sums)


def call_small(kernel, name, outs, operands, scratch=()):
    return pl.pallas_call(
        kernel,
        in_specs=[VMEM] * len(operands),
        out_specs=[VMEM] * len(outs),
        out_shape=[pltpu.VMEM(shape, F32) for shape in outs],
        scratch_shapes=[pltpu.VMEM(shape, F32) for shape in scratch],
        compiler_params=pltpu.CompilerParams(vmem_limit_bytes=4 * MIB),
        name=name,
    )(*operands)


def store_rows(ref, tiles):
    for i, tile in enumerate(tiles):
        ref[i * SUB : (i + 1) * SUB, :] = tile


def merge_kernel(shift, const_ref, mine_ref, theirs_ref, *refs):
    bit = (depth_place() >> shift) & 1
    store_rows(refs[-1], merged_state(mine_ref[...], theirs_ref[...], bit, row_masks(const_ref, mine_ref.shape[1])))


def merge_four_kernel(const_ref, mine_ref, both_ref, far_ref, near_ref, pair_ref, other_ref, whole_ref):
    place = depth_place()
    masks = row_masks(const_ref, mine_ref.shape[1])
    pair = merged_state(mine_ref[...], near_ref[...], (place >> 1) & 1, masks)
    other = merged_state(far_ref[...], both_ref[...], (place >> 1) & 1, masks)
    store_rows(pair_ref, pair)
    store_rows(other_ref, other)
    store_rows(whole_ref, merged_state(pair_ref[...], other_ref[...], (place >> 2) & 1, masks))


def depth_place():
    return lax.axis_index("far") * NEAR + lax.axis_index("near")


def result_kernel(levels, const_ref, target_ref, *refs):
    states, outs = refs[: 2 * levels], refs[-4:]
    depth, width = states[0].shape
    views = depth // SUB - 1
    place = depth_place()
    size = 2 * LANES
    start = (place & 1) * width
    masks = row_masks(const_ref, size)
    behind = (row_ids(size) & (SCALE - 1)) == 0
    for c in range(width // size):
        span = slice(c * size, (c + 1) * size)
        factor, sums = None, None
        for level in reversed(range(levels)):
            mine, theirs = states[2 * level][:, span], states[2 * level + 1][:, span]
            bit = (place >> level) & 1
            if level == levels - 1:
                signals = merged_state(mine, theirs, bit, masks)[1:]
                there = pl.ds(pl.multiple_of(start + c * size, LANES), size)
                misfits = [signals[v] - target_ref[v * SUB : (v + 1) * SUB, there] for v in range(views)]
            contexts = children(factor, sums, mine, theirs, bit, misfits, masks)
            factor, sums = contexts[0]
        for i, (state, (factor, sums)) in enumerate(zip((mine, theirs), contexts)):
            own = jnp.where(behind, weighted_rows(factor, state, misfits, masks), 0.0)
            rest = [factor * state[0:SUB], sums + own]
            for ref, first in ((outs[i], signals), (outs[2 + i], misfits)):
                for j, tile in enumerate(first + rest):
                    ref[j * SUB : (j + 1) * SUB, span] = tile


def assemble_kernel(target_ref, here_ref, there_ref, package_ref, signal_ref):
    half = here_ref.shape[1]
    count = signal_ref.shape[0]
    at = pl.multiple_of((lax.axis_index("near") & 1) * half, LANES)
    for ref, start in ((here_ref, at), (there_ref, pl.multiple_of(half - at, LANES))):
        span = pl.ds(start, half)
        signal_ref[:, span] = ref[0:count, :]
        package_ref[0:count, span] = ref[0:count, :] - target_ref[:, span]
        package_ref[count:, span] = ref[count:, :]


def assemble_other_kernel(here_ref, there_ref, package_ref):
    half = here_ref.shape[1]
    at = pl.multiple_of((lax.axis_index("near") & 1) * half, LANES)
    package_ref[:, pl.ds(at, half)] = here_ref[...]
    package_ref[:, pl.ds(pl.multiple_of(half - at, LANES), half)] = there_ref[...]


def backward_kernel(places, cells, finish, given, const_ref, package_ref, weight_ref, *refs):
    count = len(places)
    if given:
        mat, refs = refs[0], refs[1:]
    u_refs, n_refs, refs = refs[:count], refs[count : 2 * count], refs[2 * count :]
    if finish:
        signal_ref, refs = refs[0], refs[1:]
        prior, refs = refs[: finish - 1], refs[finish - 1 :]
        grad_hbm, signal_hbm, cell_ref, grad_ref, signal_rows = refs[:5]
        refs = refs[5:]
    else:
        left_sum, diff_sum, refs = refs[0], refs[1], refs[2:]
    gain, carry, scaled, left_pad, diff_pad, index_ref, sems = refs[-7:]
    _, slab, width = weight_ref.shape
    slab = slab - SUB
    emissions = SCALE - 1
    tiles = width // LANES
    blocks = slab // BLOCK
    lanes, rows = lane_ids(), row_ids()
    shift_copy = column_in(weight_ref, pl.ds(0, count), index_ref, sems.at[blocks])
    shift_copy.start()
    if finish:
        for v in range(signal_rows.shape[0]):
            signal_rows[v] = signal_ref[v * SUB : (v + 1) * SUB, :].reshape(SUB, 1, width)
        signal_copy = pltpu.make_async_copy(signal_rows, signal_hbm, sems.at[blocks + 1])
        signal_copy.start()
        out_copies = [
            pltpu.make_async_copy(grad_ref.at[b], grad_hbm.at[:, pl.ds(b * BLOCK, BLOCK), :], sems.at[b])
            for b in range(blocks)
        ]
    if not given:
        mat = refs[0]
        backward_matrix(mat, const_ref)
    masks = [const_ref[LINE_ROWS] == k for k in range(emissions)]
    scale = const_ref[SCALE]
    columns = [const_ref[k] * cells for k in range(emissions + 1)]
    for j in range(tiles):
        span = slice(j * LANES, (j + 1) * LANES)
        factor = package_ref[count * SUB : (count + 1) * SUB, span]
        sums = package_ref[(count + 1) * SUB : (count + 2) * SUB, span]
        for v in range(count):
            base = v * SCALE
            gain[v, :, span] = package_ref[v * SUB : (v + 1) * SUB, span] * scale * line_rows(factor, base, masks)
            back = columns[0] * jnp.broadcast_to(sums[base : base + 1], rows.shape)
            for k in range(1, emissions + 1):
                back = back + columns[k] * jnp.broadcast_to(sums[base + k : base + k + 1], rows.shape)
            carry[v, :, span] = back
    wide_masks = row_masks(const_ref, CHUNK)
    wide_columns = [jnp.concatenate([const_ref[k]] * (CHUNK // LANES), axis=1) for k in range(1, emissions + 1)]
    zero = jnp.zeros((SUB, LANES), F32)
    for ref in (left_pad, diff_pad):
        edge = jnp.zeros(ref.shape[:3] + (LANES,), F32)
        ref[:, :, :, 0:LANES] = edge
        ref[:, :, :, width + 2 * LANES :] = edge

    def place(v, d, cell, first):
        _, rest = shift_of(index_ref, v, cell, width)
        stay = lanes >= rest
        turn = rest & (LANES - 1)
        at = (first + d) * SUB
        plain = [scaled[v, at : at + SUB, j * LANES : (j + 1) * LANES] for j in range(tiles)]
        moved = [plain[j] * weight_ref[v, cell : cell + 1, j * LANES : (j + 1) * LANES] for j in range(tiles)]
        for ref, values in ((left_pad, plain), (diff_pad, moved)):
            turned = [zero] + [pltpu.roll(value, turn, 1) for value in values] + [zero]
            for j in range(tiles + 1):
                ref[v, first + d, :, (j + 1) * LANES : (j + 2) * LANES] = jnp.where(stay, turned[j + 1], turned[j])

    def gathered(ref, before, cell, slot):
        sums = [None] * (tiles + 2)
        if before is not None:
            sums = [before[cell, :, j * LANES : (j + 1) * LANES] for j in range(tiles + 2)]
        for v in range(count):
            whole, _ = shift_of(index_ref, v, cell, width)
            for j in range(tiles + 2):
                start = pl.multiple_of((1 + j - whole) * LANES, LANES)
                value = ref[v, slot, :, pl.ds(start, LANES)]
                sums[j] = value if sums[j] is None else sums[j] + value
        return sums

    def folded(sums):
        low = jnp.sum(sums[0], axis=1, keepdims=True)
        beyond = sums[tiles + 1] + jnp.where(lanes == LANES - 1, sums[tiles], 0.0)
        high = jnp.sum(beyond, axis=1, keepdims=True)
        core = sums[1 : tiles + 1]
        core[0] = core[0] + jnp.where(lanes == 0, low, 0.0)
        core[-1] = jnp.where(lanes == LANES - 1, 0.0, core[-1] + jnp.where(lanes == LANES - 2, high, 0.0))
        return core

    for block in range(blocks):
        first = block % 2 * BLOCK
        for v in range(count):
            for c in range(width // CHUNK):
                span = slice(c * CHUNK, (c + 1) * CHUNK)
                factor = gain[v, :, span][None]
                weighted = n_refs[v][places[v], block_rows(block), span].reshape(BLOCK, SUB, CHUNK) * factor
                direct = u_refs[v][places[v], block_rows(block), span].reshape(BLOCK, SUB, CHUNK) * factor
                lines = multiply(mat, weighted.reshape(ROWS, CHUNK)).reshape(BLOCK, SUB, CHUNK)
                lines = lines + carry[v, :, span][None]
                scaled[v, first * SUB : first * SUB + ROWS, span] = (direct - lines).reshape(ROWS, CHUNK)
                if block + 1 < blocks:
                    total = lines[-1]
                    for mask, column in zip(wide_masks, wide_columns):
                        part = jnp.sum(jnp.where(mask, weighted[-1], 0.0), axis=0, keepdims=True)
                        total = total + column * part
                    carry[v, :, span] = total
        if block == 0:
            shift_copy.wait()
        for v in range(count):
            for d in range(BLOCK):
                place(v, d, block * BLOCK + d, first)
        for d in range(BLOCK):
            cell = block * BLOCK + d
            left = gathered(left_pad, prior[0] if finish > 1 else None, cell, first + d)
            diff = gathered(diff_pad, prior[1] if finish > 1 else None, cell, first + d)
            if not finish:
                for j in range(tiles + 2):
                    left_sum[cell, :, j * LANES : (j + 1) * LANES] = left[j]
                    diff_sum[cell, :, j * LANES : (j + 1) * LANES] = diff[j]
                continue
            left, diff = folded([left[j] - diff[j] for j in range(tiles + 2)]), folded(diff)
            turned = [zero] + [pltpu.roll(value, 1, 1) for value in diff]
            for j in range(tiles):
                value = left[j] + jnp.where(lanes == 0, turned[j], turned[j + 1])
                cell_ref[first + d, :, j * LANES : (j + 1) * LANES] = value
        if finish:
            grad_ref[block] = jnp.swapaxes(cell_ref[first : first + BLOCK], 0, 1)
            out_copies[block].start()
    if finish:
        for copy in out_copies + [signal_copy]:
            copy.wait()


def backward(package, const, weights, mats, pieces, cells, signal, prior):
    views, slab, width = weights.shape
    slab = slab - SUB
    blocks = slab // BLOCK
    finish = signal is not None
    line = pltpu.VMEM((views, SUB, width), F32)
    sums = pltpu.VMEM((slab, SUB, width + 2 * LANES), F32)
    scratch = [] if mats else [pltpu.VMEM(MATRIX, BF16)]
    scratch += [
        line,
        line,
        pltpu.VMEM((views, 2 * ROWS, width), F32),
        pltpu.VMEM((views, 2 * BLOCK, SUB, width + 3 * LANES), F32),
        pltpu.VMEM((views, 2 * BLOCK, SUB, width + 3 * LANES), F32),
        pltpu.SMEM((views, SUB, LANES), F32),
        pltpu.SemaphoreType.DMA((blocks + 2,)),
    ]
    operands = [const, package, weights, *mats, *[u for u, _, _ in pieces], *[n for _, n, _ in pieces]]
    if finish:
        operands += [signal[0], *prior]
        scratch = [
            pltpu.VMEM((2 * BLOCK, SUB, width), F32),
            pltpu.VMEM((blocks, SUB, BLOCK, width), F32),
            pltpu.VMEM(signal[1], F32),
        ] + scratch
    return pl.pallas_call(
        functools.partial(
            backward_kernel, tuple(at for _, _, at in pieces), cells, 1 + len(prior) if finish else 0, len(mats)
        ),
        in_specs=[VMEM] * len(operands),
        out_specs=[HBM, HBM] if finish else [VMEM, VMEM],
        out_shape=[pltpu.HBM((SUB, slab, width), F32), pltpu.HBM(signal[1], F32)] if finish else [sums, sums],
        scratch_shapes=scratch,
        compiler_params=pltpu.CompilerParams(vmem_limit_bytes=16 * MIB),
        name="backward_last" if finish else "backward_first",
    )(*operands)


def body(concentration, shear_index, shear_weight, attenuation, yields, line_energy, measured):
    elements, _, slab, width = concentration.shape
    views = shear_weight.shape[0]
    emissions = attenuation.shape[0] - 1
    groups = lax.axis_size("far")
    both = lax.axis_size("views") == 2
    cells = float(slab * groups * NEAR)
    conc = concentration.reshape(elements, slab, width)
    scalars = (attenuation, line_energy, yields)

    def to_other(value):
        return lax.ppermute(value, "views", [(0, 1), (1, 0)])

    fillers = []

    def fill(after):
        if not both or len(fillers) == views:
            return ()
        fillers.append(forward_other(len(fillers), other_weight, mat, pads, const, after))
        return (fillers[-1][2],)

    u, n, const, target, mat, pads, weight, state, send = forward(
        conc, shear_index, shear_weight, scalars, measured, cells
    )
    def swap(value, axis, step):
        return lax.ppermute(value, axis, [(s, s ^ step) for s in range(lax.axis_size(axis))])

    states = [state, swap(send, "near", 1)]
    if both:
        other_weight = to_other(weight)
    tokens = ()
    levels = groups.bit_length() + 1

    def merge(level):
        (merged,) = call_small(
            functools.partial(merge_kernel, level), "merge", [state.shape], (const, *states[-2:])
        )
        return merged

    state = merge(0)
    pairs = [(s, s ^ 6) for s in range(groups * NEAR)]
    four = (state, lax.ppermute(state, ("far", "near"), pairs), swap(state, "far", 1), swap(state, "near", 2))
    pair, other, whole = call_small(merge_four_kernel, "merge_four", [state.shape] * 3, (const, *four))
    states += [state, four[3], pair, other]
    state = whole
    for level in range(3, levels):
        states += [state, swap(state, "far", 1 << (level - 2))]
        if level < levels - 1:
            state = merge(level)
    for _ in range(views):
        tokens += fill(state)
    half = ((views + 2) * SUB, width // 2)
    here, there, here_other, there_other = call_small(
        functools.partial(result_kernel, levels), "result", [half] * 4, (const, target, *states, *tokens)
    )
    there = swap(there, "near", 1)
    if both:
        pairs = [(v * NEAR + s, (1 - v) * NEAR + (s ^ 1)) for v in range(2) for s in range(NEAR)]
        here_other = to_other(here_other)
        there_other = lax.ppermute(there_other, ("views", "near"), pairs)
    package = (half[0], width)
    shapes = [package, target.shape]
    package, signal = call_small(assemble_kernel, "assemble", shapes, (target, here, there))
    own = [(u, n, v) for v in range(views)]
    signal = (signal, measured.shape)
    if both:
        sums = backward(package, const, weight, tokens[:1], own, cells, None, ())
        (other_package,) = call_small(
            assemble_other_kernel, "assemble_other", [package.shape], (here_other, there_other)
        )
        pieces = [(fillers[v][0], fillers[v][1], 0) for v in range(views)]
        gradient, signal = backward(other_package, const, other_weight, tokens[:1], pieces, cells, signal, sums)
    else:
        gradient, signal = backward(package, const, weight, (), own, cells, signal, ())
        gradient = lax.psum(gradient, "views")
    return gradient.reshape(concentration.shape), signal


def solution(mesh):
    views, depth = mesh.shape["views"], mesh.shape["depth"]
    devices = mesh.devices.reshape(views, depth // NEAR, NEAR)
    split = jax.sharding.Mesh(devices, ("views", "far", "near"))
    depths = ("far", "near")
    return jax.shard_map(
        body,
        mesh=split,
        in_specs=(
            P(None, None, depths, None),
            P("views", depths, None),
            P("views", depths, None),
            P(),
            P(),
            P(),
            P("views", None, None, None),
        ),
        out_specs=(P(None, None, depths, None), P("views", None, None, None)),
        check_vma=False,
    )
```

```python
import functools

import jax
import jax.numpy as jnp
from jax import lax
from jax.experimental import pallas as pl
from jax.experimental.pallas import tpu as pltpu
from jax.sharding import PartitionSpec as P

LANES = 128
SUB = 8
BLOCK = 8
ROWS = BLOCK * SUB
NEAR = 4
CHUNK = 256
MIB = 1024 * 1024
F32 = jnp.float32
BF16 = jnp.bfloat16
HBM = pl.BlockSpec(memory_space=pltpu.HBM)
VMEM = pl.BlockSpec(memory_space=pltpu.VMEM)
SCALE, LINE_ROWS, LINE_LANES = 4, 5, 6
ANY = pl.BlockSpec(memory_space=pl.ANY)


def in_hbm(value):
    return pltpu.with_memory_space_constraint(value, pltpu.HBM)


def lane_ids(width=LANES):
    return lax.broadcasted_iota(jnp.int32, (SUB, width), 1)


def row_ids(width=LANES):
    return lax.broadcasted_iota(jnp.int32, (SUB, width), 0)


def tile_of(values, ids):
    tile = jnp.zeros(ids.shape, F32)
    for e in range(SUB):
        tile = jnp.where(ids == e, values[e], tile)
    return tile


def select_line(masks, values):
    result = values[0]
    for mask, value in zip(masks[1:], values[1:]):
        result = jnp.where(mask, value, result)
    return result


def fill_matrix(mat_ref, first_tile, second_tile, first_incl, second_incl):
    depth = (lane_ids() & (ROWS - 1)) >> 3
    tiles = []
    for d in range(BLOCK):
        one = jnp.where(depth <= d if first_incl else depth < d, first_tile, 0.0)
        two = jnp.where(depth <= d if second_incl else depth < d, second_tile, 0.0)
        tiles.append(one + two)
    tiles.append(first_tile + second_tile)
    tiles.append(jnp.zeros((SUB, LANES), F32))
    whole = jnp.concatenate(tiles, axis=0)
    high = whole.astype(BF16)
    mat_ref[:, 0:LANES] = high
    mat_ref[:, LANES : 2 * LANES] = (whole - high.astype(F32)).astype(BF16)


def multiply(mat_ref, values):
    high = values.astype(BF16)
    low = (values - high.astype(F32)).astype(BF16)
    stacked = jnp.concatenate([high, low, high], axis=0)
    product = jnp.dot(mat_ref[:, 0 : 3 * ROWS], stacked, preferred_element_type=F32)
    return product[0:ROWS], product[ROWS : ROWS + SUB]


MATRIX = (ROWS + 2 * SUB, 2 * LANES)


def copies_in(pairs, sems):
    return [pltpu.make_async_copy(source, target, sems.at[i]) for i, (source, target) in enumerate(pairs)]


def block_rows(block):
    return slice(block * ROWS, (block + 1) * ROWS)


def block_cells(block):
    return slice(block * BLOCK, (block + 1) * BLOCK)


def offset_of(index_ref, v, cell, width):
    if index_ref.dtype == jnp.int32:
        at = index_ref[v, cell, 0]
    else:
        at = index_ref[v, cell % SUB, cell // SUB].astype(jnp.int32)
    return at - (width // 2 - LANES)


def shift_of(index_ref, v, cell, width):
    offset = offset_of(index_ref, v, cell, width)
    whole = jnp.minimum(offset >> 7, 1)
    return whole, offset - (whole << 7)


def pad_cells(pad_ref, cell, pieces):
    tiles = len(pieces)

    def spread(piece, lane):
        return jnp.broadcast_to(piece[:, lane : lane + 1], (SUB, LANES))

    last = spread(pieces[-1], LANES - 1)
    edges = [spread(pieces[0], 1), spread(pieces[-1], LANES - 2)]
    for j, piece in enumerate([spread(pieces[0], 0)] + pieces + [last, last] + edges):
        pad_ref[cell, :, j * LANES : (j + 1) * LANES] = piece


def shear(field, pad_ref, index_ref, weight_ref, block, views, tiles):
    lanes = lane_ids()
    for i, v in enumerate(views):
        for d in range(BLOCK):
            cell = block * BLOCK + d
            offset = offset_of(index_ref, v, cell, tiles * LANES)
            whole, rest = offset >> 7, offset & (LANES - 1)
            starts = [pl.multiple_of((whole + j) * LANES, LANES) for j in range(tiles + 1)]
            values = [pad_ref[cell, :, pl.ds(start, LANES)] for start in starts]

            def turned(rest):
                stay = lanes < LANES - rest
                turn = (LANES - rest) & (LANES - 1)
                rolled = [pltpu.roll(value, turn, 1) for value in values]
                return [jnp.where(stay, rolled[j], rolled[j + 1]) for j in range(tiles)]

            left, right = turned(rest), turned(rest + 1)
            second, last_but_one = [
                pad_ref[cell, :, (tiles + 3 + j) * LANES : (tiles + 4 + j) * LANES] for j in range(2)
            ]
            right[0] = jnp.where(lanes < LANES - offset, second, right[0])
            for j in (tiles - 2, tiles - 1):
                first = (tiles + 1 - j) * LANES - 1 - offset
                left[j] = jnp.where(lanes >= first, last_but_one, left[j])
            for j in range(tiles):
                span = slice(j * LANES, (j + 1) * LANES)
                weight = weight_ref[i, cell : cell + 1, span]
                field[i, d * SUB : (d + 1) * SUB, span] = left[j] + weight * (right[j] - left[j])


def transmit(u_ref, n_ref, field, mat, carry, block, sums):
    views, _, width = field.shape
    for v in range(views):
        for c in range(width // CHUNK):
            span = slice(c * CHUNK, (c + 1) * CHUNK)
            value = field[v, :, span]
            lines, total = multiply(mat, value)
            before = carry[v, :, span]
            through = jnp.exp(lines.reshape(BLOCK, SUB, CHUNK) + before[None])
            value = value.reshape(BLOCK, SUB, CHUNK)
            emit = value * through
            u_ref[v, block_rows(block), span] = through.reshape(ROWS, CHUNK)
            n_ref[v, block_rows(block), span] = emit.reshape(ROWS, CHUNK)
            carry[v, :, span] = before + total
            if sums:
                sums[0][v, :, span] += jnp.sum(value, axis=0)
                sums[1][v, :, span] += jnp.sum(emit, axis=0)


def forward_kernel(cells, *refs):
    att_hbm, line_hbm, yield_hbm, index_hbm, conc_hbm, weight_hbm, measured_hbm = refs[:7]
    u_ref, n_ref, const_ref, target_ref, mat, pad_ref, weight_ref = refs[7:14]
    state_refs = refs[14:16]
    refs = refs[16:]
    conc_ref, field, carry, field_sum, emit_sum, measured_ref, column_ref = refs[:7]
    att_ref, line_ref, yield_ref, index_ref, sems = refs[7:]
    views, _, width = weight_ref.shape
    slab = conc_ref.shape[1]
    emissions = att_ref.shape[0] - 1
    tiles = width // LANES
    blocks = slab // BLOCK
    lanes, rows = lane_ids(), row_ids()
    conc_copies = [
        pltpu.make_async_copy(
            conc_hbm.at[:, pl.ds(b * BLOCK, BLOCK), :], conc_ref.at[:, pl.ds(b * BLOCK, BLOCK), :], sems.at[b]
        )
        for b in range(blocks)
    ]
    pairs = [
        (att_hbm, att_ref),
        (line_hbm, line_ref),
        (yield_hbm, yield_ref),
        (weight_hbm, weight_ref.at[:, pl.ds(0, slab), :]),
        (measured_hbm, measured_ref),
        (index_hbm.at[:, :, pl.ds(width // 2, LANES)], column_ref),
    ]
    copies = copies_in(pairs, sems.at[pl.ds(2 * blocks, len(pairs))])
    index_copies = [
        pltpu.make_async_copy(
            index_hbm.at[:, pl.ds(b * BLOCK, BLOCK), pl.ds(width // 2, LANES)],
            index_ref.at[:, pl.ds(b * BLOCK, BLOCK), :],
            sems.at[blocks + b],
        )
        for b in range(blocks)
    ]
    for copy in conc_copies[:1] + copies[:3] + index_copies[:1] + copies[3:4]:
        copy.start()
    for copy in conc_copies[1:] + index_copies[1:] + copies[4:]:
        copy.start()
    for ref in (carry, field_sum, emit_sum):
        ref[...] = jnp.zeros_like(ref)

    def pad(block):
        conc_copies[block].wait()
        by_depth = jnp.swapaxes(conc_ref[:, block_cells(block), :], 0, 1)
        for d in range(BLOCK):
            pieces = [by_depth[d, :, j * LANES : (j + 1) * LANES] for j in range(tiles)]
            pad_cells(pad_ref, block * BLOCK + d, pieces)

    pad(0)
    for copy in copies[:3]:
        copy.wait()
    line_by_row = tile_of([line_ref[e].astype(F32) for e in range(SUB)], rows)
    masks = [line_by_row == k for k in range(emissions)]
    by_lane = [tile_of([att_ref[k, e] for e in range(SUB)], lanes & 7) for k in range(emissions + 1)]
    fill_matrix(mat, -by_lane[0], select_line(masks, by_lane[1:]), False, True)
    for k in range(emissions + 1):
        const_ref[k] = tile_of([att_ref[k, e] for e in range(SUB)], rows)
    const_ref[SCALE] = tile_of([yield_ref[e] for e in range(SUB)], rows)
    const_ref[LINE_ROWS] = line_by_row
    const_ref[LINE_LANES] = tile_of([line_ref[e].astype(F32) for e in range(SUB)], lanes & 7)
    copies[3].wait()
    for block in range(blocks):
        if block:
            pad(block)
        index_copies[block].wait()
        shear(field, pad_ref, index_ref, weight_ref, block, range(views), tiles)
        transmit(u_ref, n_ref, field, mat, carry, block, (field_sum, emit_sum))
    for copy in copies[4:]:
        copy.wait()
    for v in range(views):
        shifts = jnp.zeros((SUB, LANES), jnp.int32)
        for octet in range(slab // SUB):
            values = column_ref[v, octet * SUB : (octet + 1) * SUB, :] - lanes
            shifts = jnp.where(lanes == octet, values, shifts)
        weight_ref[v, slab : slab + SUB, 0:LANES] = shifts.astype(F32)
    columns = [const_ref[k] for k in range(emissions + 1)]
    masks = [const_ref[LINE_ROWS] == k for k in range(emissions)]
    scale = const_ref[SCALE] * (1.0 / cells)
    share = width // 2
    core = lax.axis_index("near") & 1
    for r in range(2):
        for j in range(share // LANES):
            start = pl.multiple_of((core ^ r) * share + j * LANES, LANES)
            span = slice(j * LANES, (j + 1) * LANES)
            totals = jnp.zeros((SUB, LANES), F32)
            for v in range(views):
                values = field_sum[v, :, pl.ds(start, LANES)]
                sums = [jnp.sum(column * values, axis=0, keepdims=True) for column in columns]
                for k in range(emissions + 1):
                    totals = jnp.where(rows == v * (emissions + 1) + k, sums[k], totals)
                line_total = select_line(masks, [jnp.broadcast_to(value, rows.shape) for value in sums[1:]])
                signal = scale * emit_sum[v, :, pl.ds(start, LANES)] * jnp.exp(-line_total)
                state_refs[r][(v + 1) * SUB : (v + 2) * SUB, span] = signal
            state_refs[r][0:SUB, span] = jnp.exp(-totals)
    for v in range(views):
        target_ref[v * SUB : (v + 1) * SUB, :] = measured_ref[v].reshape(SUB, width)


def forward(conc, index, weights, scalars, measured, cells):
    views, slab, width = weights.shape
    attenuation, line_energy, yields = scalars
    values = pltpu.VMEM((views, slab * SUB, width), F32)
    padded = pltpu.VMEM((slab, SUB, width + 5 * LANES), F32)
    state = pltpu.VMEM(((views + 1) * SUB, width // 2), F32)
    line = pltpu.VMEM((views, SUB, width), F32)
    operands = [in_hbm(value) for value in (attenuation, line_energy, yields, index, conc, weights, measured)]
    return pl.pallas_call(
        functools.partial(forward_kernel, cells),
        in_specs=[HBM] * len(operands),
        out_specs=[VMEM] * 9,
        out_shape=[
            values,
            values,
            pltpu.VMEM((LINE_LANES + 1, SUB, LANES), F32),
            pltpu.VMEM((views * SUB, width), F32),
            pltpu.VMEM(MATRIX, BF16),
            padded,
            pltpu.VMEM((views, slab + SUB, width), F32),
            state,
            state,
        ],
        scratch_shapes=[
            pltpu.VMEM((SUB, slab, width), F32),
            pltpu.VMEM((views, ROWS, width), F32),
            line,
            line,
            line,
            pltpu.VMEM(measured.shape, F32),
            pltpu.VMEM((views, slab, LANES), jnp.int32),
            pltpu.SMEM(attenuation.shape, F32),
            pltpu.SMEM(line_energy.shape, jnp.int32),
            pltpu.SMEM(yields.shape, F32),
            pltpu.SMEM((views, slab, LANES), jnp.int32),
            pltpu.SemaphoreType.DMA((2 * (slab // BLOCK) + 6,)),
        ],
        compiler_params=pltpu.CompilerParams(vmem_limit_bytes=16 * MIB),
        name="forward",
    )(*operands)


def column_in(package_any, views, index_ref, sem):
    first = package_any.shape[1] - SUB
    source = package_any.at[views, pl.ds(first, SUB), pl.ds(0, index_ref.shape[2])]
    return pltpu.make_async_copy(source, index_ref, sem)


def backward_matrix(mat_ref, const_ref):
    masks = [const_ref[LINE_LANES] == k for k in range(SCALE - 1)]
    columns = [const_ref[k] for k in range(SCALE)]
    fill_matrix(mat_ref, -columns[0], select_line(masks, columns[1:]), True, False)


def forward_other_kernel(view, weight_ref, mat, pad_ref, const_ref, order_ref, *refs):
    u_ref, n_ref, back_mat, field, carry, index_ref, sem = refs
    _, slab, width = weight_ref.shape
    slab = slab - SUB
    copy = column_in(weight_ref, pl.ds(view, 1), index_ref, sem)
    copy.start()
    carry[...] = jnp.zeros_like(carry)
    backward_matrix(back_mat, const_ref)
    copy.wait()
    for block in range(slab // BLOCK):
        shear(field, pad_ref, index_ref, weight_ref.at[pl.ds(view, 1)], block, (0,), width // LANES)
        transmit(u_ref, n_ref, field, mat, carry, block, None)


def forward_other(view, weights, mat, pads, const, after):
    _, slab, width = weights.shape
    slab = slab - SUB
    values = pltpu.VMEM((1, slab * SUB, width), F32)
    return pl.pallas_call(
        functools.partial(forward_other_kernel, view),
        in_specs=[VMEM] * 5,
        out_specs=[VMEM] * 3,
        out_shape=[values, values, pltpu.VMEM(MATRIX, BF16)],
        scratch_shapes=[
            pltpu.VMEM((1, ROWS, width), F32),
            pltpu.VMEM((1, SUB, width), F32),
            pltpu.SMEM((1, SUB, LANES), F32),
            pltpu.SemaphoreType.DMA,
        ],
        compiler_params=pltpu.CompilerParams(vmem_limit_bytes=8 * MIB),
        name="forward_other",
    )(weights, mat, pads, const, after)


def line_rows(tile, base, masks):
    shape = masks[0].shape
    return select_line(masks, [jnp.broadcast_to(tile[base + 1 + k : base + 2 + k], shape) for k in range(len(masks))])


def incident_rows(tile, step):
    rows = row_ids(tile.shape[1])
    result = jnp.broadcast_to(tile[0:1], tile.shape)
    for base in range(step, SUB, step):
        result = jnp.where(rows >= base, jnp.broadcast_to(tile[base : base + 1], tile.shape), result)
    return result


def row_masks(const_ref, width):
    tile = const_ref[LINE_ROWS]
    return [jnp.concatenate([tile] * (width // LANES), axis=1) == k for k in range(SCALE - 1)]


def factors_of(mine, theirs, bit):
    mine_factor = jnp.where(bit == 0, theirs, incident_rows(theirs, SCALE))
    return mine_factor, jnp.where(bit == 0, incident_rows(mine, SCALE), mine)


def merged_state(mine, theirs, bit, masks):
    mine_factor, theirs_factor = factors_of(mine[0:SUB], theirs[0:SUB], bit)
    result = [mine[0:SUB] * theirs[0:SUB]]
    for v in range(mine.shape[0] // SUB - 1):
        span = slice((v + 1) * SUB, (v + 2) * SUB)
        result.append(
            mine[span] * line_rows(mine_factor, v * SCALE, masks)
            + theirs[span] * line_rows(theirs_factor, v * SCALE, masks)
        )
    return result


def weighted_rows(factor, state, misfits, masks):
    rows = row_ids(state.shape[1])
    result = jnp.zeros((SUB, state.shape[1]), F32)
    for v, misfit in enumerate(misfits):
        base = v * SCALE
        value = misfit * state[(v + 1) * SUB : (v + 2) * SUB] * line_rows(factor, base, masks)
        whole = None
        for k, mask in enumerate(masks):
            part = jnp.sum(jnp.where(mask, value, 0.0), axis=0, keepdims=True)
            result = jnp.where(rows == base + 1 + k, part, result)
            whole = part if whole is None else whole + part
        result = jnp.where(rows == base, whole, result)
    return result


def children(factor, sums, mine, theirs, bit, misfits, masks):
    mine_factor, theirs_factor = factors_of(mine[0:SUB], theirs[0:SUB], bit)
    if factor is not None:
        mine_factor, theirs_factor = factor * mine_factor, factor * theirs_factor
    behind = (row_ids(mine.shape[1]) & (SCALE - 1)) == 0
    mine_sums = jnp.where(behind == (bit == 0), weighted_rows(theirs_factor, theirs, misfits, masks), 0.0)
    theirs_sums = jnp.where(behind == (bit == 1), weighted_rows(mine_factor, mine, misfits, masks), 0.0)
    if sums is not None:
        mine_sums, theirs_sums = sums + mine_sums, sums + theirs_sums
    return (mine_factor, mine_sums), (theirs_factor, theirs_sums)


def call_small(kernel, name, outs, operands, scratch=()):
    return pl.pallas_call(
        kernel,
        in_specs=[VMEM] * len(operands),
        out_specs=[VMEM] * len(outs),
        out_shape=[pltpu.VMEM(shape, F32) for shape in outs],
        scratch_shapes=[pltpu.VMEM(shape, F32) for shape in scratch],
        compiler_params=pltpu.CompilerParams(vmem_limit_bytes=4 * MIB),
        name=name,
    )(*operands)


def store_rows(ref, tiles):
    for i, tile in enumerate(tiles):
        ref[i * SUB : (i + 1) * SUB, :] = tile


def merge_kernel(shift, const_ref, mine_ref, theirs_ref, *refs):
    bit = (depth_place() >> shift) & 1
    store_rows(refs[-1], merged_state(mine_ref[...], theirs_ref[...], bit, row_masks(const_ref, mine_ref.shape[1])))


def merge_four_kernel(const_ref, mine_ref, both_ref, far_ref, near_ref, pair_ref, other_ref, whole_ref):
    place = depth_place()
    masks = row_masks(const_ref, mine_ref.shape[1])
    pair = merged_state(mine_ref[...], near_ref[...], (place >> 1) & 1, masks)
    other = merged_state(far_ref[...], both_ref[...], (place >> 1) & 1, masks)
    store_rows(pair_ref, pair)
    store_rows(other_ref, other)
    store_rows(whole_ref, merged_state(pair_ref[...], other_ref[...], (place >> 2) & 1, masks))


def depth_place():
    return lax.axis_index("far") * NEAR + lax.axis_index("near")


def result_kernel(levels, const_ref, target_ref, *refs):
    states, outs = refs[: 2 * levels], refs[-4:]
    depth, width = states[0].shape
    views = depth // SUB - 1
    place = depth_place()
    size = 2 * LANES
    start = (place & 1) * width
    masks = row_masks(const_ref, size)
    behind = (row_ids(size) & (SCALE - 1)) == 0
    for c in range(width // size):
        span = slice(c * size, (c + 1) * size)
        factor, sums = None, None
        for level in reversed(range(levels)):
            mine, theirs = states[2 * level][:, span], states[2 * level + 1][:, span]
            bit = (place >> level) & 1
            if level == levels - 1:
                signals = merged_state(mine, theirs, bit, masks)[1:]
                there = pl.ds(pl.multiple_of(start + c * size, LANES), size)
                misfits = [signals[v] - target_ref[v * SUB : (v + 1) * SUB, there] for v in range(views)]
            contexts = children(factor, sums, mine, theirs, bit, misfits, masks)
            factor, sums = contexts[0]
        for i, (state, (factor, sums)) in enumerate(zip((mine, theirs), contexts)):
            own = jnp.where(behind, weighted_rows(factor, state, misfits, masks), 0.0)
            rest = [factor * state[0:SUB], sums + own]
            for ref, first in ((outs[i], signals), (outs[2 + i], misfits)):
                for j, tile in enumerate(first + rest):
                    ref[j * SUB : (j + 1) * SUB, span] = tile


def assemble_kernel(target_ref, here_ref, there_ref, package_ref, signal_ref):
    half = here_ref.shape[1]
    count = signal_ref.shape[0]
    at = pl.multiple_of((lax.axis_index("near") & 1) * half, LANES)
    for ref, start in ((here_ref, at), (there_ref, pl.multiple_of(half - at, LANES))):
        span = pl.ds(start, half)
        signal_ref[:, span] = ref[0:count, :]
        package_ref[0:count, span] = ref[0:count, :] - target_ref[:, span]
        package_ref[count:, span] = ref[count:, :]


def assemble_other_kernel(here_ref, there_ref, package_ref):
    half = here_ref.shape[1]
    at = pl.multiple_of((lax.axis_index("near") & 1) * half, LANES)
    package_ref[:, pl.ds(at, half)] = here_ref[...]
    package_ref[:, pl.ds(pl.multiple_of(half - at, LANES), half)] = there_ref[...]


def backward_kernel(places, cells, finish, given, const_ref, package_ref, weight_ref, *refs):
    count = len(places)
    if given:
        mat, refs = refs[0], refs[1:]
    u_refs, n_refs, refs = refs[:count], refs[count : 2 * count], refs[2 * count :]
    if finish:
        signal_ref, refs = refs[0], refs[1:]
        prior, refs = refs[: finish - 1], refs[finish - 1 :]
        grad_hbm, signal_hbm, cell_ref, grad_ref, signal_rows = refs[:5]
        refs = refs[5:]
    else:
        left_sum, diff_sum, refs = refs[0], refs[1], refs[2:]
    gain, carry, scaled, left_pad, diff_pad, index_ref, sems = refs[-7:]
    _, slab, width = weight_ref.shape
    slab = slab - SUB
    emissions = SCALE - 1
    tiles = width // LANES
    blocks = slab // BLOCK
    lanes, rows = lane_ids(), row_ids()
    column = column_in(weight_ref, pl.ds(0, count), index_ref, sems.at[blocks])
    column.start()
    if finish:
        for v in range(signal_rows.shape[0]):
            signal_rows[v] = signal_ref[v * SUB : (v + 1) * SUB, :].reshape(SUB, 1, width)
        signal_copy = pltpu.make_async_copy(signal_rows, signal_hbm, sems.at[blocks + 1])
        signal_copy.start()
        out_copies = [
            pltpu.make_async_copy(grad_ref.at[b], grad_hbm.at[:, pl.ds(b * BLOCK, BLOCK), :], sems.at[b])
            for b in range(blocks)
        ]
    if not given:
        mat = refs[0]
        backward_matrix(mat, const_ref)
    masks = [const_ref[LINE_ROWS] == k for k in range(emissions)]
    scale = const_ref[SCALE]
    columns = [const_ref[k] * cells for k in range(emissions + 1)]
    for j in range(tiles):
        span = slice(j * LANES, (j + 1) * LANES)
        factor = package_ref[count * SUB : (count + 1) * SUB, span]
        sums = package_ref[(count + 1) * SUB : (count + 2) * SUB, span]
        for v in range(count):
            base = v * SCALE
            gain[v, :, span] = package_ref[v * SUB : (v + 1) * SUB, span] * scale * line_rows(factor, base, masks)
            back = columns[0] * jnp.broadcast_to(sums[base : base + 1], rows.shape)
            for k in range(1, emissions + 1):
                back = back + columns[k] * jnp.broadcast_to(sums[base + k : base + k + 1], rows.shape)
            carry[v, :, span] = back
    zero = jnp.zeros((SUB, LANES), F32)
    for ref in (left_pad, diff_pad):
        edge = jnp.zeros(ref.shape[:3] + (LANES,), F32)
        ref[:, :, :, 0:LANES] = edge
        ref[:, :, :, width + 2 * LANES :] = edge

    def place(v, d, cell, first):
        _, rest = shift_of(index_ref, v, cell, width)
        stay = lanes >= rest
        turn = rest & (LANES - 1)
        at = (first + d) * SUB
        plain = [scaled[v, at : at + SUB, j * LANES : (j + 1) * LANES] for j in range(tiles)]
        moved = [plain[j] * weight_ref[v, cell : cell + 1, j * LANES : (j + 1) * LANES] for j in range(tiles)]
        for ref, values in ((left_pad, plain), (diff_pad, moved)):
            turned = [zero] + [pltpu.roll(value, turn, 1) for value in values] + [zero]
            for j in range(tiles + 1):
                ref[v, first + d, :, (j + 1) * LANES : (j + 2) * LANES] = jnp.where(stay, turned[j + 1], turned[j])

    def gathered(ref, before, cell, slot):
        sums = [None] * (tiles + 2)
        if before is not None:
            sums = [before[cell, :, j * LANES : (j + 1) * LANES] for j in range(tiles + 2)]
        for v in range(count):
            whole, _ = shift_of(index_ref, v, cell, width)
            for j in range(tiles + 2):
                start = pl.multiple_of((1 + j - whole) * LANES, LANES)
                value = ref[v, slot, :, pl.ds(start, LANES)]
                sums[j] = value if sums[j] is None else sums[j] + value
        return sums

    def folded(sums):
        low = jnp.sum(sums[0], axis=1, keepdims=True)
        beyond = sums[tiles + 1] + jnp.where(lanes == LANES - 1, sums[tiles], 0.0)
        high = jnp.sum(beyond, axis=1, keepdims=True)
        core = sums[1 : tiles + 1]
        core[0] = core[0] + jnp.where(lanes == 0, low, 0.0)
        core[-1] = jnp.where(lanes == LANES - 1, 0.0, core[-1] + jnp.where(lanes == LANES - 2, high, 0.0))
        return core

    for block in range(blocks):
        first = block % 2 * BLOCK
        for v in range(count):
            for c in range(width // CHUNK):
                span = slice(c * CHUNK, (c + 1) * CHUNK)
                factor = gain[v, :, span][None]
                weighted = n_refs[v][places[v], block_rows(block), span].reshape(BLOCK, SUB, CHUNK) * factor
                direct = u_refs[v][places[v], block_rows(block), span].reshape(BLOCK, SUB, CHUNK) * factor
                lines, total = multiply(mat, weighted.reshape(ROWS, CHUNK))
                before = carry[v, :, span]
                lines = lines.reshape(BLOCK, SUB, CHUNK) + before[None]
                scaled[v, first * SUB : first * SUB + ROWS, span] = (direct - lines).reshape(ROWS, CHUNK)
                carry[v, :, span] = before + total
        if block == 0:
            column.wait()
        for v in range(count):
            for d in range(BLOCK):
                place(v, d, block * BLOCK + d, first)
        for d in range(BLOCK):
            cell = block * BLOCK + d
            left = gathered(left_pad, prior[0] if finish > 1 else None, cell, first + d)
            diff = gathered(diff_pad, prior[1] if finish > 1 else None, cell, first + d)
            if not finish:
                for j in range(tiles + 2):
                    left_sum[cell, :, j * LANES : (j + 1) * LANES] = left[j]
                    diff_sum[cell, :, j * LANES : (j + 1) * LANES] = diff[j]
                continue
            left, diff = folded([left[j] - diff[j] for j in range(tiles + 2)]), folded(diff)
            turned = [zero] + [pltpu.roll(value, 1, 1) for value in diff]
            for j in range(tiles):
                value = left[j] + jnp.where(lanes == 0, turned[j], turned[j + 1])
                cell_ref[first + d, :, j * LANES : (j + 1) * LANES] = value
        if finish:
            grad_ref[block] = jnp.swapaxes(cell_ref[first : first + BLOCK], 0, 1)
            out_copies[block].start()
    if finish:
        for copy in out_copies + [signal_copy]:
            copy.wait()


def backward(package, const, weights, mats, pieces, cells, signal, prior):
    views, slab, width = weights.shape
    slab = slab - SUB
    blocks = slab // BLOCK
    finish = signal is not None
    line = pltpu.VMEM((views, SUB, width), F32)
    sums = pltpu.VMEM((slab, SUB, width + 2 * LANES), F32)
    scratch = [] if mats else [pltpu.VMEM(MATRIX, BF16)]
    scratch += [
        line,
        line,
        pltpu.VMEM((views, 2 * ROWS, width), F32),
        pltpu.VMEM((views, 2 * BLOCK, SUB, width + 3 * LANES), F32),
        pltpu.VMEM((views, 2 * BLOCK, SUB, width + 3 * LANES), F32),
        pltpu.SMEM((views, SUB, LANES), F32),
        pltpu.SemaphoreType.DMA((blocks + 2,)),
    ]
    operands = [const, package, weights, *mats, *[u for u, _, _ in pieces], *[n for _, n, _ in pieces]]
    if finish:
        operands += [signal[0], *prior]
        scratch = [
            pltpu.VMEM((2 * BLOCK, SUB, width), F32),
            pltpu.VMEM((blocks, SUB, BLOCK, width), F32),
            pltpu.VMEM(signal[1], F32),
        ] + scratch
    return pl.pallas_call(
        functools.partial(
            backward_kernel, tuple(at for _, _, at in pieces), cells, 1 + len(prior) if finish else 0, len(mats)
        ),
        in_specs=[VMEM] * len(operands),
        out_specs=[HBM, HBM] if finish else [VMEM, VMEM],
        out_shape=[pltpu.HBM((SUB, slab, width), F32), pltpu.HBM(signal[1], F32)] if finish else [sums, sums],
        scratch_shapes=scratch,
        compiler_params=pltpu.CompilerParams(vmem_limit_bytes=16 * MIB),
        name="backward_last" if finish else "backward_first",
    )(*operands)


def body(concentration, shear_index, shear_weight, attenuation, yields, line_energy, measured):
    elements, _, slab, width = concentration.shape
    views = shear_weight.shape[0]
    emissions = attenuation.shape[0] - 1
    groups = lax.axis_size("far")
    both = lax.axis_size("views") == 2
    cells = float(slab * groups * NEAR)
    conc = concentration.reshape(elements, slab, width)
    scalars = (attenuation, line_energy, yields)

    def to_other(value):
        return lax.ppermute(value, "views", [(0, 1), (1, 0)])

    fillers = []

    def fill(after):
        if not both or len(fillers) == views:
            return ()
        fillers.append(forward_other(len(fillers), other_weight, mat, pads, const, after))
        return (fillers[-1][2],)

    u, n, const, target, mat, pads, weight, state, send = forward(
        conc, shear_index, shear_weight, scalars, measured, cells
    )
    def swap(value, axis, step):
        return lax.ppermute(value, axis, [(s, s ^ step) for s in range(lax.axis_size(axis))])

    states = [state, swap(send, "near", 1)]
    if both:
        other_weight = to_other(weight)
    tokens = ()
    levels = groups.bit_length() + 1

    def merge(level):
        (merged,) = call_small(
            functools.partial(merge_kernel, level), "merge", [state.shape], (const, *states[-2:])
        )
        return merged

    state = merge(0)
    pairs = [(s, s ^ 6) for s in range(groups * NEAR)]
    four = (state, lax.ppermute(state, ("far", "near"), pairs), swap(state, "far", 1), swap(state, "near", 2))
    pair, other, whole = call_small(merge_four_kernel, "merge_four", [state.shape] * 3, (const, *four))
    states += [state, four[3], pair, other]
    state = whole
    for level in range(3, levels):
        states += [state, swap(state, "far", 1 << (level - 2))]
        if level < levels - 1:
            state = merge(level)
    for _ in range(views):
        tokens += fill(state)
    half = ((views + 2) * SUB, width // 2)
    here, there, here_other, there_other = call_small(
        functools.partial(result_kernel, levels), "result", [half] * 4, (const, target, *states, *tokens)
    )
    there = swap(there, "near", 1)
    if both:
        pairs = [(v * NEAR + s, (1 - v) * NEAR + (s ^ 1)) for v in range(2) for s in range(NEAR)]
        here_other = to_other(here_other)
        there_other = lax.ppermute(there_other, ("views", "near"), pairs)
    package = (half[0], width)
    shapes = [package, target.shape]
    package, signal = call_small(assemble_kernel, "assemble", shapes, (target, here, there))
    own = [(u, n, v) for v in range(views)]
    signal = (signal, measured.shape)
    if both:
        sums = backward(package, const, weight, tokens[:1], own, cells, None, ())
        (other_package,) = call_small(
            assemble_other_kernel, "assemble_other", [package.shape], (here_other, there_other)
        )
        pieces = [(fillers[v][0], fillers[v][1], 0) for v in range(views)]
        gradient, signal = backward(other_package, const, other_weight, tokens[:1], pieces, cells, signal, sums)
    else:
        gradient, signal = backward(package, const, weight, (), own, cells, signal, ())
        gradient = lax.psum(gradient, "views")
    return gradient.reshape(concentration.shape), signal


def solution(mesh):
    views, depth = mesh.shape["views"], mesh.shape["depth"]
    devices = mesh.devices.reshape(views, depth // NEAR, NEAR)
    split = jax.sharding.Mesh(devices, ("views", "far", "near"))
    depths = ("far", "near")
    return jax.shard_map(
        body,
        mesh=split,
        in_specs=(
            P(None, None, depths, None),
            P("views", depths, None),
            P("views", depths, None),
            P(),
            P(),
            P(),
            P("views", None, None, None),
        ),
        out_specs=(P(None, None, depths, None), P("views", None, None, None)),
        check_vma=False,
    )
```

```python
import functools

import jax
import jax.numpy as jnp
from jax import lax
from jax.experimental import pallas as pl
from jax.experimental.pallas import tpu as pltpu
from jax.sharding import PartitionSpec as P

LANES = 128
SUB = 8
BLOCK = 8
ROWS = BLOCK * SUB
NEAR = 4
CHUNK = 256
MIB = 1024 * 1024
F32 = jnp.float32
BF16 = jnp.bfloat16
HBM = pl.BlockSpec(memory_space=pltpu.HBM)
VMEM = pl.BlockSpec(memory_space=pltpu.VMEM)
SCALE, LINE_ROWS, LINE_LANES = 4, 5, 6
ANY = pl.BlockSpec(memory_space=pl.ANY)


def in_hbm(value):
    return pltpu.with_memory_space_constraint(value, pltpu.HBM)


def lane_ids(width=LANES):
    return lax.broadcasted_iota(jnp.int32, (SUB, width), 1)


def row_ids(width=LANES):
    return lax.broadcasted_iota(jnp.int32, (SUB, width), 0)


def tile_of(values, ids):
    tile = jnp.zeros(ids.shape, F32)
    for e in range(SUB):
        tile = jnp.where(ids == e, values[e], tile)
    return tile


def select_line(masks, values):
    result = values[0]
    for mask, value in zip(masks[1:], values[1:]):
        result = jnp.where(mask, value, result)
    return result


def fill_matrix(mat_ref, first_tile, second_tile, first_incl, second_incl):
    depth = (lane_ids() & (ROWS - 1)) >> 3
    tiles = []
    for d in range(BLOCK):
        one = jnp.where(depth <= d if first_incl else depth < d, first_tile, 0.0)
        two = jnp.where(depth <= d if second_incl else depth < d, second_tile, 0.0)
        tiles.append(one + two)
    tiles.append(first_tile + second_tile)
    tiles.append(jnp.zeros((SUB, LANES), F32))
    whole = jnp.concatenate(tiles, axis=0)
    high = whole.astype(BF16)
    mat_ref[:, 0:LANES] = high
    mat_ref[:, LANES : 2 * LANES] = (whole - high.astype(F32)).astype(BF16)


def multiply(mat_ref, values):
    high = values.astype(BF16)
    low = (values - high.astype(F32)).astype(BF16)
    stacked = jnp.concatenate([high, low, high], axis=0)
    product = jnp.dot(mat_ref[:, 0 : 3 * ROWS], stacked, preferred_element_type=F32)
    return product[0:ROWS], product[ROWS : ROWS + SUB]


MATRIX = (ROWS + 2 * SUB, 2 * LANES)


def copies_in(pairs, sems):
    return [pltpu.make_async_copy(source, target, sems.at[i]) for i, (source, target) in enumerate(pairs)]


def block_rows(block):
    return slice(block * ROWS, (block + 1) * ROWS)


def block_cells(block):
    return slice(block * BLOCK, (block + 1) * BLOCK)


def offset_of(index_ref, v, cell, width):
    if index_ref.dtype == jnp.int32:
        at = index_ref[v, cell, 0]
    else:
        at = index_ref[v, cell % SUB, cell // SUB].astype(jnp.int32)
    return at - (width // 2 - LANES)


def shift_of(index_ref, v, cell, width):
    offset = offset_of(index_ref, v, cell, width)
    whole = jnp.minimum(offset >> 7, 1)
    return whole, offset - (whole << 7)


def pad_cells(pad_ref, cell, pieces):
    tiles = len(pieces)

    def spread(piece, lane):
        return jnp.broadcast_to(piece[:, lane : lane + 1], (SUB, LANES))

    last = spread(pieces[-1], LANES - 1)
    edges = [spread(pieces[0], 1), spread(pieces[-1], LANES - 2)]
    for j, piece in enumerate([spread(pieces[0], 0)] + pieces + [last, last] + edges):
        pad_ref[cell, :, j * LANES : (j + 1) * LANES] = piece


def shear(field, pad_ref, index_ref, weight_ref, block, views, tiles):
    lanes = lane_ids()
    for i, v in enumerate(views):
        for d in range(BLOCK):
            cell = block * BLOCK + d
            offset = offset_of(index_ref, v, cell, tiles * LANES)
            whole, rest = offset >> 7, offset & (LANES - 1)
            starts = [pl.multiple_of((whole + j) * LANES, LANES) for j in range(tiles + 1)]
            values = [pad_ref[cell, :, pl.ds(start, LANES)] for start in starts]

            def turned(rest):
                stay = lanes < LANES - rest
                turn = (LANES - rest) & (LANES - 1)
                rolled = [pltpu.roll(value, turn, 1) for value in values]
                return [jnp.where(stay, rolled[j], rolled[j + 1]) for j in range(tiles)]

            left, right = turned(rest), turned(rest + 1)
            second, last_but_one = [
                pad_ref[cell, :, (tiles + 3 + j) * LANES : (tiles + 4 + j) * LANES] for j in range(2)
            ]
            right[0] = jnp.where(lanes < LANES - offset, second, right[0])
            for j in (tiles - 2, tiles - 1):
                first = (tiles + 1 - j) * LANES - 1 - offset
                left[j] = jnp.where(lanes >= first, last_but_one, left[j])
            for j in range(tiles):
                span = slice(j * LANES, (j + 1) * LANES)
                weight = weight_ref[i, cell : cell + 1, span]
                field[i, d * SUB : (d + 1) * SUB, span] = left[j] + weight * (right[j] - left[j])


def transmit(u_ref, n_ref, field, mat, carry, block, sums):
    views, _, width = field.shape
    for v in range(views):
        for c in range(width // CHUNK):
            span = slice(c * CHUNK, (c + 1) * CHUNK)
            value = field[v, :, span]
            lines, total = multiply(mat, value)
            before = carry[v, :, span]
            through = jnp.exp(lines.reshape(BLOCK, SUB, CHUNK) + before[None])
            value = value.reshape(BLOCK, SUB, CHUNK)
            emit = value * through
            u_ref[v, block_rows(block), span] = through.reshape(ROWS, CHUNK)
            n_ref[v, block_rows(block), span] = emit.reshape(ROWS, CHUNK)
            carry[v, :, span] = before + total
            if sums:
                sums[0][v, :, span] += jnp.sum(value, axis=0)
                sums[1][v, :, span] += jnp.sum(emit, axis=0)


def forward_kernel(cells, *refs):
    att_hbm, line_hbm, yield_hbm, index_hbm, conc_hbm, weight_hbm, measured_hbm = refs[:7]
    u_ref, n_ref, const_ref, target_ref, mat, pad_ref, weight_ref = refs[7:14]
    state_refs = refs[14:16]
    refs = refs[16:]
    conc_ref, field, carry, field_sum, emit_sum, measured_ref, column_ref = refs[:7]
    att_ref, line_ref, yield_ref, index_ref, sems = refs[7:]
    views, _, width = weight_ref.shape
    slab = conc_ref.shape[1]
    emissions = att_ref.shape[0] - 1
    tiles = width // LANES
    blocks = slab // BLOCK
    lanes, rows = lane_ids(), row_ids()
    conc_copies = [
        pltpu.make_async_copy(
            conc_hbm.at[:, pl.ds(b * BLOCK, BLOCK), :], conc_ref.at[:, pl.ds(b * BLOCK, BLOCK), :], sems.at[b]
        )
        for b in range(blocks)
    ]
    pairs = [
        (att_hbm, att_ref),
        (line_hbm, line_ref),
        (yield_hbm, yield_ref),
        (weight_hbm, weight_ref.at[:, pl.ds(0, slab), :]),
        (measured_hbm, measured_ref),
        (index_hbm.at[:, :, pl.ds(width // 2, LANES)], column_ref),
    ]
    copies = copies_in(pairs, sems.at[pl.ds(2 * blocks, len(pairs))])
    index_copies = [
        pltpu.make_async_copy(
            index_hbm.at[:, pl.ds(b * BLOCK, BLOCK), pl.ds(width // 2, LANES)],
            index_ref.at[:, pl.ds(b * BLOCK, BLOCK), :],
            sems.at[blocks + b],
        )
        for b in range(blocks)
    ]
    for copy in conc_copies[:1] + copies[:3] + index_copies[:1] + copies[3:4]:
        copy.start()
    for copy in conc_copies[1:] + index_copies[1:] + copies[4:]:
        copy.start()
    for ref in (carry, field_sum, emit_sum):
        ref[...] = jnp.zeros_like(ref)

    def pad(block):
        conc_copies[block].wait()
        by_depth = jnp.swapaxes(conc_ref[:, block_cells(block), :], 0, 1)
        for d in range(BLOCK):
            pieces = [by_depth[d, :, j * LANES : (j + 1) * LANES] for j in range(tiles)]
            pad_cells(pad_ref, block * BLOCK + d, pieces)

    pad(0)
    for copy in copies[:3]:
        copy.wait()
    line_by_row = tile_of([line_ref[e].astype(F32) for e in range(SUB)], rows)
    masks = [line_by_row == k for k in range(emissions)]
    by_lane = [tile_of([att_ref[k, e] for e in range(SUB)], lanes & 7) for k in range(emissions + 1)]
    fill_matrix(mat, -by_lane[0], select_line(masks, by_lane[1:]), False, True)
    for k in range(emissions + 1):
        const_ref[k] = tile_of([att_ref[k, e] for e in range(SUB)], rows)
    const_ref[SCALE] = tile_of([yield_ref[e] for e in range(SUB)], rows)
    const_ref[LINE_ROWS] = line_by_row
    const_ref[LINE_LANES] = tile_of([line_ref[e].astype(F32) for e in range(SUB)], lanes & 7)
    copies[3].wait()
    for block in range(blocks):
        if block:
            pad(block)
        index_copies[block].wait()
        shear(field, pad_ref, index_ref, weight_ref, block, range(views), tiles)
        transmit(u_ref, n_ref, field, mat, carry, block, (field_sum, emit_sum))
    for copy in copies[4:]:
        copy.wait()
    for v in range(views):
        shifts = jnp.zeros((SUB, LANES), jnp.int32)
        for octet in range(slab // SUB):
            values = column_ref[v, octet * SUB : (octet + 1) * SUB, :] - lanes
            shifts = jnp.where(lanes == octet, values, shifts)
        weight_ref[v, slab : slab + SUB, 0:LANES] = shifts.astype(F32)
    columns = [const_ref[k] for k in range(emissions + 1)]
    masks = [const_ref[LINE_ROWS] == k for k in range(emissions)]
    scale = const_ref[SCALE] * (1.0 / cells)
    share = width // 2
    core = lax.axis_index("near") & 1
    for r in range(2):
        for j in range(share // LANES):
            start = pl.multiple_of((core ^ r) * share + j * LANES, LANES)
            span = slice(j * LANES, (j + 1) * LANES)
            totals = jnp.zeros((SUB, LANES), F32)
            for v in range(views):
                values = field_sum[v, :, pl.ds(start, LANES)]
                sums = [jnp.sum(column * values, axis=0, keepdims=True) for column in columns]
                for k in range(emissions + 1):
                    totals = jnp.where(rows == v * (emissions + 1) + k, sums[k], totals)
                line_total = select_line(masks, [jnp.broadcast_to(value, rows.shape) for value in sums[1:]])
                signal = scale * emit_sum[v, :, pl.ds(start, LANES)] * jnp.exp(-line_total)
                state_refs[r][(v + 1) * SUB : (v + 2) * SUB, span] = signal
            state_refs[r][0:SUB, span] = jnp.exp(-totals)
    for v in range(views):
        target_ref[v * SUB : (v + 1) * SUB, :] = measured_ref[v].reshape(SUB, width)


def forward(conc, index, weights, scalars, measured, cells):
    views, slab, width = weights.shape
    attenuation, line_energy, yields = scalars
    values = pltpu.VMEM((views, slab * SUB, width), F32)
    padded = pltpu.VMEM((slab, SUB, width + 5 * LANES), F32)
    state = pltpu.VMEM(((views + 1) * SUB, width // 2), F32)
    line = pltpu.VMEM((views, SUB, width), F32)
    operands = [in_hbm(value) for value in (attenuation, line_energy, yields, index, conc, weights, measured)]
    return pl.pallas_call(
        functools.partial(forward_kernel, cells),
        in_specs=[HBM] * len(operands),
        out_specs=[VMEM] * 9,
        out_shape=[
            values,
            values,
            pltpu.VMEM((LINE_LANES + 1, SUB, LANES), F32),
            pltpu.VMEM((views * SUB, width), F32),
            pltpu.VMEM(MATRIX, BF16),
            padded,
            pltpu.VMEM((views, slab + SUB, width), F32),
            state,
            state,
        ],
        scratch_shapes=[
            pltpu.VMEM((SUB, slab, width), F32),
            pltpu.VMEM((views, ROWS, width), F32),
            line,
            line,
            line,
            pltpu.VMEM(measured.shape, F32),
            pltpu.VMEM((views, slab, LANES), jnp.int32),
            pltpu.SMEM(attenuation.shape, F32),
            pltpu.SMEM(line_energy.shape, jnp.int32),
            pltpu.SMEM(yields.shape, F32),
            pltpu.SMEM((views, slab, LANES), jnp.int32),
            pltpu.SemaphoreType.DMA((2 * (slab // BLOCK) + 6,)),
        ],
        compiler_params=pltpu.CompilerParams(vmem_limit_bytes=16 * MIB),
        name="forward",
    )(*operands)


def column_in(package_any, views, index_ref, sem):
    first = package_any.shape[1] - SUB
    source = package_any.at[views, pl.ds(first, SUB), pl.ds(0, index_ref.shape[2])]
    return pltpu.make_async_copy(source, index_ref, sem)


def backward_matrix(mat_ref, const_ref):
    masks = [const_ref[LINE_LANES] == k for k in range(SCALE - 1)]
    columns = [const_ref[k] for k in range(SCALE)]
    fill_matrix(mat_ref, -columns[0], select_line(masks, columns[1:]), True, False)


def forward_other_kernel(view, weight_ref, mat, pad_ref, const_ref, order_ref, *refs):
    u_ref, n_ref, back_mat, field, carry, index_ref, sem = refs
    _, slab, width = weight_ref.shape
    slab = slab - SUB
    copy = column_in(weight_ref, pl.ds(view, 1), index_ref, sem)
    copy.start()
    carry[...] = jnp.zeros_like(carry)
    backward_matrix(back_mat, const_ref)
    copy.wait()
    for block in range(slab // BLOCK):
        shear(field, pad_ref, index_ref, weight_ref.at[pl.ds(view, 1)], block, (0,), width // LANES)
        transmit(u_ref, n_ref, field, mat, carry, block, None)


def forward_other(view, weights, mat, pads, const, after):
    _, slab, width = weights.shape
    slab = slab - SUB
    values = pltpu.VMEM((1, slab * SUB, width), F32)
    return pl.pallas_call(
        functools.partial(forward_other_kernel, view),
        in_specs=[VMEM] * 5,
        out_specs=[VMEM] * 3,
        out_shape=[values, values, pltpu.VMEM(MATRIX, BF16)],
        scratch_shapes=[
            pltpu.VMEM((1, ROWS, width), F32),
            pltpu.VMEM((1, SUB, width), F32),
            pltpu.SMEM((1, SUB, LANES), F32),
            pltpu.SemaphoreType.DMA,
        ],
        compiler_params=pltpu.CompilerParams(vmem_limit_bytes=8 * MIB),
        name="forward_other",
    )(weights, mat, pads, const, after)


def line_rows(tile, base, masks):
    shape = masks[0].shape
    return select_line(masks, [jnp.broadcast_to(tile[base + 1 + k : base + 2 + k], shape) for k in range(len(masks))])


def incident_rows(tile, step):
    rows = row_ids(tile.shape[1])
    result = jnp.broadcast_to(tile[0:1], tile.shape)
    for base in range(step, SUB, step):
        result = jnp.where(rows >= base, jnp.broadcast_to(tile[base : base + 1], tile.shape), result)
    return result


def row_masks(const_ref, width):
    tile = const_ref[LINE_ROWS]
    return [jnp.concatenate([tile] * (width // LANES), axis=1) == k for k in range(SCALE - 1)]


def factors_of(mine, theirs, bit):
    mine_factor = jnp.where(bit == 0, theirs, incident_rows(theirs, SCALE))
    return mine_factor, jnp.where(bit == 0, incident_rows(mine, SCALE), mine)


def merged_state(mine, theirs, bit, masks):
    mine_factor, theirs_factor = factors_of(mine[0:SUB], theirs[0:SUB], bit)
    result = [mine[0:SUB] * theirs[0:SUB]]
    for v in range(mine.shape[0] // SUB - 1):
        span = slice((v + 1) * SUB, (v + 2) * SUB)
        result.append(
            mine[span] * line_rows(mine_factor, v * SCALE, masks)
            + theirs[span] * line_rows(theirs_factor, v * SCALE, masks)
        )
    return result


def weighted_rows(factor, state, misfits, masks):
    rows = row_ids(state.shape[1])
    result = jnp.zeros((SUB, state.shape[1]), F32)
    for v, misfit in enumerate(misfits):
        base = v * SCALE
        value = misfit * state[(v + 1) * SUB : (v + 2) * SUB] * line_rows(factor, base, masks)
        whole = None
        for k, mask in enumerate(masks):
            part = jnp.sum(jnp.where(mask, value, 0.0), axis=0, keepdims=True)
            result = jnp.where(rows == base + 1 + k, part, result)
            whole = part if whole is None else whole + part
        result = jnp.where(rows == base, whole, result)
    return result


def children(factor, sums, mine, theirs, bit, misfits, masks):
    mine_factor, theirs_factor = factors_of(mine[0:SUB], theirs[0:SUB], bit)
    if factor is not None:
        mine_factor, theirs_factor = factor * mine_factor, factor * theirs_factor
    behind = (row_ids(mine.shape[1]) & (SCALE - 1)) == 0
    mine_sums = jnp.where(behind == (bit == 0), weighted_rows(theirs_factor, theirs, misfits, masks), 0.0)
    theirs_sums = jnp.where(behind == (bit == 1), weighted_rows(mine_factor, mine, misfits, masks), 0.0)
    if sums is not None:
        mine_sums, theirs_sums = sums + mine_sums, sums + theirs_sums
    return (mine_factor, mine_sums), (theirs_factor, theirs_sums)


def call_small(kernel, name, outs, operands, scratch=()):
    return pl.pallas_call(
        kernel,
        in_specs=[VMEM] * len(operands),
        out_specs=[VMEM] * len(outs),
        out_shape=[pltpu.VMEM(shape, F32) for shape in outs],
        scratch_shapes=[pltpu.VMEM(shape, F32) for shape in scratch],
        compiler_params=pltpu.CompilerParams(vmem_limit_bytes=4 * MIB),
        name=name,
    )(*operands)


def store_rows(ref, tiles):
    for i, tile in enumerate(tiles):
        ref[i * SUB : (i + 1) * SUB, :] = tile


def merge_kernel(shift, const_ref, mine_ref, theirs_ref, *refs):
    bit = (depth_place() >> shift) & 1
    store_rows(refs[-1], merged_state(mine_ref[...], theirs_ref[...], bit, row_masks(const_ref, mine_ref.shape[1])))


def merge_four_kernel(const_ref, mine_ref, both_ref, far_ref, near_ref, pair_ref, other_ref, whole_ref, near_out):
    place = depth_place()
    masks = row_masks(const_ref, mine_ref.shape[1])
    pair = merged_state(mine_ref[...], near_ref[...], (place >> 1) & 1, masks)
    other = merged_state(far_ref[...], both_ref[...], (place >> 1) & 1, masks)
    store_rows(pair_ref, pair)
    near_out[...] = near_ref[...]
    store_rows(other_ref, other)
    store_rows(whole_ref, merged_state(pair_ref[...], other_ref[...], (place >> 2) & 1, masks))


def depth_place():
    return lax.axis_index("far") * NEAR + lax.axis_index("near")


def result_kernel(levels, const_ref, target_ref, *refs):
    states, outs = refs[: 2 * levels], refs[-4:]
    depth, width = states[0].shape
    views = depth // SUB - 1
    place = depth_place()
    size = 2 * LANES
    start = (place & 1) * width
    masks = row_masks(const_ref, size)
    behind = (row_ids(size) & (SCALE - 1)) == 0
    for c in range(width // size):
        span = slice(c * size, (c + 1) * size)
        factor, sums = None, None
        for level in reversed(range(levels)):
            mine, theirs = states[2 * level][:, span], states[2 * level + 1][:, span]
            bit = (place >> level) & 1
            if level == levels - 1:
                signals = merged_state(mine, theirs, bit, masks)[1:]
                there = pl.ds(pl.multiple_of(start + c * size, LANES), size)
                misfits = [signals[v] - target_ref[v * SUB : (v + 1) * SUB, there] for v in range(views)]
            contexts = children(factor, sums, mine, theirs, bit, misfits, masks)
            factor, sums = contexts[0]
        for i, (state, (factor, sums)) in enumerate(zip((mine, theirs), contexts)):
            own = jnp.where(behind, weighted_rows(factor, state, misfits, masks), 0.0)
            rest = [factor * state[0:SUB], sums + own]
            for ref, first in ((outs[i], signals), (outs[2 + i], misfits)):
                for j, tile in enumerate(first + rest):
                    ref[j * SUB : (j + 1) * SUB, span] = tile


def assemble_kernel(target_ref, here_ref, there_ref, package_ref, signal_ref):
    half = here_ref.shape[1]
    count = signal_ref.shape[0]
    at = pl.multiple_of((lax.axis_index("near") & 1) * half, LANES)
    for ref, start in ((here_ref, at), (there_ref, pl.multiple_of(half - at, LANES))):
        span = pl.ds(start, half)
        signal_ref[:, span] = ref[0:count, :]
        package_ref[0:count, span] = ref[0:count, :] - target_ref[:, span]
        package_ref[count:, span] = ref[count:, :]


def assemble_other_kernel(here_ref, there_ref, package_ref):
    half = here_ref.shape[1]
    at = pl.multiple_of((lax.axis_index("near") & 1) * half, LANES)
    package_ref[:, pl.ds(at, half)] = here_ref[...]
    package_ref[:, pl.ds(pl.multiple_of(half - at, LANES), half)] = there_ref[...]


def backward_kernel(places, cells, finish, given, const_ref, package_ref, weight_ref, *refs):
    count = len(places)
    if given:
        mat, refs = refs[0], refs[1:]
    u_refs, n_refs, refs = refs[:count], refs[count : 2 * count], refs[2 * count :]
    if finish:
        signal_ref, refs = refs[0], refs[1:]
        prior, refs = refs[: finish - 1], refs[finish - 1 :]
        grad_hbm, signal_hbm, cell_ref, grad_ref, signal_rows = refs[:5]
        refs = refs[5:]
    else:
        left_sum, diff_sum, refs = refs[0], refs[1], refs[2:]
    gain, carry, scaled, left_pad, diff_pad, index_ref, sems = refs[-7:]
    _, slab, width = weight_ref.shape
    slab = slab - SUB
    emissions = SCALE - 1
    tiles = width // LANES
    blocks = slab // BLOCK
    lanes, rows = lane_ids(), row_ids()
    column = column_in(weight_ref, pl.ds(0, count), index_ref, sems.at[blocks])
    column.start()
    if finish:
        for v in range(signal_rows.shape[0]):
            signal_rows[v] = signal_ref[v * SUB : (v + 1) * SUB, :].reshape(SUB, 1, width)
        signal_copy = pltpu.make_async_copy(signal_rows, signal_hbm, sems.at[blocks + 1])
        signal_copy.start()
        out_copies = [
            pltpu.make_async_copy(grad_ref.at[b], grad_hbm.at[:, pl.ds(b * BLOCK, BLOCK), :], sems.at[b])
            for b in range(blocks)
        ]
    if not given:
        mat = refs[0]
        backward_matrix(mat, const_ref)
    masks = [const_ref[LINE_ROWS] == k for k in range(emissions)]
    scale = const_ref[SCALE]
    columns = [const_ref[k] * cells for k in range(emissions + 1)]
    for j in range(tiles):
        span = slice(j * LANES, (j + 1) * LANES)
        factor = package_ref[count * SUB : (count + 1) * SUB, span]
        sums = package_ref[(count + 1) * SUB : (count + 2) * SUB, span]
        for v in range(count):
            base = v * SCALE
            gain[v, :, span] = package_ref[v * SUB : (v + 1) * SUB, span] * scale * line_rows(factor, base, masks)
            back = columns[0] * jnp.broadcast_to(sums[base : base + 1], rows.shape)
            for k in range(1, emissions + 1):
                back = back + columns[k] * jnp.broadcast_to(sums[base + k : base + k + 1], rows.shape)
            carry[v, :, span] = back
    zero = jnp.zeros((SUB, LANES), F32)
    for ref in (left_pad, diff_pad):
        edge = jnp.zeros(ref.shape[:3] + (LANES,), F32)
        ref[:, :, :, 0:LANES] = edge
        ref[:, :, :, width + 2 * LANES :] = edge

    def place(v, d, cell, first):
        _, rest = shift_of(index_ref, v, cell, width)
        stay = lanes >= rest
        turn = rest & (LANES - 1)
        at = (first + d) * SUB
        plain = [scaled[v, at : at + SUB, j * LANES : (j + 1) * LANES] for j in range(tiles)]
        moved = [plain[j] * weight_ref[v, cell : cell + 1, j * LANES : (j + 1) * LANES] for j in range(tiles)]
        for ref, values in ((left_pad, plain), (diff_pad, moved)):
            turned = [zero] + [pltpu.roll(value, turn, 1) for value in values] + [zero]
            for j in range(tiles + 1):
                ref[v, first + d, :, (j + 1) * LANES : (j + 2) * LANES] = jnp.where(stay, turned[j + 1], turned[j])

    def gathered(ref, before, cell, slot):
        sums = [None] * (tiles + 2)
        if before is not None:
            sums = [before[cell, :, j * LANES : (j + 1) * LANES] for j in range(tiles + 2)]
        for v in range(count):
            whole, _ = shift_of(index_ref, v, cell, width)
            for j in range(tiles + 2):
                start = pl.multiple_of((1 + j - whole) * LANES, LANES)
                value = ref[v, slot, :, pl.ds(start, LANES)]
                sums[j] = value if sums[j] is None else sums[j] + value
        return sums

    def folded(sums):
        low = jnp.sum(sums[0], axis=1, keepdims=True)
        beyond = sums[tiles + 1] + jnp.where(lanes == LANES - 1, sums[tiles], 0.0)
        high = jnp.sum(beyond, axis=1, keepdims=True)
        core = sums[1 : tiles + 1]
        core[0] = core[0] + jnp.where(lanes == 0, low, 0.0)
        core[-1] = jnp.where(lanes == LANES - 1, 0.0, core[-1] + jnp.where(lanes == LANES - 2, high, 0.0))
        return core

    for block in range(blocks):
        first = block % 2 * BLOCK
        for v in range(count):
            for c in range(width // CHUNK):
                span = slice(c * CHUNK, (c + 1) * CHUNK)
                factor = gain[v, :, span][None]
                weighted = n_refs[v][places[v], block_rows(block), span].reshape(BLOCK, SUB, CHUNK) * factor
                direct = u_refs[v][places[v], block_rows(block), span].reshape(BLOCK, SUB, CHUNK) * factor
                lines, total = multiply(mat, weighted.reshape(ROWS, CHUNK))
                before = carry[v, :, span]
                lines = lines.reshape(BLOCK, SUB, CHUNK) + before[None]
                scaled[v, first * SUB : first * SUB + ROWS, span] = (direct - lines).reshape(ROWS, CHUNK)
                carry[v, :, span] = before + total
        if block == 0:
            column.wait()
        for v in range(count):
            for d in range(BLOCK):
                place(v, d, block * BLOCK + d, first)
        for d in range(BLOCK):
            cell = block * BLOCK + d
            left = gathered(left_pad, prior[0] if finish > 1 else None, cell, first + d)
            diff = gathered(diff_pad, prior[1] if finish > 1 else None, cell, first + d)
            if not finish:
                for j in range(tiles + 2):
                    left_sum[cell, :, j * LANES : (j + 1) * LANES] = left[j]
                    diff_sum[cell, :, j * LANES : (j + 1) * LANES] = diff[j]
                continue
            left, diff = folded([left[j] - diff[j] for j in range(tiles + 2)]), folded(diff)
            turned = [zero] + [pltpu.roll(value, 1, 1) for value in diff]
            for j in range(tiles):
                value = left[j] + jnp.where(lanes == 0, turned[j], turned[j + 1])
                cell_ref[first + d, :, j * LANES : (j + 1) * LANES] = value
        if finish:
            grad_ref[block] = jnp.swapaxes(cell_ref[first : first + BLOCK], 0, 1)
            out_copies[block].start()
    if finish:
        for copy in out_copies + [signal_copy]:
            copy.wait()


def backward(package, const, weights, mats, pieces, cells, signal, prior):
    views, slab, width = weights.shape
    slab = slab - SUB
    blocks = slab // BLOCK
    finish = signal is not None
    line = pltpu.VMEM((views, SUB, width), F32)
    sums = pltpu.VMEM((slab, SUB, width + 2 * LANES), F32)
    scratch = [] if mats else [pltpu.VMEM(MATRIX, BF16)]
    scratch += [
        line,
        line,
        pltpu.VMEM((views, 2 * ROWS, width), F32),
        pltpu.VMEM((views, 2 * BLOCK, SUB, width + 3 * LANES), F32),
        pltpu.VMEM((views, 2 * BLOCK, SUB, width + 3 * LANES), F32),
        pltpu.SMEM((views, SUB, LANES), F32),
        pltpu.SemaphoreType.DMA((blocks + 2,)),
    ]
    operands = [const, package, weights, *mats, *[u for u, _, _ in pieces], *[n for _, n, _ in pieces]]
    if finish:
        operands += [signal[0], *prior]
        scratch = [
            pltpu.VMEM((2 * BLOCK, SUB, width), F32),
            pltpu.VMEM((blocks, SUB, BLOCK, width), F32),
            pltpu.VMEM(signal[1], F32),
        ] + scratch
    return pl.pallas_call(
        functools.partial(
            backward_kernel, tuple(at for _, _, at in pieces), cells, 1 + len(prior) if finish else 0, len(mats)
        ),
        in_specs=[VMEM] * len(operands),
        out_specs=[HBM, HBM] if finish else [VMEM, VMEM],
        out_shape=[pltpu.HBM((SUB, slab, width), F32), pltpu.HBM(signal[1], F32)] if finish else [sums, sums],
        scratch_shapes=scratch,
        compiler_params=pltpu.CompilerParams(vmem_limit_bytes=16 * MIB),
        name="backward_last" if finish else "backward_first",
    )(*operands)


def body(concentration, shear_index, shear_weight, attenuation, yields, line_energy, measured):
    elements, _, slab, width = concentration.shape
    views = shear_weight.shape[0]
    emissions = attenuation.shape[0] - 1
    groups = lax.axis_size("far")
    both = lax.axis_size("views") == 2
    cells = float(slab * groups * NEAR)
    conc = concentration.reshape(elements, slab, width)
    scalars = (attenuation, line_energy, yields)

    def to_other(value):
        return lax.ppermute(value, "views", [(0, 1), (1, 0)])

    fillers = []

    def fill(after):
        if not both or len(fillers) == views:
            return ()
        fillers.append(forward_other(len(fillers), other_weight, mat, pads, const, after))
        return (fillers[-1][2],)

    u, n, const, target, mat, pads, weight, state, send = forward(
        conc, shear_index, shear_weight, scalars, measured, cells
    )
    def swap(value, axis, step):
        return lax.ppermute(value, axis, [(s, s ^ step) for s in range(lax.axis_size(axis))])

    states = [state, swap(send, "near", 1)]
    if both:
        other_weight = to_other(weight)
    tokens = ()
    levels = groups.bit_length() + 1

    def merge(level):
        (merged,) = call_small(
            functools.partial(merge_kernel, level), "merge", [state.shape], (const, *states[-2:])
        )
        return merged

    state = merge(0)
    pairs = [(s, s ^ 6) for s in range(groups * NEAR)]
    four = (state, lax.ppermute(state, ("far", "near"), pairs), swap(state, "far", 1), swap(state, "near", 2))
    pair, other, whole, beside = call_small(merge_four_kernel, "merge_four", [state.shape] * 4, (const, *four))
    states += [state, beside, pair, other]
    state = whole
    for level in range(3, levels):
        states += [state, swap(state, "far", 1 << (level - 2))]
        if level < levels - 1:
            state = merge(level)
    for _ in range(views):
        tokens += fill(state)
    half = ((views + 2) * SUB, width // 2)
    here, there, here_other, there_other = call_small(
        functools.partial(result_kernel, levels), "result", [half] * 4, (const, target, *states, *tokens)
    )
    there = swap(there, "near", 1)
    if both:
        pairs = [(v * NEAR + s, (1 - v) * NEAR + (s ^ 1)) for v in range(2) for s in range(NEAR)]
        here_other = to_other(here_other)
        there_other = lax.ppermute(there_other, ("views", "near"), pairs)
    package = (half[0], width)
    shapes = [package, target.shape]
    package, signal = call_small(assemble_kernel, "assemble", shapes, (target, here, there))
    own = [(u, n, v) for v in range(views)]
    signal = (signal, measured.shape)
    if both:
        sums = backward(package, const, weight, tokens[:1], own, cells, None, ())
        (other_package,) = call_small(
            assemble_other_kernel, "assemble_other", [package.shape], (here_other, there_other)
        )
        pieces = [(fillers[v][0], fillers[v][1], 0) for v in range(views)]
        gradient, signal = backward(other_package, const, other_weight, tokens[:1], pieces, cells, signal, sums)
    else:
        gradient, signal = backward(package, const, weight, (), own, cells, signal, ())
        gradient = lax.psum(gradient, "views")
    return gradient.reshape(concentration.shape), signal


def solution(mesh):
    views, depth = mesh.shape["views"], mesh.shape["depth"]
    devices = mesh.devices.reshape(views, depth // NEAR, NEAR)
    split = jax.sharding.Mesh(devices, ("views", "far", "near"))
    depths = ("far", "near")
    return jax.shard_map(
        body,
        mesh=split,
        in_specs=(
            P(None, None, depths, None),
            P("views", depths, None),
            P("views", depths, None),
            P(),
            P(),
            P(),
            P("views", None, None, None),
        ),
        out_specs=(P(None, None, depths, None), P("views", None, None, None)),
        check_vma=False,
    )
```
